32 devices in a mesh: scene: 2 (over y), queue: 4 (over z), tok: 2 (over x), cfg: 2 (over core).
Axes of the slice: x: 2, y: 2, z: 4, core: 2. Of those that a mesh axis runs over, the one named last changes fastest.
Arguments:
- latents: float32 [32, 16, 96], P(('scene', 'queue'), None, 'tok'), parts along dimension 0, may hold values from -6 to 6
- fresh_noise: float32 [32, 96], P(('scene', 'cfg'), 'tok'), parts along dimension 0, may hold values from -6 to 6
- levels: int32 [32], P(('scene', 'queue')), parts along dimension 0, may hold values from 0 to 15, as said below
- window_mask: int32 [32, 9], P(('scene', 'queue')), parts along dimension 0, may hold values from 0 to 1, as said below
- cond_embed: float32 [4, 1152], P(('scene', 'cfg')), parts along dimension 0, may hold values from -6 to 6
- level_mod: float32 [16, 3, 1152], replicated, may hold values from -3 to 3
- embed_weight: bfloat16 [16, 1152], replicated, may hold values from -1.5 to 1.5
- qkv_weight: bfloat16 [1152, 3, 1152], P(('queue', 'cfg'), None, 'tok'), may hold values from -0.1875 to 0.1875
- query_gain: float32 [72], replicated, may hold values from 0.25 to 1.75
- key_gain: float32 [72], replicated, may hold values from 0.25 to 1.75
- out_weight: bfloat16 [1152, 1152], P('tok', ('queue', 'cfg')), may hold values from -0.1875 to 0.1875
- final_gain: float32 [1152], replicated, may hold values from 0.5 to 1.5
- final_weight: bfloat16 [1152, 16], replicated, may hold values from -0.1875 to 0.1875
- guide_table: float32 [8], replicated, may hold values from 2 to 8
- guide_index: int32 [1], replicated, may hold values from 0 to 7
Outputs:
- velocity: float32 [32, 16, 96], P(('scene', 'queue'), 'cfg', 'tok'), parts along dimension 0
- new_queue: float32 [32, 16, 96], P(('scene', 'queue'), 'cfg', 'tok'), parts along dimension 0
The draws below stay inside these ranges and needn't reach their ends.
There are 2 independent parts, one for each index of `scene`. The reference program is written for one: setup_inputs(seed, part) draws one part's arguments, and reference() takes and returns one part's arrays. A program takes and returns all parts, laid end to end along the dimension named above; an argument that names none is the same for every part. Nothing has to cross between parts.
Inputs may be any that keep to these rules, and one draw needn't show every extreme that they name: levels[f] differs from 16 * f // 16 by at most one; the first frame has level 0 and the last 15. window_mask[f, o] = 1 lets frame f attend frame f + o - 4; window_mask[f, 4] = 1; entries whose frame lies outside 0 to 15 are 0.
All inputs are finite; a program needn't handle non-finite values.
Results may differ from the reference program's by a relative error of at most 0.0065.
Values may be sent and summed in bfloat16 or wider, within the bound.
No kernel may reach another device: no remote copies, remote signals or barrier semaphores. Data moves between devices by JAX's collectives and lax.ppermute only.
A program may use at most 64 MiB of HBM per device.

```python
import jax
import jax.numpy as jnp
from jax import lax

D = 1152
HEADS = 16
HD = 72
C = 16
G = 8
F = 16
S = 96
LEVELS = 16
WIN = 4
HEAD_GROUP = 576
N_TOK = 2


def draw_levels(key, part):
    frame_ids = jnp.arange(F, dtype=jnp.int32)
    jitter = jax.random.randint(key, (F,), -1, 2, dtype=jnp.int32)
    base = frame_ids * LEVELS // F
    result = jnp.clip(base + jitter, 0, LEVELS - 1)
    result = jnp.where(frame_ids == 0, 0, result)
    result = jnp.where(frame_ids == F - 1, LEVELS - 1, result)
    return result.astype(jnp.int32)


def draw_window_mask(key, part):
    span = 2 * WIN + 1
    picks = jax.random.randint(key, (F, span), 0, 4, dtype=jnp.int32)
    allowed = (picks != 0).astype(jnp.int32)
    offsets = jnp.arange(span, dtype=jnp.int32)[None, :] - WIN
    target = jnp.arange(F, dtype=jnp.int32)[:, None] + offsets
    inside = (target >= 0) & (target < F)
    result = jnp.where(offsets == 0, 1, jnp.where(inside, allowed, 0))
    return result.astype(jnp.int32)


def level_of(rng, shape, cuts, low, high):
    gain, own = 1.0, jax.random.fold_in(rng, 6)
    for dim, parts in cuts:
        draws = jnp.exp(jax.random.uniform(jax.random.fold_in(own, dim), (parts,), jnp.float32, low / len(cuts), high / len(cuts)))
        gain = gain * jnp.repeat(draws, shape[dim] // parts).reshape([-1 if axis == dim else 1 for axis in range(len(shape))])
    return gain


def normal_values(key, shape, scale, most, cuts=(), kind=jnp.bfloat16):
    array = scale * jax.random.normal(key, shape, jnp.float32)
    if cuts:
        array = array * level_of(key, shape, cuts, -0.22, 0.18)
    return jnp.clip(array, -most, most).astype(kind)


def setup_inputs(seed: int = 0, part: int = 0) -> dict:
    streams_of = jax.random.split(jax.random.key(seed), 16)
    part_keys = jax.random.split(jax.random.fold_in(streams_of[15], part), 16)
    return {
        "latents": normal_values(part_keys[0], (F, C, S), 1.0, 6.0, ((0, 4), (2, 2)), jnp.float32),
        "fresh_noise": normal_values(part_keys[1], (C, S), 1.0, 6.0, ((0, 2), (1, 2)), jnp.float32),
        "levels": draw_levels(jax.random.fold_in(jax.random.fold_in(streams_of[15], part), 71), part),
        "window_mask": draw_window_mask(jax.random.fold_in(jax.random.fold_in(streams_of[15], part), 71), part),
        "cond_embed": normal_values(part_keys[4], (2, D), 1.0, 6.0, ((0, 2),), jnp.float32),
        "level_mod": normal_values(streams_of[5], (LEVELS, 3, D), 0.5, 3.0, (), jnp.float32),
        "embed_weight": normal_values(streams_of[6], (C, D), C ** -0.5, 1.5),
        "qkv_weight": normal_values(streams_of[7], (D, 3, D), D ** -0.5, 0.1875, ((0, 8), (2, 2))),
        "query_gain": jnp.clip(1.0 + 0.15 * jax.random.normal(streams_of[8], (HD,), jnp.float32), 0.25, 1.75),
        "key_gain": jnp.clip(1.0 + 0.15 * jax.random.normal(streams_of[9], (HD,), jnp.float32), 0.25, 1.75),
        "out_weight": normal_values(streams_of[10], (D, D), D ** -0.5, 0.1875, ((0, 2), (1, 8))),
        "final_gain": jnp.clip(1.0 + 0.1 * jax.random.normal(streams_of[11], (D,), jnp.float32), 0.5, 1.5),
        "final_weight": normal_values(streams_of[12], (D, C), D ** -0.5, 0.1875),
        "guide_table": jnp.clip(jax.random.uniform(streams_of[13], (G,), jnp.float32, 2.0, 8.0), 2.0, 8.0),
        "guide_index": jax.random.randint(streams_of[14], (1,), 0, G).astype(jnp.int32),
    }


EPS_NORM = 1e-06
TIME_SHIFT = 3.0

def layer_norm(values):
    center = lax.optimization_barrier(jnp.mean(values, axis=-1, keepdims=True))
    deviate = values - center
    spread = lax.optimization_barrier(jnp.mean(deviate * deviate, axis=-1, keepdims=True))
    return deviate * lax.rsqrt(spread + EPS_NORM)

def rms_norm(values, scaling):
    return values * lax.rsqrt(lax.optimization_barrier(jnp.mean(values * values, axis=-1, keepdims=True)) + EPS_NORM) * scaling

def noise_sigma(fraction):
    return TIME_SHIFT * fraction / (1.0 + (TIME_SHIFT - 1.0) * fraction)

def temporal_attention(queries, key_rows, value_rows, window_mask, first_frame, total_frames, window):
    frames = queries.shape[0]
    numerator = jnp.zeros(queries.shape, jnp.float32)
    denominator = jnp.zeros(queries.shape[:-1], jnp.float32)
    for offset in range(2 * window + 1):
        near_keys = key_rows[offset:offset + frames].astype(jnp.float32)
        near_values = value_rows[offset:offset + frames].astype(jnp.float32)
        scores = lax.optimization_barrier(jnp.sum(queries * near_keys, axis=-1)) * queries.shape[-1] ** (-0.5)
        target = first_frame + jnp.arange(frames, dtype=jnp.int32) + (offset - window)
        allowed = (window_mask[:, offset] == 1) & (target >= 0) & (target < total_frames)
        weights = jnp.exp(scores) * allowed.astype(jnp.float32)[:, None, None]
        numerator = numerator + weights[..., None] * near_values
        denominator = denominator + weights
    return numerator / denominator[..., None]

def branch_velocity(latents, levels, window_mask, cond_row, level_mod, embed_weight, qkv_weight, query_gain, key_gain, out_weight, final_gain, final_weight):
    embedded = jnp.einsum('fcs,cd->fsd', latents.astype(jnp.bfloat16).astype(jnp.float32), embed_weight.astype(jnp.float32)) + cond_row
    one_hot = (levels[:, None] == jnp.arange(LEVELS, dtype=jnp.int32)[None, :]).astype(jnp.float32)
    modulate = jnp.dot(one_hot, level_mod.reshape(LEVELS, 3 * D), precision=lax.Precision.HIGHEST).reshape(F, 3, D)
    normed = (layer_norm(embedded) * (1.0 + modulate[:, None, 1]) + modulate[:, None, 0]).astype(jnp.bfloat16)
    projected = jnp.dot(normed.reshape(F * S, D), qkv_weight.reshape(D, 3 * D), preferred_element_type=jnp.float32).reshape(F, S, 3, HEADS, HD)
    queries = rms_norm(projected[:, :, 0], query_gain)
    key_rows = rms_norm(projected[:, :, 1], key_gain).astype(jnp.bfloat16)
    value_rows = projected[:, :, 2].astype(jnp.bfloat16)
    padding = ((WIN, WIN), (0, 0), (0, 0), (0, 0))
    attended = temporal_attention(queries, jnp.pad(key_rows, padding), jnp.pad(value_rows, padding), window_mask, jnp.int32(0), F, WIN)
    attended = attended.astype(jnp.bfloat16).reshape(F * S, D)
    mixed = jnp.zeros((F * S, D), jnp.float32)
    for group_index in range(N_TOK):
        lower_edge = group_index * HEAD_GROUP
        group_term = jnp.dot(attended[:, lower_edge:lower_edge + HEAD_GROUP], out_weight[lower_edge:lower_edge + HEAD_GROUP], preferred_element_type=jnp.float32)
        mixed = mixed + group_term.astype(jnp.bfloat16).astype(jnp.float32)
    summed = embedded + modulate[:, None, 2] * mixed.reshape(F, S, D)
    final_rows = (layer_norm(summed) * final_gain).astype(jnp.bfloat16)
    result = jnp.dot(final_rows.reshape(F * S, D), final_weight, preferred_element_type=jnp.float32)
    return result.reshape(F, S, C).transpose(0, 2, 1)

def reference(latents, fresh_noise, levels, window_mask, cond_embed, level_mod, embed_weight, qkv_weight, query_gain, key_gain, out_weight, final_gain, final_weight, guide_table, guide_index):
    cond_vel = branch_velocity(latents, levels, window_mask, cond_embed[0], level_mod, embed_weight, qkv_weight, query_gain, key_gain, out_weight, final_gain, final_weight)
    uncond_vel = branch_velocity(latents, levels, window_mask, cond_embed[1], level_mod, embed_weight, qkv_weight, query_gain, key_gain, out_weight, final_gain, final_weight)
    guidance = jnp.sum(guide_table * (jnp.arange(G, dtype=jnp.int32) == guide_index[0]).astype(jnp.float32))
    velocity = uncond_vel + guidance * (cond_vel - uncond_vel)
    current = noise_sigma((levels + 1).astype(jnp.float32) / LEVELS)
    upcoming = noise_sigma(levels.astype(jnp.float32) / LEVELS)
    updated = latents + (upcoming - current)[:, None, None] * velocity
    new_queue = jnp.concatenate([updated[1:], fresh_noise[None]], axis=0)
    return (velocity, new_queue)
```

```python
import functools

import jax
import jax.numpy as jnp
from jax import lax
from jax.experimental import pallas as pl
from jax.experimental.pallas import tpu as pltpu
from jax.sharding import PartitionSpec as P

EPS_NORM = 1e-06
TIME_SHIFT = 3.0
LANES = 128
VMEM_BYTES = 40 * 1024 * 1024
F32 = jnp.float32
BF16 = jnp.bfloat16


def noise_sigma(fraction):
    return TIME_SHIFT * fraction / (1.0 + (TIME_SHIFT - 1.0) * fraction)


def from_partner(value, axis, bit):
    return lax.ppermute(value, axis, [(i, i ^ 1 << bit) for i in range(lax.axis_size(axis))])


def with_halo(cells, sides, width):
    for axis, dim in sides:
        count = lax.axis_size(axis)
        ends = count - 1
        head = lax.slice_in_dim(cells, 0, width, axis=dim)
        tail = lax.slice_in_dim(cells, cells.shape[dim] - width, cells.shape[dim], axis=dim)
        cells = jnp.concatenate(
            [
                lax.ppermute(tail, axis, [(i, (i + 1) % count) for i in range(ends)]),
                cells,
                lax.ppermute(head, axis, [((i + 1) % count, i) for i in range(ends)]),
            ],
            axis=dim,
        )
    return cells


def shifted(value, axis, steps):
    count = lax.axis_size(axis)
    initial, last = (max(0, -steps), min(count, count - steps))
    return lax.ppermute(value, axis, [(source, source + steps) for source in range(initial, last)])


def layer_norm(values):
    center = jnp.mean(values, axis=-1, keepdims=True)
    deviate = values - center
    spread = jnp.mean(deviate * deviate, axis=-1, keepdims=True)
    return deviate * lax.rsqrt(spread + EPS_NORM)


def rms_norm(values, scaling):
    return (
        values * lax.rsqrt(jnp.mean(values * values, axis=-1, keepdims=True) + EPS_NORM) * scaling
    )


def temporal_attention(
    queries, key_rows, value_rows, window_mask, first_frame, total_frames, window
):
    frames = queries.shape[0]
    numerator = jnp.zeros(queries.shape, jnp.float32)
    denominator = jnp.zeros(queries.shape[:-1], jnp.float32)
    for offset in range(2 * window + 1):
        near_keys = key_rows[offset : offset + frames].astype(jnp.float32)
        near_values = value_rows[offset : offset + frames].astype(jnp.float32)
        scores = jnp.sum(queries * near_keys, axis=-1) * queries.shape[-1] ** (-0.5)
        target = first_frame + jnp.arange(frames, dtype=jnp.int32) + (offset - window)
        allowed = (window_mask[:, offset] == 1) & (target >= 0) & (target < total_frames)
        weights = jnp.exp(scores) * allowed.astype(jnp.float32)[:, None, None]
        numerator = numerator + weights[..., None] * near_values
        denominator = denominator + weights
    return numerator / denominator[..., None]


def on_device_general(
    latents,
    fresh_noise,
    levels,
    window_mask,
    cond_embed,
    level_mod,
    embed_weight,
    qkv_weight,
    query_gain,
    key_gain,
    out_weight,
    final_gain,
    final_weight,
    guide_table,
    guide_index,
):
    frames = latents.shape[0]
    tok_count = latents.shape[2]
    model_width = embed_weight.shape[1]
    head_dim = query_gain.shape[0]
    levels_all = level_mod.shape[0]
    queue_count = lax.axis_size("queue")
    all_tokens = lax.all_gather(latents, "tok", axis=2, tiled=True)
    seq_tokens = all_tokens.shape[2]
    row_count = frames * seq_tokens
    embedded = (
        jnp.einsum(
            "fcs,cd->fsd",
            all_tokens.astype(jnp.bfloat16),
            embed_weight,
            preferred_element_type=jnp.float32,
        )
        + cond_embed[0]
    )
    one_hot = (levels[:, None] == jnp.arange(levels_all, dtype=jnp.int32)[None, :]).astype(
        jnp.float32
    )
    modulate = jnp.dot(
        one_hot, level_mod.reshape(levels_all, 3 * model_width), precision=lax.Precision.HIGHEST
    ).reshape(frames, 3, model_width)
    normed = (layer_norm(embedded) * (1.0 + modulate[:, None, 1]) + modulate[:, None, 0]).astype(
        jnp.bfloat16
    )
    norm_rows = normed.reshape(row_count, model_width)
    local_cols = qkv_weight.shape[2]
    shard_piece = lax.all_gather(qkv_weight, ("queue", "cfg"), axis=0, tiled=True)
    flat_piece = shard_piece.reshape(shard_piece.shape[0], 3 * local_cols)
    projected = jnp.dot(norm_rows, flat_piece, preferred_element_type=jnp.float32)
    projected = projected.reshape(frames, seq_tokens, 3, local_cols // head_dim, head_dim)
    queries = rms_norm(projected[:, :, 0], query_gain)
    keys_values = jnp.stack(
        [
            rms_norm(projected[:, :, 1], key_gain).astype(jnp.bfloat16),
            projected[:, :, 2].astype(jnp.bfloat16),
        ]
    )
    window = window_mask.shape[1] // 2
    widened = with_halo(keys_values, (("queue", 1),), window)
    first_frame = lax.axis_index("queue") * frames
    attended = temporal_attention(
        queries, widened[0], widened[1], window_mask, first_frame, frames * queue_count, window
    )
    attended = attended.astype(jnp.bfloat16).reshape(frames, seq_tokens, local_cols)
    flat_heads = attended.reshape(row_count, local_cols)
    partial_value = jnp.dot(
        flat_heads,
        lax.all_gather(out_weight, ("queue", "cfg"), axis=1, tiled=True),
        preferred_element_type=jnp.float32,
    )
    mixed_out = lax.psum_scatter(
        partial_value.reshape(frames, seq_tokens, model_width).astype(jnp.bfloat16),
        "tok",
        scatter_dimension=1,
        tiled=True,
    ).astype(jnp.float32)
    own_start = lax.axis_index("tok") * tok_count
    own_embed = lax.dynamic_slice_in_dim(embedded, own_start, tok_count, 1)
    summed = own_embed + modulate[:, None, 2] * mixed_out
    final_rows = (layer_norm(summed) * final_gain).astype(jnp.bfloat16)
    velocity = jnp.einsum(
        "ftd,dc->fct", final_rows, final_weight, preferred_element_type=jnp.float32
    )
    half_values = velocity.shape[1] // 2
    branch_index = lax.axis_index("cfg")
    own_first = branch_index * half_values
    other_first = (1 - branch_index) * half_values
    outgoing = lax.dynamic_slice_in_dim(velocity, other_first, half_values, 1)
    partner = from_partner(outgoing, "cfg", 0)
    mine = lax.dynamic_slice_in_dim(velocity, own_first, half_values, 1)
    is_cond = branch_index == 0
    cond_vel = jnp.where(is_cond, mine, partner)
    uncond_vel = jnp.where(is_cond, partner, mine)
    entries = guide_table.shape[0]
    guidance = jnp.sum(
        guide_table * (jnp.arange(entries, dtype=jnp.int32) == guide_index[0]).astype(jnp.float32)
    )
    guided = uncond_vel + guidance * (cond_vel - uncond_vel)
    current = noise_sigma((levels + 1).astype(jnp.float32) / levels_all)
    upcoming = noise_sigma(levels.astype(jnp.float32) / levels_all)
    own_latents = lax.dynamic_slice_in_dim(latents, own_first, half_values, 1)
    updated = own_latents + (upcoming - current)[:, None, None] * guided
    incoming = shifted(updated[:1], "queue", -1)
    is_last = lax.axis_index("queue") == queue_count - 1
    incoming = jnp.where(is_last, fresh_noise[None], incoming)
    new_queue = jnp.concatenate([updated[1:], incoming], axis=0)
    return (guided, new_queue)


def kernel_call(body, out_shapes, spaces, scratch=(), **cost):
    kinds = {"v": pltpu.VMEM, "s": pltpu.SMEM}
    many = isinstance(out_shapes, (list, tuple))
    return pl.pallas_call(
        body,
        out_shape=out_shapes,
        in_specs=[pl.BlockSpec(memory_space=kinds[k]) for k in spaces],
        out_specs=[pl.BlockSpec(memory_space=pltpu.VMEM) for _ in out_shapes]
        if many
        else pl.BlockSpec(memory_space=pltpu.VMEM),
        scratch_shapes=list(scratch),
        compiler_params=pltpu.CompilerParams(vmem_limit_bytes=VMEM_BYTES),
        cost_estimate=pl.CostEstimate(
            flops=cost.get("flops", 1000000),
            bytes_accessed=cost.get("bytes_accessed", 1000000),
            transcendentals=0,
        ),
    )


def split_terms(values, terms):
    parts = []
    for _ in range(terms):
        part = values.astype(BF16)
        parts.append(part)
        values = values - part.astype(F32)
    return parts


def dot_tn(left, right):
    return lax.dot_general(
        left, right, (((0,), (0,)), ((), ())), preferred_element_type=F32
    )


def pack_kernel(head_dim, latents, levels, window_mask, qkv, chunks, packed):
    for h in range(chunks.shape[0]):
        first = h * head_dim
        chunks[h] = jnp.concatenate(
            [qkv[part, :, first : first + head_dim] for part in range(3)], axis=1
        )
    frames, values, tokens = latents.shape
    span = window_mask.shape[1]
    pieces = []
    for f in range(frames):
        rows = [latents[f]]
        side = jnp.zeros((packed.shape[0] - values, tokens), F32)
        row_id = lax.broadcasted_iota(jnp.int32, side.shape, 0)
        for o in range(span):
            side = jnp.where(row_id == o, window_mask[f, o].astype(F32), side)
        side = jnp.where(row_id == span, levels[f].astype(F32), side)
        rows.append(side)
        pieces.append(jnp.concatenate(rows, axis=0))
    packed[...] = jnp.concatenate(pieces, axis=1)


def prepare_kernel(
    frames, values, span, gathered, cond, level_mod, embed, lhs, xin, rstd_out, mask_out
):
    width = embed.shape[1]
    rows = xin.shape[1]
    queue_tok = gathered.shape[0]
    branches = cond.shape[0]
    all_frames = xin.shape[0]
    toks = queue_tok * frames // all_frames
    tokens = gathered.shape[2] // frames
    weights = embed[...].astype(F32)
    weights = weights - jnp.mean(weights, axis=1, keepdims=True)
    conds = cond[...]
    conds = conds - jnp.mean(conds, axis=1, keepdims=True)
    basis = jnp.concatenate(
        [weights, conds, jnp.zeros((rows - values - branches, width), F32)], axis=0
    )
    gram = lax.dot_general(
        basis,
        basis,
        (((1,), (1,)), ((), ())),
        preferred_element_type=F32,
        precision=lax.Precision.HIGHEST,
    ) * (1.0 / width)
    row_id = lax.broadcasted_iota(jnp.int32, (rows, LANES), 0)
    wide_id = lax.broadcasted_iota(jnp.int32, (rows, width), 0)
    level_id = lax.broadcasted_iota(jnp.int32, (level_mod.shape[1], width), 0).astype(F32)
    shift_row = values + branches
    fill = LANES - toks * tokens
    for f in range(all_frames):
        q, part = divmod(f, frames)
        info = [
            gathered[q * toks + t, :, part * tokens : (part + 1) * tokens] for t in range(toks)
        ]
        level = info[0][values + span : values + span + 1, 0:1]
        chosen = level_id == level
        shift = jnp.sum(jnp.where(chosen, level_mod[0], 0.0), axis=0, keepdims=True)
        scale = jnp.sum(jnp.where(chosen, level_mod[1], 0.0), axis=0, keepdims=True)
        block = basis * (1.0 + scale)
        block = jnp.where((wide_id == shift_row) | (wide_id == shift_row + 1), shift, block)
        lhs[f * rows : (f + 1) * rows, :] = block.astype(BF16)
        info = jnp.concatenate(info + [jnp.ones((info[0].shape[0], fill), F32)], axis=1)
        mask_out[f] = info[values : values + mask_out.shape[1]]
        base = jnp.where(row_id < values, info[:rows], 0.0).astype(BF16).astype(F32)
        for b in range(branches):
            vec = jnp.where(row_id == values + b, 1.0, base)
            spread = jnp.sum(
                vec
                * jnp.dot(gram, vec, preferred_element_type=F32, precision=lax.Precision.HIGHEST),
                axis=0,
                keepdims=True,
            )
            spread = jnp.maximum(spread, 0.0) + EPS_NORM
            rstd = lax.rsqrt(spread)
            std = spread * rstd
            high = std.astype(BF16).astype(F32)
            vec = jnp.where(row_id == shift_row, high, vec)
            vec = jnp.where(row_id == shift_row + 1, std - high, vec)
            xin[f, :, b * LANES : (b + 1) * LANES] = vec.astype(BF16)
            rstd_out[f, :, b * LANES : (b + 1) * LANES] = rstd


def attend_kernel(
    frames, tokens, weight, lhs, xin, rstd_in, mask_in, gain_q, gain_k, out, proj, kfac, vfac, att
):
    all_frames, rows, lanes = xin.shape
    head_dim = gain_q.shape[0]
    window = (proj.shape[0] - all_frames) // 2
    span = 2 * window + 1
    branches = lanes // LANES
    folded = jnp.dot(lhs[...], weight[...], preferred_element_type=F32)
    high, low = split_terms(folded, 2)
    gains = gain_q[...] * gain_k[...] * head_dim ** (-0.5)
    gains = jnp.broadcast_to(gains, (head_dim, LANES))
    for side in range(window):
        for at in (side, all_frames + window + side):
            proj[at] = jnp.zeros(proj.shape[1:], F32)
            kfac[at] = jnp.zeros(kfac.shape[1:], F32)
            vfac[at] = jnp.zeros(vfac.shape[1:], F32)
    for f in range(all_frames):
        piece = slice(f * rows, (f + 1) * rows)
        made = dot_tn(high[piece], xin[f]) + dot_tn(low[piece], xin[f])
        proj[f + window] = made
        rstd = rstd_in[f]
        keys = made[head_dim : 2 * head_dim]
        square = jnp.mean(keys * keys, axis=0, keepdims=True)
        kfac[f + window] = rstd * lax.rsqrt(rstd * rstd * square + EPS_NORM)
        vfac[f + window] = rstd

    def one_frame(f, carry):
        for b in range(branches):
            lane = slice(b * LANES, (b + 1) * LANES)
            query = proj[f + window, 0:head_dim, lane]
            rstd = vfac[f + window, :, lane]
            square = jnp.mean(query * query, axis=0, keepdims=True)
            qfac = rstd * lax.rsqrt(rstd * rstd * square + EPS_NORM)
            query = query * gains
            total = jnp.zeros((head_dim, LANES), F32)
            norm = jnp.zeros((1, LANES), F32)
            for o in range(span):
                keys = proj[f + o, head_dim : 2 * head_dim, lane]
                score = jnp.sum(query * keys, axis=0, keepdims=True)
                score = score * (qfac * kfac[f + o, :, lane])
                part = jnp.exp(score) * mask_in[f, o : o + 1, :]
                norm = norm + part
                total = total + (part * vfac[f + o, :, lane]) * proj[f + o, 2 * head_dim :, lane]
            att[f, b] = total / norm
        return carry

    lax.fori_loop(0, all_frames, one_frame, 0)
    toks = out.shape[0] * frames // (all_frames * branches)
    queues = all_frames // frames
    for t in range(toks):
        for q in range(queues):
            for b in range(branches):
                pieces = [
                    att[min(q * frames + i, all_frames - 1), b, :, t * tokens : (t + 1) * tokens]
                    for i in range(frames + 1)
                ]
                at = (t * queues + q) * branches + b
                out[at] = jnp.concatenate(pieces, axis=1).astype(BF16)


def rows_kernel(
    values, span, packed, following, cond, level_mod, embed, final_gain, emb_out, gate_out, gain_out
):
    levels_all, width = level_mod.shape
    info = jnp.concatenate([packed[...], following[...]], axis=1)
    lanes = info.shape[1]
    vec = info[:values].astype(BF16)
    ones = jnp.ones((16, lanes), BF16)
    zero = jnp.zeros((13, width), BF16)
    weights = jnp.concatenate([embed[...]] + split_terms(cond[...], 3) + [zero], axis=0)
    emb_out[...] = dot_tn(weights, jnp.concatenate([vec, ones], axis=0))
    level = info[values + span : values + span + 1]
    one_hot = (lax.broadcasted_iota(jnp.int32, (levels_all, lanes), 0).astype(F32) == level).astype(
        F32
    ).astype(BF16)
    gates = jnp.concatenate(split_terms(level_mod[...], 3), axis=0)
    gate_out[...] = dot_tn(gates, jnp.concatenate([one_hot] * 3, axis=0))
    gains = jnp.concatenate(split_terms(final_gain[...], 3) + [zero], axis=0)
    gain_out[...] = dot_tn(gains, ones)


def finish_kernel(half, attended, out_w, emb, gate, gain, final_w, branch, mine, send, scratch):
    group = out_w.shape[2]
    mixed = jnp.zeros(emb.shape, F32)
    for g in range(out_w.shape[0]):
        made = jnp.dot(
            out_w[g], attended[g * group : (g + 1) * group, :], preferred_element_type=F32
        )
        mixed = mixed + made.astype(BF16).astype(F32)
    summed = emb[...] + gate[...] * mixed
    center = jnp.mean(summed, axis=0, keepdims=True)
    deviate = summed - center
    spread = jnp.mean(deviate * deviate, axis=0, keepdims=True)
    final = (deviate * lax.rsqrt(spread + EPS_NORM) * gain[...]).astype(BF16)
    scratch[...] = jnp.dot(final_w[...], final, preferred_element_type=F32)
    own = pl.multiple_of(branch[0] * half, half)
    other = pl.multiple_of((1 - branch[0]) * half, half)
    mine[...] = scratch[pl.ds(own, half), :]
    send[...] = scratch[pl.ds(other, half), :]


def update_kernel(
    values, span, levels_all, mine, partner, packed, following, noise, table, index, place, vel, new
):
    half = mine.shape[0]
    frames, _, tokens = vel.shape
    is_cond = place[0] == 0
    own = pl.multiple_of(place[0] * half, half)
    here, there = mine[...], partner[...]
    cond = jnp.where(is_cond, here, there)
    uncond = jnp.where(is_cond, there, here)
    guided = uncond + table[index[0]] * (cond - uncond)
    level = jnp.concatenate(
        [packed[values + span : values + span + 1], following[values + span : values + span + 1]],
        axis=1,
    )
    current = noise_sigma((level + 1.0) / levels_all)
    upcoming = noise_sigma(level / levels_all)
    latents = jnp.concatenate([packed[pl.ds(own, half), :], following[pl.ds(own, half), :]], axis=1)
    updated = latents + (upcoming - current) * guided
    is_last = place[1] == 1
    for f in range(frames):
        vel[f] = guided[:, f * tokens : (f + 1) * tokens]
        moved = updated[:, (f + 1) * tokens : (f + 2) * tokens]
        if f == frames - 1:
            moved = jnp.where(is_last, noise[...], moved)
        new[f] = moved


def on_device_heads(
    latents,
    fresh_noise,
    levels,
    window_mask,
    cond_embed,
    level_mod,
    embed_weight,
    qkv_weight,
    query_gain,
    key_gain,
    out_weight,
    final_gain,
    final_weight,
    guide_table,
    guide_index,
):
    frames, values, tokens = latents.shape
    width = embed_weight.shape[1]
    head_dim = query_gain.shape[0]
    levels_all = level_mod.shape[0]
    span = window_mask.shape[1]
    window = span // 2
    queues, toks, branches = (lax.axis_size(a) for a in ("queue", "tok", "cfg"))
    group = queues * branches
    q_at, branch = lax.axis_index("queue"), lax.axis_index("cfg")
    all_frames = queues * frames
    rows = -(-max(values + 4, values + span + 1) // 16) * 16
    local_rows = qkv_weight.shape[0]
    lanes = branches * LANES
    row_lanes = (frames + 1) * tokens

    chunks, packed = kernel_call(
        functools.partial(pack_kernel, head_dim),
        [
            jax.ShapeDtypeStruct((group, local_rows, 3 * head_dim), BF16),
            jax.ShapeDtypeStruct((rows, frames * tokens), F32),
        ],
        "vssv",
    )(latents, levels, window_mask, jnp.transpose(qkv_weight, (1, 0, 2)))
    gathered = lax.all_gather(packed, ("queue", "tok"), axis=0)
    cond_other = from_partner(cond_embed, "cfg", 0)
    weight = lax.all_to_all(chunks, ("queue", "cfg"), 0, 0).reshape(width, 3 * head_dim)
    out_all = lax.all_gather(out_weight.T, ("tok", "queue", "cfg"), axis=0)
    out_all = out_all.reshape(toks, width, out_weight.shape[0])

    conds = jnp.where(
        branch == 0,
        jnp.concatenate([cond_embed, cond_other], axis=0),
        jnp.concatenate([cond_other, cond_embed], axis=0),
    )
    mods = jnp.transpose(level_mod, (1, 0, 2))
    lhs, xin, rstd, masks = kernel_call(
        functools.partial(prepare_kernel, frames, values, span),
        [
            jax.ShapeDtypeStruct((all_frames * rows, width), BF16),
            jax.ShapeDtypeStruct((all_frames, rows, lanes), BF16),
            jax.ShapeDtypeStruct((all_frames, 1, lanes), F32),
            jax.ShapeDtypeStruct((all_frames, rows - values, LANES), F32),
        ],
        "vvvv",
    )(gathered, conds, mods, embed_weight)
    attended = kernel_call(
        functools.partial(attend_kernel, frames, tokens),
        jax.ShapeDtypeStruct((toks * group, head_dim, row_lanes), BF16),
        "vvvvvvv",
        [
            pltpu.VMEM((all_frames + 2 * window, 3 * head_dim, lanes), F32),
            pltpu.VMEM((all_frames + 2 * window, 1, lanes), F32),
            pltpu.VMEM((all_frames + 2 * window, 1, lanes), F32),
            pltpu.VMEM((all_frames, branches, head_dim, LANES), F32),
        ],
    )(weight, lhs, xin, rstd, masks, query_gain[:, None], key_gain[:, None])
    received = lax.all_to_all(attended, ("tok", "queue", "cfg"), 0, 0).reshape(width, row_lanes)

    following = lax.dynamic_index_in_dim(
        gathered,
        jnp.minimum(q_at + 1, queues - 1) * toks + lax.axis_index("tok"),
        0,
        keepdims=False,
    )[:, :tokens]
    wide = jax.ShapeDtypeStruct((width, row_lanes), F32)
    emb, gate, gain = kernel_call(
        functools.partial(rows_kernel, values, span), [wide, wide, wide], "vvvvvv"
    )(packed, following, cond_embed, mods[2], embed_weight, final_gain[None])
    half = values // 2
    half_shape = jax.ShapeDtypeStruct((half, row_lanes), F32)
    mine, send = kernel_call(
        functools.partial(finish_kernel, half),
        [half_shape, half_shape],
        "vvvvvvs",
        [pltpu.VMEM((values, row_lanes), F32)],
    )(received, out_all, emb, gate, gain, final_weight.T, branch[None])
    partner = from_partner(send, "cfg", 0)
    place = jnp.stack([branch, (q_at == queues - 1).astype(jnp.int32)])
    shape = jax.ShapeDtypeStruct((frames, half, tokens), F32)
    return kernel_call(
        functools.partial(update_kernel, values, span, levels_all),
        [shape, shape],
        "vvvvvsss",
    )(mine, partner, packed, following, fresh_noise, guide_table, guide_index, place)


def on_device(*args):
    latents, qkv_weight, query_gain = args[0], args[7], args[8]
    local_heads = qkv_weight.shape[2] // query_gain.shape[0]
    one_head_each = local_heads == lax.axis_size("queue") * lax.axis_size("cfg")
    fits = latents.shape[2] * lax.axis_size("tok") <= LANES
    if one_head_each and fits:
        return tuple(on_device_heads(*args))
    return on_device_general(*args)


def solution(mesh):
    placed = (
        P(("scene", "queue"), None, "tok"),
        P(("scene", "cfg"), "tok"),
        P(("scene", "queue")),
        P(("scene", "queue"), None),
        P(("scene", "cfg"), None),
        P(),
        P(),
        P(("queue", "cfg"), None, "tok"),
        P(),
        P(),
        P("tok", ("queue", "cfg")),
        P(),
        P(),
        P(),
        P(),
    )
    return jax.shard_map(
        on_device,
        mesh=mesh,
        in_specs=placed,
        out_specs=(P(("scene", "queue"), "cfg", "tok"), P(("scene", "queue"), "cfg", "tok")),
        check_vma=False,
    )
```

```python
import functools

import jax
import jax.numpy as jnp
from jax import lax
from jax.experimental import pallas as pl
from jax.experimental.pallas import tpu as pltpu
from jax.sharding import PartitionSpec as P

EPS_NORM = 1e-06
TIME_SHIFT = 3.0
LANES = 128
VMEM_BYTES = 40 * 1024 * 1024
WHOLE_VMEM = 62 * 1024 * 1024
F32 = jnp.float32
BF16 = jnp.bfloat16


def noise_sigma(fraction):
    return TIME_SHIFT * fraction / (1.0 + (TIME_SHIFT - 1.0) * fraction)


def from_partner(value, axis, bit):
    return lax.ppermute(value, axis, [(i, i ^ 1 << bit) for i in range(lax.axis_size(axis))])


def with_halo(cells, sides, width):
    for axis, dim in sides:
        count = lax.axis_size(axis)
        ends = count - 1
        head = lax.slice_in_dim(cells, 0, width, axis=dim)
        tail = lax.slice_in_dim(cells, cells.shape[dim] - width, cells.shape[dim], axis=dim)
        cells = jnp.concatenate(
            [
                lax.ppermute(tail, axis, [(i, (i + 1) % count) for i in range(ends)]),
                cells,
                lax.ppermute(head, axis, [((i + 1) % count, i) for i in range(ends)]),
            ],
            axis=dim,
        )
    return cells


def shifted(value, axis, steps):
    count = lax.axis_size(axis)
    initial, last = (max(0, -steps), min(count, count - steps))
    return lax.ppermute(value, axis, [(source, source + steps) for source in range(initial, last)])


def layer_norm(values):
    center = jnp.mean(values, axis=-1, keepdims=True)
    deviate = values - center
    spread = jnp.mean(deviate * deviate, axis=-1, keepdims=True)
    return deviate * lax.rsqrt(spread + EPS_NORM)


def rms_norm(values, scaling):
    return (
        values * lax.rsqrt(jnp.mean(values * values, axis=-1, keepdims=True) + EPS_NORM) * scaling
    )


def temporal_attention(
    queries, key_rows, value_rows, window_mask, first_frame, total_frames, window
):
    frames = queries.shape[0]
    numerator = jnp.zeros(queries.shape, jnp.float32)
    denominator = jnp.zeros(queries.shape[:-1], jnp.float32)
    for offset in range(2 * window + 1):
        near_keys = key_rows[offset : offset + frames].astype(jnp.float32)
        near_values = value_rows[offset : offset + frames].astype(jnp.float32)
        scores = jnp.sum(queries * near_keys, axis=-1) * queries.shape[-1] ** (-0.5)
        target = first_frame + jnp.arange(frames, dtype=jnp.int32) + (offset - window)
        allowed = (window_mask[:, offset] == 1) & (target >= 0) & (target < total_frames)
        weights = jnp.exp(scores) * allowed.astype(jnp.float32)[:, None, None]
        numerator = numerator + weights[..., None] * near_values
        denominator = denominator + weights
    return numerator / denominator[..., None]


def on_device_general(
    latents,
    fresh_noise,
    levels,
    window_mask,
    cond_embed,
    level_mod,
    embed_weight,
    qkv_weight,
    query_gain,
    key_gain,
    out_weight,
    final_gain,
    final_weight,
    guide_table,
    guide_index,
):
    frames = latents.shape[0]
    tok_count = latents.shape[2]
    model_width = embed_weight.shape[1]
    head_dim = query_gain.shape[0]
    levels_all = level_mod.shape[0]
    queue_count = lax.axis_size("queue")
    all_tokens = lax.all_gather(latents, "tok", axis=2, tiled=True)
    seq_tokens = all_tokens.shape[2]
    row_count = frames * seq_tokens
    embedded = (
        jnp.einsum(
            "fcs,cd->fsd",
            all_tokens.astype(jnp.bfloat16),
            embed_weight,
            preferred_element_type=jnp.float32,
        )
        + cond_embed[0]
    )
    one_hot = (levels[:, None] == jnp.arange(levels_all, dtype=jnp.int32)[None, :]).astype(
        jnp.float32
    )
    modulate = jnp.dot(
        one_hot, level_mod.reshape(levels_all, 3 * model_width), precision=lax.Precision.HIGHEST
    ).reshape(frames, 3, model_width)
    normed = (layer_norm(embedded) * (1.0 + modulate[:, None, 1]) + modulate[:, None, 0]).astype(
        jnp.bfloat16
    )
    norm_rows = normed.reshape(row_count, model_width)
    local_cols = qkv_weight.shape[2]
    shard_piece = lax.all_gather(qkv_weight, ("queue", "cfg"), axis=0, tiled=True)
    flat_piece = shard_piece.reshape(shard_piece.shape[0], 3 * local_cols)
    projected = jnp.dot(norm_rows, flat_piece, preferred_element_type=jnp.float32)
    projected = projected.reshape(frames, seq_tokens, 3, local_cols // head_dim, head_dim)
    queries = rms_norm(projected[:, :, 0], query_gain)
    keys_values = jnp.stack(
        [
            rms_norm(projected[:, :, 1], key_gain).astype(jnp.bfloat16),
            projected[:, :, 2].astype(jnp.bfloat16),
        ]
    )
    window = window_mask.shape[1] // 2
    widened = with_halo(keys_values, (("queue", 1),), window)
    first_frame = lax.axis_index("queue") * frames
    attended = temporal_attention(
        queries, widened[0], widened[1], window_mask, first_frame, frames * queue_count, window
    )
    attended = attended.astype(jnp.bfloat16).reshape(frames, seq_tokens, local_cols)
    flat_heads = attended.reshape(row_count, local_cols)
    partial_value = jnp.dot(
        flat_heads,
        lax.all_gather(out_weight, ("queue", "cfg"), axis=1, tiled=True),
        preferred_element_type=jnp.float32,
    )
    mixed_out = lax.psum_scatter(
        partial_value.reshape(frames, seq_tokens, model_width).astype(jnp.bfloat16),
        "tok",
        scatter_dimension=1,
        tiled=True,
    ).astype(jnp.float32)
    own_start = lax.axis_index("tok") * tok_count
    own_embed = lax.dynamic_slice_in_dim(embedded, own_start, tok_count, 1)
    summed = own_embed + modulate[:, None, 2] * mixed_out
    final_rows = (layer_norm(summed) * final_gain).astype(jnp.bfloat16)
    velocity = jnp.einsum(
        "ftd,dc->fct", final_rows, final_weight, preferred_element_type=jnp.float32
    )
    half_values = velocity.shape[1] // 2
    branch_index = lax.axis_index("cfg")
    own_first = branch_index * half_values
    other_first = (1 - branch_index) * half_values
    outgoing = lax.dynamic_slice_in_dim(velocity, other_first, half_values, 1)
    partner = from_partner(outgoing, "cfg", 0)
    mine = lax.dynamic_slice_in_dim(velocity, own_first, half_values, 1)
    is_cond = branch_index == 0
    cond_vel = jnp.where(is_cond, mine, partner)
    uncond_vel = jnp.where(is_cond, partner, mine)
    entries = guide_table.shape[0]
    guidance = jnp.sum(
        guide_table * (jnp.arange(entries, dtype=jnp.int32) == guide_index[0]).astype(jnp.float32)
    )
    guided = uncond_vel + guidance * (cond_vel - uncond_vel)
    current = noise_sigma((levels + 1).astype(jnp.float32) / levels_all)
    upcoming = noise_sigma(levels.astype(jnp.float32) / levels_all)
    own_latents = lax.dynamic_slice_in_dim(latents, own_first, half_values, 1)
    updated = own_latents + (upcoming - current)[:, None, None] * guided
    incoming = shifted(updated[:1], "queue", -1)
    is_last = lax.axis_index("queue") == queue_count - 1
    incoming = jnp.where(is_last, fresh_noise[None], incoming)
    new_queue = jnp.concatenate([updated[1:], incoming], axis=0)
    return (guided, new_queue)


def kernel_call(body, out_shapes, spaces, scratch=(), vmem=VMEM_BYTES, **cost):
    kinds = {"v": pl.BlockSpec(), "s": pl.BlockSpec(memory_space=pltpu.SMEM)}
    many = isinstance(out_shapes, (list, tuple))
    return pl.pallas_call(
        body,
        out_shape=out_shapes,
        in_specs=[kinds[k] for k in spaces],
        out_specs=[pl.BlockSpec() for _ in out_shapes] if many else pl.BlockSpec(),
        scratch_shapes=list(scratch),
        compiler_params=pltpu.CompilerParams(vmem_limit_bytes=vmem),
        cost_estimate=pl.CostEstimate(
            flops=cost.get("flops", 1000000),
            bytes_accessed=cost.get("bytes_accessed", 1000000),
            transcendentals=0,
        ),
    )


def split_terms(values, terms):
    parts = []
    for _ in range(terms):
        part = values.astype(BF16)
        parts.append(part)
        values = values - part.astype(F32)
    return parts


def dot_tn(left, right):
    return lax.dot_general(
        left, right, (((0,), (0,)), ((), ())), preferred_element_type=F32
    )


def pack_kernel(head_dim, latents, levels, window_mask, qkv, chunks, packed):
    for h in range(chunks.shape[0]):
        first = h * head_dim
        chunks[h] = jnp.concatenate(
            [qkv[part, :, first : first + head_dim] for part in range(3)], axis=1
        )
    frames, values, tokens = latents.shape
    span = window_mask.shape[1]
    pieces = []
    for f in range(frames):
        rows = [latents[f]]
        side = jnp.zeros((packed.shape[0] - values, tokens), F32)
        row_id = lax.broadcasted_iota(jnp.int32, side.shape, 0)
        for o in range(span):
            side = jnp.where(row_id == o, window_mask[f : f + 1, o : o + 1].astype(F32), side)
        side = jnp.where(row_id == span, levels[:, f : f + 1].astype(F32), side)
        rows.append(side)
        pieces.append(jnp.concatenate(rows, axis=0))
    packed[...] = jnp.concatenate(pieces, axis=1)


def prepare_kernel(
    frames, values, span, gathered, cond, level_mod, embed, lhs, xin, rstd_out, mask_out
):
    width = embed.shape[1]
    rows = xin.shape[1]
    queue_tok = gathered.shape[0]
    branches = cond.shape[0]
    all_frames = xin.shape[0]
    toks = queue_tok * frames // all_frames
    tokens = gathered.shape[2] // frames
    weights = embed[...].astype(F32)
    weights = weights - jnp.mean(weights, axis=1, keepdims=True)
    conds = cond[...]
    conds = conds - jnp.mean(conds, axis=1, keepdims=True)
    basis = jnp.concatenate(
        [weights, conds, jnp.zeros((rows - values - branches, width), F32)], axis=0
    )
    gram = lax.dot_general(
        basis,
        basis,
        (((1,), (1,)), ((), ())),
        preferred_element_type=F32,
        precision=lax.Precision.HIGHEST,
    ) * (1.0 / width)
    row_id = lax.broadcasted_iota(jnp.int32, (rows, LANES), 0)
    wide_id = lax.broadcasted_iota(jnp.int32, (rows, width), 0)
    level_id = lax.broadcasted_iota(jnp.int32, (level_mod.shape[1], width), 0).astype(F32)
    shift_row = values + branches
    fill = LANES - toks * tokens
    for f in range(all_frames):
        q, part = divmod(f, frames)
        info = [
            gathered[q * toks + t, :, part * tokens : (part + 1) * tokens] for t in range(toks)
        ]
        level = info[0][values + span : values + span + 1, 0:1]
        chosen = level_id == level
        shift = jnp.sum(jnp.where(chosen, level_mod[0], 0.0), axis=0, keepdims=True)
        scale = jnp.sum(jnp.where(chosen, level_mod[1], 0.0), axis=0, keepdims=True)
        block = basis * (1.0 + scale)
        block = jnp.where((wide_id == shift_row) | (wide_id == shift_row + 1), shift, block)
        lhs[f * rows : (f + 1) * rows, :] = block.astype(BF16)
        info = jnp.concatenate(info + [jnp.ones((info[0].shape[0], fill), F32)], axis=1)
        mask_out[f] = info[values : values + mask_out.shape[1]]
        base = jnp.where(row_id < values, info[:rows], 0.0).astype(BF16).astype(F32)
        for b in range(branches):
            vec = jnp.where(row_id == values + b, 1.0, base)
            spread = jnp.sum(
                vec
                * jnp.dot(gram, vec, preferred_element_type=F32, precision=lax.Precision.HIGHEST),
                axis=0,
                keepdims=True,
            )
            spread = jnp.maximum(spread, 0.0) + EPS_NORM
            rstd = lax.rsqrt(spread)
            std = spread * rstd
            high = std.astype(BF16).astype(F32)
            vec = jnp.where(row_id == shift_row, high, vec)
            vec = jnp.where(row_id == shift_row + 1, std - high, vec)
            xin[f, :, b * LANES : (b + 1) * LANES] = vec.astype(BF16)
            rstd_out[f, :, b * LANES : (b + 1) * LANES] = rstd


def attend_kernel(
    frames, tokens, weight, lhs, xin, rstd_in, mask_in, gain_q, gain_k, out, proj, kfac, vfac, att
):
    all_frames, rows, lanes = xin.shape
    head_dim = gain_q.shape[0]
    window = (proj.shape[0] - all_frames) // 2
    span = 2 * window + 1
    branches = lanes // LANES
    folded = jnp.dot(lhs[...], weight[...], preferred_element_type=F32)
    high, low = split_terms(folded, 2)
    gains = gain_q[...] * gain_k[...] * head_dim ** (-0.5)
    gains = jnp.broadcast_to(gains, (head_dim, LANES))
    for side in range(window):
        for at in (side, all_frames + window + side):
            proj[at] = jnp.zeros(proj.shape[1:], F32)
            kfac[at] = jnp.zeros(kfac.shape[1:], F32)
            vfac[at] = jnp.zeros(vfac.shape[1:], F32)
    for f in range(all_frames):
        piece = slice(f * rows, (f + 1) * rows)
        made = dot_tn(high[piece], xin[f]) + dot_tn(low[piece], xin[f])
        proj[f + window] = made
        rstd = rstd_in[f]
        keys = made[head_dim : 2 * head_dim]
        square = jnp.mean(keys * keys, axis=0, keepdims=True)
        kfac[f + window] = rstd * lax.rsqrt(rstd * rstd * square + EPS_NORM)
        vfac[f + window] = rstd

    def one_frame(f, carry):
        for b in range(branches):
            lane = slice(b * LANES, (b + 1) * LANES)
            query = proj[f + window, 0:head_dim, lane]
            rstd = vfac[f + window, :, lane]
            square = jnp.mean(query * query, axis=0, keepdims=True)
            qfac = rstd * lax.rsqrt(rstd * rstd * square + EPS_NORM)
            query = query * gains
            total = jnp.zeros((head_dim, LANES), F32)
            norm = jnp.zeros((1, LANES), F32)
            for o in range(span):
                keys = proj[f + o, head_dim : 2 * head_dim, lane]
                score = jnp.sum(query * keys, axis=0, keepdims=True)
                score = score * (qfac * kfac[f + o, :, lane])
                part = jnp.exp(score) * mask_in[f, o : o + 1, :]
                norm = norm + part
                total = total + (part * vfac[f + o, :, lane]) * proj[f + o, 2 * head_dim :, lane]
            att[f, b] = total / norm
        return carry

    lax.fori_loop(0, all_frames, one_frame, 0)
    toks = out.shape[0] * frames // (all_frames * branches)
    queues = all_frames // frames
    for t in range(toks):
        for q in range(queues):
            for b in range(branches):
                pieces = [
                    att[min(q * frames + i, all_frames - 1), b, :, t * tokens : (t + 1) * tokens]
                    for i in range(frames + 1)
                ]
                at = (t * queues + q) * branches + b
                out[at] = jnp.concatenate(pieces, axis=1).astype(BF16)


def rows_kernel(
    values, span, packed, following, cond, level_mod, embed, final_gain, emb_out, gate_out, gain_out
):
    levels_all, width = level_mod.shape
    info = jnp.concatenate([packed[...], following[...]], axis=1)
    lanes = info.shape[1]
    vec = info[:values].astype(BF16)
    ones = jnp.ones((16, lanes), BF16)
    zero = jnp.zeros((13, width), BF16)
    weights = jnp.concatenate([embed[...]] + split_terms(cond[...], 3) + [zero], axis=0)
    emb_out[...] = dot_tn(weights, jnp.concatenate([vec, ones], axis=0))
    level = info[values + span : values + span + 1]
    one_hot = (lax.broadcasted_iota(jnp.int32, (levels_all, lanes), 0).astype(F32) == level).astype(
        F32
    ).astype(BF16)
    gates = jnp.concatenate(split_terms(level_mod[...], 3), axis=0)
    gate_out[...] = dot_tn(gates, jnp.concatenate([one_hot] * 3, axis=0))
    gains = jnp.concatenate(split_terms(final_gain[...], 3) + [zero], axis=0)
    gain_out[...] = dot_tn(gains, ones)


def finish_kernel(
    half,
    toks,
    attended,
    out_own,
    out_other,
    emb,
    gate,
    gain,
    final_w,
    branch,
    mine,
    send,
    scratch,
    mixed,
):
    queues, columns, group = out_own.shape[0] // toks, out_own.shape[1], out_own.shape[2]
    for core, held in ((branch[0], out_own), (1 - branch[0], out_other)):
        for q in range(queues):
            total = jnp.zeros((columns, attended.shape[1]), F32)
            for t in range(toks):
                made = jnp.dot(
                    held[t * queues + q],
                    attended[t * group : (t + 1) * group, :],
                    preferred_element_type=F32,
                )
                total = total + made.astype(BF16).astype(F32)
            first = pl.multiple_of((2 * q + core) * columns, 8)
            mixed[pl.ds(first, columns), :] = total
    summed = emb[...] + gate[...] * mixed[...]
    center = jnp.mean(summed, axis=0, keepdims=True)
    deviate = summed - center
    spread = jnp.mean(deviate * deviate, axis=0, keepdims=True)
    final = (deviate * lax.rsqrt(spread + EPS_NORM) * gain[...]).astype(BF16)
    scratch[...] = jnp.dot(final_w[...], final, preferred_element_type=F32)
    own = pl.multiple_of(branch[0] * half, half)
    other = pl.multiple_of((1 - branch[0]) * half, half)
    mine[...] = scratch[pl.ds(own, half), :]
    send[...] = scratch[pl.ds(other, half), :]


def update_kernel(
    values, span, levels_all, mine, partner, packed, following, noise, table, index, place, vel, new
):
    half = mine.shape[0]
    frames, _, tokens = vel.shape
    is_cond = place[0] == 0
    own = pl.multiple_of(place[0] * half, half)
    here, there = mine[...], partner[...]
    cond = jnp.where(is_cond, here, there)
    uncond = jnp.where(is_cond, there, here)
    guided = uncond + table[index[0]] * (cond - uncond)
    level = jnp.concatenate(
        [packed[values + span : values + span + 1], following[values + span : values + span + 1]],
        axis=1,
    )
    current = noise_sigma((level + 1.0) / levels_all)
    upcoming = noise_sigma(level / levels_all)
    latents = jnp.concatenate([packed[pl.ds(own, half), :], following[pl.ds(own, half), :]], axis=1)
    updated = latents + (upcoming - current) * guided
    is_last = place[1] == 1
    for f in range(frames):
        vel[f] = guided[:, f * tokens : (f + 1) * tokens]
        moved = updated[:, (f + 1) * tokens : (f + 2) * tokens]
        if f == frames - 1:
            moved = jnp.where(is_last, noise[...], moved)
        new[f] = moved


def on_device_heads(
    latents,
    fresh_noise,
    levels,
    window_mask,
    cond_embed,
    level_mod,
    embed_weight,
    qkv_weight,
    query_gain,
    key_gain,
    out_weight,
    final_gain,
    final_weight,
    guide_table,
    guide_index,
):
    frames, values, tokens = latents.shape
    width = embed_weight.shape[1]
    head_dim = query_gain.shape[0]
    levels_all = level_mod.shape[0]
    span = window_mask.shape[1]
    window = span // 2
    queues, toks, branches = (lax.axis_size(a) for a in ("queue", "tok", "cfg"))
    group = queues * branches
    q_at, branch = lax.axis_index("queue"), lax.axis_index("cfg")
    all_frames = queues * frames
    rows = -(-max(values + 4, values + span + 1) // 16) * 16
    local_rows = qkv_weight.shape[0]
    lanes = branches * LANES
    row_lanes = (frames + 1) * tokens

    chunks, packed = kernel_call(
        functools.partial(pack_kernel, head_dim),
        [
            jax.ShapeDtypeStruct((group, local_rows, 3 * head_dim), BF16),
            jax.ShapeDtypeStruct((rows, frames * tokens), F32),
        ],
        "vvvv",
        vmem=WHOLE_VMEM,
    )(latents, levels[None], window_mask, jnp.transpose(qkv_weight, (1, 0, 2)))
    gathered = lax.all_gather(packed, ("queue", "tok"), axis=0)
    cond_other = from_partner(cond_embed, "cfg", 0)
    weight = lax.all_to_all(chunks, ("queue", "cfg"), 0, 0).reshape(width, 3 * head_dim)
    out_own, gathered = lax.optimization_barrier((out_weight.T, gathered))
    out_own = jnp.broadcast_to(out_own[None], (toks * queues,) + out_own.shape)
    out_own = lax.all_to_all(out_own, ("tok", "queue"), 0, 0)
    out_other = from_partner(out_own, "cfg", 0)

    conds = jnp.where(
        branch == 0,
        jnp.concatenate([cond_embed, cond_other], axis=0),
        jnp.concatenate([cond_other, cond_embed], axis=0),
    )
    mods = jnp.transpose(level_mod, (1, 0, 2))
    lhs, xin, rstd, masks = kernel_call(
        functools.partial(prepare_kernel, frames, values, span),
        [
            jax.ShapeDtypeStruct((all_frames * rows, width), BF16),
            jax.ShapeDtypeStruct((all_frames, rows, lanes), BF16),
            jax.ShapeDtypeStruct((all_frames, 1, lanes), F32),
            jax.ShapeDtypeStruct((all_frames, rows - values, LANES), F32),
        ],
        "vvvv",
    )(gathered, conds, mods, embed_weight)
    attended = kernel_call(
        functools.partial(attend_kernel, frames, tokens),
        jax.ShapeDtypeStruct((toks * group, head_dim, row_lanes), BF16),
        "vvvvvvv",
        [
            pltpu.VMEM((all_frames + 2 * window, 3 * head_dim, lanes), F32),
            pltpu.VMEM((all_frames + 2 * window, 1, lanes), F32),
            pltpu.VMEM((all_frames + 2 * window, 1, lanes), F32),
            pltpu.VMEM((all_frames, branches, head_dim, LANES), F32),
        ],
    )(weight, lhs, xin, rstd, masks, query_gain[:, None], key_gain[:, None])
    received = lax.all_to_all(attended, ("tok", "queue", "cfg"), 0, 0).reshape(width, row_lanes)

    following = lax.dynamic_index_in_dim(
        gathered,
        jnp.minimum(q_at + 1, queues - 1) * toks + lax.axis_index("tok"),
        0,
        keepdims=False,
    )[:, :tokens]
    wide = jax.ShapeDtypeStruct((width, row_lanes), F32)
    emb, gate, gain = kernel_call(
        functools.partial(rows_kernel, values, span), [wide, wide, wide], "vvvvvv"
    )(packed, following, cond_embed, mods[2], embed_weight, final_gain[None])
    half = values // 2
    half_shape = jax.ShapeDtypeStruct((half, row_lanes), F32)
    mine, send = kernel_call(
        functools.partial(finish_kernel, half, toks),
        [half_shape, half_shape],
        "vvvvvvvs",
        [pltpu.VMEM((values, row_lanes), F32), pltpu.VMEM((width, row_lanes), F32)],
    )(received, out_own, out_other, emb, gate, gain, final_weight.T, branch[None])
    partner = from_partner(send, "cfg", 0)
    place = jnp.stack([branch, (q_at == queues - 1).astype(jnp.int32)])
    shape = jax.ShapeDtypeStruct((frames, half, tokens), F32)
    return kernel_call(
        functools.partial(update_kernel, values, span, levels_all),
        [shape, shape],
        "vvvvvsss",
    )(mine, partner, packed, following, fresh_noise, guide_table, guide_index, place)


def on_device(*args):
    latents, qkv_weight, query_gain = args[0], args[7], args[8]
    local_heads = qkv_weight.shape[2] // query_gain.shape[0]
    one_head_each = local_heads == lax.axis_size("queue") * lax.axis_size("cfg")
    fits = latents.shape[2] * lax.axis_size("tok") <= LANES
    if one_head_each and fits:
        return tuple(on_device_heads(*args))
    return on_device_general(*args)


def solution(mesh):
    placed = (
        P(("scene", "queue"), None, "tok"),
        P(("scene", "cfg"), "tok"),
        P(("scene", "queue")),
        P(("scene", "queue"), None),
        P(("scene", "cfg"), None),
        P(),
        P(),
        P(("queue", "cfg"), None, "tok"),
        P(),
        P(),
        P("tok", ("queue", "cfg")),
        P(),
        P(),
        P(),
        P(),
    )
    return jax.shard_map(
        on_device,
        mesh=mesh,
        in_specs=placed,
        out_specs=(P(("scene", "queue"), "cfg", "tok"), P(("scene", "queue"), "cfg", "tok")),
        check_vma=False,
    )
```

```python
import functools

import jax
import jax.numpy as jnp
from jax import lax
from jax.experimental import pallas as pl
from jax.experimental.pallas import tpu as pltpu
from jax.sharding import PartitionSpec as P

EPS_NORM = 1e-06
TIME_SHIFT = 3.0
LANES = 128
VMEM_BYTES = 20 * 1024 * 1024
WHOLE_VMEM = 62 * 1024 * 1024
F32 = jnp.float32
BF16 = jnp.bfloat16


def noise_sigma(fraction):
    return TIME_SHIFT * fraction / (1.0 + (TIME_SHIFT - 1.0) * fraction)


def from_partner(value, axis, bit):
    return lax.ppermute(value, axis, [(i, i ^ 1 << bit) for i in range(lax.axis_size(axis))])


def with_halo(cells, sides, width):
    for axis, dim in sides:
        count = lax.axis_size(axis)
        ends = count - 1
        head = lax.slice_in_dim(cells, 0, width, axis=dim)
        tail = lax.slice_in_dim(cells, cells.shape[dim] - width, cells.shape[dim], axis=dim)
        cells = jnp.concatenate(
            [
                lax.ppermute(tail, axis, [(i, (i + 1) % count) for i in range(ends)]),
                cells,
                lax.ppermute(head, axis, [((i + 1) % count, i) for i in range(ends)]),
            ],
            axis=dim,
        )
    return cells


def shifted(value, axis, steps):
    count = lax.axis_size(axis)
    initial, last = (max(0, -steps), min(count, count - steps))
    return lax.ppermute(value, axis, [(source, source + steps) for source in range(initial, last)])


def layer_norm(values):
    center = jnp.mean(values, axis=-1, keepdims=True)
    deviate = values - center
    spread = jnp.mean(deviate * deviate, axis=-1, keepdims=True)
    return deviate * lax.rsqrt(spread + EPS_NORM)


def rms_norm(values, scaling):
    return (
        values * lax.rsqrt(jnp.mean(values * values, axis=-1, keepdims=True) + EPS_NORM) * scaling
    )


def temporal_attention(
    queries, key_rows, value_rows, window_mask, first_frame, total_frames, window
):
    frames = queries.shape[0]
    numerator = jnp.zeros(queries.shape, jnp.float32)
    denominator = jnp.zeros(queries.shape[:-1], jnp.float32)
    for offset in range(2 * window + 1):
        near_keys = key_rows[offset : offset + frames].astype(jnp.float32)
        near_values = value_rows[offset : offset + frames].astype(jnp.float32)
        scores = jnp.sum(queries * near_keys, axis=-1) * queries.shape[-1] ** (-0.5)
        target = first_frame + jnp.arange(frames, dtype=jnp.int32) + (offset - window)
        allowed = (window_mask[:, offset] == 1) & (target >= 0) & (target < total_frames)
        weights = jnp.exp(scores) * allowed.astype(jnp.float32)[:, None, None]
        numerator = numerator + weights[..., None] * near_values
        denominator = denominator + weights
    return numerator / denominator[..., None]


def on_device_general(
    latents,
    fresh_noise,
    levels,
    window_mask,
    cond_embed,
    level_mod,
    embed_weight,
    qkv_weight,
    query_gain,
    key_gain,
    out_weight,
    final_gain,
    final_weight,
    guide_table,
    guide_index,
):
    frames = latents.shape[0]
    tok_count = latents.shape[2]
    model_width = embed_weight.shape[1]
    head_dim = query_gain.shape[0]
    levels_all = level_mod.shape[0]
    queue_count = lax.axis_size("queue")
    all_tokens = lax.all_gather(latents, "tok", axis=2, tiled=True)
    seq_tokens = all_tokens.shape[2]
    row_count = frames * seq_tokens
    embedded = (
        jnp.einsum(
            "fcs,cd->fsd",
            all_tokens.astype(jnp.bfloat16),
            embed_weight,
            preferred_element_type=jnp.float32,
        )
        + cond_embed[0]
    )
    one_hot = (levels[:, None] == jnp.arange(levels_all, dtype=jnp.int32)[None, :]).astype(
        jnp.float32
    )
    modulate = jnp.dot(
        one_hot, level_mod.reshape(levels_all, 3 * model_width), precision=lax.Precision.HIGHEST
    ).reshape(frames, 3, model_width)
    normed = (layer_norm(embedded) * (1.0 + modulate[:, None, 1]) + modulate[:, None, 0]).astype(
        jnp.bfloat16
    )
    norm_rows = normed.reshape(row_count, model_width)
    local_cols = qkv_weight.shape[2]
    shard_piece = lax.all_gather(qkv_weight, ("queue", "cfg"), axis=0, tiled=True)
    flat_piece = shard_piece.reshape(shard_piece.shape[0], 3 * local_cols)
    projected = jnp.dot(norm_rows, flat_piece, preferred_element_type=jnp.float32)
    projected = projected.reshape(frames, seq_tokens, 3, local_cols // head_dim, head_dim)
    queries = rms_norm(projected[:, :, 0], query_gain)
    keys_values = jnp.stack(
        [
            rms_norm(projected[:, :, 1], key_gain).astype(jnp.bfloat16),
            projected[:, :, 2].astype(jnp.bfloat16),
        ]
    )
    window = window_mask.shape[1] // 2
    widened = with_halo(keys_values, (("queue", 1),), window)
    first_frame = lax.axis_index("queue") * frames
    attended = temporal_attention(
        queries, widened[0], widened[1], window_mask, first_frame, frames * queue_count, window
    )
    attended = attended.astype(jnp.bfloat16).reshape(frames, seq_tokens, local_cols)
    flat_heads = attended.reshape(row_count, local_cols)
    partial_value = jnp.dot(
        flat_heads,
        lax.all_gather(out_weight, ("queue", "cfg"), axis=1, tiled=True),
        preferred_element_type=jnp.float32,
    )
    mixed_out = lax.psum_scatter(
        partial_value.reshape(frames, seq_tokens, model_width).astype(jnp.bfloat16),
        "tok",
        scatter_dimension=1,
        tiled=True,
    ).astype(jnp.float32)
    own_start = lax.axis_index("tok") * tok_count
    own_embed = lax.dynamic_slice_in_dim(embedded, own_start, tok_count, 1)
    summed = own_embed + modulate[:, None, 2] * mixed_out
    final_rows = (layer_norm(summed) * final_gain).astype(jnp.bfloat16)
    velocity = jnp.einsum(
        "ftd,dc->fct", final_rows, final_weight, preferred_element_type=jnp.float32
    )
    half_values = velocity.shape[1] // 2
    branch_index = lax.axis_index("cfg")
    own_first = branch_index * half_values
    other_first = (1 - branch_index) * half_values
    outgoing = lax.dynamic_slice_in_dim(velocity, other_first, half_values, 1)
    partner = from_partner(outgoing, "cfg", 0)
    mine = lax.dynamic_slice_in_dim(velocity, own_first, half_values, 1)
    is_cond = branch_index == 0
    cond_vel = jnp.where(is_cond, mine, partner)
    uncond_vel = jnp.where(is_cond, partner, mine)
    entries = guide_table.shape[0]
    guidance = jnp.sum(
        guide_table * (jnp.arange(entries, dtype=jnp.int32) == guide_index[0]).astype(jnp.float32)
    )
    guided = uncond_vel + guidance * (cond_vel - uncond_vel)
    current = noise_sigma((levels + 1).astype(jnp.float32) / levels_all)
    upcoming = noise_sigma(levels.astype(jnp.float32) / levels_all)
    own_latents = lax.dynamic_slice_in_dim(latents, own_first, half_values, 1)
    updated = own_latents + (upcoming - current)[:, None, None] * guided
    incoming = shifted(updated[:1], "queue", -1)
    is_last = lax.axis_index("queue") == queue_count - 1
    incoming = jnp.where(is_last, fresh_noise[None], incoming)
    new_queue = jnp.concatenate([updated[1:], incoming], axis=0)
    return (guided, new_queue)


def kernel_call(body, out_shapes, spaces, scratch=(), vmem=VMEM_BYTES, **cost):
    kinds = {"v": pl.BlockSpec(), "s": pl.BlockSpec(memory_space=pltpu.SMEM)}
    many = isinstance(out_shapes, (list, tuple))
    return pl.pallas_call(
        body,
        out_shape=out_shapes,
        in_specs=[kinds[k] for k in spaces],
        out_specs=[pl.BlockSpec() for _ in out_shapes] if many else pl.BlockSpec(),
        scratch_shapes=list(scratch),
        compiler_params=pltpu.CompilerParams(vmem_limit_bytes=vmem),
        cost_estimate=pl.CostEstimate(
            flops=cost.get("flops", 1000000),
            bytes_accessed=cost.get("bytes_accessed", 1000000),
            transcendentals=0,
        ),
    )


def split_terms(values, terms):
    parts = []
    for _ in range(terms):
        part = values.astype(BF16)
        parts.append(part)
        values = values - part.astype(F32)
    return parts


def dot_tn(left, right):
    return lax.dot_general(
        left, right, (((0,), (0,)), ((), ())), preferred_element_type=F32
    )


def place_of(axis):
    return lax.axis_index(axis)


def pack_kernel(head_dim, copies_frames, latents, levels, window_mask, qkv, *outs):
    scratch = outs[-1]
    copies, packed, first = outs[-4:-1]
    chunks = outs[:-4]
    scene, q, core = (place_of(a) for a in ("scene", "queue", "cfg"))
    for h in range(scratch.shape[0]):
        start = h * head_dim
        scratch[h] = jnp.concatenate(
            [qkv[part, :, start : start + head_dim] for part in range(3)], axis=1
        )
    for k, chunk in enumerate(chunks):
        chunk[...] = scratch[scene * len(chunks) + (q ^ k)]
    frames, values, tokens = latents.shape
    span = window_mask.shape[1]
    shares = []
    own = []
    for f in range(frames):
        level = levels[:, f : f + 1].astype(F32)
        side = jnp.zeros((copies.shape[1] - values, tokens), F32)
        row_id = lax.broadcasted_iota(jnp.int32, side.shape, 0)
        for o in range(span):
            side = jnp.where(row_id == o, window_mask[f : f + 1, o : o + 1].astype(F32), side)
        side = jnp.where(row_id == span, level, side)
        shares.append(jnp.concatenate([latents[f], side], axis=0))
        fill = jnp.broadcast_to(level, (packed.shape[0] - values, tokens))
        own.append(jnp.concatenate([latents[f], fill], axis=0))
    lower = jnp.concatenate(shares[:copies_frames], axis=1)
    upper = jnp.concatenate(shares[copies_frames:], axis=1)
    share = jnp.where(core == 0, lower, upper).astype(BF16)
    for at in range(copies.shape[0]):
        copies[at] = share
    packed[...] = jnp.concatenate(own, axis=1)
    first[...] = own[0]


def prepare_kernel(
    frames, values, span, mine, other, cond, level_mod, embed, lhs, xin, rstd_out, mask_out
):
    width = embed.shape[1]
    scenes, all_frames, rows, _ = xin.shape
    queues = all_frames // frames
    toks = mine.shape[0] // (scenes * queues)
    per_core = frames // 2
    tokens = mine.shape[2] // per_core
    core = place_of("cfg")
    weights = embed[...].astype(F32)
    weights = weights - jnp.mean(weights, axis=1, keepdims=True)
    conds = cond[...]
    conds = conds - jnp.mean(conds, axis=1, keepdims=True)
    basis = jnp.concatenate(
        [weights, conds, jnp.zeros((rows - values - scenes, width), F32)], axis=0
    )
    gram = lax.dot_general(
        basis,
        basis,
        (((1,), (1,)), ((), ())),
        preferred_element_type=F32,
        precision=lax.Precision.HIGHEST,
    ) * (1.0 / width)
    row_id = lax.broadcasted_iota(jnp.int32, (rows, LANES), 0)
    wide_id = lax.broadcasted_iota(jnp.int32, (rows, width), 0)
    level_id = lax.broadcasted_iota(jnp.int32, (level_mod.shape[1], width), 0).astype(F32)
    shift_row = values + scenes
    fill = LANES - toks * tokens
    for y in range(scenes):
        for q in range(queues):
            first = (y * queues + q) * toks
            held = []
            for t in range(toks):
                one, two = mine[first + t].astype(F32), other[first + t].astype(F32)
                held.append((jnp.where(core == 0, one, two), jnp.where(core == 0, two, one)))
            for part in range(frames):
                f = q * frames + part
                at = part % per_core * tokens
                info = [pair[part // per_core][:, at : at + tokens] for pair in held]
                level = info[0][values + span : values + span + 1, 0:1]
                chosen = level_id == level
                shift = jnp.sum(jnp.where(chosen, level_mod[0], 0.0), axis=0, keepdims=True)
                scale = jnp.sum(jnp.where(chosen, level_mod[1], 0.0), axis=0, keepdims=True)
                block = basis * (1.0 + scale)
                block = jnp.where((wide_id == shift_row) | (wide_id == shift_row + 1), shift, block)
                to = (y * all_frames + f) * rows
                lhs[to : to + rows, :] = block.astype(BF16)
                info = jnp.concatenate(info + [jnp.ones((info[0].shape[0], fill), F32)], axis=1)
                mask_out[y, f] = info[values : values + mask_out.shape[2]]
                vec = jnp.where(row_id < values, info[:rows], 0.0)
                vec = jnp.where(row_id == values + y, 1.0, vec)
                spread = jnp.sum(
                    vec
                    * jnp.dot(
                        gram, vec, preferred_element_type=F32, precision=lax.Precision.HIGHEST
                    ),
                    axis=0,
                    keepdims=True,
                )
                spread = jnp.maximum(spread, 0.0) + EPS_NORM
                rstd = lax.rsqrt(spread)
                std = spread * rstd
                high = std.astype(BF16).astype(F32)
                vec = jnp.where(row_id == shift_row, high, vec)
                vec = jnp.where(row_id == shift_row + 1, std - high, vec)
                xin[y, f] = vec.astype(BF16)
                rstd_out[f, :, y * LANES : (y + 1) * LANES] = rstd


def attend_kernel(frames, tokens, queues, *refs):
    pieces = refs[: 2 * queues]
    lhs, xin, rstd_in, mask_in, gain_q, gain_k, out, whole, proj, kfac, vfac, att = refs[
        2 * queues :
    ]
    scenes, all_frames, rows, _ = xin.shape
    head_dim = gain_q.shape[0]
    window = (proj.shape[0] - all_frames) // 2
    span = 2 * window + 1
    q_at, core = place_of("queue"), place_of("cfg")
    part_rows = pieces[0].shape[0]
    for k in range(queues):
        for side in range(2):
            owner = core if side == 0 else 1 - core
            first = pl.multiple_of(((q_at ^ k) * 2 + owner) * part_rows, 16)
            whole[pl.ds(first, part_rows), :] = pieces[side * queues + k][...]
    folded = jnp.dot(lhs[...], whole[...], preferred_element_type=F32)
    high, low = split_terms(folded, 2)
    gains = gain_q[...] * gain_k[...] * head_dim ** (-0.5)
    gains = jnp.broadcast_to(gains, (head_dim, LANES))
    for side in range(window):
        for at in (side, all_frames + window + side):
            proj[at] = jnp.zeros(proj.shape[1:], F32)
            kfac[at] = jnp.zeros(kfac.shape[1:], F32)
            vfac[at] = jnp.zeros(vfac.shape[1:], F32)
    for y in range(scenes):
        lane = slice(y * LANES, (y + 1) * LANES)
        for f in range(all_frames):
            first = (y * all_frames + f) * rows
            piece = slice(first, first + rows)
            made = dot_tn(high[piece], xin[y, f]) + dot_tn(low[piece], xin[y, f])
            proj[f + window, :, lane] = made
            rstd = rstd_in[f, :, lane]
            keys = made[head_dim : 2 * head_dim]
            square = jnp.mean(keys * keys, axis=0, keepdims=True)
            kfac[f + window, :, lane] = rstd * lax.rsqrt(rstd * rstd * square + EPS_NORM)
            vfac[f + window, :, lane] = rstd

    def one_frame(f, carry):
        for y in range(scenes):
            lane = slice(y * LANES, (y + 1) * LANES)
            query = proj[f + window, 0:head_dim, lane]
            rstd = vfac[f + window, :, lane]
            square = jnp.mean(query * query, axis=0, keepdims=True)
            qfac = rstd * lax.rsqrt(rstd * rstd * square + EPS_NORM)
            query = query * gains
            total = jnp.zeros((head_dim, LANES), F32)
            norm = jnp.zeros((1, LANES), F32)
            for o in range(span):
                keys = proj[f + o, head_dim : 2 * head_dim, lane]
                score = jnp.sum(query * keys, axis=0, keepdims=True)
                score = score * (qfac * kfac[f + o, :, lane])
                part = jnp.exp(score) * mask_in[y, f, o : o + 1, :]
                norm = norm + part
                total = total + (part * vfac[f + o, :, lane]) * proj[f + o, 2 * head_dim :, lane]
            att[f, y] = total / norm
        return carry

    lax.fori_loop(0, all_frames, one_frame, 0)
    toks = out.shape[0] // (scenes * queues)
    for t in range(toks):
        for y in range(scenes):
            for q in range(queues):
                parts = [
                    att[min(q * frames + i, all_frames - 1), y, :, t * tokens : (t + 1) * tokens]
                    for i in range(frames + 1)
                ]
                at = (t * scenes + y) * queues + q
                out[at] = jnp.concatenate(parts, axis=1).astype(BF16)


def rows_kernel(
    values, packed, following, cond, level_mod, embed, final_gain, emb_out, gate_out, gain_out
):
    levels_all, width = level_mod.shape[1:]
    info = jnp.concatenate([packed[...], following[...]], axis=1)
    lanes = info.shape[1]
    vec = info[:values].astype(BF16)
    ones = jnp.ones((16, lanes), BF16)
    zero = jnp.zeros((13, width), BF16)
    weights = jnp.concatenate([embed[...]] + split_terms(cond[...], 3) + [zero], axis=0)
    emb_out[...] = dot_tn(weights, jnp.concatenate([vec, ones], axis=0))
    level = info[values : values + 1]
    one_hot = (lax.broadcasted_iota(jnp.int32, (levels_all, lanes), 0).astype(F32) == level).astype(
        F32
    ).astype(BF16)
    gates = jnp.concatenate(split_terms(level_mod[2], 3), axis=0)
    gate_out[...] = dot_tn(gates, jnp.concatenate([one_hot] * 3, axis=0))
    gains = jnp.concatenate(split_terms(final_gain[...], 3) + [zero], axis=0)
    gain_out[...] = dot_tn(gains, ones)


def finish_kernel(half, queues, attended, *refs):
    parts = refs[:8]
    emb, gate, gain, final_w, mine, send, scratch, mixed = refs[8:]
    scene, q_at, tok, core = (place_of(a) for a in ("scene", "queue", "tok", "cfg"))
    group = parts[0].shape[1]
    columns = parts[0].shape[0] // queues
    held = [
        attended[pl.ds(pl.multiple_of(at * group, 16), group), :] for at in (tok, 1 - tok)
    ]
    for n in range(4):
        owner = core if n // 2 == 0 else 1 - core
        plane = scene if n % 2 == 0 else 1 - scene
        total = None
        for t in range(2):
            made = jnp.dot(parts[2 * n + t][...], held[t], preferred_element_type=F32)
            made = made.astype(BF16).astype(F32)
            total = made if total is None else total + made
        for k in range(queues):
            first = (((q_at ^ k) * 2 + owner) * 2 + plane) * columns
            mixed[pl.ds(pl.multiple_of(first, 8), columns), :] = total[
                k * columns : (k + 1) * columns
            ]
    summed = emb[...] + gate[...] * mixed[...]
    center = jnp.mean(summed, axis=0, keepdims=True)
    deviate = summed - center
    spread = jnp.mean(deviate * deviate, axis=0, keepdims=True)
    final = (deviate * lax.rsqrt(spread + EPS_NORM) * gain[...]).astype(BF16)
    scratch[...] = jnp.dot(final_w[...], final, preferred_element_type=F32)
    own = pl.multiple_of(core * half, half)
    other = pl.multiple_of((1 - core) * half, half)
    mine[...] = scratch[pl.ds(own, half), :]
    send[...] = scratch[pl.ds(other, half), :]


def update_kernel(
    values, levels_all, mine, partner, packed, following, noise, table, index, vel, new
):
    half = mine.shape[0]
    frames, _, tokens = vel.shape
    core = place_of("cfg")
    own = pl.multiple_of(core * half, half)
    here, there = mine[...], partner[...]
    cond = jnp.where(core == 0, here, there)
    uncond = jnp.where(core == 0, there, here)
    guided = uncond + table[index[0]] * (cond - uncond)
    level = jnp.concatenate(
        [packed[values : values + 1], following[values : values + 1]], axis=1
    )
    current = noise_sigma((level + 1.0) / levels_all)
    upcoming = noise_sigma(level / levels_all)
    latents = jnp.concatenate([packed[pl.ds(own, half), :], following[pl.ds(own, half), :]], axis=1)
    updated = latents + (upcoming - current) * guided
    is_last = place_of("queue") == lax.axis_size("queue") - 1
    for f in range(frames):
        vel[f] = guided[:, f * tokens : (f + 1) * tokens]
        moved = updated[:, (f + 1) * tokens : (f + 2) * tokens]
        if f == frames - 1:
            moved = jnp.where(is_last, noise[...], moved)
        new[f] = moved


def swapped(value, axis, mask):
    return lax.ppermute(value, axis, [(i, i ^ mask) for i in range(lax.axis_size(axis))])


def on_device_heads(
    latents,
    fresh_noise,
    levels,
    window_mask,
    cond_embed,
    level_mod,
    embed_weight,
    qkv_weight,
    query_gain,
    key_gain,
    out_weight,
    final_gain,
    final_weight,
    guide_table,
    guide_index,
):
    frames, values, tokens = latents.shape
    width = embed_weight.shape[1]
    head_dim = query_gain.shape[0]
    levels_all = level_mod.shape[0]
    span = window_mask.shape[1]
    window = span // 2
    scenes, queues, toks = (lax.axis_size(a) for a in ("scene", "queue", "tok"))
    chips = scenes * queues * toks
    all_frames = queues * frames
    rows = -(-max(values + scenes + 2, values + span + 1) // 16) * 16
    own_rows = -(-(values + 1) // 8) * 8
    local_rows = qkv_weight.shape[0]
    local_heads = qkv_weight.shape[2] // head_dim
    lanes = scenes * LANES
    row_lanes = (frames + 1) * tokens
    per_core = frames // 2
    mods = jnp.transpose(level_mod, (1, 0, 2))

    chunk = jax.ShapeDtypeStruct((local_rows, 3 * head_dim), BF16)
    *chunks, copies, packed, first = kernel_call(
        functools.partial(pack_kernel, head_dim, per_core),
        [chunk] * queues
        + [
            jax.ShapeDtypeStruct((chips, rows, per_core * tokens), BF16),
            jax.ShapeDtypeStruct((own_rows, frames * tokens), F32),
            jax.ShapeDtypeStruct((own_rows, tokens), F32),
        ],
        "vvvv",
        [pltpu.VMEM((local_heads, local_rows, 3 * head_dim), BF16)],
        vmem=WHOLE_VMEM,
    )(latents, levels[None], window_mask, jnp.transpose(qkv_weight, (1, 0, 2)))

    near = [chunks[0]] + [swapped(chunks[k], "queue", k) for k in range(1, queues)]
    far = [swapped(piece, "cfg", 1) for piece in near]
    shares = lax.all_to_all(copies, ("scene", "queue", "tok"), 0, 0)
    other_shares = swapped(shares, "cfg", 1)
    cond_far = swapped(cond_embed, "scene", 1)
    following = lax.ppermute(first, "queue", [(i + 1, i) for i in range(queues - 1)])

    columns = out_weight.shape[1] // scenes
    out_half = lax.dynamic_slice_in_dim(
        out_weight.T, lax.axis_index("scene") * columns, columns, 0
    )
    out_half, shares = lax.optimization_barrier((out_half, shares))
    part = jnp.concatenate(
        [out_half] + [swapped(out_half, "queue", k) for k in range(1, queues)], axis=0
    )
    part_tok = swapped(part, "tok", 1)
    parts = [part, part_tok, swapped(part, "scene", 1), swapped(part_tok, "scene", 1)]
    parts = parts + [swapped(piece, "cfg", 1) for piece in parts]

    conds = jnp.where(
        lax.axis_index("scene") == 0,
        jnp.concatenate([cond_embed, cond_far], axis=0),
        jnp.concatenate([cond_far, cond_embed], axis=0),
    )
    lhs, xin, rstd, masks = kernel_call(
        functools.partial(prepare_kernel, frames, values, span),
        [
            jax.ShapeDtypeStruct((scenes * all_frames * rows, width), BF16),
            jax.ShapeDtypeStruct((scenes, all_frames, rows, LANES), BF16),
            jax.ShapeDtypeStruct((all_frames, 1, lanes), F32),
            jax.ShapeDtypeStruct((scenes, all_frames, rows - values, LANES), F32),
        ],
        "vvvvv",
    )(shares, other_shares, conds, mods, embed_weight)
    attended = kernel_call(
        functools.partial(attend_kernel, frames, tokens, queues),
        jax.ShapeDtypeStruct((chips, head_dim, row_lanes), BF16),
        "v" * (2 * queues + 6),
        [
            pltpu.VMEM((width, 3 * head_dim), BF16),
            pltpu.VMEM((all_frames + 2 * window, 3 * head_dim, lanes), F32),
            pltpu.VMEM((all_frames + 2 * window, 1, lanes), F32),
            pltpu.VMEM((all_frames + 2 * window, 1, lanes), F32),
            pltpu.VMEM((all_frames, scenes, head_dim, LANES), F32),
        ],
    )(*near, *far, lhs, xin, rstd, masks, query_gain[:, None], key_gain[:, None])
    received = lax.all_to_all(attended, ("tok", "scene", "queue"), 0, 0)
    received = received.reshape(width, row_lanes)

    wide = jax.ShapeDtypeStruct((width, row_lanes), F32)
    emb, gate, gain = kernel_call(
        functools.partial(rows_kernel, values), [wide, wide, wide], "vvvvvv"
    )(packed, following, cond_embed, mods, embed_weight, final_gain[None])
    half = values // 2
    half_shape = jax.ShapeDtypeStruct((half, row_lanes), F32)
    mine, send = kernel_call(
        functools.partial(finish_kernel, half, queues),
        [half_shape, half_shape],
        "v" * 13,
        [pltpu.VMEM((values, row_lanes), F32), pltpu.VMEM((width, row_lanes), F32)],
    )(received, *parts, emb, gate, gain, final_weight.T)
    partner = swapped(send, "cfg", 1)
    shape = jax.ShapeDtypeStruct((frames, half, tokens), F32)
    return kernel_call(
        functools.partial(update_kernel, values, levels_all), [shape, shape], "vvvvvss"
    )(mine, partner, packed, following, fresh_noise, guide_table, guide_index)


def on_device(*args):
    latents, qkv_weight, query_gain = args[0], args[7], args[8]
    local_heads = qkv_weight.shape[2] // query_gain.shape[0]
    scenes, queues, toks, cores = (lax.axis_size(a) for a in ("scene", "queue", "tok", "cfg"))
    pairs = scenes == toks == cores == 2 and queues & (queues - 1) == 0
    fits = latents.shape[2] * toks <= LANES and latents.shape[0] % cores == 0
    if pairs and fits and local_heads == scenes * queues:
        return tuple(on_device_heads(*args))
    return on_device_general(*args)


def solution(mesh):
    placed = (
        P(("scene", "queue"), None, "tok"),
        P(("scene", "cfg"), "tok"),
        P(("scene", "queue")),
        P(("scene", "queue"), None),
        P(("scene", "cfg"), None),
        P(),
        P(),
        P(("queue", "cfg"), None, "tok"),
        P(),
        P(),
        P("tok", ("queue", "cfg")),
        P(),
        P(),
        P(),
        P(),
    )
    return jax.shard_map(
        on_device,
        mesh=mesh,
        in_specs=placed,
        out_specs=(P(("scene", "queue"), "cfg", "tok"), P(("scene", "queue"), "cfg", "tok")),
        check_vma=False,
    )
```

```python
import functools

import jax
import jax.numpy as jnp
from jax import lax
from jax.experimental import pallas as pl
from jax.experimental.pallas import tpu as pltpu
from jax.sharding import PartitionSpec as P

EPS_NORM = 1e-06
TIME_SHIFT = 3.0
LANES = 128
VMEM_BYTES = 20 * 1024 * 1024
WHOLE_VMEM = 62 * 1024 * 1024
F32 = jnp.float32
BF16 = jnp.bfloat16


def noise_sigma(fraction):
    return TIME_SHIFT * fraction / (1.0 + (TIME_SHIFT - 1.0) * fraction)


def from_partner(value, axis, bit):
    return lax.ppermute(value, axis, [(i, i ^ 1 << bit) for i in range(lax.axis_size(axis))])


def with_halo(cells, sides, width):
    for axis, dim in sides:
        count = lax.axis_size(axis)
        ends = count - 1
        head = lax.slice_in_dim(cells, 0, width, axis=dim)
        tail = lax.slice_in_dim(cells, cells.shape[dim] - width, cells.shape[dim], axis=dim)
        cells = jnp.concatenate(
            [
                lax.ppermute(tail, axis, [(i, (i + 1) % count) for i in range(ends)]),
                cells,
                lax.ppermute(head, axis, [((i + 1) % count, i) for i in range(ends)]),
            ],
            axis=dim,
        )
    return cells


def shifted(value, axis, steps):
    count = lax.axis_size(axis)
    initial, last = (max(0, -steps), min(count, count - steps))
    return lax.ppermute(value, axis, [(source, source + steps) for source in range(initial, last)])


def layer_norm(values):
    center = jnp.mean(values, axis=-1, keepdims=True)
    deviate = values - center
    spread = jnp.mean(deviate * deviate, axis=-1, keepdims=True)
    return deviate * lax.rsqrt(spread + EPS_NORM)


def rms_norm(values, scaling):
    return (
        values * lax.rsqrt(jnp.mean(values * values, axis=-1, keepdims=True) + EPS_NORM) * scaling
    )


def temporal_attention(
    queries, key_rows, value_rows, window_mask, first_frame, total_frames, window
):
    frames = queries.shape[0]
    numerator = jnp.zeros(queries.shape, jnp.float32)
    denominator = jnp.zeros(queries.shape[:-1], jnp.float32)
    for offset in range(2 * window + 1):
        near_keys = key_rows[offset : offset + frames].astype(jnp.float32)
        near_values = value_rows[offset : offset + frames].astype(jnp.float32)
        scores = jnp.sum(queries * near_keys, axis=-1) * queries.shape[-1] ** (-0.5)
        target = first_frame + jnp.arange(frames, dtype=jnp.int32) + (offset - window)
        allowed = (window_mask[:, offset] == 1) & (target >= 0) & (target < total_frames)
        weights = jnp.exp(scores) * allowed.astype(jnp.float32)[:, None, None]
        numerator = numerator + weights[..., None] * near_values
        denominator = denominator + weights
    return numerator / denominator[..., None]


def on_device_general(
    latents,
    fresh_noise,
    levels,
    window_mask,
    cond_embed,
    level_mod,
    embed_weight,
    qkv_weight,
    query_gain,
    key_gain,
    out_weight,
    final_gain,
    final_weight,
    guide_table,
    guide_index,
):
    frames = latents.shape[0]
    tok_count = latents.shape[2]
    model_width = embed_weight.shape[1]
    head_dim = query_gain.shape[0]
    levels_all = level_mod.shape[0]
    queue_count = lax.axis_size("queue")
    all_tokens = lax.all_gather(latents, "tok", axis=2, tiled=True)
    seq_tokens = all_tokens.shape[2]
    row_count = frames * seq_tokens
    embedded = (
        jnp.einsum(
            "fcs,cd->fsd",
            all_tokens.astype(jnp.bfloat16),
            embed_weight,
            preferred_element_type=jnp.float32,
        )
        + cond_embed[0]
    )
    one_hot = (levels[:, None] == jnp.arange(levels_all, dtype=jnp.int32)[None, :]).astype(
        jnp.float32
    )
    modulate = jnp.dot(
        one_hot, level_mod.reshape(levels_all, 3 * model_width), precision=lax.Precision.HIGHEST
    ).reshape(frames, 3, model_width)
    normed = (layer_norm(embedded) * (1.0 + modulate[:, None, 1]) + modulate[:, None, 0]).astype(
        jnp.bfloat16
    )
    norm_rows = normed.reshape(row_count, model_width)
    local_cols = qkv_weight.shape[2]
    shard_piece = lax.all_gather(qkv_weight, ("queue", "cfg"), axis=0, tiled=True)
    flat_piece = shard_piece.reshape(shard_piece.shape[0], 3 * local_cols)
    projected = jnp.dot(norm_rows, flat_piece, preferred_element_type=jnp.float32)
    projected = projected.reshape(frames, seq_tokens, 3, local_cols // head_dim, head_dim)
    queries = rms_norm(projected[:, :, 0], query_gain)
    keys_values = jnp.stack(
        [
            rms_norm(projected[:, :, 1], key_gain).astype(jnp.bfloat16),
            projected[:, :, 2].astype(jnp.bfloat16),
        ]
    )
    window = window_mask.shape[1] // 2
    widened = with_halo(keys_values, (("queue", 1),), window)
    first_frame = lax.axis_index("queue") * frames
    attended = temporal_attention(
        queries, widened[0], widened[1], window_mask, first_frame, frames * queue_count, window
    )
    attended = attended.astype(jnp.bfloat16).reshape(frames, seq_tokens, local_cols)
    flat_heads = attended.reshape(row_count, local_cols)
    partial_value = jnp.dot(
        flat_heads,
        lax.all_gather(out_weight, ("queue", "cfg"), axis=1, tiled=True),
        preferred_element_type=jnp.float32,
    )
    mixed_out = lax.psum_scatter(
        partial_value.reshape(frames, seq_tokens, model_width).astype(jnp.bfloat16),
        "tok",
        scatter_dimension=1,
        tiled=True,
    ).astype(jnp.float32)
    own_start = lax.axis_index("tok") * tok_count
    own_embed = lax.dynamic_slice_in_dim(embedded, own_start, tok_count, 1)
    summed = own_embed + modulate[:, None, 2] * mixed_out
    final_rows = (layer_norm(summed) * final_gain).astype(jnp.bfloat16)
    velocity = jnp.einsum(
        "ftd,dc->fct", final_rows, final_weight, preferred_element_type=jnp.float32
    )
    half_values = velocity.shape[1] // 2
    branch_index = lax.axis_index("cfg")
    own_first = branch_index * half_values
    other_first = (1 - branch_index) * half_values
    outgoing = lax.dynamic_slice_in_dim(velocity, other_first, half_values, 1)
    partner = from_partner(outgoing, "cfg", 0)
    mine = lax.dynamic_slice_in_dim(velocity, own_first, half_values, 1)
    is_cond = branch_index == 0
    cond_vel = jnp.where(is_cond, mine, partner)
    uncond_vel = jnp.where(is_cond, partner, mine)
    entries = guide_table.shape[0]
    guidance = jnp.sum(
        guide_table * (jnp.arange(entries, dtype=jnp.int32) == guide_index[0]).astype(jnp.float32)
    )
    guided = uncond_vel + guidance * (cond_vel - uncond_vel)
    current = noise_sigma((levels + 1).astype(jnp.float32) / levels_all)
    upcoming = noise_sigma(levels.astype(jnp.float32) / levels_all)
    own_latents = lax.dynamic_slice_in_dim(latents, own_first, half_values, 1)
    updated = own_latents + (upcoming - current)[:, None, None] * guided
    incoming = shifted(updated[:1], "queue", -1)
    is_last = lax.axis_index("queue") == queue_count - 1
    incoming = jnp.where(is_last, fresh_noise[None], incoming)
    new_queue = jnp.concatenate([updated[1:], incoming], axis=0)
    return (guided, new_queue)


def kernel_call(body, out_shapes, spaces, scratch=(), vmem=VMEM_BYTES, **cost):
    kinds = {
        "v": pl.BlockSpec(),
        "s": pl.BlockSpec(memory_space=pltpu.SMEM),
        "a": pl.BlockSpec(memory_space=pl.ANY),
    }
    many = isinstance(out_shapes, (list, tuple))
    return pl.pallas_call(
        body,
        out_shape=out_shapes,
        in_specs=[kinds[k] for k in spaces],
        out_specs=[pl.BlockSpec() for _ in out_shapes] if many else pl.BlockSpec(),
        scratch_shapes=list(scratch),
        compiler_params=pltpu.CompilerParams(vmem_limit_bytes=vmem),
        cost_estimate=pl.CostEstimate(
            flops=cost.get("flops", 1000000),
            bytes_accessed=cost.get("bytes_accessed", 1000000),
            transcendentals=0,
        ),
    )


def split_terms(values, terms):
    parts = []
    for _ in range(terms):
        part = values.astype(BF16)
        parts.append(part)
        values = values - part.astype(F32)
    return parts


def dot_tn(left, right):
    return lax.dot_general(
        left, right, (((0,), (0,)), ((), ())), preferred_element_type=F32
    )


def place_of(axis):
    return lax.axis_index(axis)


def pack_kernel(head_dim, copies_frames, latents, levels, window_mask, qkv, *outs):
    scratch = outs[-1]
    copies, packed, first = outs[-4:-1]
    chunks = outs[:-4]
    scene, q, core = (place_of(a) for a in ("scene", "queue", "cfg"))
    for h in range(scratch.shape[0]):
        start = h * head_dim
        scratch[h] = jnp.concatenate(
            [qkv[part, :, start : start + head_dim] for part in range(3)], axis=1
        )
    for k, chunk in enumerate(chunks):
        chunk[...] = scratch[scene * len(chunks) + (q ^ k)]
    frames, values, tokens = latents.shape
    span = window_mask.shape[1]
    shares = []
    own = []
    for f in range(frames):
        level = levels[:, f : f + 1].astype(F32)
        side = jnp.zeros((copies.shape[1] - values, tokens), F32)
        row_id = lax.broadcasted_iota(jnp.int32, side.shape, 0)
        for o in range(span):
            side = jnp.where(row_id == o, window_mask[f : f + 1, o : o + 1].astype(F32), side)
        side = jnp.where(row_id == span, level, side)
        shares.append(jnp.concatenate([latents[f], side], axis=0))
        fill = jnp.broadcast_to(level, (packed.shape[0] - values, tokens))
        own.append(jnp.concatenate([latents[f], fill], axis=0))
    lower = jnp.concatenate(shares[:copies_frames], axis=1)
    upper = jnp.concatenate(shares[copies_frames:], axis=1)
    share = jnp.where(core == 0, lower, upper).astype(BF16)
    for at in range(copies.shape[0]):
        copies[at] = share
    packed[...] = jnp.concatenate(own, axis=1)
    first[...] = own[0]


def prepare_kernel(
    frames,
    values,
    span,
    mine,
    other,
    cond,
    cond_far,
    level_mod,
    embed,
    lhs,
    xin,
    rstd_out,
    mask_out,
):
    width = embed.shape[1]
    scenes, all_frames, rows, _ = xin.shape
    queues = all_frames // frames
    toks = mine.shape[0] // (scenes * queues)
    per_core = frames // 2
    tokens = mine.shape[2] // per_core
    core = place_of("cfg")
    weights = embed[...].astype(F32)
    weights = weights - jnp.mean(weights, axis=1, keepdims=True)
    here, there = cond[...], cond_far[...]
    is_first = place_of("scene") == 0
    conds = jnp.concatenate(
        [jnp.where(is_first, here, there), jnp.where(is_first, there, here)], axis=0
    )
    conds = conds - jnp.mean(conds, axis=1, keepdims=True)
    basis = jnp.concatenate(
        [weights, conds, jnp.zeros((rows - values - scenes, width), F32)], axis=0
    )
    gram = lax.dot_general(
        basis,
        basis,
        (((1,), (1,)), ((), ())),
        preferred_element_type=F32,
        precision=lax.Precision.HIGHEST,
    ) * (1.0 / width)
    row_id = lax.broadcasted_iota(jnp.int32, (rows, LANES), 0)
    wide_id = lax.broadcasted_iota(jnp.int32, (rows, width), 0)
    level_id = lax.broadcasted_iota(jnp.int32, (level_mod.shape[1], width), 0).astype(F32)
    shift_row = values + scenes
    fill = LANES - toks * tokens
    for y in range(scenes):
        for q in range(queues):
            first = (y * queues + q) * toks
            held = []
            for t in range(toks):
                one, two = mine[first + t].astype(F32), other[first + t].astype(F32)
                held.append((jnp.where(core == 0, one, two), jnp.where(core == 0, two, one)))
            for part in range(frames):
                f = q * frames + part
                at = part % per_core * tokens
                info = [pair[part // per_core][:, at : at + tokens] for pair in held]
                level = info[0][values + span : values + span + 1, 0:1]
                chosen = level_id == level
                shift = jnp.sum(jnp.where(chosen, level_mod[0], 0.0), axis=0, keepdims=True)
                scale = jnp.sum(jnp.where(chosen, level_mod[1], 0.0), axis=0, keepdims=True)
                block = basis * (1.0 + scale)
                block = jnp.where((wide_id == shift_row) | (wide_id == shift_row + 1), shift, block)
                to = (y * all_frames + f) * rows
                lhs[to : to + rows, :] = block.astype(BF16)
                info = jnp.concatenate(info + [jnp.ones((info[0].shape[0], fill), F32)], axis=1)
                mask_out[y, f] = info[values : values + mask_out.shape[2]]
                vec = jnp.where(row_id < values, info[:rows], 0.0)
                vec = jnp.where(row_id == values + y, 1.0, vec)
                spread = jnp.sum(
                    vec
                    * jnp.dot(
                        gram, vec, preferred_element_type=F32, precision=lax.Precision.HIGHEST
                    ),
                    axis=0,
                    keepdims=True,
                )
                spread = jnp.maximum(spread, 0.0) + EPS_NORM
                rstd = lax.rsqrt(spread)
                std = spread * rstd
                high = std.astype(BF16).astype(F32)
                vec = jnp.where(row_id == shift_row, high, vec)
                vec = jnp.where(row_id == shift_row + 1, std - high, vec)
                xin[y, f] = vec.astype(BF16)
                rstd_out[f, :, y * LANES : (y + 1) * LANES] = rstd


def attend_kernel(frames, tokens, queues, *refs):
    pieces = refs[: 2 * queues]
    lhs, xin, rstd_in, mask_in, gain_q, gain_k, out, whole, proj, kfac, vfac, att = refs[
        2 * queues :
    ]
    scenes, all_frames, rows, _ = xin.shape
    head_dim = gain_q.shape[1]
    window = (proj.shape[0] - all_frames) // 2
    span = 2 * window + 1
    q_at, core = place_of("queue"), place_of("cfg")
    part_rows = pieces[0].shape[0]
    for k in range(queues):
        for side in range(2):
            owner = core if side == 0 else 1 - core
            first = pl.multiple_of(((q_at ^ k) * 2 + owner) * part_rows, 16)
            whole[pl.ds(first, part_rows), :] = pieces[side * queues + k][...]
    folded = jnp.dot(lhs[...], whole[...], preferred_element_type=F32)
    high, low = split_terms(folded, 2)
    gains = split_terms(gain_q[...] * gain_k[...] * head_dim ** (-0.5), 3)
    gains = jnp.concatenate(gains + [jnp.zeros((13, head_dim), BF16)], axis=0)
    gains = dot_tn(gains, jnp.ones((16, LANES), BF16))
    for side in range(window):
        for at in (side, all_frames + window + side):
            proj[at] = jnp.zeros(proj.shape[1:], F32)
            kfac[at] = jnp.zeros(kfac.shape[1:], F32)
            vfac[at] = jnp.zeros(vfac.shape[1:], F32)
    for y in range(scenes):
        lane = slice(y * LANES, (y + 1) * LANES)
        for f in range(all_frames):
            first = (y * all_frames + f) * rows
            piece = slice(first, first + rows)
            made = dot_tn(high[piece], xin[y, f]) + dot_tn(low[piece], xin[y, f])
            proj[f + window, :, lane] = made
            rstd = rstd_in[f, :, lane]
            keys = made[head_dim : 2 * head_dim]
            square = jnp.mean(keys * keys, axis=0, keepdims=True)
            kfac[f + window, :, lane] = rstd * lax.rsqrt(rstd * rstd * square + EPS_NORM)
            vfac[f + window, :, lane] = rstd

    def one_frame(f, carry):
        for y in range(scenes):
            lane = slice(y * LANES, (y + 1) * LANES)
            query = proj[f + window, 0:head_dim, lane]
            rstd = vfac[f + window, :, lane]
            square = jnp.mean(query * query, axis=0, keepdims=True)
            qfac = rstd * lax.rsqrt(rstd * rstd * square + EPS_NORM)
            query = query * gains
            total = jnp.zeros((head_dim, LANES), F32)
            norm = jnp.zeros((1, LANES), F32)
            for o in range(span):
                keys = proj[f + o, head_dim : 2 * head_dim, lane]
                score = jnp.sum(query * keys, axis=0, keepdims=True)
                score = score * (qfac * kfac[f + o, :, lane])
                part = jnp.exp(score) * mask_in[y, f, o : o + 1, :]
                norm = norm + part
                total = total + (part * vfac[f + o, :, lane]) * proj[f + o, 2 * head_dim :, lane]
            att[f, y] = total / norm
        return carry

    lax.fori_loop(0, all_frames, one_frame, 0)
    toks = out.shape[0] // (scenes * queues)
    for t in range(toks):
        for y in range(scenes):
            for q in range(queues):
                parts = [
                    att[min(q * frames + i, all_frames - 1), y, :, t * tokens : (t + 1) * tokens]
                    for i in range(frames + 1)
                ]
                at = (t * scenes + y) * queues + q
                out[at] = jnp.concatenate(parts, axis=1).astype(BF16)


def finish_kernel(half, values, queues, *refs):
    count = 16
    sources, mine, send, held = refs[:count], refs[count], refs[count + 1], refs[count + 2 : -5]
    scratch, mixed, emb, gate, sems = refs[-5:]
    copies = []
    for i in range(count):
        source = sources[i].at[2] if i == 3 else sources[i]
        copies.append(pltpu.make_async_copy(source, held[i], sems.at[i]))
    for copy in copies:
        copy.start()
    for copy in copies[:7]:
        copy.wait()
    packed, following, cond, gates, embed, final_gain, final_w, attended = held[:8]
    parts = held[8:]
    scene, q_at, tok, core = (place_of(a) for a in ("scene", "queue", "tok", "cfg"))

    levels_all, width = gates.shape
    info = jnp.concatenate([packed[...], following[...]], axis=1)
    lanes = info.shape[1]
    vec = info[:values].astype(BF16)
    ones = jnp.ones((16, lanes), BF16)
    zero = jnp.zeros((13, width), BF16)
    weights = jnp.concatenate([embed[...]] + split_terms(cond[...], 3) + [zero], axis=0)
    emb[...] = dot_tn(weights, jnp.concatenate([vec, ones], axis=0))
    level = info[values : values + 1]
    one_hot = (lax.broadcasted_iota(jnp.int32, (levels_all, lanes), 0).astype(F32) == level).astype(
        F32
    ).astype(BF16)
    gate_terms = jnp.concatenate(split_terms(gates[...], 3), axis=0)
    gate[...] = dot_tn(gate_terms, jnp.concatenate([one_hot] * 3, axis=0))

    group = parts[0].shape[1]
    columns = parts[0].shape[0] // queues
    copies[7].wait()
    rows = [attended[pl.ds(pl.multiple_of(at * group, 16), group), :] for at in (tok, 1 - tok)]
    for n in range(4):
        owner = core if n // 2 == 0 else 1 - core
        plane = scene if n % 2 == 0 else 1 - scene
        total = None
        for t in range(2):
            copies[8 + 2 * n + t].wait()
            made = jnp.dot(parts[2 * n + t][...], rows[t], preferred_element_type=F32)
            made = made.astype(BF16).astype(F32)
            total = made if total is None else total + made
        for k in range(queues):
            first = (((q_at ^ k) * 2 + owner) * 2 + plane) * columns
            mixed[pl.ds(pl.multiple_of(first, 8), columns), :] = total[
                k * columns : (k + 1) * columns
            ]
    summed = emb[...] + gate[...] * mixed[...]
    center = jnp.mean(summed, axis=0, keepdims=True)
    deviate = summed - center
    spread = jnp.mean(deviate * deviate, axis=0, keepdims=True)
    gain_terms = jnp.concatenate(split_terms(final_gain[...], 3) + [zero], axis=0)
    gain = dot_tn(gain_terms, ones)
    final = (deviate * lax.rsqrt(spread + EPS_NORM) * gain).astype(BF16)
    scratch[...] = jnp.dot(final_w[...], final, preferred_element_type=F32)
    own = pl.multiple_of(core * half, half)
    other = pl.multiple_of((1 - core) * half, half)
    mine[...] = scratch[pl.ds(own, half), :]
    send[...] = scratch[pl.ds(other, half), :]


def update_kernel(
    values, levels_all, mine, partner, packed, following, noise, table, index, vel, new
):
    half = mine.shape[0]
    frames, _, tokens = vel.shape
    core = place_of("cfg")
    own = pl.multiple_of(core * half, half)
    here, there = mine[...], partner[...]
    cond = jnp.where(core == 0, here, there)
    uncond = jnp.where(core == 0, there, here)
    guided = uncond + table[index[0]] * (cond - uncond)
    level = jnp.concatenate(
        [packed[values : values + 1], following[values : values + 1]], axis=1
    )
    current = noise_sigma((level + 1.0) / levels_all)
    upcoming = noise_sigma(level / levels_all)
    latents = jnp.concatenate([packed[pl.ds(own, half), :], following[pl.ds(own, half), :]], axis=1)
    updated = latents + (upcoming - current) * guided
    is_last = place_of("queue") == lax.axis_size("queue") - 1
    for f in range(frames):
        vel[f] = guided[:, f * tokens : (f + 1) * tokens]
        moved = updated[:, (f + 1) * tokens : (f + 2) * tokens]
        if f == frames - 1:
            moved = jnp.where(is_last, noise[...], moved)
        new[f] = moved


def swapped(value, axis, mask):
    count = lax.axis_size(axis)
    return lax.ppermute(value, axis, [(i, i ^ mask) for i in range(count)])


def on_device_heads(
    latents,
    fresh_noise,
    levels,
    window_mask,
    cond_embed,
    level_mod,
    embed_weight,
    qkv_weight,
    query_gain,
    key_gain,
    out_weight,
    final_gain,
    final_weight,
    guide_table,
    guide_index,
):
    frames, values, tokens = latents.shape
    width = embed_weight.shape[1]
    head_dim = query_gain.shape[0]
    levels_all = level_mod.shape[0]
    span = window_mask.shape[1]
    window = span // 2
    scenes, queues, toks = (lax.axis_size(a) for a in ("scene", "queue", "tok"))
    chips = scenes * queues * toks
    all_frames = queues * frames
    rows = -(-max(values + scenes + 2, values + span + 1) // 16) * 16
    own_rows = -(-(values + 1) // 8) * 8
    local_rows = qkv_weight.shape[0]
    local_heads = qkv_weight.shape[2] // head_dim
    lanes = scenes * LANES
    row_lanes = (frames + 1) * tokens
    per_core = frames // 2
    mods = jnp.transpose(level_mod, (1, 0, 2))

    chunk = jax.ShapeDtypeStruct((local_rows, 3 * head_dim), BF16)
    *chunks, copies, packed, first = kernel_call(
        functools.partial(pack_kernel, head_dim, per_core),
        [chunk] * queues
        + [
            jax.ShapeDtypeStruct((chips, rows, per_core * tokens), BF16),
            jax.ShapeDtypeStruct((own_rows, frames * tokens), F32),
            jax.ShapeDtypeStruct((own_rows, tokens), F32),
        ],
        "vvvv",
        [pltpu.VMEM((local_heads, local_rows, 3 * head_dim), BF16)],
        vmem=WHOLE_VMEM,
    )(latents, levels[None], window_mask, jnp.transpose(qkv_weight, (1, 0, 2)))

    near = [chunks[0]] + [swapped(chunks[k], "queue", k) for k in range(1, queues)]
    far = [swapped(piece, "cfg", 1) for piece in near]
    shares = lax.all_to_all(copies, ("scene", "queue", "tok"), 0, 0)
    other_shares = swapped(shares, "cfg", 1)
    cond_far = swapped(cond_embed, "scene", 1)
    following = lax.ppermute(first, "queue", [(i + 1, i) for i in range(queues - 1)])

    columns = out_weight.shape[1] // scenes
    out_half = lax.dynamic_slice_in_dim(
        out_weight.T, lax.axis_index("scene") * columns, columns, 0
    )
    part = jnp.concatenate(
        [out_half] + [swapped(out_half, "queue", k) for k in range(1, queues)], axis=0
    )
    parts = [
        part,
        swapped(part, "tok", 1),
        swapped(part, "scene", 1),
        swapped(part, ("scene", "tok"), 3),
    ]
    parts = parts + [swapped(piece, "cfg", 1) for piece in parts]

    lhs, xin, rstd, masks = kernel_call(
        functools.partial(prepare_kernel, frames, values, span),
        [
            jax.ShapeDtypeStruct((scenes * all_frames * rows, width), BF16),
            jax.ShapeDtypeStruct((scenes, all_frames, rows, LANES), BF16),
            jax.ShapeDtypeStruct((all_frames, 1, lanes), F32),
            jax.ShapeDtypeStruct((scenes, all_frames, rows - values, LANES), F32),
        ],
        "vvvvvv",
        bytes_accessed=8_000_000,
    )(shares, other_shares, cond_embed, cond_far, mods, embed_weight)
    lhs, part = lax.optimization_barrier((lhs, part))
    attended = kernel_call(
        functools.partial(attend_kernel, frames, tokens, queues),
        jax.ShapeDtypeStruct((chips, head_dim, row_lanes), BF16),
        "v" * (2 * queues + 6),
        [
            pltpu.VMEM((width, 3 * head_dim), BF16),
            pltpu.VMEM((all_frames + 2 * window, 3 * head_dim, lanes), F32),
            pltpu.VMEM((all_frames + 2 * window, 1, lanes), F32),
            pltpu.VMEM((all_frames + 2 * window, 1, lanes), F32),
            pltpu.VMEM((all_frames, scenes, head_dim, LANES), F32),
        ],
        bytes_accessed=24_000_000,
    )(*near, *far, lhs, xin, rstd, masks, query_gain[None], key_gain[None])
    received = lax.all_to_all(attended, ("tok", "scene", "queue"), 0, 0)
    received = received.reshape(width, row_lanes)

    half = values // 2
    half_shape = jax.ShapeDtypeStruct((half, row_lanes), F32)
    wide = pltpu.VMEM((width, row_lanes), F32)
    operands = (
        packed,
        following,
        cond_embed,
        mods,
        embed_weight,
        final_gain[None],
        final_weight.T,
        received,
        *parts,
    )
    places = [
        pltpu.VMEM(a.shape[1:] if i == 3 else a.shape, a.dtype) for i, a in enumerate(operands)
    ]
    mine, send = kernel_call(
        functools.partial(finish_kernel, half, values, queues),
        [half_shape, half_shape],
        "a" * len(operands),
        places
        + [pltpu.VMEM((values, row_lanes), F32)]
        + [wide] * 3
        + [pltpu.SemaphoreType.DMA((len(operands),))],
        vmem=WHOLE_VMEM,
        bytes_accessed=8_000_000,
    )(*operands)
    partner = swapped(send, "cfg", 1)
    shape = jax.ShapeDtypeStruct((frames, half, tokens), F32)
    return kernel_call(
        functools.partial(update_kernel, values, levels_all), [shape, shape], "vvvvvss"
    )(mine, partner, packed, following, fresh_noise, guide_table, guide_index)


def on_device(*args):
    latents, qkv_weight, query_gain = args[0], args[7], args[8]
    local_heads = qkv_weight.shape[2] // query_gain.shape[0]
    scenes, queues, toks, cores = (lax.axis_size(a) for a in ("scene", "queue", "tok", "cfg"))
    pairs = scenes == toks == cores == 2 and queues & (queues - 1) == 0
    fits = latents.shape[2] * toks <= LANES and latents.shape[0] % cores == 0
    if pairs and fits and local_heads == scenes * queues:
        return tuple(on_device_heads(*args))
    return on_device_general(*args)


def solution(mesh):
    placed = (
        P(("scene", "queue"), None, "tok"),
        P(("scene", "cfg"), "tok"),
        P(("scene", "queue")),
        P(("scene", "queue"), None),
        P(("scene", "cfg"), None),
        P(),
        P(),
        P(("queue", "cfg"), None, "tok"),
        P(),
        P(),
        P("tok", ("queue", "cfg")),
        P(),
        P(),
        P(),
        P(),
    )
    return jax.shard_map(
        on_device,
        mesh=mesh,
        in_specs=placed,
        out_specs=(P(("scene", "queue"), "cfg", "tok"), P(("scene", "queue"), "cfg", "tok")),
        check_vma=False,
    )
```

```python
import functools

import jax
import jax.numpy as jnp
from jax import lax
from jax.experimental import pallas as pl
from jax.experimental.pallas import tpu as pltpu
from jax.sharding import PartitionSpec as P

EPS_NORM = 1e-06
TIME_SHIFT = 3.0
LANES = 128
VMEM_BYTES = 20 * 1024 * 1024
WHOLE_VMEM = 62 * 1024 * 1024
HOLD_BYTES = 80_000_000
F32 = jnp.float32
BF16 = jnp.bfloat16


def noise_sigma(fraction):
    return TIME_SHIFT * fraction / (1.0 + (TIME_SHIFT - 1.0) * fraction)


def from_partner(value, axis, bit):
    return lax.ppermute(value, axis, [(i, i ^ 1 << bit) for i in range(lax.axis_size(axis))])


def with_halo(cells, sides, width):
    for axis, dim in sides:
        count = lax.axis_size(axis)
        ends = count - 1
        head = lax.slice_in_dim(cells, 0, width, axis=dim)
        tail = lax.slice_in_dim(cells, cells.shape[dim] - width, cells.shape[dim], axis=dim)
        cells = jnp.concatenate(
            [
                lax.ppermute(tail, axis, [(i, (i + 1) % count) for i in range(ends)]),
                cells,
                lax.ppermute(head, axis, [((i + 1) % count, i) for i in range(ends)]),
            ],
            axis=dim,
        )
    return cells


def shifted(value, axis, steps):
    count = lax.axis_size(axis)
    initial, last = (max(0, -steps), min(count, count - steps))
    return lax.ppermute(value, axis, [(source, source + steps) for source in range(initial, last)])


def layer_norm(values):
    center = jnp.mean(values, axis=-1, keepdims=True)
    deviate = values - center
    spread = jnp.mean(deviate * deviate, axis=-1, keepdims=True)
    return deviate * lax.rsqrt(spread + EPS_NORM)


def rms_norm(values, scaling):
    return (
        values * lax.rsqrt(jnp.mean(values * values, axis=-1, keepdims=True) + EPS_NORM) * scaling
    )


def temporal_attention(
    queries, key_rows, value_rows, window_mask, first_frame, total_frames, window
):
    frames = queries.shape[0]
    numerator = jnp.zeros(queries.shape, jnp.float32)
    denominator = jnp.zeros(queries.shape[:-1], jnp.float32)
    for offset in range(2 * window + 1):
        near_keys = key_rows[offset : offset + frames].astype(jnp.float32)
        near_values = value_rows[offset : offset + frames].astype(jnp.float32)
        scores = jnp.sum(queries * near_keys, axis=-1) * queries.shape[-1] ** (-0.5)
        target = first_frame + jnp.arange(frames, dtype=jnp.int32) + (offset - window)
        allowed = (window_mask[:, offset] == 1) & (target >= 0) & (target < total_frames)
        weights = jnp.exp(scores) * allowed.astype(jnp.float32)[:, None, None]
        numerator = numerator + weights[..., None] * near_values
        denominator = denominator + weights
    return numerator / denominator[..., None]


def on_device_general(
    latents,
    fresh_noise,
    levels,
    window_mask,
    cond_embed,
    level_mod,
    embed_weight,
    qkv_weight,
    query_gain,
    key_gain,
    out_weight,
    final_gain,
    final_weight,
    guide_table,
    guide_index,
):
    frames = latents.shape[0]
    tok_count = latents.shape[2]
    model_width = embed_weight.shape[1]
    head_dim = query_gain.shape[0]
    levels_all = level_mod.shape[0]
    queue_count = lax.axis_size("queue")
    all_tokens = lax.all_gather(latents, "tok", axis=2, tiled=True)
    seq_tokens = all_tokens.shape[2]
    row_count = frames * seq_tokens
    embedded = (
        jnp.einsum(
            "fcs,cd->fsd",
            all_tokens.astype(jnp.bfloat16),
            embed_weight,
            preferred_element_type=jnp.float32,
        )
        + cond_embed[0]
    )
    one_hot = (levels[:, None] == jnp.arange(levels_all, dtype=jnp.int32)[None, :]).astype(
        jnp.float32
    )
    modulate = jnp.dot(
        one_hot, level_mod.reshape(levels_all, 3 * model_width), precision=lax.Precision.HIGHEST
    ).reshape(frames, 3, model_width)
    normed = (layer_norm(embedded) * (1.0 + modulate[:, None, 1]) + modulate[:, None, 0]).astype(
        jnp.bfloat16
    )
    norm_rows = normed.reshape(row_count, model_width)
    local_cols = qkv_weight.shape[2]
    shard_piece = lax.all_gather(qkv_weight, ("queue", "cfg"), axis=0, tiled=True)
    flat_piece = shard_piece.reshape(shard_piece.shape[0], 3 * local_cols)
    projected = jnp.dot(norm_rows, flat_piece, preferred_element_type=jnp.float32)
    projected = projected.reshape(frames, seq_tokens, 3, local_cols // head_dim, head_dim)
    queries = rms_norm(projected[:, :, 0], query_gain)
    keys_values = jnp.stack(
        [
            rms_norm(projected[:, :, 1], key_gain).astype(jnp.bfloat16),
            projected[:, :, 2].astype(jnp.bfloat16),
        ]
    )
    window = window_mask.shape[1] // 2
    widened = with_halo(keys_values, (("queue", 1),), window)
    first_frame = lax.axis_index("queue") * frames
    attended = temporal_attention(
        queries, widened[0], widened[1], window_mask, first_frame, frames * queue_count, window
    )
    attended = attended.astype(jnp.bfloat16).reshape(frames, seq_tokens, local_cols)
    flat_heads = attended.reshape(row_count, local_cols)
    partial_value = jnp.dot(
        flat_heads,
        lax.all_gather(out_weight, ("queue", "cfg"), axis=1, tiled=True),
        preferred_element_type=jnp.float32,
    )
    mixed_out = lax.psum_scatter(
        partial_value.reshape(frames, seq_tokens, model_width).astype(jnp.bfloat16),
        "tok",
        scatter_dimension=1,
        tiled=True,
    ).astype(jnp.float32)
    own_start = lax.axis_index("tok") * tok_count
    own_embed = lax.dynamic_slice_in_dim(embedded, own_start, tok_count, 1)
    summed = own_embed + modulate[:, None, 2] * mixed_out
    final_rows = (layer_norm(summed) * final_gain).astype(jnp.bfloat16)
    velocity = jnp.einsum(
        "ftd,dc->fct", final_rows, final_weight, preferred_element_type=jnp.float32
    )
    half_values = velocity.shape[1] // 2
    branch_index = lax.axis_index("cfg")
    own_first = branch_index * half_values
    other_first = (1 - branch_index) * half_values
    outgoing = lax.dynamic_slice_in_dim(velocity, other_first, half_values, 1)
    partner = from_partner(outgoing, "cfg", 0)
    mine = lax.dynamic_slice_in_dim(velocity, own_first, half_values, 1)
    is_cond = branch_index == 0
    cond_vel = jnp.where(is_cond, mine, partner)
    uncond_vel = jnp.where(is_cond, partner, mine)
    entries = guide_table.shape[0]
    guidance = jnp.sum(
        guide_table * (jnp.arange(entries, dtype=jnp.int32) == guide_index[0]).astype(jnp.float32)
    )
    guided = uncond_vel + guidance * (cond_vel - uncond_vel)
    current = noise_sigma((levels + 1).astype(jnp.float32) / levels_all)
    upcoming = noise_sigma(levels.astype(jnp.float32) / levels_all)
    own_latents = lax.dynamic_slice_in_dim(latents, own_first, half_values, 1)
    updated = own_latents + (upcoming - current)[:, None, None] * guided
    incoming = shifted(updated[:1], "queue", -1)
    is_last = lax.axis_index("queue") == queue_count - 1
    incoming = jnp.where(is_last, fresh_noise[None], incoming)
    new_queue = jnp.concatenate([updated[1:], incoming], axis=0)
    return (guided, new_queue)


def kernel_call(body, out_shapes, spaces, scratch=(), vmem=VMEM_BYTES, **cost):
    kinds = {
        "v": pl.BlockSpec(),
        "s": pl.BlockSpec(memory_space=pltpu.SMEM),
        "a": pl.BlockSpec(memory_space=pl.ANY),
    }
    many = isinstance(out_shapes, (list, tuple))
    return pl.pallas_call(
        body,
        out_shape=out_shapes,
        in_specs=[kinds[k] for k in spaces],
        out_specs=[pl.BlockSpec() for _ in out_shapes] if many else pl.BlockSpec(),
        scratch_shapes=list(scratch),
        compiler_params=pltpu.CompilerParams(vmem_limit_bytes=vmem),
        cost_estimate=pl.CostEstimate(
            flops=cost.get("flops", 1000000),
            bytes_accessed=cost.get("bytes_accessed", 1000000),
            transcendentals=0,
        ),
    )


def split_terms(values, terms):
    parts = []
    for _ in range(terms):
        part = values.astype(BF16)
        parts.append(part)
        values = values - part.astype(F32)
    return parts


def dot_tn(left, right):
    return lax.dot_general(
        left, right, (((0,), (0,)), ((), ())), preferred_element_type=F32
    )


def place_of(axis):
    return lax.axis_index(axis)


def pack_kernel(head_dim, copies_frames, latents, levels, window_mask, qkv, out_w, *outs):
    scratch = outs[-1]
    copies, packed, first = outs[-4:-1]
    chunks = outs[:-4]
    scene, q, core = (place_of(a) for a in ("scene", "queue", "cfg"))
    for h in range(scratch.shape[0]):
        start = h * head_dim
        scratch[h] = jnp.concatenate(
            [qkv[part, :, start : start + head_dim] for part in range(3)], axis=1
        )
    group = out_w.shape[1] // 2
    half = jnp.where(scene == 0, out_w[:, :group], out_w[:, group:])
    for k, chunk in enumerate(chunks):
        chunk[...] = jnp.concatenate([half, scratch[scene * len(chunks) + (q ^ k)]], axis=1)
    frames, values, tokens = latents.shape
    span = window_mask.shape[1]
    shares = []
    own = []
    for f in range(frames):
        level = levels[:, f : f + 1].astype(F32)
        side = jnp.zeros((copies.shape[1] - values, tokens), F32)
        row_id = lax.broadcasted_iota(jnp.int32, side.shape, 0)
        for o in range(span):
            side = jnp.where(row_id == o, window_mask[f : f + 1, o : o + 1].astype(F32), side)
        side = jnp.where(row_id == span, level, side)
        shares.append(jnp.concatenate([latents[f], side], axis=0))
        fill = jnp.broadcast_to(level, (packed.shape[0] - values, tokens))
        own.append(jnp.concatenate([latents[f], fill], axis=0))
    lower = jnp.concatenate(shares[:copies_frames], axis=1)
    upper = jnp.concatenate(shares[copies_frames:], axis=1)
    share = jnp.where(core == 0, lower, upper).astype(BF16)
    for at in range(copies.shape[0]):
        copies[at] = share
    packed[...] = jnp.concatenate(own, axis=1)
    first[...] = own[0]


def prepare_kernel(
    frames,
    values,
    span,
    mine,
    other,
    cond,
    cond_far,
    level_mod,
    embed,
    lhs,
    xin,
    rstd_out,
    mask_out,
):
    width = embed.shape[1]
    scenes, all_frames, rows, _ = xin.shape
    queues = all_frames // frames
    toks = mine.shape[0] // (scenes * queues)
    per_core = frames // 2
    tokens = mine.shape[2] // per_core
    core = place_of("cfg")
    weights = embed[...].astype(F32)
    weights = weights - jnp.mean(weights, axis=1, keepdims=True)
    here, there = cond[...], cond_far[...]
    is_first = place_of("scene") == 0
    conds = jnp.concatenate(
        [jnp.where(is_first, here, there), jnp.where(is_first, there, here)], axis=0
    )
    conds = conds - jnp.mean(conds, axis=1, keepdims=True)
    basis = jnp.concatenate(
        [weights, conds, jnp.zeros((rows - values - scenes, width), F32)], axis=0
    )
    gram = lax.dot_general(
        basis,
        basis,
        (((1,), (1,)), ((), ())),
        preferred_element_type=F32,
        precision=lax.Precision.HIGHEST,
    ) * (1.0 / width)
    row_id = lax.broadcasted_iota(jnp.int32, (rows, LANES), 0)
    wide_id = lax.broadcasted_iota(jnp.int32, (rows, width), 0)
    level_id = lax.broadcasted_iota(jnp.int32, (level_mod.shape[1], width), 0).astype(F32)
    shift_row = values + scenes
    fill = LANES - toks * tokens
    for y in range(scenes):
        for q in range(queues):
            first = (y * queues + q) * toks
            held = []
            for t in range(toks):
                one, two = mine[first + t].astype(F32), other[first + t].astype(F32)
                held.append((jnp.where(core == 0, one, two), jnp.where(core == 0, two, one)))
            for part in range(frames):
                f = q * frames + part
                at = part % per_core * tokens
                info = [pair[part // per_core][:, at : at + tokens] for pair in held]
                level = info[0][values + span : values + span + 1, 0:1]
                chosen = level_id == level
                shift = jnp.sum(jnp.where(chosen, level_mod[0], 0.0), axis=0, keepdims=True)
                scale = jnp.sum(jnp.where(chosen, level_mod[1], 0.0), axis=0, keepdims=True)
                block = basis * (1.0 + scale)
                block = jnp.where((wide_id == shift_row) | (wide_id == shift_row + 1), shift, block)
                to = (y * all_frames + f) * rows
                lhs[to : to + rows, :] = block.astype(BF16)
                info = jnp.concatenate(info + [jnp.ones((info[0].shape[0], fill), F32)], axis=1)
                mask_out[y, f] = info[values : values + mask_out.shape[2]]
                vec = jnp.where(row_id < values, info[:rows], 0.0)
                vec = jnp.where(row_id == values + y, 1.0, vec)
                spread = jnp.sum(
                    vec
                    * jnp.dot(
                        gram, vec, preferred_element_type=F32, precision=lax.Precision.HIGHEST
                    ),
                    axis=0,
                    keepdims=True,
                )
                spread = jnp.maximum(spread, 0.0) + EPS_NORM
                rstd = lax.rsqrt(spread)
                std = spread * rstd
                high = std.astype(BF16).astype(F32)
                vec = jnp.where(row_id == shift_row, high, vec)
                vec = jnp.where(row_id == shift_row + 1, std - high, vec)
                xin[y, f] = vec.astype(BF16)
                rstd_out[f, :, y * LANES : (y + 1) * LANES] = rstd


def attend_kernel(frames, tokens, queues, *refs):
    pieces = refs[: 2 * queues]
    lhs, xin, rstd_in, mask_in, gain_q, gain_k, out, whole, proj, kfac, vfac, att = refs[
        2 * queues :
    ]
    scenes, all_frames, rows, _ = xin.shape
    head_dim = gain_q.shape[1]
    window = (proj.shape[0] - all_frames) // 2
    span = 2 * window + 1
    q_at, core = place_of("queue"), place_of("cfg")
    part_rows = pieces[0].shape[0]
    for k in range(queues):
        for side in range(2):
            owner = core if side == 0 else 1 - core
            first = pl.multiple_of(((q_at ^ k) * 2 + owner) * part_rows, 16)
            piece = pieces[side * queues + k]
            whole[pl.ds(first, part_rows), :] = piece[:, piece.shape[1] - 3 * head_dim :]
    folded = jnp.dot(lhs[...], whole[...], preferred_element_type=F32)
    high, low = split_terms(folded, 2)
    gains = split_terms(gain_q[...] * gain_k[...] * head_dim ** (-0.5), 3)
    gains = jnp.concatenate(gains + [jnp.zeros((13, head_dim), BF16)], axis=0)
    gains = dot_tn(gains, jnp.ones((16, LANES), BF16))
    for side in range(window):
        for at in (side, all_frames + window + side):
            proj[at] = jnp.zeros(proj.shape[1:], F32)
            kfac[at] = jnp.zeros(kfac.shape[1:], F32)
            vfac[at] = jnp.zeros(vfac.shape[1:], F32)
    for y in range(scenes):
        lane = slice(y * LANES, (y + 1) * LANES)
        for f in range(all_frames):
            first = (y * all_frames + f) * rows
            piece = slice(first, first + rows)
            made = dot_tn(high[piece], xin[y, f]) + dot_tn(low[piece], xin[y, f])
            proj[f + window, :, lane] = made
            rstd = rstd_in[f, :, lane]
            keys = made[head_dim : 2 * head_dim]
            square = jnp.mean(keys * keys, axis=0, keepdims=True)
            kfac[f + window, :, lane] = rstd * lax.rsqrt(rstd * rstd * square + EPS_NORM)
            vfac[f + window, :, lane] = rstd

    def one_frame(f, carry):
        for y in range(scenes):
            lane = slice(y * LANES, (y + 1) * LANES)
            query = proj[f + window, 0:head_dim, lane]
            rstd = vfac[f + window, :, lane]
            square = jnp.mean(query * query, axis=0, keepdims=True)
            qfac = rstd * lax.rsqrt(rstd * rstd * square + EPS_NORM)
            query = query * gains
            total = jnp.zeros((head_dim, LANES), F32)
            norm = jnp.zeros((1, LANES), F32)
            for o in range(span):
                keys = proj[f + o, head_dim : 2 * head_dim, lane]
                score = jnp.sum(query * keys, axis=0, keepdims=True)
                score = score * (qfac * kfac[f + o, :, lane])
                part = jnp.exp(score) * mask_in[y, f, o : o + 1, :]
                norm = norm + part
                total = total + (part * vfac[f + o, :, lane]) * proj[f + o, 2 * head_dim :, lane]
            att[f, y] = total / norm
        return carry

    lax.fori_loop(0, all_frames, one_frame, 0)
    toks = out.shape[0] // (scenes * queues)
    for t in range(toks):
        for y in range(scenes):
            for q in range(queues):
                parts = [
                    att[min(q * frames + i, all_frames - 1), y, :, t * tokens : (t + 1) * tokens]
                    for i in range(frames + 1)
                ]
                at = (t * scenes + y) * queues + q
                out[at] = jnp.concatenate(parts, axis=1).astype(BF16)


def hold_kernel(*refs):
    refs[-1][...] = jnp.zeros(refs[-1].shape, F32)


def finish_kernel(half, values, queues, *refs):
    near = [refs[:queues], refs[queues : 2 * queues]]
    away = [refs[2 * queues : 2 * queues + 3], refs[2 * queues + 3 : 2 * queues + 6]]
    (
        attended,
        packed,
        following,
        cond,
        level_mod,
        embed,
        final_gain,
        final_w,
        _,
        mine,
        send,
        scratch,
        mixed,
    ) = refs[2 * queues + 6 :]
    scene, q_at, tok, core = (place_of(a) for a in ("scene", "queue", "tok", "cfg"))
    group = away[0][0].shape[1] // queues
    columns = away[0][0].shape[0]
    total = None
    for t in range(2):
        made = None
        for y in range(2):
            if t == y == 0:
                pieces = [near[c][k][:, :group] for c in range(2) for k in range(queues)]
            else:
                pieces = [
                    away[c][2 * y + t - 1][:, k * group : (k + 1) * group]
                    for c in range(2)
                    for k in range(queues)
                ]
            first = ((tok ^ t) * 2 + (scene ^ y)) * group
            rows = attended[pl.ds(pl.multiple_of(first, 16), group), :]
            term = jnp.dot(jnp.concatenate(pieces, axis=0), rows, preferred_element_type=F32)
            made = term if made is None else made + term
        made = made.astype(BF16).astype(F32)
        total = made if total is None else total + made
    for c in range(2):
        for k in range(queues):
            first = ((q_at ^ k) * 2 + (core ^ c)) * columns
            at = (c * queues + k) * columns
            mixed[pl.ds(pl.multiple_of(first, 8), columns), :] = total[at : at + columns]

    levels_all, width = level_mod.shape[1:]
    info = jnp.concatenate([packed[...], following[...]], axis=1)
    lanes = info.shape[1]
    vec = info[:values].astype(BF16)
    ones = jnp.ones((16, lanes), BF16)
    zero = jnp.zeros((13, width), BF16)
    weights = jnp.concatenate([embed[...]] + split_terms(cond[...], 3) + [zero], axis=0)
    emb = dot_tn(weights, jnp.concatenate([vec, ones], axis=0))
    level = info[values : values + 1]
    one_hot = (lax.broadcasted_iota(jnp.int32, (levels_all, lanes), 0).astype(F32) == level).astype(
        F32
    ).astype(BF16)
    gate_terms = jnp.concatenate(split_terms(level_mod[2], 3), axis=0)
    gate = dot_tn(gate_terms, jnp.concatenate([one_hot] * 3, axis=0))
    gain_terms = jnp.concatenate(split_terms(final_gain[...], 3) + [zero], axis=0)
    gain = dot_tn(gain_terms, ones)
    summed = emb + gate * mixed[...]
    center = jnp.mean(summed, axis=0, keepdims=True)
    deviate = summed - center
    spread = jnp.mean(deviate * deviate, axis=0, keepdims=True)
    final = (deviate * lax.rsqrt(spread + EPS_NORM) * gain).astype(BF16)
    scratch[...] = jnp.dot(final_w[...], final, preferred_element_type=F32)
    own = pl.multiple_of(core * half, half)
    other = pl.multiple_of((1 - core) * half, half)
    mine[...] = scratch[pl.ds(own, half), :]
    send[...] = scratch[pl.ds(other, half), :]


def update_kernel(
    values, levels_all, mine, partner, packed, following, noise, table, index, vel, new
):
    half = mine.shape[0]
    frames, _, tokens = vel.shape
    core = place_of("cfg")
    own = pl.multiple_of(core * half, half)
    here, there = mine[...], partner[...]
    cond = jnp.where(core == 0, here, there)
    uncond = jnp.where(core == 0, there, here)
    guided = uncond + table[index[0]] * (cond - uncond)
    level = jnp.concatenate(
        [packed[values : values + 1], following[values : values + 1]], axis=1
    )
    current = noise_sigma((level + 1.0) / levels_all)
    upcoming = noise_sigma(level / levels_all)
    latents = jnp.concatenate([packed[pl.ds(own, half), :], following[pl.ds(own, half), :]], axis=1)
    updated = latents + (upcoming - current) * guided
    is_last = place_of("queue") == lax.axis_size("queue") - 1
    for f in range(frames):
        vel[f] = guided[:, f * tokens : (f + 1) * tokens]
        moved = updated[:, (f + 1) * tokens : (f + 2) * tokens]
        if f == frames - 1:
            moved = jnp.where(is_last, noise[...], moved)
        new[f] = moved


def swapped(value, axis, mask):
    count = lax.axis_size(axis)
    return lax.ppermute(value, axis, [(i, i ^ mask) for i in range(count)])


def on_device_heads(
    latents,
    fresh_noise,
    levels,
    window_mask,
    cond_embed,
    level_mod,
    embed_weight,
    qkv_weight,
    query_gain,
    key_gain,
    out_weight,
    final_gain,
    final_weight,
    guide_table,
    guide_index,
):
    frames, values, tokens = latents.shape
    width = embed_weight.shape[1]
    head_dim = query_gain.shape[0]
    levels_all = level_mod.shape[0]
    span = window_mask.shape[1]
    window = span // 2
    scenes, queues, toks = (lax.axis_size(a) for a in ("scene", "queue", "tok"))
    chips = scenes * queues * toks
    all_frames = queues * frames
    rows = -(-max(values + scenes + 2, values + span + 1) // 16) * 16
    own_rows = -(-(values + 1) // 8) * 8
    local_rows = qkv_weight.shape[0]
    local_heads = qkv_weight.shape[2] // head_dim
    lanes = scenes * LANES
    row_lanes = (frames + 1) * tokens
    per_core = frames // 2
    mods = jnp.transpose(level_mod, (1, 0, 2))

    group = out_weight.shape[0] // scenes
    chunk = jax.ShapeDtypeStruct((local_rows, group + 3 * head_dim), BF16)
    *chunks, copies, packed, first = kernel_call(
        functools.partial(pack_kernel, head_dim, per_core),
        [chunk] * queues
        + [
            jax.ShapeDtypeStruct((chips, rows, per_core * tokens), BF16),
            jax.ShapeDtypeStruct((own_rows, frames * tokens), F32),
            jax.ShapeDtypeStruct((own_rows, tokens), F32),
        ],
        "vvvvv",
        [pltpu.VMEM((local_heads, local_rows, 3 * head_dim), BF16)],
        vmem=WHOLE_VMEM,
        bytes_accessed=8_000_000,
    )(latents, levels[None], window_mask, jnp.transpose(qkv_weight, (1, 0, 2)), out_weight.T)

    near = [chunks[0]] + [swapped(chunks[k], "queue", k) for k in range(1, queues)]
    far = [swapped(piece, "cfg", 1) for piece in near]
    shares = lax.all_to_all(copies, ("scene", "queue", "tok"), 0, 0)
    other_shares = swapped(shares, "cfg", 1)
    cond_far = swapped(cond_embed, "scene", 1)
    following = lax.ppermute(first, "queue", [(i + 1, i) for i in range(queues - 1)])

    part = jnp.concatenate([piece[:, :group] for piece in near], axis=1)
    away = [
        swapped(part, "tok", 1),
        swapped(part, "scene", 1),
        swapped(part, ("scene", "tok"), 3),
    ]
    token = kernel_call(
        hold_kernel, jax.ShapeDtypeStruct((8, LANES), F32), "aaa", bytes_accessed=HOLD_BYTES
    )(*away)
    *away, token = lax.optimization_barrier((*away, token))
    away_far = [swapped(piece, "cfg", 1) for piece in away]

    lhs, xin, rstd, masks = kernel_call(
        functools.partial(prepare_kernel, frames, values, span),
        [
            jax.ShapeDtypeStruct((scenes * all_frames * rows, width), BF16),
            jax.ShapeDtypeStruct((scenes, all_frames, rows, LANES), BF16),
            jax.ShapeDtypeStruct((all_frames, 1, lanes), F32),
            jax.ShapeDtypeStruct((scenes, all_frames, rows - values, LANES), F32),
        ],
        "vvvvvv",
        bytes_accessed=8_000_000,
    )(shares, other_shares, cond_embed, cond_far, mods, embed_weight)
    lhs, part, following = lax.optimization_barrier((lhs, part, following))
    attended = kernel_call(
        functools.partial(attend_kernel, frames, tokens, queues),
        jax.ShapeDtypeStruct((chips, head_dim, row_lanes), BF16),
        "v" * (2 * queues + 6),
        [
            pltpu.VMEM((width, 3 * head_dim), BF16),
            pltpu.VMEM((all_frames + 2 * window, 3 * head_dim, lanes), F32),
            pltpu.VMEM((all_frames + 2 * window, 1, lanes), F32),
            pltpu.VMEM((all_frames + 2 * window, 1, lanes), F32),
            pltpu.VMEM((all_frames, scenes, head_dim, LANES), F32),
        ],
        bytes_accessed=24_000_000,
    )(*near, *far, lhs, xin, rstd, masks, query_gain[None], key_gain[None])
    received = lax.all_to_all(attended, ("tok", "scene", "queue"), 0, 0)
    received = received.reshape(width, row_lanes)

    half = values // 2
    half_shape = jax.ShapeDtypeStruct((half, row_lanes), F32)
    mine, send = kernel_call(
        functools.partial(finish_kernel, half, values, queues),
        [half_shape, half_shape],
        "v" * (2 * queues + 15),
        [pltpu.VMEM((values, row_lanes), F32), pltpu.VMEM((width, row_lanes), F32)],
        bytes_accessed=8_000_000,
    )(
        *near,
        *far,
        *away,
        *away_far,
        received,
        packed,
        following,
        cond_embed,
        mods,
        embed_weight,
        final_gain[None],
        final_weight.T,
        token,
    )
    partner = swapped(send, "cfg", 1)
    shape = jax.ShapeDtypeStruct((frames, half, tokens), F32)
    return kernel_call(
        functools.partial(update_kernel, values, levels_all), [shape, shape], "vvvvvss"
    )(mine, partner, packed, following, fresh_noise, guide_table, guide_index)


def on_device(*args):
    latents, qkv_weight, query_gain = args[0], args[7], args[8]
    local_heads = qkv_weight.shape[2] // query_gain.shape[0]
    scenes, queues, toks, cores = (lax.axis_size(a) for a in ("scene", "queue", "tok", "cfg"))
    pairs = scenes == toks == cores == 2 and queues & (queues - 1) == 0
    fits = latents.shape[2] * toks <= LANES and latents.shape[0] % cores == 0
    if pairs and fits and local_heads == scenes * queues:
        return tuple(on_device_heads(*args))
    return on_device_general(*args)


def solution(mesh):
    placed = (
        P(("scene", "queue"), None, "tok"),
        P(("scene", "cfg"), "tok"),
        P(("scene", "queue")),
        P(("scene", "queue"), None),
        P(("scene", "cfg"), None),
        P(),
        P(),
        P(("queue", "cfg"), None, "tok"),
        P(),
        P(),
        P("tok", ("queue", "cfg")),
        P(),
        P(),
        P(),
        P(),
    )
    return jax.shard_map(
        on_device,
        mesh=mesh,
        in_specs=placed,
        out_specs=(P(("scene", "queue"), "cfg", "tok"), P(("scene", "queue"), "cfg", "tok")),
        check_vma=False,
    )
```

```python
import functools

import jax
import jax.numpy as jnp
from jax import lax
from jax.experimental import pallas as pl
from jax.experimental.pallas import tpu as pltpu
from jax.sharding import PartitionSpec as P

EPS_NORM = 1e-06
TIME_SHIFT = 3.0
LANES = 128
VMEM_BYTES = 20 * 1024 * 1024
WHOLE_VMEM = 62 * 1024 * 1024
HOLD_BYTES = 2_000_000_000
F32 = jnp.float32
BF16 = jnp.bfloat16


def noise_sigma(fraction):
    return TIME_SHIFT * fraction / (1.0 + (TIME_SHIFT - 1.0) * fraction)


def from_partner(value, axis, bit):
    return lax.ppermute(value, axis, [(i, i ^ 1 << bit) for i in range(lax.axis_size(axis))])


def with_halo(cells, sides, width):
    for axis, dim in sides:
        count = lax.axis_size(axis)
        ends = count - 1
        head = lax.slice_in_dim(cells, 0, width, axis=dim)
        tail = lax.slice_in_dim(cells, cells.shape[dim] - width, cells.shape[dim], axis=dim)
        cells = jnp.concatenate(
            [
                lax.ppermute(tail, axis, [(i, (i + 1) % count) for i in range(ends)]),
                cells,
                lax.ppermute(head, axis, [((i + 1) % count, i) for i in range(ends)]),
            ],
            axis=dim,
        )
    return cells


def shifted(value, axis, steps):
    count = lax.axis_size(axis)
    initial, last = (max(0, -steps), min(count, count - steps))
    return lax.ppermute(value, axis, [(source, source + steps) for source in range(initial, last)])


def layer_norm(values):
    center = jnp.mean(values, axis=-1, keepdims=True)
    deviate = values - center
    spread = jnp.mean(deviate * deviate, axis=-1, keepdims=True)
    return deviate * lax.rsqrt(spread + EPS_NORM)


def rms_norm(values, scaling):
    return (
        values * lax.rsqrt(jnp.mean(values * values, axis=-1, keepdims=True) + EPS_NORM) * scaling
    )


def temporal_attention(
    queries, key_rows, value_rows, window_mask, first_frame, total_frames, window
):
    frames = queries.shape[0]
    numerator = jnp.zeros(queries.shape, jnp.float32)
    denominator = jnp.zeros(queries.shape[:-1], jnp.float32)
    for offset in range(2 * window + 1):
        near_keys = key_rows[offset : offset + frames].astype(jnp.float32)
        near_values = value_rows[offset : offset + frames].astype(jnp.float32)
        scores = jnp.sum(queries * near_keys, axis=-1) * queries.shape[-1] ** (-0.5)
        target = first_frame + jnp.arange(frames, dtype=jnp.int32) + (offset - window)
        allowed = (window_mask[:, offset] == 1) & (target >= 0) & (target < total_frames)
        weights = jnp.exp(scores) * allowed.astype(jnp.float32)[:, None, None]
        numerator = numerator + weights[..., None] * near_values
        denominator = denominator + weights
    return numerator / denominator[..., None]


def on_device_general(
    latents,
    fresh_noise,
    levels,
    window_mask,
    cond_embed,
    level_mod,
    embed_weight,
    qkv_weight,
    query_gain,
    key_gain,
    out_weight,
    final_gain,
    final_weight,
    guide_table,
    guide_index,
):
    frames = latents.shape[0]
    tok_count = latents.shape[2]
    model_width = embed_weight.shape[1]
    head_dim = query_gain.shape[0]
    levels_all = level_mod.shape[0]
    queue_count = lax.axis_size("queue")
    all_tokens = lax.all_gather(latents, "tok", axis=2, tiled=True)
    seq_tokens = all_tokens.shape[2]
    row_count = frames * seq_tokens
    embedded = (
        jnp.einsum(
            "fcs,cd->fsd",
            all_tokens.astype(jnp.bfloat16),
            embed_weight,
            preferred_element_type=jnp.float32,
        )
        + cond_embed[0]
    )
    one_hot = (levels[:, None] == jnp.arange(levels_all, dtype=jnp.int32)[None, :]).astype(
        jnp.float32
    )
    modulate = jnp.dot(
        one_hot, level_mod.reshape(levels_all, 3 * model_width), precision=lax.Precision.HIGHEST
    ).reshape(frames, 3, model_width)
    normed = (layer_norm(embedded) * (1.0 + modulate[:, None, 1]) + modulate[:, None, 0]).astype(
        jnp.bfloat16
    )
    norm_rows = normed.reshape(row_count, model_width)
    local_cols = qkv_weight.shape[2]
    shard_piece = lax.all_gather(qkv_weight, ("queue", "cfg"), axis=0, tiled=True)
    flat_piece = shard_piece.reshape(shard_piece.shape[0], 3 * local_cols)
    projected = jnp.dot(norm_rows, flat_piece, preferred_element_type=jnp.float32)
    projected = projected.reshape(frames, seq_tokens, 3, local_cols // head_dim, head_dim)
    queries = rms_norm(projected[:, :, 0], query_gain)
    keys_values = jnp.stack(
        [
            rms_norm(projected[:, :, 1], key_gain).astype(jnp.bfloat16),
            projected[:, :, 2].astype(jnp.bfloat16),
        ]
    )
    window = window_mask.shape[1] // 2
    widened = with_halo(keys_values, (("queue", 1),), window)
    first_frame = lax.axis_index("queue") * frames
    attended = temporal_attention(
        queries, widened[0], widened[1], window_mask, first_frame, frames * queue_count, window
    )
    attended = attended.astype(jnp.bfloat16).reshape(frames, seq_tokens, local_cols)
    flat_heads = attended.reshape(row_count, local_cols)
    partial_value = jnp.dot(
        flat_heads,
        lax.all_gather(out_weight, ("queue", "cfg"), axis=1, tiled=True),
        preferred_element_type=jnp.float32,
    )
    mixed_out = lax.psum_scatter(
        partial_value.reshape(frames, seq_tokens, model_width).astype(jnp.bfloat16),
        "tok",
        scatter_dimension=1,
        tiled=True,
    ).astype(jnp.float32)
    own_start = lax.axis_index("tok") * tok_count
    own_embed = lax.dynamic_slice_in_dim(embedded, own_start, tok_count, 1)
    summed = own_embed + modulate[:, None, 2] * mixed_out
    final_rows = (layer_norm(summed) * final_gain).astype(jnp.bfloat16)
    velocity = jnp.einsum(
        "ftd,dc->fct", final_rows, final_weight, preferred_element_type=jnp.float32
    )
    half_values = velocity.shape[1] // 2
    branch_index = lax.axis_index("cfg")
    own_first = branch_index * half_values
    other_first = (1 - branch_index) * half_values
    outgoing = lax.dynamic_slice_in_dim(velocity, other_first, half_values, 1)
    partner = from_partner(outgoing, "cfg", 0)
    mine = lax.dynamic_slice_in_dim(velocity, own_first, half_values, 1)
    is_cond = branch_index == 0
    cond_vel = jnp.where(is_cond, mine, partner)
    uncond_vel = jnp.where(is_cond, partner, mine)
    entries = guide_table.shape[0]
    guidance = jnp.sum(
        guide_table * (jnp.arange(entries, dtype=jnp.int32) == guide_index[0]).astype(jnp.float32)
    )
    guided = uncond_vel + guidance * (cond_vel - uncond_vel)
    current = noise_sigma((levels + 1).astype(jnp.float32) / levels_all)
    upcoming = noise_sigma(levels.astype(jnp.float32) / levels_all)
    own_latents = lax.dynamic_slice_in_dim(latents, own_first, half_values, 1)
    updated = own_latents + (upcoming - current)[:, None, None] * guided
    incoming = shifted(updated[:1], "queue", -1)
    is_last = lax.axis_index("queue") == queue_count - 1
    incoming = jnp.where(is_last, fresh_noise[None], incoming)
    new_queue = jnp.concatenate([updated[1:], incoming], axis=0)
    return (guided, new_queue)


def kernel_call(body, out_shapes, spaces, scratch=(), vmem=VMEM_BYTES, **cost):
    kinds = {
        "v": pl.BlockSpec(),
        "s": pl.BlockSpec(memory_space=pltpu.SMEM),
        "a": pl.BlockSpec(memory_space=pl.ANY),
    }
    many = isinstance(out_shapes, (list, tuple))
    return pl.pallas_call(
        body,
        out_shape=out_shapes,
        in_specs=[kinds[k] for k in spaces],
        out_specs=[pl.BlockSpec() for _ in out_shapes] if many else pl.BlockSpec(),
        scratch_shapes=list(scratch),
        compiler_params=pltpu.CompilerParams(vmem_limit_bytes=vmem),
        cost_estimate=pl.CostEstimate(
            flops=cost.get("flops", 1000000),
            bytes_accessed=cost.get("bytes_accessed", 1000000),
            transcendentals=0,
        ),
    )


def split_terms(values, terms):
    parts = []
    for _ in range(terms):
        part = values.astype(BF16)
        parts.append(part)
        values = values - part.astype(F32)
    return parts


def dot_tn(left, right):
    return lax.dot_general(
        left, right, (((0,), (0,)), ((), ())), preferred_element_type=F32
    )


def place_of(axis):
    return lax.axis_index(axis)


def pack_kernel(head_dim, copies_frames, latents, levels, window_mask, qkv, out_w, cond, *outs):
    scratch = outs[-1]
    copies, packed, first = outs[-4:-1]
    chunks = outs[:-4]
    scene, q, tok, core = (place_of(a) for a in ("scene", "queue", "tok", "cfg"))
    for h in range(scratch.shape[0]):
        start = h * head_dim
        scratch[h] = jnp.concatenate(
            [qkv[part, :, start : start + head_dim] for part in range(3)], axis=1
        )
    group = out_w.shape[1] // 2
    half = jnp.where(scene == 0, out_w[:, :group], out_w[:, group:])
    for k, chunk in enumerate(chunks):
        chunk[...] = jnp.concatenate([half, scratch[scene * len(chunks) + (q ^ k)]], axis=1)
    frames, values, tokens = latents.shape
    span = window_mask.shape[1]
    shares = []
    own = []
    for f in range(frames):
        level = levels[:, f : f + 1].astype(F32)
        side = jnp.zeros((copies.shape[1] - values, tokens), F32)
        row_id = lax.broadcasted_iota(jnp.int32, side.shape, 0)
        for o in range(span):
            side = jnp.where(row_id == o, window_mask[f : f + 1, o : o + 1].astype(F32), side)
        side = jnp.where(row_id == span, level, side)
        shares.append(jnp.concatenate([latents[f], side], axis=0))
        fill = jnp.broadcast_to(level, (packed.shape[0] - values, tokens))
        own.append(jnp.concatenate([latents[f], fill], axis=0))
    lower = jnp.concatenate(shares[:copies_frames], axis=1)
    upper = jnp.concatenate(shares[copies_frames:], axis=1)
    share = jnp.where(core == 0, lower, upper)
    spots = lax.axis_size("queue") * lax.axis_size("tok")
    length = cond.shape[1] // spots
    piece = jnp.zeros((1, length), F32)
    for i in range(spots):
        chosen = q * lax.axis_size("tok") + tok == i
        piece = jnp.where(chosen, cond[:, i * length : (i + 1) * length], piece)
    row_id = lax.broadcasted_iota(jnp.int32, share.shape, 0)
    at_row, step = values + span + 1, share.shape[1]
    for term in split_terms(piece, 3):
        for start in range(0, length, step):
            line = term.astype(F32)[:, start : start + step]
            fill = jnp.zeros((1, step - line.shape[1]), F32)
            line = jnp.concatenate([line, fill], axis=1) if fill.shape[1] else line
            share = jnp.where(row_id == at_row, line, share)
            at_row += 1
    share = share.astype(BF16)
    for at in range(copies.shape[0]):
        copies[at] = share
    packed[...] = jnp.concatenate(own, axis=1)
    first[...] = own[0]


def prepare_kernel(
    frames,
    values,
    span,
    mine,
    other,
    level_mod,
    embed,
    lhs,
    xin,
    rstd_out,
    mask_out,
):
    width = embed.shape[1]
    scenes, all_frames, rows, _ = xin.shape
    queues = all_frames // frames
    toks = mine.shape[0] // (scenes * queues)
    per_core = frames // 2
    tokens = mine.shape[2] // per_core
    core = place_of("cfg")
    weights = embed[...].astype(F32)
    weights = weights - jnp.mean(weights, axis=1, keepdims=True)
    length, step = width // (queues * toks), mine.shape[2]
    lines = -(-length // step)
    conds = []
    for y in range(scenes):
        pieces = []
        for at in range(y * queues * toks, (y + 1) * queues * toks):
            info = mine[at].astype(F32)
            first = values + span + 1
            terms = sum(info[first + i * lines : first + (i + 1) * lines] for i in range(3))
            for i in range(lines):
                pieces.append(terms[i : i + 1, : min(step, length - i * step)])
        conds.append(jnp.concatenate(pieces, axis=1))
    conds = jnp.concatenate(conds, axis=0)
    conds = conds - jnp.mean(conds, axis=1, keepdims=True)
    basis = jnp.concatenate(
        [weights, conds, jnp.zeros((rows - values - scenes, width), F32)], axis=0
    )
    gram = lax.dot_general(
        basis,
        basis,
        (((1,), (1,)), ((), ())),
        preferred_element_type=F32,
        precision=lax.Precision.HIGHEST,
    ) * (1.0 / width)
    row_id = lax.broadcasted_iota(jnp.int32, (rows, LANES), 0)
    wide_id = lax.broadcasted_iota(jnp.int32, (rows, width), 0)
    level_id = lax.broadcasted_iota(jnp.int32, (level_mod.shape[1], width), 0).astype(F32)
    shift_row = values + scenes
    fill = LANES - toks * tokens
    for y in range(scenes):
        for q in range(queues):
            first = (y * queues + q) * toks
            held = []
            for t in range(toks):
                one, two = mine[first + t].astype(F32), other[first + t].astype(F32)
                held.append((jnp.where(core == 0, one, two), jnp.where(core == 0, two, one)))
            for part in range(frames):
                f = q * frames + part
                at = part % per_core * tokens
                info = [pair[part // per_core][:, at : at + tokens] for pair in held]
                level = info[0][values + span : values + span + 1, 0:1]
                chosen = level_id == level
                shift = jnp.sum(jnp.where(chosen, level_mod[0], 0.0), axis=0, keepdims=True)
                scale = jnp.sum(jnp.where(chosen, level_mod[1], 0.0), axis=0, keepdims=True)
                block = basis * (1.0 + scale)
                block = jnp.where((wide_id == shift_row) | (wide_id == shift_row + 1), shift, block)
                to = (y * all_frames + f) * rows
                lhs[to : to + rows, :] = block.astype(BF16)
                info = jnp.concatenate(info + [jnp.ones((info[0].shape[0], fill), F32)], axis=1)
                mask_out[y, f] = info[values : values + mask_out.shape[2]]
                vec = jnp.where(row_id < values, info[:rows], 0.0)
                vec = jnp.where(row_id == values + y, 1.0, vec)
                spread = jnp.sum(
                    vec
                    * jnp.dot(
                        gram, vec, preferred_element_type=F32, precision=lax.Precision.HIGHEST
                    ),
                    axis=0,
                    keepdims=True,
                )
                spread = jnp.maximum(spread, 0.0) + EPS_NORM
                rstd = lax.rsqrt(spread)
                std = spread * rstd
                high = std.astype(BF16).astype(F32)
                vec = jnp.where(row_id == shift_row, high, vec)
                vec = jnp.where(row_id == shift_row + 1, std - high, vec)
                xin[y, f] = vec.astype(BF16)
                rstd_out[f, :, y * LANES : (y + 1) * LANES] = rstd


def attend_kernel(frames, tokens, queues, *refs):
    pieces = refs[: 2 * queues]
    lhs, xin, rstd_in, mask_in, gain_q, gain_k, out, whole, proj, kfac, vfac, att = refs[
        2 * queues :
    ]
    scenes, all_frames, rows, _ = xin.shape
    head_dim = gain_q.shape[1]
    window = (proj.shape[0] - all_frames) // 2
    span = 2 * window + 1
    q_at, core = place_of("queue"), place_of("cfg")
    part_rows = pieces[0].shape[0]
    for k in range(queues):
        for side in range(2):
            owner = core if side == 0 else 1 - core
            first = pl.multiple_of(((q_at ^ k) * 2 + owner) * part_rows, 16)
            piece = pieces[side * queues + k]
            whole[pl.ds(first, part_rows), :] = piece[:, piece.shape[1] - 3 * head_dim :]
    folded = jnp.dot(lhs[...], whole[...], preferred_element_type=F32)
    high, low = split_terms(folded, 2)
    gains = split_terms(gain_q[...] * gain_k[...] * head_dim ** (-0.5), 3)
    gains = jnp.concatenate(gains + [jnp.zeros((13, head_dim), BF16)], axis=0)
    gains = dot_tn(gains, jnp.ones((16, LANES), BF16))
    for side in range(window):
        for at in (side, all_frames + window + side):
            proj[at] = jnp.zeros(proj.shape[1:], F32)
            kfac[at] = jnp.zeros(kfac.shape[1:], F32)
            vfac[at] = jnp.zeros(vfac.shape[1:], F32)
    for y in range(scenes):
        lane = slice(y * LANES, (y + 1) * LANES)
        for f in range(all_frames):
            first = (y * all_frames + f) * rows
            piece = slice(first, first + rows)
            made = dot_tn(high[piece], xin[y, f]) + dot_tn(low[piece], xin[y, f])
            proj[f + window, :, lane] = made
            rstd = rstd_in[f, :, lane]
            keys = made[head_dim : 2 * head_dim]
            square = jnp.mean(keys * keys, axis=0, keepdims=True)
            kfac[f + window, :, lane] = rstd * lax.rsqrt(rstd * rstd * square + EPS_NORM)
            vfac[f + window, :, lane] = rstd

    def one_frame(f, carry):
        for y in range(scenes):
            lane = slice(y * LANES, (y + 1) * LANES)
            query = proj[f + window, 0:head_dim, lane]
            rstd = vfac[f + window, :, lane]
            square = jnp.mean(query * query, axis=0, keepdims=True)
            qfac = rstd * lax.rsqrt(rstd * rstd * square + EPS_NORM)
            query = query * gains
            total = jnp.zeros((head_dim, LANES), F32)
            norm = jnp.zeros((1, LANES), F32)
            for o in range(span):
                keys = proj[f + o, head_dim : 2 * head_dim, lane]
                score = jnp.sum(query * keys, axis=0, keepdims=True)
                score = score * (qfac * kfac[f + o, :, lane])
                part = jnp.exp(score) * mask_in[y, f, o : o + 1, :]
                norm = norm + part
                total = total + (part * vfac[f + o, :, lane]) * proj[f + o, 2 * head_dim :, lane]
            att[f, y] = total / norm
        return carry

    lax.fori_loop(0, all_frames, one_frame, 0)
    toks = out.shape[0] // (scenes * queues)
    for t in range(toks):
        for y in range(scenes):
            for q in range(queues):
                parts = [
                    att[min(q * frames + i, all_frames - 1), y, :, t * tokens : (t + 1) * tokens]
                    for i in range(frames + 1)
                ]
                at = (t * scenes + y) * queues + q
                out[at] = jnp.concatenate(parts, axis=1).astype(BF16)


def side_kernel(group, *refs):
    for k, piece in enumerate(refs[:-1]):
        refs[-1][:, k * group : (k + 1) * group] = piece[:, :group]


def hold_kernel(*refs):
    refs[-1][...] = jnp.zeros(refs[-1].shape, F32)


def finish_kernel(half, values, queues, *refs):
    parts = [refs[:4], refs[4:8]]
    (
        attended,
        packed,
        following,
        cond,
        level_mod,
        embed,
        final_gain,
        final_w,
        _,
        mine,
        send,
        scratch,
        mixed,
    ) = refs[8:]
    scene, q_at, tok, core = (place_of(a) for a in ("scene", "queue", "tok", "cfg"))
    group = parts[0][0].shape[1] // queues
    columns = parts[0][0].shape[0]
    total = None
    for t in range(2):
        made = None
        for y in range(2):
            pieces = [
                parts[c][2 * y + t][:, k * group : (k + 1) * group]
                for c in range(2)
                for k in range(queues)
            ]
            first = ((tok ^ t) * 2 + (scene ^ y)) * group
            rows = attended[pl.ds(pl.multiple_of(first, 16), group), :]
            term = jnp.dot(jnp.concatenate(pieces, axis=0), rows, preferred_element_type=F32)
            made = term if made is None else made + term
        made = made.astype(BF16).astype(F32)
        total = made if total is None else total + made
    for c in range(2):
        for k in range(queues):
            first = ((q_at ^ k) * 2 + (core ^ c)) * columns
            at = (c * queues + k) * columns
            mixed[pl.ds(pl.multiple_of(first, 8), columns), :] = total[at : at + columns]

    levels_all, width = level_mod.shape[1:]
    info = jnp.concatenate([packed[...], following[...]], axis=1)
    lanes = info.shape[1]
    vec = info[:values].astype(BF16)
    ones = jnp.ones((16, lanes), BF16)
    zero = jnp.zeros((13, width), BF16)
    weights = jnp.concatenate([embed[...]] + split_terms(cond[...], 3) + [zero], axis=0)
    emb = dot_tn(weights, jnp.concatenate([vec, ones], axis=0))
    level = info[values : values + 1]
    one_hot = (lax.broadcasted_iota(jnp.int32, (levels_all, lanes), 0).astype(F32) == level).astype(
        F32
    ).astype(BF16)
    gate_terms = jnp.concatenate(split_terms(level_mod[2], 3), axis=0)
    gate = dot_tn(gate_terms, jnp.concatenate([one_hot] * 3, axis=0))
    gain_terms = jnp.concatenate(split_terms(final_gain[...], 3) + [zero], axis=0)
    gain = dot_tn(gain_terms, ones)
    summed = emb + gate * mixed[...]
    center = jnp.mean(summed, axis=0, keepdims=True)
    deviate = summed - center
    spread = jnp.mean(deviate * deviate, axis=0, keepdims=True)
    final = (deviate * lax.rsqrt(spread + EPS_NORM) * gain).astype(BF16)
    scratch[...] = jnp.dot(final_w[...], final, preferred_element_type=F32)
    own = pl.multiple_of(core * half, half)
    other = pl.multiple_of((1 - core) * half, half)
    mine[...] = scratch[pl.ds(own, half), :]
    send[...] = scratch[pl.ds(other, half), :]


def update_kernel(
    values, levels_all, mine, partner, packed, following, noise, table, index, vel, new
):
    half = mine.shape[0]
    frames, _, tokens = vel.shape
    core = place_of("cfg")
    own = pl.multiple_of(core * half, half)
    here, there = mine[...], partner[...]
    cond = jnp.where(core == 0, here, there)
    uncond = jnp.where(core == 0, there, here)
    guided = uncond + table[index[0]] * (cond - uncond)
    level = jnp.concatenate(
        [packed[values : values + 1], following[values : values + 1]], axis=1
    )
    current = noise_sigma((level + 1.0) / levels_all)
    upcoming = noise_sigma(level / levels_all)
    latents = jnp.concatenate([packed[pl.ds(own, half), :], following[pl.ds(own, half), :]], axis=1)
    updated = latents + (upcoming - current) * guided
    is_last = place_of("queue") == lax.axis_size("queue") - 1
    for f in range(frames):
        vel[f] = guided[:, f * tokens : (f + 1) * tokens]
        moved = updated[:, (f + 1) * tokens : (f + 2) * tokens]
        if f == frames - 1:
            moved = jnp.where(is_last, noise[...], moved)
        new[f] = moved


def swapped(value, axis, mask):
    count = lax.axis_size(axis)
    return lax.ppermute(value, axis, [(i, i ^ mask) for i in range(count)])


def on_device_heads(
    latents,
    fresh_noise,
    levels,
    window_mask,
    cond_embed,
    level_mod,
    embed_weight,
    qkv_weight,
    query_gain,
    key_gain,
    out_weight,
    final_gain,
    final_weight,
    guide_table,
    guide_index,
):
    frames, values, tokens = latents.shape
    width = embed_weight.shape[1]
    head_dim = query_gain.shape[0]
    levels_all = level_mod.shape[0]
    span = window_mask.shape[1]
    window = span // 2
    scenes, queues, toks = (lax.axis_size(a) for a in ("scene", "queue", "tok"))
    chips = scenes * queues * toks
    all_frames = queues * frames
    per_core = frames // 2
    cond_rows = 3 * -(-(width // (queues * toks)) // (per_core * tokens))
    rows = -(-max(values + scenes + 2, values + span + 1 + cond_rows) // 16) * 16
    own_rows = -(-(values + 1) // 8) * 8
    local_rows = qkv_weight.shape[0]
    local_heads = qkv_weight.shape[2] // head_dim
    lanes = scenes * LANES
    row_lanes = (frames + 1) * tokens
    mods = jnp.transpose(level_mod, (1, 0, 2))

    group = out_weight.shape[0] // scenes
    chunk = jax.ShapeDtypeStruct((local_rows, group + 3 * head_dim), BF16)
    *chunks, copies, packed, first = kernel_call(
        functools.partial(pack_kernel, head_dim, per_core),
        [chunk] * queues
        + [
            jax.ShapeDtypeStruct((chips, rows, per_core * tokens), BF16),
            jax.ShapeDtypeStruct((own_rows, frames * tokens), F32),
            jax.ShapeDtypeStruct((own_rows, tokens), F32),
        ],
        "vvvvvv",
        [pltpu.VMEM((local_heads, local_rows, 3 * head_dim), BF16)],
        vmem=WHOLE_VMEM,
        bytes_accessed=8_000_000,
    )(
        latents,
        levels[None],
        window_mask,
        jnp.transpose(qkv_weight, (1, 0, 2)),
        out_weight.T,
        cond_embed,
    )

    near = [chunks[0]] + [swapped(chunks[k], "queue", k) for k in range(1, queues)]
    far = [swapped(piece, "cfg", 1) for piece in near]
    shares = lax.all_to_all(copies, ("scene", "queue", "tok"), 0, 0)
    other_shares = swapped(shares, "cfg", 1)
    following = lax.ppermute(first, "queue", [(i + 1, i) for i in range(queues - 1)])

    part = kernel_call(
        functools.partial(side_kernel, group),
        jax.ShapeDtypeStruct((local_rows, queues * group), BF16),
        "v" * queues,
    )(*near)
    away = [
        swapped(part, "tok", 1),
        swapped(part, "scene", 1),
        swapped(part, ("scene", "tok"), 3),
    ]
    token = kernel_call(
        hold_kernel, jax.ShapeDtypeStruct((8, LANES), F32), "aaaa", bytes_accessed=HOLD_BYTES
    )(*away, following)
    *away, token = lax.optimization_barrier((part, *away, token))
    away_far = [swapped(piece, "cfg", 1) for piece in away]

    lhs, xin, rstd, masks = kernel_call(
        functools.partial(prepare_kernel, frames, values, span),
        [
            jax.ShapeDtypeStruct((scenes * all_frames * rows, width), BF16),
            jax.ShapeDtypeStruct((scenes, all_frames, rows, LANES), BF16),
            jax.ShapeDtypeStruct((all_frames, 1, lanes), F32),
            jax.ShapeDtypeStruct((scenes, all_frames, rows - values, LANES), F32),
        ],
        "vvvv",
        bytes_accessed=8_000_000,
    )(shares, other_shares, mods, embed_weight)
    lhs, part = lax.optimization_barrier((lhs, part))
    attended = kernel_call(
        functools.partial(attend_kernel, frames, tokens, queues),
        jax.ShapeDtypeStruct((chips, head_dim, row_lanes), BF16),
        "v" * (2 * queues + 6),
        [
            pltpu.VMEM((width, 3 * head_dim), BF16),
            pltpu.VMEM((all_frames + 2 * window, 3 * head_dim, lanes), F32),
            pltpu.VMEM((all_frames + 2 * window, 1, lanes), F32),
            pltpu.VMEM((all_frames + 2 * window, 1, lanes), F32),
            pltpu.VMEM((all_frames, scenes, head_dim, LANES), F32),
        ],
        bytes_accessed=24_000_000,
    )(*near, *far, lhs, xin, rstd, masks, query_gain[None], key_gain[None])
    received = lax.all_to_all(attended, ("tok", "scene", "queue"), 0, 0)
    received = received.reshape(width, row_lanes)

    half = values // 2
    half_shape = jax.ShapeDtypeStruct((half, row_lanes), F32)
    mine, send = kernel_call(
        functools.partial(finish_kernel, half, values, queues),
        [half_shape, half_shape],
        "v" * 17,
        [pltpu.VMEM((values, row_lanes), F32), pltpu.VMEM((width, row_lanes), F32)],
        bytes_accessed=8_000_000,
    )(
        *away,
        *away_far,
        received,
        packed,
        following,
        cond_embed,
        mods,
        embed_weight,
        final_gain[None],
        final_weight.T,
        token,
    )
    partner = swapped(send, "cfg", 1)
    shape = jax.ShapeDtypeStruct((frames, half, tokens), F32)
    return kernel_call(
        functools.partial(update_kernel, values, levels_all), [shape, shape], "vvvvvss"
    )(mine, partner, packed, following, fresh_noise, guide_table, guide_index)


def on_device(*args):
    latents, qkv_weight, query_gain = args[0], args[7], args[8]
    local_heads = qkv_weight.shape[2] // query_gain.shape[0]
    scenes, queues, toks, cores = (lax.axis_size(a) for a in ("scene", "queue", "tok", "cfg"))
    pairs = scenes == toks == cores == 2 and queues & (queues - 1) == 0
    fits = latents.shape[2] * toks <= LANES and latents.shape[0] % cores == 0
    if pairs and fits and local_heads == scenes * queues:
        return tuple(on_device_heads(*args))
    return on_device_general(*args)


def solution(mesh):
    placed = (
        P(("scene", "queue"), None, "tok"),
        P(("scene", "cfg"), "tok"),
        P(("scene", "queue")),
        P(("scene", "queue"), None),
        P(("scene", "cfg"), None),
        P(),
        P(),
        P(("queue", "cfg"), None, "tok"),
        P(),
        P(),
        P("tok", ("queue", "cfg")),
        P(),
        P(),
        P(),
        P(),
    )
    return jax.shard_map(
        on_device,
        mesh=mesh,
        in_specs=placed,
        out_specs=(P(("scene", "queue"), "cfg", "tok"), P(("scene", "queue"), "cfg", "tok")),
        check_vma=False,
    )
```

```python
import functools

import jax
import jax.numpy as jnp
from jax import lax
from jax.experimental import pallas as pl
from jax.experimental.pallas import tpu as pltpu
from jax.sharding import PartitionSpec as P

EPS_NORM = 1e-06
TIME_SHIFT = 3.0
LANES = 128
VMEM_BYTES = 20 * 1024 * 1024
WHOLE_VMEM = 62 * 1024 * 1024
F32 = jnp.float32
BF16 = jnp.bfloat16


def noise_sigma(fraction):
    return TIME_SHIFT * fraction / (1.0 + (TIME_SHIFT - 1.0) * fraction)


def from_partner(value, axis, bit):
    return lax.ppermute(value, axis, [(i, i ^ 1 << bit) for i in range(lax.axis_size(axis))])


def with_halo(cells, sides, width):
    for axis, dim in sides:
        count = lax.axis_size(axis)
        ends = count - 1
        head = lax.slice_in_dim(cells, 0, width, axis=dim)
        tail = lax.slice_in_dim(cells, cells.shape[dim] - width, cells.shape[dim], axis=dim)
        cells = jnp.concatenate(
            [
                lax.ppermute(tail, axis, [(i, (i + 1) % count) for i in range(ends)]),
                cells,
                lax.ppermute(head, axis, [((i + 1) % count, i) for i in range(ends)]),
            ],
            axis=dim,
        )
    return cells


def shifted(value, axis, steps):
    count = lax.axis_size(axis)
    initial, last = (max(0, -steps), min(count, count - steps))
    return lax.ppermute(value, axis, [(source, source + steps) for source in range(initial, last)])


def layer_norm(values):
    center = jnp.mean(values, axis=-1, keepdims=True)
    deviate = values - center
    spread = jnp.mean(deviate * deviate, axis=-1, keepdims=True)
    return deviate * lax.rsqrt(spread + EPS_NORM)


def rms_norm(values, scaling):
    return (
        values * lax.rsqrt(jnp.mean(values * values, axis=-1, keepdims=True) + EPS_NORM) * scaling
    )


def temporal_attention(
    queries, key_rows, value_rows, window_mask, first_frame, total_frames, window
):
    frames = queries.shape[0]
    numerator = jnp.zeros(queries.shape, jnp.float32)
    denominator = jnp.zeros(queries.shape[:-1], jnp.float32)
    for offset in range(2 * window + 1):
        near_keys = key_rows[offset : offset + frames].astype(jnp.float32)
        near_values = value_rows[offset : offset + frames].astype(jnp.float32)
        scores = jnp.sum(queries * near_keys, axis=-1) * queries.shape[-1] ** (-0.5)
        target = first_frame + jnp.arange(frames, dtype=jnp.int32) + (offset - window)
        allowed = (window_mask[:, offset] == 1) & (target >= 0) & (target < total_frames)
        weights = jnp.exp(scores) * allowed.astype(jnp.float32)[:, None, None]
        numerator = numerator + weights[..., None] * near_values
        denominator = denominator + weights
    return numerator / denominator[..., None]


def on_device_general(
    latents,
    fresh_noise,
    levels,
    window_mask,
    cond_embed,
    level_mod,
    embed_weight,
    qkv_weight,
    query_gain,
    key_gain,
    out_weight,
    final_gain,
    final_weight,
    guide_table,
    guide_index,
):
    frames = latents.shape[0]
    tok_count = latents.shape[2]
    model_width = embed_weight.shape[1]
    head_dim = query_gain.shape[0]
    levels_all = level_mod.shape[0]
    queue_count = lax.axis_size("queue")
    all_tokens = lax.all_gather(latents, "tok", axis=2, tiled=True)
    seq_tokens = all_tokens.shape[2]
    row_count = frames * seq_tokens
    embedded = (
        jnp.einsum(
            "fcs,cd->fsd",
            all_tokens.astype(jnp.bfloat16),
            embed_weight,
            preferred_element_type=jnp.float32,
        )
        + cond_embed[0]
    )
    one_hot = (levels[:, None] == jnp.arange(levels_all, dtype=jnp.int32)[None, :]).astype(
        jnp.float32
    )
    modulate = jnp.dot(
        one_hot, level_mod.reshape(levels_all, 3 * model_width), precision=lax.Precision.HIGHEST
    ).reshape(frames, 3, model_width)
    normed = (layer_norm(embedded) * (1.0 + modulate[:, None, 1]) + modulate[:, None, 0]).astype(
        jnp.bfloat16
    )
    norm_rows = normed.reshape(row_count, model_width)
    local_cols = qkv_weight.shape[2]
    shard_piece = lax.all_gather(qkv_weight, ("queue", "cfg"), axis=0, tiled=True)
    flat_piece = shard_piece.reshape(shard_piece.shape[0], 3 * local_cols)
    projected = jnp.dot(norm_rows, flat_piece, preferred_element_type=jnp.float32)
    projected = projected.reshape(frames, seq_tokens, 3, local_cols // head_dim, head_dim)
    queries = rms_norm(projected[:, :, 0], query_gain)
    keys_values = jnp.stack(
        [
            rms_norm(projected[:, :, 1], key_gain).astype(jnp.bfloat16),
            projected[:, :, 2].astype(jnp.bfloat16),
        ]
    )
    window = window_mask.shape[1] // 2
    widened = with_halo(keys_values, (("queue", 1),), window)
    first_frame = lax.axis_index("queue") * frames
    attended = temporal_attention(
        queries, widened[0], widened[1], window_mask, first_frame, frames * queue_count, window
    )
    attended = attended.astype(jnp.bfloat16).reshape(frames, seq_tokens, local_cols)
    flat_heads = attended.reshape(row_count, local_cols)
    partial_value = jnp.dot(
        flat_heads,
        lax.all_gather(out_weight, ("queue", "cfg"), axis=1, tiled=True),
        preferred_element_type=jnp.float32,
    )
    mixed_out = lax.psum_scatter(
        partial_value.reshape(frames, seq_tokens, model_width).astype(jnp.bfloat16),
        "tok",
        scatter_dimension=1,
        tiled=True,
    ).astype(jnp.float32)
    own_start = lax.axis_index("tok") * tok_count
    own_embed = lax.dynamic_slice_in_dim(embedded, own_start, tok_count, 1)
    summed = own_embed + modulate[:, None, 2] * mixed_out
    final_rows = (layer_norm(summed) * final_gain).astype(jnp.bfloat16)
    velocity = jnp.einsum(
        "ftd,dc->fct", final_rows, final_weight, preferred_element_type=jnp.float32
    )
    half_values = velocity.shape[1] // 2
    branch_index = lax.axis_index("cfg")
    own_first = branch_index * half_values
    other_first = (1 - branch_index) * half_values
    outgoing = lax.dynamic_slice_in_dim(velocity, other_first, half_values, 1)
    partner = from_partner(outgoing, "cfg", 0)
    mine = lax.dynamic_slice_in_dim(velocity, own_first, half_values, 1)
    is_cond = branch_index == 0
    cond_vel = jnp.where(is_cond, mine, partner)
    uncond_vel = jnp.where(is_cond, partner, mine)
    entries = guide_table.shape[0]
    guidance = jnp.sum(
        guide_table * (jnp.arange(entries, dtype=jnp.int32) == guide_index[0]).astype(jnp.float32)
    )
    guided = uncond_vel + guidance * (cond_vel - uncond_vel)
    current = noise_sigma((levels + 1).astype(jnp.float32) / levels_all)
    upcoming = noise_sigma(levels.astype(jnp.float32) / levels_all)
    own_latents = lax.dynamic_slice_in_dim(latents, own_first, half_values, 1)
    updated = own_latents + (upcoming - current)[:, None, None] * guided
    incoming = shifted(updated[:1], "queue", -1)
    is_last = lax.axis_index("queue") == queue_count - 1
    incoming = jnp.where(is_last, fresh_noise[None], incoming)
    new_queue = jnp.concatenate([updated[1:], incoming], axis=0)
    return (guided, new_queue)


def kernel_call(body, out_shapes, spaces, scratch=(), vmem=VMEM_BYTES, **cost):
    kinds = {
        "v": pl.BlockSpec(),
        "s": pl.BlockSpec(memory_space=pltpu.SMEM),
        "a": pl.BlockSpec(memory_space=pl.ANY),
    }
    many = isinstance(out_shapes, (list, tuple))
    return pl.pallas_call(
        body,
        out_shape=out_shapes,
        in_specs=[kinds[k] for k in spaces],
        out_specs=[pl.BlockSpec() for _ in out_shapes] if many else pl.BlockSpec(),
        scratch_shapes=list(scratch),
        compiler_params=pltpu.CompilerParams(vmem_limit_bytes=vmem),
        cost_estimate=pl.CostEstimate(
            flops=cost.get("flops", 1000000),
            bytes_accessed=cost.get("bytes_accessed", 1000000),
            transcendentals=0,
        ),
    )


def split_terms(values, terms):
    parts = []
    for _ in range(terms):
        part = values.astype(BF16)
        parts.append(part)
        values = values - part.astype(F32)
    return parts


def dot_tn(left, right):
    return lax.dot_general(
        left, right, (((0,), (0,)), ((), ())), preferred_element_type=F32
    )


def place_of(axis):
    return lax.axis_index(axis)


def pack_kernel(head_dim, copies_frames, latents, levels, window_mask, qkv, out_w, cond, *outs):
    scratch = outs[-1]
    copies, packed, first = outs[-4:-1]
    chunks = outs[:-4]
    scene, q, tok, core = (place_of(a) for a in ("scene", "queue", "tok", "cfg"))
    for h in range(scratch.shape[0]):
        start = h * head_dim
        scratch[h] = jnp.concatenate(
            [qkv[part, :, start : start + head_dim] for part in range(3)], axis=1
        )
    group = out_w.shape[1] // 2
    half = jnp.where(scene == 0, out_w[:, :group], out_w[:, group:])
    for k, chunk in enumerate(chunks):
        chunk[...] = jnp.concatenate([half, scratch[scene * len(chunks) + (q ^ k)]], axis=1)
    frames, values, tokens = latents.shape
    span = window_mask.shape[1]
    shares = []
    own = []
    for f in range(frames):
        level = levels[:, f : f + 1].astype(F32)
        side = jnp.zeros((copies.shape[1] - values, tokens), F32)
        row_id = lax.broadcasted_iota(jnp.int32, side.shape, 0)
        for o in range(span):
            side = jnp.where(row_id == o, window_mask[f : f + 1, o : o + 1].astype(F32), side)
        side = jnp.where(row_id == span, level, side)
        shares.append(jnp.concatenate([latents[f], side], axis=0))
        fill = jnp.broadcast_to(level, (packed.shape[0] - values, tokens))
        own.append(jnp.concatenate([latents[f], fill], axis=0))
    lower = jnp.concatenate(shares[:copies_frames], axis=1)
    upper = jnp.concatenate(shares[copies_frames:], axis=1)
    share = jnp.where(core == 0, lower, upper)
    spots = lax.axis_size("queue") * lax.axis_size("tok")
    length = cond.shape[1] // spots
    piece = jnp.zeros((1, length), F32)
    for i in range(spots):
        chosen = q * lax.axis_size("tok") + tok == i
        piece = jnp.where(chosen, cond[:, i * length : (i + 1) * length], piece)
    row_id = lax.broadcasted_iota(jnp.int32, share.shape, 0)
    at_row, step = values + span + 1, share.shape[1]
    for term in split_terms(piece, 3):
        for start in range(0, length, step):
            line = term.astype(F32)[:, start : start + step]
            fill = jnp.zeros((1, step - line.shape[1]), F32)
            line = jnp.concatenate([line, fill], axis=1) if fill.shape[1] else line
            share = jnp.where(row_id == at_row, line, share)
            at_row += 1
    share = share.astype(BF16)
    for at in range(copies.shape[0]):
        copies[at] = share
    packed[...] = jnp.concatenate(own, axis=1)
    first[...] = own[0]


def prepare_kernel(
    frames,
    values,
    span,
    mine,
    other,
    level_source,
    embed,
    lhs,
    xin,
    rstd_out,
    mask_out,
    level_mod,
    sem,
):
    width = embed.shape[1]
    scenes, all_frames, rows, _ = xin.shape
    queues = all_frames // frames
    toks = mine.shape[0] // (scenes * queues)
    per_core = frames // 2
    tokens = mine.shape[2] // per_core
    core = place_of("cfg")
    copy = pltpu.make_async_copy(level_source.at[pl.ds(0, 2)], level_mod, sem)
    copy.start()
    weights = embed[...].astype(F32)
    weights = weights - jnp.mean(weights, axis=1, keepdims=True)
    length, step = width // (queues * toks), mine.shape[2]
    lines = -(-length // step)
    conds = []
    for y in range(scenes):
        pieces = []
        for at in range(y * queues * toks, (y + 1) * queues * toks):
            info = mine[at].astype(F32)
            first = values + span + 1
            terms = sum(info[first + i * lines : first + (i + 1) * lines] for i in range(3))
            for i in range(lines):
                pieces.append(terms[i : i + 1, : min(step, length - i * step)])
        conds.append(jnp.concatenate(pieces, axis=1))
    conds = jnp.concatenate(conds, axis=0)
    conds = conds - jnp.mean(conds, axis=1, keepdims=True)
    basis = jnp.concatenate(
        [weights, conds, jnp.zeros((rows - values - scenes, width), F32)], axis=0
    )
    gram = lax.dot_general(
        basis,
        basis,
        (((1,), (1,)), ((), ())),
        preferred_element_type=F32,
        precision=lax.Precision.HIGHEST,
    ) * (1.0 / width)
    row_id = lax.broadcasted_iota(jnp.int32, (rows, LANES), 0)
    wide_id = lax.broadcasted_iota(jnp.int32, (rows, width), 0)
    level_id = lax.broadcasted_iota(jnp.int32, (level_mod.shape[1], width), 0).astype(F32)
    shift_row = values + scenes
    fill = LANES - toks * tokens
    copy.wait()
    for y in range(scenes):
        for q in range(queues):
            first = (y * queues + q) * toks
            held = []
            for t in range(toks):
                one, two = mine[first + t].astype(F32), other[first + t].astype(F32)
                held.append((jnp.where(core == 0, one, two), jnp.where(core == 0, two, one)))
            for part in range(frames):
                f = q * frames + part
                at = part % per_core * tokens
                info = [pair[part // per_core][:, at : at + tokens] for pair in held]
                level = info[0][values + span : values + span + 1, 0:1]
                chosen = level_id == level
                shift = jnp.sum(jnp.where(chosen, level_mod[0], 0.0), axis=0, keepdims=True)
                scale = jnp.sum(jnp.where(chosen, level_mod[1], 0.0), axis=0, keepdims=True)
                block = basis * (1.0 + scale)
                block = jnp.where((wide_id == shift_row) | (wide_id == shift_row + 1), shift, block)
                to = (y * all_frames + f) * rows
                lhs[to : to + rows, :] = block.astype(BF16)
                info = jnp.concatenate(info + [jnp.ones((info[0].shape[0], fill), F32)], axis=1)
                mask_out[y, f] = info[values : values + mask_out.shape[2]]
                vec = jnp.where(row_id < values, info[:rows], 0.0)
                vec = jnp.where(row_id == values + y, 1.0, vec)
                spread = jnp.sum(
                    vec
                    * jnp.dot(
                        gram, vec, preferred_element_type=F32, precision=lax.Precision.HIGHEST
                    ),
                    axis=0,
                    keepdims=True,
                )
                spread = jnp.maximum(spread, 0.0) + EPS_NORM
                rstd = lax.rsqrt(spread)
                std = spread * rstd
                high = std.astype(BF16).astype(F32)
                vec = jnp.where(row_id == shift_row, high, vec)
                vec = jnp.where(row_id == shift_row + 1, std - high, vec)
                xin[y, f] = vec.astype(BF16)
                rstd_out[f, :, y * LANES : (y + 1) * LANES] = rstd


def attend_kernel(frames, tokens, queues, *refs):
    pieces = refs[: 2 * queues]
    lhs, xin, rstd_in, mask_in, gain_q, gain_k, out, whole, proj, kfac, vfac, att, own, sem = refs[
        2 * queues :
    ]
    copy = pltpu.make_async_copy(pieces[0], own, sem)
    copy.start()
    scenes, all_frames, rows, _ = xin.shape
    head_dim = gain_q.shape[1]
    window = (proj.shape[0] - all_frames) // 2
    span = 2 * window + 1
    q_at, core = place_of("queue"), place_of("cfg")
    part_rows = pieces[0].shape[0]
    for k in reversed(range(queues)):
        for side in reversed(range(2)):
            owner = core if side == 0 else 1 - core
            first = pl.multiple_of(((q_at ^ k) * 2 + owner) * part_rows, 16)
            piece = pieces[side * queues + k]
            if k == side == 0:
                copy.wait()
                piece = own
            whole[pl.ds(first, part_rows), :] = piece[:, piece.shape[1] - 3 * head_dim :]
    folded = jnp.dot(lhs[...], whole[...], preferred_element_type=F32)
    high, low = split_terms(folded, 2)
    gains = split_terms(gain_q[...] * gain_k[...] * head_dim ** (-0.5), 3)
    gains = jnp.concatenate(gains + [jnp.zeros((13, head_dim), BF16)], axis=0)
    gains = dot_tn(gains, jnp.ones((16, LANES), BF16))
    for side in range(window):
        for at in (side, all_frames + window + side):
            proj[at] = jnp.zeros(proj.shape[1:], F32)
            kfac[at] = jnp.zeros(kfac.shape[1:], F32)
            vfac[at] = jnp.zeros(vfac.shape[1:], F32)
    for y in range(scenes):
        lane = slice(y * LANES, (y + 1) * LANES)
        for f in range(all_frames):
            first = (y * all_frames + f) * rows
            piece = slice(first, first + rows)
            made = dot_tn(high[piece], xin[y, f]) + dot_tn(low[piece], xin[y, f])
            proj[f + window, :, lane] = made
            rstd = rstd_in[f, :, lane]
            keys = made[head_dim : 2 * head_dim]
            square = jnp.mean(keys * keys, axis=0, keepdims=True)
            kfac[f + window, :, lane] = rstd * lax.rsqrt(rstd * rstd * square + EPS_NORM)
            vfac[f + window, :, lane] = rstd

    def one_frame(f, carry):
        for y in range(scenes):
            lane = slice(y * LANES, (y + 1) * LANES)
            query = proj[f + window, 0:head_dim, lane]
            rstd = vfac[f + window, :, lane]
            square = jnp.mean(query * query, axis=0, keepdims=True)
            qfac = rstd * lax.rsqrt(rstd * rstd * square + EPS_NORM)
            query = query * gains
            total = jnp.zeros((head_dim, LANES), F32)
            norm = jnp.zeros((1, LANES), F32)
            for o in range(span):
                keys = proj[f + o, head_dim : 2 * head_dim, lane]
                score = jnp.sum(query * keys, axis=0, keepdims=True)
                score = score * (qfac * kfac[f + o, :, lane])
                part = jnp.exp(score) * mask_in[y, f, o : o + 1, :]
                norm = norm + part
                total = total + (part * vfac[f + o, :, lane]) * proj[f + o, 2 * head_dim :, lane]
            att[f, y] = total / norm
        return carry

    lax.fori_loop(0, all_frames, one_frame, 0)
    toks = out.shape[0] // (scenes * queues)
    for t in range(toks):
        for y in range(scenes):
            for q in range(queues):
                parts = [
                    att[min(q * frames + i, all_frames - 1), y, :, t * tokens : (t + 1) * tokens]
                    for i in range(frames + 1)
                ]
                at = (t * scenes + y) * queues + q
                out[at] = jnp.concatenate(parts, axis=1).astype(BF16)


def side_kernel(group, *refs):
    *pieces, out, own, sem = refs
    copy = pltpu.make_async_copy(pieces[0], own, sem)
    copy.start()
    for k, piece in reversed(list(enumerate(pieces))):
        if k == 0:
            copy.wait()
            piece = own
        out[:, k * group : (k + 1) * group] = piece[:, :group]


def hold_kernel(*refs):
    refs[-1][...] = jnp.zeros(refs[-1].shape, F32)


def finish_kernel(half, values, queues, *refs):
    parts = [refs[:5], refs[5:10]]
    attended, _, table, index = refs[10:14]
    sources = refs[14:22]
    mine, send, base, factor, noise_out, guide = refs[22:28]
    held = refs[28:36]
    scratch, mixed, sems = refs[36:]
    copies = []
    for i, (source, to) in enumerate(zip(sources, held)):
        source = source.at[2] if i == 3 else source
        copies.append(pltpu.make_async_copy(source, to, sems.at[i]))
    for copy in copies:
        copy.start()
    packed, following, cond, gates, embed, final_gain, final_w, noise = held
    scene, q_at, tok, core = (place_of(a) for a in ("scene", "queue", "tok", "cfg"))
    group = parts[0][0].shape[1] // queues
    columns = parts[0][0].shape[0]

    def weights_of(c, t, y, k):
        lane = slice(k * group, (k + 1) * group)
        if t == y == 1:
            return [parts[c][3][:, lane], parts[c][4][:, lane]]
        return [parts[c][2 * y + t][:, lane]]

    total = None
    for t in range(2):
        made = None
        for y in range(2):
            pieces = []
            for c in range(2):
                for k in range(queues):
                    pieces += weights_of(c, t, y, k)
            first = ((tok ^ t) * 2 + (scene ^ y)) * group
            rows = attended[pl.ds(pl.multiple_of(first, 16), group), :]
            term = jnp.dot(jnp.concatenate(pieces, axis=0), rows, preferred_element_type=F32)
            made = term if made is None else made + term
        made = made.astype(BF16).astype(F32)
        total = made if total is None else total + made
    for c in range(2):
        for k in range(queues):
            first = ((q_at ^ k) * 2 + (core ^ c)) * columns
            at = (c * queues + k) * columns
            mixed[pl.ds(pl.multiple_of(first, 8), columns), :] = total[at : at + columns]

    for copy in copies:
        copy.wait()
    levels_all, width = gates.shape
    info = jnp.concatenate([packed[...], following[...]], axis=1)
    lanes = info.shape[1]
    vec = info[:values].astype(BF16)
    ones = jnp.ones((16, lanes), BF16)
    zero = jnp.zeros((13, width), BF16)
    weights = jnp.concatenate([embed[...]] + split_terms(cond[...], 3) + [zero], axis=0)
    emb = dot_tn(weights, jnp.concatenate([vec, ones], axis=0))
    level = info[values : values + 1]
    one_hot = (lax.broadcasted_iota(jnp.int32, (levels_all, lanes), 0).astype(F32) == level).astype(
        F32
    ).astype(BF16)
    gate_terms = jnp.concatenate(split_terms(gates[...], 3), axis=0)
    gate = dot_tn(gate_terms, jnp.concatenate([one_hot] * 3, axis=0))
    gain_terms = jnp.concatenate(split_terms(final_gain[...], 3) + [zero], axis=0)
    gain = dot_tn(gain_terms, ones)
    summed = emb + gate * mixed[...]
    center = jnp.mean(summed, axis=0, keepdims=True)
    deviate = summed - center
    spread = jnp.mean(deviate * deviate, axis=0, keepdims=True)
    final = (deviate * lax.rsqrt(spread + EPS_NORM) * gain).astype(BF16)
    scratch[...] = jnp.dot(final_w[...], final, preferred_element_type=F32)
    own = pl.multiple_of(core * half, half)
    other = pl.multiple_of((1 - core) * half, half)
    mine[...] = scratch[pl.ds(own, half), :]
    send[...] = scratch[pl.ds(other, half), :]

    current = noise_sigma((level + 1.0) / levels_all)
    upcoming = noise_sigma(level / levels_all)
    factor[...] = jnp.broadcast_to(upcoming - current, factor.shape)
    base[...] = jnp.concatenate(
        [packed[pl.ds(own, half), :], following[pl.ds(own, half), :]], axis=1
    )
    noise_out[...] = noise[...]
    guide[...] = jnp.full(guide.shape, table[index[0]], F32)


def update_kernel(mine, partner, base, factor, noise, guide, vel, new):
    frames, _, tokens = vel.shape
    is_cond = place_of("cfg") == 0
    here, there = mine[...], partner[...]
    cond = jnp.where(is_cond, here, there)
    uncond = jnp.where(is_cond, there, here)
    guided = uncond + guide[0:1, 0:1] * (cond - uncond)
    updated = base[...] + factor[...] * guided
    is_last = place_of("queue") == lax.axis_size("queue") - 1
    for f in range(frames):
        vel[f] = guided[:, f * tokens : (f + 1) * tokens]
        moved = updated[:, (f + 1) * tokens : (f + 2) * tokens]
        if f == frames - 1:
            moved = jnp.where(is_last, noise[...], moved)
        new[f] = moved


def swapped(value, axis, mask):
    count = lax.axis_size(axis)
    return lax.ppermute(value, axis, [(i, i ^ mask) for i in range(count)])


def on_device_heads(
    latents,
    fresh_noise,
    levels,
    window_mask,
    cond_embed,
    level_mod,
    embed_weight,
    qkv_weight,
    query_gain,
    key_gain,
    out_weight,
    final_gain,
    final_weight,
    guide_table,
    guide_index,
):
    frames, values, tokens = latents.shape
    width = embed_weight.shape[1]
    head_dim = query_gain.shape[0]
    levels_all = level_mod.shape[0]
    span = window_mask.shape[1]
    window = span // 2
    scenes, queues, toks = (lax.axis_size(a) for a in ("scene", "queue", "tok"))
    chips = scenes * queues * toks
    all_frames = queues * frames
    per_core = frames // 2
    cond_rows = 3 * -(-(width // (queues * toks)) // (per_core * tokens))
    rows = -(-max(values + scenes + 2, values + span + 1 + cond_rows) // 16) * 16
    own_rows = -(-(values + 1) // 8) * 8
    local_rows = qkv_weight.shape[0]
    local_heads = qkv_weight.shape[2] // head_dim
    lanes = scenes * LANES
    row_lanes = (frames + 1) * tokens
    mods = jnp.transpose(level_mod, (1, 0, 2))

    group = out_weight.shape[0] // scenes
    chunk = jax.ShapeDtypeStruct((local_rows, group + 3 * head_dim), BF16)
    *chunks, copies, packed, first = kernel_call(
        functools.partial(pack_kernel, head_dim, per_core),
        [chunk] * queues
        + [
            jax.ShapeDtypeStruct((chips, rows, per_core * tokens), BF16),
            jax.ShapeDtypeStruct((own_rows, frames * tokens), F32),
            jax.ShapeDtypeStruct((own_rows, tokens), F32),
        ],
        "vvvvvv",
        [pltpu.VMEM((local_heads, local_rows, 3 * head_dim), BF16)],
        vmem=WHOLE_VMEM,
        bytes_accessed=8_000_000,
    )(
        latents,
        levels[None],
        window_mask,
        jnp.transpose(qkv_weight, (1, 0, 2)),
        out_weight.T,
        cond_embed,
    )

    near = [chunks[0]] + [swapped(chunks[k], "queue", k) for k in range(1, queues)]
    far = [swapped(piece, "cfg", 1) for piece in near]
    shares = lax.all_to_all(copies, ("scene", "queue", "tok"), 0, 0)
    other_shares = swapped(shares, "cfg", 1)

    part = kernel_call(
        functools.partial(side_kernel, group),
        jax.ShapeDtypeStruct((local_rows, queues * group), BF16),
        "a" + "v" * (queues - 1),
        [pltpu.VMEM(chunk.shape, BF16), pltpu.SemaphoreType.DMA],
    )(*near)
    part_tok, part_scene = swapped(part, "tok", 1), swapped(part, "scene", 1)

    lhs, xin, rstd, masks = kernel_call(
        functools.partial(prepare_kernel, frames, values, span),
        [
            jax.ShapeDtypeStruct((scenes * all_frames * rows, width), BF16),
            jax.ShapeDtypeStruct((scenes, all_frames, rows, LANES), BF16),
            jax.ShapeDtypeStruct((all_frames, 1, lanes), F32),
            jax.ShapeDtypeStruct((scenes, all_frames, rows - values, LANES), F32),
        ],
        "vvav",
        [pltpu.VMEM((2, levels_all, width), F32), pltpu.SemaphoreType.DMA],
        bytes_accessed=8_000_000,
    )(shares, other_shares, mods, embed_weight)
    attended = kernel_call(
        functools.partial(attend_kernel, frames, tokens, queues),
        jax.ShapeDtypeStruct((chips, head_dim, row_lanes), BF16),
        "a" + "v" * (2 * queues + 5),
        [
            pltpu.VMEM((width, 3 * head_dim), BF16),
            pltpu.VMEM((all_frames + 2 * window, 3 * head_dim, lanes), F32),
            pltpu.VMEM((all_frames + 2 * window, 1, lanes), F32),
            pltpu.VMEM((all_frames + 2 * window, 1, lanes), F32),
            pltpu.VMEM((all_frames, scenes, head_dim, LANES), F32),
            pltpu.VMEM(chunk.shape, BF16),
            pltpu.SemaphoreType.DMA,
        ],
        bytes_accessed=100_000_000,
    )(*near, *far, lhs, xin, rstd, masks, query_gain[None], key_gain[None])
    attended, part, part_tok, part_scene, first = lax.optimization_barrier(
        (attended, part, part_tok, part_scene, first)
    )
    received = lax.all_to_all(attended, ("tok", "scene", "queue"), 0, 0)
    following = lax.ppermute(first, "queue", [(i + 1, i) for i in range(queues - 1)])
    cut = -(-local_rows // 32) * 16
    upper = swapped(part_tok[:cut], "scene", 1)
    lower = swapped(part_scene[cut:], "tok", 1)
    token = kernel_call(hold_kernel, jax.ShapeDtypeStruct((8, LANES), F32), "a")(following)
    upper, lower, token = lax.optimization_barrier((upper, lower, token))
    away = [part, part_tok, part_scene, upper, lower]
    away_far = [swapped(piece, "cfg", 1) for piece in away]
    received = received.reshape(width, row_lanes)

    half = values // 2
    half_shape = jax.ShapeDtypeStruct((half, row_lanes), F32)
    smalls = (
        packed,
        following,
        cond_embed,
        mods,
        embed_weight,
        final_gain[None],
        final_weight.T,
        fresh_noise,
    )
    places = [
        pltpu.VMEM(a.shape[1:] if i == 3 else a.shape, a.dtype) for i, a in enumerate(smalls)
    ]
    mine, send, *rest = kernel_call(
        functools.partial(finish_kernel, half, values, queues),
        [half_shape] * 4
        + [
            jax.ShapeDtypeStruct(fresh_noise.shape, F32),
            jax.ShapeDtypeStruct((8, LANES), F32),
        ],
        "v" * 12 + "ss" + "a" * len(smalls),
        places
        + [
            pltpu.VMEM((values, row_lanes), F32),
            pltpu.VMEM((width, row_lanes), F32),
            pltpu.SemaphoreType.DMA((len(smalls),)),
        ],
        bytes_accessed=8_000_000,
    )(*away, *away_far, received, token, guide_table, guide_index, *smalls)
    partner = swapped(send, "cfg", 1)
    shape = jax.ShapeDtypeStruct((frames, half, tokens), F32)
    return kernel_call(update_kernel, [shape, shape], "v" * 6)(mine, partner, *rest)


def on_device(*args):
    latents, qkv_weight, query_gain = args[0], args[7], args[8]
    local_heads = qkv_weight.shape[2] // query_gain.shape[0]
    scenes, queues, toks, cores = (lax.axis_size(a) for a in ("scene", "queue", "tok", "cfg"))
    pairs = scenes == toks == cores == 2 and queues & (queues - 1) == 0
    fits = latents.shape[2] * toks <= LANES and latents.shape[0] % cores == 0
    if pairs and fits and local_heads == scenes * queues:
        return tuple(on_device_heads(*args))
    return on_device_general(*args)


def solution(mesh):
    placed = (
        P(("scene", "queue"), None, "tok"),
        P(("scene", "cfg"), "tok"),
        P(("scene", "queue")),
        P(("scene", "queue"), None),
        P(("scene", "cfg"), None),
        P(),
        P(),
        P(("queue", "cfg"), None, "tok"),
        P(),
        P(),
        P("tok", ("queue", "cfg")),
        P(),
        P(),
        P(),
        P(),
    )
    return jax.shard_map(
        on_device,
        mesh=mesh,
        in_specs=placed,
        out_specs=(P(("scene", "queue"), "cfg", "tok"), P(("scene", "queue"), "cfg", "tok")),
        check_vma=False,
    )
```

```python
import functools

import jax
import jax.numpy as jnp
from jax import lax
from jax.experimental import pallas as pl
from jax.experimental.pallas import tpu as pltpu
from jax.sharding import PartitionSpec as P

EPS_NORM = 1e-06
TIME_SHIFT = 3.0
LANES = 128
VMEM_BYTES = 20 * 1024 * 1024
WHOLE_VMEM = 62 * 1024 * 1024
F32 = jnp.float32
BF16 = jnp.bfloat16


def noise_sigma(fraction):
    return TIME_SHIFT * fraction / (1.0 + (TIME_SHIFT - 1.0) * fraction)


def from_partner(value, axis, bit):
    return lax.ppermute(value, axis, [(i, i ^ 1 << bit) for i in range(lax.axis_size(axis))])


def with_halo(cells, sides, width):
    for axis, dim in sides:
        count = lax.axis_size(axis)
        ends = count - 1
        head = lax.slice_in_dim(cells, 0, width, axis=dim)
        tail = lax.slice_in_dim(cells, cells.shape[dim] - width, cells.shape[dim], axis=dim)
        cells = jnp.concatenate(
            [
                lax.ppermute(tail, axis, [(i, (i + 1) % count) for i in range(ends)]),
                cells,
                lax.ppermute(head, axis, [((i + 1) % count, i) for i in range(ends)]),
            ],
            axis=dim,
        )
    return cells


def shifted(value, axis, steps):
    count = lax.axis_size(axis)
    initial, last = (max(0, -steps), min(count, count - steps))
    return lax.ppermute(value, axis, [(source, source + steps) for source in range(initial, last)])


def layer_norm(values):
    center = jnp.mean(values, axis=-1, keepdims=True)
    deviate = values - center
    spread = jnp.mean(deviate * deviate, axis=-1, keepdims=True)
    return deviate * lax.rsqrt(spread + EPS_NORM)


def rms_norm(values, scaling):
    return (
        values * lax.rsqrt(jnp.mean(values * values, axis=-1, keepdims=True) + EPS_NORM) * scaling
    )


def temporal_attention(
    queries, key_rows, value_rows, window_mask, first_frame, total_frames, window
):
    frames = queries.shape[0]
    numerator = jnp.zeros(queries.shape, jnp.float32)
    denominator = jnp.zeros(queries.shape[:-1], jnp.float32)
    for offset in range(2 * window + 1):
        near_keys = key_rows[offset : offset + frames].astype(jnp.float32)
        near_values = value_rows[offset : offset + frames].astype(jnp.float32)
        scores = jnp.sum(queries * near_keys, axis=-1) * queries.shape[-1] ** (-0.5)
        target = first_frame + jnp.arange(frames, dtype=jnp.int32) + (offset - window)
        allowed = (window_mask[:, offset] == 1) & (target >= 0) & (target < total_frames)
        weights = jnp.exp(scores) * allowed.astype(jnp.float32)[:, None, None]
        numerator = numerator + weights[..., None] * near_values
        denominator = denominator + weights
    return numerator / denominator[..., None]


def on_device_general(
    latents,
    fresh_noise,
    levels,
    window_mask,
    cond_embed,
    level_mod,
    embed_weight,
    qkv_weight,
    query_gain,
    key_gain,
    out_weight,
    final_gain,
    final_weight,
    guide_table,
    guide_index,
):
    frames = latents.shape[0]
    tok_count = latents.shape[2]
    model_width = embed_weight.shape[1]
    head_dim = query_gain.shape[0]
    levels_all = level_mod.shape[0]
    queue_count = lax.axis_size("queue")
    all_tokens = lax.all_gather(latents, "tok", axis=2, tiled=True)
    seq_tokens = all_tokens.shape[2]
    row_count = frames * seq_tokens
    embedded = (
        jnp.einsum(
            "fcs,cd->fsd",
            all_tokens.astype(jnp.bfloat16),
            embed_weight,
            preferred_element_type=jnp.float32,
        )
        + cond_embed[0]
    )
    one_hot = (levels[:, None] == jnp.arange(levels_all, dtype=jnp.int32)[None, :]).astype(
        jnp.float32
    )
    modulate = jnp.dot(
        one_hot, level_mod.reshape(levels_all, 3 * model_width), precision=lax.Precision.HIGHEST
    ).reshape(frames, 3, model_width)
    normed = (layer_norm(embedded) * (1.0 + modulate[:, None, 1]) + modulate[:, None, 0]).astype(
        jnp.bfloat16
    )
    norm_rows = normed.reshape(row_count, model_width)
    local_cols = qkv_weight.shape[2]
    shard_piece = lax.all_gather(qkv_weight, ("queue", "cfg"), axis=0, tiled=True)
    flat_piece = shard_piece.reshape(shard_piece.shape[0], 3 * local_cols)
    projected = jnp.dot(norm_rows, flat_piece, preferred_element_type=jnp.float32)
    projected = projected.reshape(frames, seq_tokens, 3, local_cols // head_dim, head_dim)
    queries = rms_norm(projected[:, :, 0], query_gain)
    keys_values = jnp.stack(
        [
            rms_norm(projected[:, :, 1], key_gain).astype(jnp.bfloat16),
            projected[:, :, 2].astype(jnp.bfloat16),
        ]
    )
    window = window_mask.shape[1] // 2
    widened = with_halo(keys_values, (("queue", 1),), window)
    first_frame = lax.axis_index("queue") * frames
    attended = temporal_attention(
        queries, widened[0], widened[1], window_mask, first_frame, frames * queue_count, window
    )
    attended = attended.astype(jnp.bfloat16).reshape(frames, seq_tokens, local_cols)
    flat_heads = attended.reshape(row_count, local_cols)
    partial_value = jnp.dot(
        flat_heads,
        lax.all_gather(out_weight, ("queue", "cfg"), axis=1, tiled=True),
        preferred_element_type=jnp.float32,
    )
    mixed_out = lax.psum_scatter(
        partial_value.reshape(frames, seq_tokens, model_width).astype(jnp.bfloat16),
        "tok",
        scatter_dimension=1,
        tiled=True,
    ).astype(jnp.float32)
    own_start = lax.axis_index("tok") * tok_count
    own_embed = lax.dynamic_slice_in_dim(embedded, own_start, tok_count, 1)
    summed = own_embed + modulate[:, None, 2] * mixed_out
    final_rows = (layer_norm(summed) * final_gain).astype(jnp.bfloat16)
    velocity = jnp.einsum(
        "ftd,dc->fct", final_rows, final_weight, preferred_element_type=jnp.float32
    )
    half_values = velocity.shape[1] // 2
    branch_index = lax.axis_index("cfg")
    own_first = branch_index * half_values
    other_first = (1 - branch_index) * half_values
    outgoing = lax.dynamic_slice_in_dim(velocity, other_first, half_values, 1)
    partner = from_partner(outgoing, "cfg", 0)
    mine = lax.dynamic_slice_in_dim(velocity, own_first, half_values, 1)
    is_cond = branch_index == 0
    cond_vel = jnp.where(is_cond, mine, partner)
    uncond_vel = jnp.where(is_cond, partner, mine)
    entries = guide_table.shape[0]
    guidance = jnp.sum(
        guide_table * (jnp.arange(entries, dtype=jnp.int32) == guide_index[0]).astype(jnp.float32)
    )
    guided = uncond_vel + guidance * (cond_vel - uncond_vel)
    current = noise_sigma((levels + 1).astype(jnp.float32) / levels_all)
    upcoming = noise_sigma(levels.astype(jnp.float32) / levels_all)
    own_latents = lax.dynamic_slice_in_dim(latents, own_first, half_values, 1)
    updated = own_latents + (upcoming - current)[:, None, None] * guided
    incoming = shifted(updated[:1], "queue", -1)
    is_last = lax.axis_index("queue") == queue_count - 1
    incoming = jnp.where(is_last, fresh_noise[None], incoming)
    new_queue = jnp.concatenate([updated[1:], incoming], axis=0)
    return (guided, new_queue)


def kernel_call(body, out_shapes, spaces, scratch=(), vmem=VMEM_BYTES, **cost):
    kinds = {
        "v": pl.BlockSpec(),
        "s": pl.BlockSpec(memory_space=pltpu.SMEM),
        "a": pl.BlockSpec(memory_space=pl.ANY),
        "h": pl.BlockSpec(memory_space=pltpu.HBM),
    }
    many = isinstance(out_shapes, (list, tuple))
    return pl.pallas_call(
        body,
        out_shape=out_shapes,
        in_specs=[kinds[k] for k in spaces],
        out_specs=[pl.BlockSpec() for _ in out_shapes] if many else pl.BlockSpec(),
        scratch_shapes=list(scratch),
        compiler_params=pltpu.CompilerParams(vmem_limit_bytes=vmem),
        cost_estimate=pl.CostEstimate(
            flops=cost.get("flops", 1000000),
            bytes_accessed=cost.get("bytes_accessed", 1000000),
            transcendentals=0,
        ),
    )


def split_terms(values, terms):
    parts = []
    for _ in range(terms):
        part = values.astype(BF16)
        parts.append(part)
        values = values - part.astype(F32)
    return parts


def dot_tn(left, right):
    return lax.dot_general(
        left, right, (((0,), (0,)), ((), ())), preferred_element_type=F32
    )


def place_of(axis):
    return lax.axis_index(axis)


def pack_kernel(head_dim, copies_frames, latents, levels, window_mask, qkv, out_w, cond, *outs):
    scratch = outs[-1]
    copies, packed, first = outs[-4:-1]
    chunks = outs[:-4]
    scene, q, tok, core = (place_of(a) for a in ("scene", "queue", "tok", "cfg"))
    for h in range(scratch.shape[0]):
        start = h * head_dim
        scratch[h] = jnp.concatenate(
            [qkv[part, :, start : start + head_dim] for part in range(3)], axis=1
        )
    group = out_w.shape[1] // 2
    half = jnp.where(scene == 0, out_w[:, :group], out_w[:, group:])
    for k, chunk in enumerate(chunks):
        chunk[...] = jnp.concatenate([half, scratch[scene * len(chunks) + (q ^ k)]], axis=1)
    frames, values, tokens = latents.shape
    span = window_mask.shape[1]
    shares = []
    own = []
    for f in range(frames):
        level = levels[:, f : f + 1].astype(F32)
        side = jnp.zeros((copies.shape[1] - values, tokens), F32)
        row_id = lax.broadcasted_iota(jnp.int32, side.shape, 0)
        for o in range(span):
            side = jnp.where(row_id == o, window_mask[f : f + 1, o : o + 1].astype(F32), side)
        side = jnp.where(row_id == span, level, side)
        shares.append(jnp.concatenate([latents[f], side], axis=0))
        fill = jnp.broadcast_to(level, (packed.shape[0] - values, tokens))
        own.append(jnp.concatenate([latents[f], fill], axis=0))
    lower = jnp.concatenate(shares[:copies_frames], axis=1)
    upper = jnp.concatenate(shares[copies_frames:], axis=1)
    share = jnp.where(core == 0, lower, upper)
    spots = lax.axis_size("queue") * lax.axis_size("tok")
    length = cond.shape[1] // spots
    piece = jnp.zeros((1, length), F32)
    for i in range(spots):
        chosen = q * lax.axis_size("tok") + tok == i
        piece = jnp.where(chosen, cond[:, i * length : (i + 1) * length], piece)
    row_id = lax.broadcasted_iota(jnp.int32, share.shape, 0)
    at_row, step = values + span + 1, share.shape[1]
    for term in split_terms(piece, 3):
        for start in range(0, length, step):
            line = term.astype(F32)[:, start : start + step]
            fill = jnp.zeros((1, step - line.shape[1]), F32)
            line = jnp.concatenate([line, fill], axis=1) if fill.shape[1] else line
            share = jnp.where(row_id == at_row, line, share)
            at_row += 1
    share = share.astype(BF16)
    for at in range(copies.shape[0]):
        copies[at] = share
    packed[...] = jnp.concatenate(own, axis=1)
    first[...] = own[0]


def prepare_kernel(
    frames,
    values,
    span,
    mine,
    other,
    level_mod,
    embed,
    lhs,
    xin,
    rstd_out,
    mask_out,
):
    width = embed.shape[1]
    scenes, all_frames, rows, _ = xin.shape
    queues = all_frames // frames
    toks = mine.shape[0] // (scenes * queues)
    per_core = frames // 2
    tokens = mine.shape[2] // per_core
    core = place_of("cfg")
    weights = embed[...].astype(F32)
    weights = weights - jnp.mean(weights, axis=1, keepdims=True)
    length, step = width // (queues * toks), mine.shape[2]
    lines = -(-length // step)
    conds = []
    for y in range(scenes):
        pieces = []
        for at in range(y * queues * toks, (y + 1) * queues * toks):
            info = mine[at].astype(F32)
            first = values + span + 1
            terms = sum(info[first + i * lines : first + (i + 1) * lines] for i in range(3))
            for i in range(lines):
                pieces.append(terms[i : i + 1, : min(step, length - i * step)])
        conds.append(jnp.concatenate(pieces, axis=1))
    conds = jnp.concatenate(conds, axis=0)
    conds = conds - jnp.mean(conds, axis=1, keepdims=True)
    basis = jnp.concatenate(
        [weights, conds, jnp.zeros((rows - values - scenes, width), F32)], axis=0
    )
    gram = lax.dot_general(
        basis,
        basis,
        (((1,), (1,)), ((), ())),
        preferred_element_type=F32,
        precision=lax.Precision.HIGHEST,
    ) * (1.0 / width)
    row_id = lax.broadcasted_iota(jnp.int32, (rows, LANES), 0)
    wide_id = lax.broadcasted_iota(jnp.int32, (rows, width), 0)
    level_id = lax.broadcasted_iota(jnp.int32, (level_mod.shape[1], width), 0).astype(F32)
    shift_row = values + scenes
    fill = LANES - toks * tokens
    for y in range(scenes):
        for q in range(queues):
            first = (y * queues + q) * toks
            held = []
            for t in range(toks):
                one, two = mine[first + t].astype(F32), other[first + t].astype(F32)
                held.append((jnp.where(core == 0, one, two), jnp.where(core == 0, two, one)))
            for part in range(frames):
                f = q * frames + part
                at = part % per_core * tokens
                info = [pair[part // per_core][:, at : at + tokens] for pair in held]
                level = info[0][values + span : values + span + 1, 0:1]
                chosen = level_id == level
                shift = jnp.sum(jnp.where(chosen, level_mod[0], 0.0), axis=0, keepdims=True)
                scale = jnp.sum(jnp.where(chosen, level_mod[1], 0.0), axis=0, keepdims=True)
                block = basis * (1.0 + scale)
                block = jnp.where((wide_id == shift_row) | (wide_id == shift_row + 1), shift, block)
                to = (y * all_frames + f) * rows
                lhs[to : to + rows, :] = block.astype(BF16)
                info = jnp.concatenate(info + [jnp.ones((info[0].shape[0], fill), F32)], axis=1)
                mask_out[y, f] = info[values : values + mask_out.shape[2]]
                vec = jnp.where(row_id < values, info[:rows], 0.0)
                vec = jnp.where(row_id == values + y, 1.0, vec)
                spread = jnp.sum(
                    vec
                    * jnp.dot(
                        gram, vec, preferred_element_type=F32, precision=lax.Precision.HIGHEST
                    ),
                    axis=0,
                    keepdims=True,
                )
                spread = jnp.maximum(spread, 0.0) + EPS_NORM
                rstd = lax.rsqrt(spread)
                std = spread * rstd
                high = std.astype(BF16).astype(F32)
                vec = jnp.where(row_id == shift_row, high, vec)
                vec = jnp.where(row_id == shift_row + 1, std - high, vec)
                xin[y, f] = vec.astype(BF16)
                rstd_out[f, :, y * LANES : (y + 1) * LANES] = rstd


def attend_kernel(frames, tokens, queues, *refs):
    pieces = refs[: 2 * queues]
    lhs, xin, rstd_in, mask_in, gain_q, gain_k, out, whole, proj, kfac, vfac, att = refs[
        2 * queues :
    ]
    scenes, all_frames, rows, _ = xin.shape
    head_dim = gain_q.shape[1]
    window = (proj.shape[0] - all_frames) // 2
    span = 2 * window + 1
    q_at, core = place_of("queue"), place_of("cfg")
    part_rows = pieces[0].shape[0]
    for k in range(queues):
        for side in range(2):
            owner = core if side == 0 else 1 - core
            first = pl.multiple_of(((q_at ^ k) * 2 + owner) * part_rows, 16)
            piece = pieces[side * queues + k]
            whole[pl.ds(first, part_rows), :] = piece[:, piece.shape[1] - 3 * head_dim :]
    folded = jnp.dot(lhs[...], whole[...], preferred_element_type=F32)
    high, low = split_terms(folded, 2)
    gains = split_terms(gain_q[...] * gain_k[...] * head_dim ** (-0.5), 3)
    gains = jnp.concatenate(gains + [jnp.zeros((13, head_dim), BF16)], axis=0)
    gains = dot_tn(gains, jnp.ones((16, LANES), BF16))
    for side in range(window):
        for at in (side, all_frames + window + side):
            proj[at] = jnp.zeros(proj.shape[1:], F32)
            kfac[at] = jnp.zeros(kfac.shape[1:], F32)
            vfac[at] = jnp.zeros(vfac.shape[1:], F32)
    for y in range(scenes):
        lane = slice(y * LANES, (y + 1) * LANES)
        for f in range(all_frames):
            first = (y * all_frames + f) * rows
            piece = slice(first, first + rows)
            made = dot_tn(high[piece], xin[y, f]) + dot_tn(low[piece], xin[y, f])
            proj[f + window, :, lane] = made
            rstd = rstd_in[f, :, lane]
            keys = made[head_dim : 2 * head_dim]
            square = jnp.mean(keys * keys, axis=0, keepdims=True)
            kfac[f + window, :, lane] = rstd * lax.rsqrt(rstd * rstd * square + EPS_NORM)
            vfac[f + window, :, lane] = rstd

    def one_frame(f, carry):
        for y in range(scenes):
            lane = slice(y * LANES, (y + 1) * LANES)
            query = proj[f + window, 0:head_dim, lane]
            rstd = vfac[f + window, :, lane]
            square = jnp.mean(query * query, axis=0, keepdims=True)
            qfac = rstd * lax.rsqrt(rstd * rstd * square + EPS_NORM)
            query = query * gains
            total = jnp.zeros((head_dim, LANES), F32)
            norm = jnp.zeros((1, LANES), F32)
            for o in range(span):
                keys = proj[f + o, head_dim : 2 * head_dim, lane]
                score = jnp.sum(query * keys, axis=0, keepdims=True)
                score = score * (qfac * kfac[f + o, :, lane])
                part = jnp.exp(score) * mask_in[y, f, o : o + 1, :]
                norm = norm + part
                total = total + (part * vfac[f + o, :, lane]) * proj[f + o, 2 * head_dim :, lane]
            att[f, y] = total / norm
        return carry

    lax.fori_loop(0, all_frames, one_frame, 0)
    toks = out.shape[0] // (scenes * queues)
    for t in range(toks):
        for y in range(scenes):
            for q in range(queues):
                parts = [
                    att[min(q * frames + i, all_frames - 1), y, :, t * tokens : (t + 1) * tokens]
                    for i in range(frames + 1)
                ]
                at = (t * scenes + y) * queues + q
                out[at] = jnp.concatenate(parts, axis=1).astype(BF16)


def stage_kernel(group, *refs):
    *pieces, level_source, embed_source, out, own, level_mod, embed, sems = refs
    copies = [
        pltpu.make_async_copy(pieces[0], own, sems.at[0]),
        pltpu.make_async_copy(level_source.at[pl.ds(0, 2)], level_mod, sems.at[1]),
        pltpu.make_async_copy(embed_source, embed, sems.at[2]),
    ]
    for copy in copies:
        copy.start()
    for k, piece in reversed(list(enumerate(pieces))):
        if k == 0:
            for copy in copies:
                copy.wait()
            piece = own
        out[:, k * group : (k + 1) * group] = piece[:, :group]


def ready_kernel(values, half, *refs):
    sources, table, index = refs[:8], refs[8], refs[9]
    left, right, base, factor, noise_out, guide, final_out = refs[10:17]
    held, sems = refs[17:25], refs[25]
    copies = []
    for i, (source, to) in enumerate(zip(sources, held)):
        source = source.at[2] if i == 3 else source
        copies.append(pltpu.make_async_copy(source, to, sems.at[i]))
    for copy in copies:
        copy.start()
    for copy in copies:
        copy.wait()
    packed, following, cond, gates, embed, final_gain, final_w, noise = held
    levels_all, width = gates.shape
    info = jnp.concatenate([packed[...], following[...]], axis=1)
    lanes = info.shape[1]
    ones = jnp.ones((16, lanes), BF16)
    zero = jnp.zeros((13, width), BF16)
    left[...] = jnp.concatenate(
        [embed[...]]
        + split_terms(cond[...], 3)
        + [zero]
        + split_terms(gates[...], 3)
        + split_terms(final_gain[...], 3)
        + [zero],
        axis=0,
    )
    level = info[values : values + 1]
    one_hot = (lax.broadcasted_iota(jnp.int32, (levels_all, lanes), 0).astype(F32) == level).astype(
        F32
    ).astype(BF16)
    right[...] = jnp.concatenate(
        [info[:values].astype(BF16), ones, one_hot, one_hot, one_hot, ones], axis=0
    )
    own = pl.multiple_of(place_of("cfg") * half, half)
    current = noise_sigma((level + 1.0) / levels_all)
    upcoming = noise_sigma(level / levels_all)
    factor[...] = jnp.broadcast_to(upcoming - current, factor.shape)
    base[...] = jnp.concatenate(
        [packed[pl.ds(own, half), :], following[pl.ds(own, half), :]], axis=1
    )
    noise_out[...] = noise[...]
    final_out[...] = final_w[...]
    guide[...] = jnp.full(guide.shape, table[index[0]], F32)


def finish_kernel(half, values, queues, *refs):
    parts = [refs[:5], refs[5:10]]
    attended, left, right, final_w, mine, send, scratch, mixed = refs[10:]
    scene, q_at, tok, core = (place_of(a) for a in ("scene", "queue", "tok", "cfg"))
    group = parts[0][0].shape[1] // queues
    columns = parts[0][0].shape[0]

    def weights_of(c, t, y, k):
        lane = slice(k * group, (k + 1) * group)
        if t == y == 1:
            return [parts[c][3][:, lane], parts[c][4][:, lane]]
        return [parts[c][2 * y + t][:, lane]]

    total = None
    for t in range(2):
        made = None
        for y in range(2):
            pieces = []
            for c in range(2):
                for k in range(queues):
                    pieces += weights_of(c, t, y, k)
            first = ((tok ^ t) * 2 + (scene ^ y)) * group
            rows = attended[pl.ds(pl.multiple_of(first, 16), group), :]
            term = jnp.dot(jnp.concatenate(pieces, axis=0), rows, preferred_element_type=F32)
            made = term if made is None else made + term
        made = made.astype(BF16).astype(F32)
        total = made if total is None else total + made
    for c in range(2):
        for k in range(queues):
            first = ((q_at ^ k) * 2 + (core ^ c)) * columns
            at = (c * queues + k) * columns
            mixed[pl.ds(pl.multiple_of(first, 8), columns), :] = total[at : at + columns]

    first, last = values + 16, left.shape[0] - 16
    emb = dot_tn(left[:first], right[:first])
    gate = dot_tn(left[first:last], right[first:last])
    gain = dot_tn(left[last:], right[last:])
    summed = emb + gate * mixed[...]
    center = jnp.mean(summed, axis=0, keepdims=True)
    deviate = summed - center
    spread = jnp.mean(deviate * deviate, axis=0, keepdims=True)
    final = (deviate * lax.rsqrt(spread + EPS_NORM) * gain).astype(BF16)
    scratch[...] = jnp.dot(final_w[...], final, preferred_element_type=F32)
    own = pl.multiple_of(core * half, half)
    other = pl.multiple_of((1 - core) * half, half)
    mine[...] = scratch[pl.ds(own, half), :]
    send[...] = scratch[pl.ds(other, half), :]


def update_kernel(mine, partner, base, factor, noise, guide, vel, new):
    frames, _, tokens = vel.shape
    is_cond = place_of("cfg") == 0
    here, there = mine[...], partner[...]
    cond = jnp.where(is_cond, here, there)
    uncond = jnp.where(is_cond, there, here)
    guided = uncond + guide[0:1, 0:1] * (cond - uncond)
    updated = base[...] + factor[...] * guided
    is_last = place_of("queue") == lax.axis_size("queue") - 1
    for f in range(frames):
        vel[f] = guided[:, f * tokens : (f + 1) * tokens]
        moved = updated[:, (f + 1) * tokens : (f + 2) * tokens]
        if f == frames - 1:
            moved = jnp.where(is_last, noise[...], moved)
        new[f] = moved


def swapped(value, axis, mask):
    count = lax.axis_size(axis)
    return lax.ppermute(value, axis, [(i, i ^ mask) for i in range(count)])


def on_device_heads(
    latents,
    fresh_noise,
    levels,
    window_mask,
    cond_embed,
    level_mod,
    embed_weight,
    qkv_weight,
    query_gain,
    key_gain,
    out_weight,
    final_gain,
    final_weight,
    guide_table,
    guide_index,
):
    frames, values, tokens = latents.shape
    width = embed_weight.shape[1]
    head_dim = query_gain.shape[0]
    levels_all = level_mod.shape[0]
    span = window_mask.shape[1]
    window = span // 2
    scenes, queues, toks = (lax.axis_size(a) for a in ("scene", "queue", "tok"))
    chips = scenes * queues * toks
    all_frames = queues * frames
    per_core = frames // 2
    cond_rows = 3 * -(-(width // (queues * toks)) // (per_core * tokens))
    rows = -(-max(values + scenes + 2, values + span + 1 + cond_rows) // 16) * 16
    own_rows = -(-(values + 1) // 8) * 8
    local_rows = qkv_weight.shape[0]
    local_heads = qkv_weight.shape[2] // head_dim
    lanes = scenes * LANES
    row_lanes = (frames + 1) * tokens
    mods = jnp.transpose(level_mod, (1, 0, 2))

    group = out_weight.shape[0] // scenes
    chunk = jax.ShapeDtypeStruct((local_rows, group + 3 * head_dim), BF16)
    *chunks, copies, packed, first = kernel_call(
        functools.partial(pack_kernel, head_dim, per_core),
        [chunk] * queues
        + [
            jax.ShapeDtypeStruct((chips, rows, per_core * tokens), BF16),
            jax.ShapeDtypeStruct((own_rows, frames * tokens), F32),
            jax.ShapeDtypeStruct((own_rows, tokens), F32),
        ],
        "vvvvvv",
        [pltpu.VMEM((local_heads, local_rows, 3 * head_dim), BF16)],
        vmem=WHOLE_VMEM,
        bytes_accessed=8_000_000,
    )(
        latents,
        levels[None],
        window_mask,
        jnp.transpose(qkv_weight, (1, 0, 2)),
        out_weight.T,
        cond_embed,
    )

    near = [chunks[0]] + [swapped(chunks[k], "queue", k) for k in range(1, queues)]
    far = [swapped(piece, "cfg", 1) for piece in near]
    shares = lax.all_to_all(copies, ("scene", "queue", "tok"), 0, 0)
    other_shares = swapped(shares, "cfg", 1)

    part, own, level_rows, embed_held = kernel_call(
        functools.partial(stage_kernel, group),
        [
            jax.ShapeDtypeStruct((local_rows, queues * group), BF16),
            chunk,
            jax.ShapeDtypeStruct((2, levels_all, width), F32),
            jax.ShapeDtypeStruct(embed_weight.shape, BF16),
        ],
        "h" + "v" * (queues - 1) + "hh",
        [pltpu.SemaphoreType.DMA((3,))],
    )(*near, mods, embed_weight)
    part_tok, part_scene = swapped(part, "tok", 1), swapped(part, "scene", 1)

    lhs, xin, rstd, masks = kernel_call(
        functools.partial(prepare_kernel, frames, values, span),
        [
            jax.ShapeDtypeStruct((scenes * all_frames * rows, width), BF16),
            jax.ShapeDtypeStruct((scenes, all_frames, rows, LANES), BF16),
            jax.ShapeDtypeStruct((all_frames, 1, lanes), F32),
            jax.ShapeDtypeStruct((scenes, all_frames, rows - values, LANES), F32),
        ],
        "vvvv",
        bytes_accessed=8_000_000,
    )(shares, other_shares, level_rows, embed_held)
    attended = kernel_call(
        functools.partial(attend_kernel, frames, tokens, queues),
        jax.ShapeDtypeStruct((chips, head_dim, row_lanes), BF16),
        "v" * (2 * queues + 6),
        [
            pltpu.VMEM((width, 3 * head_dim), BF16),
            pltpu.VMEM((all_frames + 2 * window, 3 * head_dim, lanes), F32),
            pltpu.VMEM((all_frames + 2 * window, 1, lanes), F32),
            pltpu.VMEM((all_frames + 2 * window, 1, lanes), F32),
            pltpu.VMEM((all_frames, scenes, head_dim, LANES), F32),
        ],
        bytes_accessed=100_000_000,
    )(own, *near[1:], *far, lhs, xin, rstd, masks, query_gain[None], key_gain[None])
    attended, part, part_tok, part_scene, first = lax.optimization_barrier(
        (attended, part, part_tok, part_scene, first)
    )
    received = lax.all_to_all(attended, ("tok", "scene", "queue"), 0, 0)
    following = lax.ppermute(first, "queue", [(i + 1, i) for i in range(queues - 1)])
    cut = -(-local_rows // 32) * 16
    upper = swapped(part_tok[:cut], "scene", 1)
    lower = swapped(part_scene[cut:], "tok", 1)
    half = values // 2
    half_shape = jax.ShapeDtypeStruct((half, row_lanes), F32)
    smalls = (
        packed,
        following,
        cond_embed,
        mods,
        embed_weight,
        final_gain[None],
        final_weight.T,
        fresh_noise,
    )
    places = [
        pltpu.VMEM(a.shape[1:] if i == 3 else a.shape, a.dtype) for i, a in enumerate(smalls)
    ]
    terms = values + 16 + 3 * levels_all + 16
    left, right, *rest, final_held = kernel_call(
        functools.partial(ready_kernel, values, half),
        [
            jax.ShapeDtypeStruct((terms, width), BF16),
            jax.ShapeDtypeStruct((terms, row_lanes), BF16),
            half_shape,
            half_shape,
            jax.ShapeDtypeStruct(fresh_noise.shape, F32),
            jax.ShapeDtypeStruct((8, LANES), F32),
            jax.ShapeDtypeStruct((values, width), BF16),
        ],
        "ha" + "h" * 6 + "ss",
        places + [pltpu.SemaphoreType.DMA((len(smalls),))],
    )(*smalls, guide_table, guide_index)
    upper, lower, right = lax.optimization_barrier((upper, lower, right))
    away = [part, part_tok, part_scene, upper, lower]
    away_far = [swapped(piece, "cfg", 1) for piece in away]
    received = received.reshape(width, row_lanes)

    mine, send = kernel_call(
        functools.partial(finish_kernel, half, values, queues),
        [half_shape] * 2,
        "v" * 14,
        [pltpu.VMEM((values, row_lanes), F32), pltpu.VMEM((width, row_lanes), F32)],
        bytes_accessed=8_000_000,
    )(*away, *away_far, received, left, right, final_held)
    partner = swapped(send, "cfg", 1)
    shape = jax.ShapeDtypeStruct((frames, half, tokens), F32)
    return kernel_call(update_kernel, [shape, shape], "v" * 6)(mine, partner, *rest)


def on_device(*args):
    latents, qkv_weight, query_gain = args[0], args[7], args[8]
    local_heads = qkv_weight.shape[2] // query_gain.shape[0]
    scenes, queues, toks, cores = (lax.axis_size(a) for a in ("scene", "queue", "tok", "cfg"))
    pairs = scenes == toks == cores == 2 and queues & (queues - 1) == 0
    fits = latents.shape[2] * toks <= LANES and latents.shape[0] % cores == 0
    if pairs and fits and local_heads == scenes * queues:
        return tuple(on_device_heads(*args))
    return on_device_general(*args)


def solution(mesh):
    placed = (
        P(("scene", "queue"), None, "tok"),
        P(("scene", "cfg"), "tok"),
        P(("scene", "queue")),
        P(("scene", "queue"), None),
        P(("scene", "cfg"), None),
        P(),
        P(),
        P(("queue", "cfg"), None, "tok"),
        P(),
        P(),
        P("tok", ("queue", "cfg")),
        P(),
        P(),
        P(),
        P(),
    )
    return jax.shard_map(
        on_device,
        mesh=mesh,
        in_specs=placed,
        out_specs=(P(("scene", "queue"), "cfg", "tok"), P(("scene", "queue"), "cfg", "tok")),
        check_vma=False,
    )
```

```python
import functools

import jax
import jax.numpy as jnp
from jax import lax
from jax.experimental import pallas as pl
from jax.experimental.pallas import tpu as pltpu
from jax.sharding import PartitionSpec as P

EPS_NORM = 1e-06
TIME_SHIFT = 3.0
LANES = 128
VMEM_BYTES = 20 * 1024 * 1024
WHOLE_VMEM = 62 * 1024 * 1024
F32 = jnp.float32
BF16 = jnp.bfloat16


def noise_sigma(fraction):
    return TIME_SHIFT * fraction / (1.0 + (TIME_SHIFT - 1.0) * fraction)


def from_partner(value, axis, bit):
    return lax.ppermute(value, axis, [(i, i ^ 1 << bit) for i in range(lax.axis_size(axis))])


def with_halo(cells, sides, width):
    for axis, dim in sides:
        count = lax.axis_size(axis)
        ends = count - 1
        head = lax.slice_in_dim(cells, 0, width, axis=dim)
        tail = lax.slice_in_dim(cells, cells.shape[dim] - width, cells.shape[dim], axis=dim)
        cells = jnp.concatenate(
            [
                lax.ppermute(tail, axis, [(i, (i + 1) % count) for i in range(ends)]),
                cells,
                lax.ppermute(head, axis, [((i + 1) % count, i) for i in range(ends)]),
            ],
            axis=dim,
        )
    return cells


def shifted(value, axis, steps):
    count = lax.axis_size(axis)
    initial, last = (max(0, -steps), min(count, count - steps))
    return lax.ppermute(value, axis, [(source, source + steps) for source in range(initial, last)])


def layer_norm(values):
    center = jnp.mean(values, axis=-1, keepdims=True)
    deviate = values - center
    spread = jnp.mean(deviate * deviate, axis=-1, keepdims=True)
    return deviate * lax.rsqrt(spread + EPS_NORM)


def rms_norm(values, scaling):
    return (
        values * lax.rsqrt(jnp.mean(values * values, axis=-1, keepdims=True) + EPS_NORM) * scaling
    )


def temporal_attention(
    queries, key_rows, value_rows, window_mask, first_frame, total_frames, window
):
    frames = queries.shape[0]
    numerator = jnp.zeros(queries.shape, jnp.float32)
    denominator = jnp.zeros(queries.shape[:-1], jnp.float32)
    for offset in range(2 * window + 1):
        near_keys = key_rows[offset : offset + frames].astype(jnp.float32)
        near_values = value_rows[offset : offset + frames].astype(jnp.float32)
        scores = jnp.sum(queries * near_keys, axis=-1) * queries.shape[-1] ** (-0.5)
        target = first_frame + jnp.arange(frames, dtype=jnp.int32) + (offset - window)
        allowed = (window_mask[:, offset] == 1) & (target >= 0) & (target < total_frames)
        weights = jnp.exp(scores) * allowed.astype(jnp.float32)[:, None, None]
        numerator = numerator + weights[..., None] * near_values
        denominator = denominator + weights
    return numerator / denominator[..., None]


def on_device_general(
    latents,
    fresh_noise,
    levels,
    window_mask,
    cond_embed,
    level_mod,
    embed_weight,
    qkv_weight,
    query_gain,
    key_gain,
    out_weight,
    final_gain,
    final_weight,
    guide_table,
    guide_index,
):
    frames = latents.shape[0]
    tok_count = latents.shape[2]
    model_width = embed_weight.shape[1]
    head_dim = query_gain.shape[0]
    levels_all = level_mod.shape[0]
    queue_count = lax.axis_size("queue")
    all_tokens = lax.all_gather(latents, "tok", axis=2, tiled=True)
    seq_tokens = all_tokens.shape[2]
    row_count = frames * seq_tokens
    embedded = (
        jnp.einsum(
            "fcs,cd->fsd",
            all_tokens.astype(jnp.bfloat16),
            embed_weight,
            preferred_element_type=jnp.float32,
        )
        + cond_embed[0]
    )
    one_hot = (levels[:, None] == jnp.arange(levels_all, dtype=jnp.int32)[None, :]).astype(
        jnp.float32
    )
    modulate = jnp.dot(
        one_hot, level_mod.reshape(levels_all, 3 * model_width), precision=lax.Precision.HIGHEST
    ).reshape(frames, 3, model_width)
    normed = (layer_norm(embedded) * (1.0 + modulate[:, None, 1]) + modulate[:, None, 0]).astype(
        jnp.bfloat16
    )
    norm_rows = normed.reshape(row_count, model_width)
    local_cols = qkv_weight.shape[2]
    shard_piece = lax.all_gather(qkv_weight, ("queue", "cfg"), axis=0, tiled=True)
    flat_piece = shard_piece.reshape(shard_piece.shape[0], 3 * local_cols)
    projected = jnp.dot(norm_rows, flat_piece, preferred_element_type=jnp.float32)
    projected = projected.reshape(frames, seq_tokens, 3, local_cols // head_dim, head_dim)
    queries = rms_norm(projected[:, :, 0], query_gain)
    keys_values = jnp.stack(
        [
            rms_norm(projected[:, :, 1], key_gain).astype(jnp.bfloat16),
            projected[:, :, 2].astype(jnp.bfloat16),
        ]
    )
    window = window_mask.shape[1] // 2
    widened = with_halo(keys_values, (("queue", 1),), window)
    first_frame = lax.axis_index("queue") * frames
    attended = temporal_attention(
        queries, widened[0], widened[1], window_mask, first_frame, frames * queue_count, window
    )
    attended = attended.astype(jnp.bfloat16).reshape(frames, seq_tokens, local_cols)
    flat_heads = attended.reshape(row_count, local_cols)
    partial_value = jnp.dot(
        flat_heads,
        lax.all_gather(out_weight, ("queue", "cfg"), axis=1, tiled=True),
        preferred_element_type=jnp.float32,
    )
    mixed_out = lax.psum_scatter(
        partial_value.reshape(frames, seq_tokens, model_width).astype(jnp.bfloat16),
        "tok",
        scatter_dimension=1,
        tiled=True,
    ).astype(jnp.float32)
    own_start = lax.axis_index("tok") * tok_count
    own_embed = lax.dynamic_slice_in_dim(embedded, own_start, tok_count, 1)
    summed = own_embed + modulate[:, None, 2] * mixed_out
    final_rows = (layer_norm(summed) * final_gain).astype(jnp.bfloat16)
    velocity = jnp.einsum(
        "ftd,dc->fct", final_rows, final_weight, preferred_element_type=jnp.float32
    )
    half_values = velocity.shape[1] // 2
    branch_index = lax.axis_index("cfg")
    own_first = branch_index * half_values
    other_first = (1 - branch_index) * half_values
    outgoing = lax.dynamic_slice_in_dim(velocity, other_first, half_values, 1)
    partner = from_partner(outgoing, "cfg", 0)
    mine = lax.dynamic_slice_in_dim(velocity, own_first, half_values, 1)
    is_cond = branch_index == 0
    cond_vel = jnp.where(is_cond, mine, partner)
    uncond_vel = jnp.where(is_cond, partner, mine)
    entries = guide_table.shape[0]
    guidance = jnp.sum(
        guide_table * (jnp.arange(entries, dtype=jnp.int32) == guide_index[0]).astype(jnp.float32)
    )
    guided = uncond_vel + guidance * (cond_vel - uncond_vel)
    current = noise_sigma((levels + 1).astype(jnp.float32) / levels_all)
    upcoming = noise_sigma(levels.astype(jnp.float32) / levels_all)
    own_latents = lax.dynamic_slice_in_dim(latents, own_first, half_values, 1)
    updated = own_latents + (upcoming - current)[:, None, None] * guided
    incoming = shifted(updated[:1], "queue", -1)
    is_last = lax.axis_index("queue") == queue_count - 1
    incoming = jnp.where(is_last, fresh_noise[None], incoming)
    new_queue = jnp.concatenate([updated[1:], incoming], axis=0)
    return (guided, new_queue)


def kernel_call(body, out_shapes, spaces, scratch=(), vmem=VMEM_BYTES, **cost):
    kinds = {
        "v": pl.BlockSpec(),
        "s": pl.BlockSpec(memory_space=pltpu.SMEM),
        "a": pl.BlockSpec(memory_space=pl.ANY),
        "h": pl.BlockSpec(memory_space=pltpu.HBM),
    }
    many = isinstance(out_shapes, (list, tuple))
    return pl.pallas_call(
        body,
        out_shape=out_shapes,
        in_specs=[kinds[k] for k in spaces],
        out_specs=[pl.BlockSpec() for _ in out_shapes] if many else pl.BlockSpec(),
        scratch_shapes=list(scratch),
        compiler_params=pltpu.CompilerParams(vmem_limit_bytes=vmem),
        cost_estimate=pl.CostEstimate(
            flops=cost.get("flops", 1000000),
            bytes_accessed=cost.get("bytes_accessed", 1000000),
            transcendentals=0,
        ),
    )


def split_terms(values, terms):
    parts = []
    for _ in range(terms):
        part = values.astype(BF16)
        parts.append(part)
        values = values - part.astype(F32)
    return parts


def dot_tn(left, right):
    return lax.dot_general(
        left, right, (((0,), (0,)), ((), ())), preferred_element_type=F32
    )


def place_of(axis):
    return lax.axis_index(axis)


def pack_kernel(head_dim, copies_frames, latents, levels, window_mask, qkv, out_w, cond, *outs):
    scratch = outs[-1]
    copies, packed, first = outs[-4:-1]
    chunks = outs[:-4]
    scene, q, tok, core = (place_of(a) for a in ("scene", "queue", "tok", "cfg"))
    for h in range(scratch.shape[0]):
        start = h * head_dim
        scratch[h] = jnp.concatenate(
            [qkv[part, :, start : start + head_dim] for part in range(3)], axis=1
        )
    group = out_w.shape[1] // 2
    half = jnp.where(scene == 0, out_w[:, :group], out_w[:, group:])
    for k, chunk in enumerate(chunks):
        chunk[...] = jnp.concatenate([half, scratch[scene * len(chunks) + (q ^ k)]], axis=1)
    frames, values, tokens = latents.shape
    span = window_mask.shape[1]
    shares = []
    own = []
    for f in range(frames):
        level = levels[:, f : f + 1].astype(F32)
        side = jnp.zeros((copies.shape[1] - values, tokens), F32)
        row_id = lax.broadcasted_iota(jnp.int32, side.shape, 0)
        for o in range(span):
            side = jnp.where(row_id == o, window_mask[f : f + 1, o : o + 1].astype(F32), side)
        side = jnp.where(row_id == span, level, side)
        shares.append(jnp.concatenate([latents[f], side], axis=0))
        fill = jnp.broadcast_to(level, (packed.shape[0] - values, tokens))
        own.append(jnp.concatenate([latents[f], fill], axis=0))
    lower = jnp.concatenate(shares[:copies_frames], axis=1)
    upper = jnp.concatenate(shares[copies_frames:], axis=1)
    share = jnp.where(core == 0, lower, upper)
    spots = lax.axis_size("queue") * lax.axis_size("tok")
    length = cond.shape[1] // spots
    piece = jnp.zeros((1, length), F32)
    for i in range(spots):
        chosen = q * lax.axis_size("tok") + tok == i
        piece = jnp.where(chosen, cond[:, i * length : (i + 1) * length], piece)
    row_id = lax.broadcasted_iota(jnp.int32, share.shape, 0)
    at_row, step = values + span + 1, share.shape[1]
    for term in split_terms(piece, 3):
        for start in range(0, length, step):
            line = term.astype(F32)[:, start : start + step]
            fill = jnp.zeros((1, step - line.shape[1]), F32)
            line = jnp.concatenate([line, fill], axis=1) if fill.shape[1] else line
            share = jnp.where(row_id == at_row, line, share)
            at_row += 1
    share = share.astype(BF16)
    for at in range(copies.shape[0]):
        copies[at] = share
    packed[...] = jnp.concatenate(own, axis=1)
    first[...] = own[0]


def prepare_kernel(
    frames,
    values,
    span,
    mine,
    other,
    level_mod,
    embed,
    lhs,
    xin,
    rstd_out,
    mask_out,
):
    width = embed.shape[1]
    scenes, all_frames = mask_out.shape[:2]
    rows = xin.shape[1] // scenes
    queues = all_frames // frames
    toks = mine.shape[0] // (scenes * queues)
    per_core = frames // 2
    tokens = mine.shape[2] // per_core
    core = place_of("cfg")
    weights = embed[...].astype(F32)
    weights = weights - jnp.mean(weights, axis=1, keepdims=True)
    length, step = width // (queues * toks), mine.shape[2]
    lines = -(-length // step)
    conds = []
    for y in range(scenes):
        pieces = []
        for at in range(y * queues * toks, (y + 1) * queues * toks):
            info = mine[at].astype(F32)
            first = values + span + 1
            terms = sum(info[first + i * lines : first + (i + 1) * lines] for i in range(3))
            for i in range(lines):
                pieces.append(terms[i : i + 1, : min(step, length - i * step)])
        conds.append(jnp.concatenate(pieces, axis=1))
    conds = jnp.concatenate(conds, axis=0)
    conds = conds - jnp.mean(conds, axis=1, keepdims=True)
    basis = jnp.concatenate(
        [weights, conds, jnp.zeros((rows - values - scenes, width), F32)], axis=0
    )
    gram = lax.dot_general(
        basis,
        basis,
        (((1,), (1,)), ((), ())),
        preferred_element_type=F32,
        precision=lax.Precision.HIGHEST,
    ) * (1.0 / width)
    row_id = lax.broadcasted_iota(jnp.int32, (rows, LANES), 0)
    wide_id = lax.broadcasted_iota(jnp.int32, (rows, width), 0)
    level_id = lax.broadcasted_iota(jnp.int32, (level_mod.shape[1], width), 0).astype(F32)
    shift_row = values + scenes
    fill = LANES - toks * tokens
    for y in range(scenes):
        for q in range(queues):
            first = (y * queues + q) * toks
            held = []
            for t in range(toks):
                one, two = mine[first + t].astype(F32), other[first + t].astype(F32)
                held.append((jnp.where(core == 0, one, two), jnp.where(core == 0, two, one)))
            for part in range(frames):
                f = q * frames + part
                at = part % per_core * tokens
                info = [pair[part // per_core][:, at : at + tokens] for pair in held]
                level = info[0][values + span : values + span + 1, 0:1]
                chosen = level_id == level
                shift = jnp.sum(jnp.where(chosen, level_mod[0], 0.0), axis=0, keepdims=True)
                scale = jnp.sum(jnp.where(chosen, level_mod[1], 0.0), axis=0, keepdims=True)
                block = basis * (1.0 + scale)
                block = jnp.where((wide_id == shift_row) | (wide_id == shift_row + 1), shift, block)
                to = (f * scenes + y) * rows
                lhs[to : to + rows, :] = block.astype(BF16)
                info = jnp.concatenate(info + [jnp.ones((info[0].shape[0], fill), F32)], axis=1)
                mask_out[y, f] = info[values : values + mask_out.shape[2]]
                vec = jnp.where(row_id < values, info[:rows], 0.0)
                vec = jnp.where(row_id == values + y, 1.0, vec)
                spread = jnp.sum(
                    vec
                    * jnp.dot(
                        gram, vec, preferred_element_type=F32, precision=lax.Precision.HIGHEST
                    ),
                    axis=0,
                    keepdims=True,
                )
                spread = jnp.maximum(spread, 0.0) + EPS_NORM
                rstd = lax.rsqrt(spread)
                std = spread * rstd
                high = std.astype(BF16).astype(F32)
                vec = jnp.where(row_id == shift_row, high, vec)
                vec = jnp.where(row_id == shift_row + 1, std - high, vec)
                blank = jnp.zeros(vec.shape, F32)
                blocks = [vec if n == y else blank for n in range(scenes)]
                xin[f, y * rows : (y + 1) * rows] = jnp.concatenate(blocks, axis=1).astype(BF16)
                rstd_out[f, :, y * LANES : (y + 1) * LANES] = rstd


def attend_kernel(frames, tokens, queues, *refs):
    pieces = refs[: 2 * queues]
    lhs, xin, rstd_in, mask_in, gain_q, gain_k, out, whole, proj, kfac, vfac, att = refs[
        2 * queues :
    ]
    scenes, all_frames = mask_in.shape[:2]
    rows = xin.shape[1]
    head_dim = gain_q.shape[1]
    window = (proj.shape[0] - all_frames) // 2
    span = 2 * window + 1
    q_at, core = place_of("queue"), place_of("cfg")
    part_rows = pieces[0].shape[0]
    for k in range(queues):
        for side in range(2):
            owner = core if side == 0 else 1 - core
            first = pl.multiple_of(((q_at ^ k) * 2 + owner) * part_rows, 16)
            piece = pieces[side * queues + k]
            whole[pl.ds(first, part_rows), :] = piece[:, piece.shape[1] - 3 * head_dim :]
    folded = jnp.dot(lhs[...], whole[...], preferred_element_type=F32)
    high, low = split_terms(folded, 2)
    gains = split_terms(gain_q[...] * gain_k[...] * head_dim ** (-0.5), 3)
    gains = jnp.concatenate(gains + [jnp.zeros((13, head_dim), BF16)], axis=0)
    gains = dot_tn(gains, jnp.ones((16, LANES), BF16))
    for side in range(window):
        for at in (side, all_frames + window + side):
            proj[at] = jnp.zeros(proj.shape[1:], F32)
            kfac[at] = jnp.zeros(kfac.shape[1:], F32)
            vfac[at] = jnp.zeros(vfac.shape[1:], F32)
    for f in range(all_frames):
        piece = slice(f * rows, (f + 1) * rows)
        made = dot_tn(
            jnp.concatenate([high[piece], low[piece]], axis=0),
            jnp.concatenate([xin[f], xin[f]], axis=0),
        )
        proj[f + window] = made
        rstd = rstd_in[f]
        keys = made[head_dim : 2 * head_dim]
        square = jnp.mean(keys * keys, axis=0, keepdims=True)
        kfac[f + window] = rstd * lax.rsqrt(rstd * rstd * square + EPS_NORM)
        vfac[f + window] = rstd

    def one_frame(f, carry):
        for y in range(scenes):
            lane = slice(y * LANES, (y + 1) * LANES)
            query = proj[f + window, 0:head_dim, lane]
            rstd = vfac[f + window, :, lane]
            square = jnp.mean(query * query, axis=0, keepdims=True)
            qfac = rstd * lax.rsqrt(rstd * rstd * square + EPS_NORM)
            query = query * gains
            total = jnp.zeros((head_dim, LANES), F32)
            norm = jnp.zeros((1, LANES), F32)
            for o in range(span):
                keys = proj[f + o, head_dim : 2 * head_dim, lane]
                score = jnp.sum(query * keys, axis=0, keepdims=True)
                score = score * (qfac * kfac[f + o, :, lane])
                part = jnp.exp(score) * mask_in[y, f, o : o + 1, :]
                norm = norm + part
                total = total + (part * vfac[f + o, :, lane]) * proj[f + o, 2 * head_dim :, lane]
            att[f, y] = total * (1.0 / norm)
        return carry

    lax.fori_loop(0, all_frames, one_frame, 0)
    toks = out.shape[0] // (scenes * queues)
    for t in range(toks):
        for y in range(scenes):
            for q in range(queues):
                parts = [
                    att[min(q * frames + i, all_frames - 1), y, :, t * tokens : (t + 1) * tokens]
                    for i in range(frames + 1)
                ]
                at = (t * queues + q) * scenes + y
                out[at] = jnp.concatenate(parts, axis=1).astype(BF16)


def stage_kernel(group, *refs):
    *pieces, level_source, embed_source, out, own, level_mod, embed, sems = refs
    copies = [
        pltpu.make_async_copy(pieces[0], own, sems.at[0]),
        pltpu.make_async_copy(level_source.at[pl.ds(0, 2)], level_mod, sems.at[1]),
        pltpu.make_async_copy(embed_source, embed, sems.at[2]),
    ]
    for copy in copies:
        copy.start()
    for k, piece in reversed(list(enumerate(pieces))):
        if k == 0:
            for copy in copies:
                copy.wait()
            piece = own
        out[:, k * group : (k + 1) * group] = piece[:, :group]


def ready_kernel(values, half, *refs):
    sources, table, index = refs[:8], refs[8], refs[9]
    left, right, base, factor, noise_out, guide, final_out = refs[10:17]
    held, sems = refs[17:25], refs[25]
    copies = []
    for i, (source, to) in enumerate(zip(sources, held)):
        source = source.at[2] if i == 3 else source
        copies.append(pltpu.make_async_copy(source, to, sems.at[i]))
    for copy in copies:
        copy.start()
    for copy in copies:
        copy.wait()
    packed, following, cond, gates, embed, final_gain, final_w, noise = held
    levels_all, width = gates.shape
    info = jnp.concatenate([packed[...], following[...]], axis=1)
    lanes = info.shape[1]
    ones = jnp.ones((16, lanes), BF16)
    zero = jnp.zeros((13, width), BF16)
    left[...] = jnp.concatenate(
        [embed[...]]
        + split_terms(cond[...], 3)
        + [zero]
        + split_terms(gates[...], 3)
        + split_terms(final_gain[...], 3)
        + [zero],
        axis=0,
    )
    level = info[values : values + 1]
    one_hot = (lax.broadcasted_iota(jnp.int32, (levels_all, lanes), 0).astype(F32) == level).astype(
        F32
    ).astype(BF16)
    right[...] = jnp.concatenate(
        [info[:values].astype(BF16), ones, one_hot, one_hot, one_hot, ones], axis=0
    )
    own = pl.multiple_of(place_of("cfg") * half, half)
    current = noise_sigma((level + 1.0) / levels_all)
    upcoming = noise_sigma(level / levels_all)
    factor[...] = jnp.broadcast_to(upcoming - current, factor.shape)
    base[...] = jnp.concatenate(
        [packed[pl.ds(own, half), :], following[pl.ds(own, half), :]], axis=1
    )
    noise_out[...] = noise[...]
    final_out[...] = final_w[...]
    guide[...] = jnp.full(guide.shape, table[index[0]], F32)


def finish_kernel(half, values, queues, *refs):
    parts = [refs[:5], refs[5:10]]
    attended, left, right, final_w, mine, send, scratch, mixed = refs[10:]
    scene, q_at, tok, core = (place_of(a) for a in ("scene", "queue", "tok", "cfg"))
    group = parts[0][0].shape[1] // queues
    columns = parts[0][0].shape[0]

    def weights_of(c, t, y, k):
        lane = slice(k * group, (k + 1) * group)
        if t == y == 1:
            return [parts[c][3][:, lane], parts[c][4][:, lane]]
        return [parts[c][2 * y + t][:, lane]]

    total = None
    for t in range(2):
        made = None
        for y in range(2):
            pieces = []
            for c in range(2):
                for k in range(queues):
                    pieces += weights_of(c, t, y, k)
            rows = [
                attended[((tok ^ t) * queues + k) * 2 + (scene ^ y)].astype(F32)
                for k in range(queues)
            ]
            rows = jnp.concatenate(rows, axis=0).astype(BF16)
            term = jnp.dot(jnp.concatenate(pieces, axis=0), rows, preferred_element_type=F32)
            made = term if made is None else made + term
        made = made.astype(BF16).astype(F32)
        total = made if total is None else total + made
    for c in range(2):
        for k in range(queues):
            first = ((q_at ^ k) * 2 + (core ^ c)) * columns
            at = (c * queues + k) * columns
            mixed[pl.ds(pl.multiple_of(first, 8), columns), :] = total[at : at + columns]

    first, last = values + 16, left.shape[0] - 16
    emb = dot_tn(left[:first], right[:first])
    gate = dot_tn(left[first:last], right[first:last])
    gain = dot_tn(left[last:], right[last:])
    summed = emb + gate * mixed[...]
    center = jnp.mean(summed, axis=0, keepdims=True)
    deviate = summed - center
    spread = jnp.mean(deviate * deviate, axis=0, keepdims=True)
    final = (deviate * lax.rsqrt(spread + EPS_NORM) * gain).astype(BF16)
    scratch[...] = jnp.dot(final_w[...], final, preferred_element_type=F32)
    own = pl.multiple_of(core * half, half)
    other = pl.multiple_of((1 - core) * half, half)
    mine[...] = scratch[pl.ds(own, half), :]
    send[...] = scratch[pl.ds(other, half), :]


def update_kernel(mine, partner, base, factor, noise, guide, vel, new):
    frames, _, tokens = vel.shape
    is_cond = place_of("cfg") == 0
    here, there = mine[...], partner[...]
    cond = jnp.where(is_cond, here, there)
    uncond = jnp.where(is_cond, there, here)
    guided = uncond + guide[0:1, 0:1] * (cond - uncond)
    updated = base[...] + factor[...] * guided
    is_last = place_of("queue") == lax.axis_size("queue") - 1
    for f in range(frames):
        vel[f] = guided[:, f * tokens : (f + 1) * tokens]
        moved = updated[:, (f + 1) * tokens : (f + 2) * tokens]
        if f == frames - 1:
            moved = jnp.where(is_last, noise[...], moved)
        new[f] = moved


def swapped(value, axis, mask):
    count = lax.axis_size(axis)
    return lax.ppermute(value, axis, [(i, i ^ mask) for i in range(count)])


def on_device_heads(
    latents,
    fresh_noise,
    levels,
    window_mask,
    cond_embed,
    level_mod,
    embed_weight,
    qkv_weight,
    query_gain,
    key_gain,
    out_weight,
    final_gain,
    final_weight,
    guide_table,
    guide_index,
):
    frames, values, tokens = latents.shape
    width = embed_weight.shape[1]
    head_dim = query_gain.shape[0]
    levels_all = level_mod.shape[0]
    span = window_mask.shape[1]
    window = span // 2
    scenes, queues, toks = (lax.axis_size(a) for a in ("scene", "queue", "tok"))
    chips = scenes * queues * toks
    all_frames = queues * frames
    per_core = frames // 2
    cond_rows = 3 * -(-(width // (queues * toks)) // (per_core * tokens))
    rows = -(-max(values + scenes + 2, values + span + 1 + cond_rows) // 16) * 16
    own_rows = -(-(values + 1) // 8) * 8
    local_rows = qkv_weight.shape[0]
    local_heads = qkv_weight.shape[2] // head_dim
    lanes = scenes * LANES
    row_lanes = (frames + 1) * tokens
    mods = jnp.transpose(level_mod, (1, 0, 2))

    group = out_weight.shape[0] // scenes
    chunk = jax.ShapeDtypeStruct((local_rows, group + 3 * head_dim), BF16)
    *chunks, copies, packed, first = kernel_call(
        functools.partial(pack_kernel, head_dim, per_core),
        [chunk] * queues
        + [
            jax.ShapeDtypeStruct((chips, rows, per_core * tokens), BF16),
            jax.ShapeDtypeStruct((own_rows, frames * tokens), F32),
            jax.ShapeDtypeStruct((own_rows, tokens), F32),
        ],
        "vvvvvv",
        [pltpu.VMEM((local_heads, local_rows, 3 * head_dim), BF16)],
        vmem=WHOLE_VMEM,
        bytes_accessed=8_000_000,
    )(
        latents,
        levels[None],
        window_mask,
        jnp.transpose(qkv_weight, (1, 0, 2)),
        out_weight.T,
        cond_embed,
    )

    near = [chunks[0]] + [swapped(chunks[k], "queue", k) for k in range(1, queues)]
    far = [swapped(piece, "cfg", 1) for piece in near]
    shares = lax.all_to_all(copies, ("scene", "queue", "tok"), 0, 0)
    other_shares = swapped(shares, "cfg", 1)

    part, own, level_rows, embed_held = kernel_call(
        functools.partial(stage_kernel, group),
        [
            jax.ShapeDtypeStruct((local_rows, queues * group), BF16),
            chunk,
            jax.ShapeDtypeStruct((2, levels_all, width), F32),
            jax.ShapeDtypeStruct(embed_weight.shape, BF16),
        ],
        "h" + "v" * (queues - 1) + "hh",
        [pltpu.SemaphoreType.DMA((3,))],
    )(*near, mods, embed_weight)
    part_tok, part_scene = swapped(part, "tok", 1), swapped(part, "scene", 1)

    lhs, xin, rstd, masks = kernel_call(
        functools.partial(prepare_kernel, frames, values, span),
        [
            jax.ShapeDtypeStruct((scenes * all_frames * rows, width), BF16),
            jax.ShapeDtypeStruct((all_frames, scenes * rows, lanes), BF16),
            jax.ShapeDtypeStruct((all_frames, 1, lanes), F32),
            jax.ShapeDtypeStruct((scenes, all_frames, rows - values, LANES), F32),
        ],
        "vvvv",
        bytes_accessed=8_000_000,
    )(shares, other_shares, level_rows, embed_held)
    attended = kernel_call(
        functools.partial(attend_kernel, frames, tokens, queues),
        jax.ShapeDtypeStruct((chips, head_dim, row_lanes), BF16),
        "v" * (2 * queues + 6),
        [
            pltpu.VMEM((width, 3 * head_dim), BF16),
            pltpu.VMEM((all_frames + 2 * window, 3 * head_dim, lanes), F32),
            pltpu.VMEM((all_frames + 2 * window, 1, lanes), F32),
            pltpu.VMEM((all_frames + 2 * window, 1, lanes), F32),
            pltpu.VMEM((all_frames, scenes, head_dim, LANES), F32),
        ],
        bytes_accessed=100_000_000,
    )(own, *near[1:], *far, lhs, xin, rstd, masks, query_gain[None], key_gain[None])
    attended, part, part_tok, part_scene, first = lax.optimization_barrier(
        (attended, part, part_tok, part_scene, first)
    )
    received = lax.all_to_all(attended, ("tok", "queue", "scene"), 0, 0)
    following = lax.ppermute(first, "queue", [(i + 1, i) for i in range(queues - 1)])
    cut = -(-local_rows // 32) * 16
    upper = swapped(part_tok[:cut], "scene", 1)
    lower = swapped(part_scene[cut:], "tok", 1)
    half = values // 2
    half_shape = jax.ShapeDtypeStruct((half, row_lanes), F32)
    smalls = (
        packed,
        following,
        cond_embed,
        mods,
        embed_weight,
        final_gain[None],
        final_weight.T,
        fresh_noise,
    )
    places = [
        pltpu.VMEM(a.shape[1:] if i == 3 else a.shape, a.dtype) for i, a in enumerate(smalls)
    ]
    terms = values + 16 + 3 * levels_all + 16
    left, right, *rest, final_held = kernel_call(
        functools.partial(ready_kernel, values, half),
        [
            jax.ShapeDtypeStruct((terms, width), BF16),
            jax.ShapeDtypeStruct((terms, row_lanes), BF16),
            half_shape,
            half_shape,
            jax.ShapeDtypeStruct(fresh_noise.shape, F32),
            jax.ShapeDtypeStruct((8, LANES), F32),
            jax.ShapeDtypeStruct((values, width), BF16),
        ],
        "ha" + "h" * 6 + "ss",
        places + [pltpu.SemaphoreType.DMA((len(smalls),))],
    )(*smalls, guide_table, guide_index)
    upper, lower, right = lax.optimization_barrier((upper, lower, right))
    away = [part, part_tok, part_scene, upper, lower]
    away_far = [swapped(piece, "cfg", 1) for piece in away]

    mine, send = kernel_call(
        functools.partial(finish_kernel, half, values, queues),
        [half_shape] * 2,
        "v" * 14,
        [pltpu.VMEM((values, row_lanes), F32), pltpu.VMEM((width, row_lanes), F32)],
        bytes_accessed=8_000_000,
    )(*away, *away_far, received, left, right, final_held)
    partner = swapped(send, "cfg", 1)
    shape = jax.ShapeDtypeStruct((frames, half, tokens), F32)
    return kernel_call(update_kernel, [shape, shape], "v" * 6)(mine, partner, *rest)


def on_device(*args):
    latents, qkv_weight, query_gain = args[0], args[7], args[8]
    local_heads = qkv_weight.shape[2] // query_gain.shape[0]
    scenes, queues, toks, cores = (lax.axis_size(a) for a in ("scene", "queue", "tok", "cfg"))
    pairs = scenes == toks == cores == 2 and queues & (queues - 1) == 0
    fits = latents.shape[2] * toks <= LANES and latents.shape[0] % cores == 0
    if pairs and fits and local_heads == scenes * queues:
        return tuple(on_device_heads(*args))
    return on_device_general(*args)


def solution(mesh):
    placed = (
        P(("scene", "queue"), None, "tok"),
        P(("scene", "cfg"), "tok"),
        P(("scene", "queue")),
        P(("scene", "queue"), None),
        P(("scene", "cfg"), None),
        P(),
        P(),
        P(("queue", "cfg"), None, "tok"),
        P(),
        P(),
        P("tok", ("queue", "cfg")),
        P(),
        P(),
        P(),
        P(),
    )
    return jax.shard_map(
        on_device,
        mesh=mesh,
        in_specs=placed,
        out_specs=(P(("scene", "queue"), "cfg", "tok"), P(("scene", "queue"), "cfg", "tok")),
        check_vma=False,
    )
```

```python
import functools

import jax
import jax.numpy as jnp
from jax import lax
from jax.experimental import pallas as pl
from jax.experimental.pallas import tpu as pltpu
from jax.sharding import PartitionSpec as P

EPS_NORM = 1e-06
TIME_SHIFT = 3.0
LANES = 128
VMEM_BYTES = 20 * 1024 * 1024
WHOLE_VMEM = 62 * 1024 * 1024
F32 = jnp.float32
BF16 = jnp.bfloat16


def noise_sigma(fraction):
    return TIME_SHIFT * fraction / (1.0 + (TIME_SHIFT - 1.0) * fraction)


def from_partner(value, axis, bit):
    return lax.ppermute(value, axis, [(i, i ^ 1 << bit) for i in range(lax.axis_size(axis))])


def with_halo(cells, sides, width):
    for axis, dim in sides:
        count = lax.axis_size(axis)
        ends = count - 1
        head = lax.slice_in_dim(cells, 0, width, axis=dim)
        tail = lax.slice_in_dim(cells, cells.shape[dim] - width, cells.shape[dim], axis=dim)
        cells = jnp.concatenate(
            [
                lax.ppermute(tail, axis, [(i, (i + 1) % count) for i in range(ends)]),
                cells,
                lax.ppermute(head, axis, [((i + 1) % count, i) for i in range(ends)]),
            ],
            axis=dim,
        )
    return cells


def shifted(value, axis, steps):
    count = lax.axis_size(axis)
    initial, last = (max(0, -steps), min(count, count - steps))
    return lax.ppermute(value, axis, [(source, source + steps) for source in range(initial, last)])


def layer_norm(values):
    center = jnp.mean(values, axis=-1, keepdims=True)
    deviate = values - center
    spread = jnp.mean(deviate * deviate, axis=-1, keepdims=True)
    return deviate * lax.rsqrt(spread + EPS_NORM)


def rms_norm(values, scaling):
    return (
        values * lax.rsqrt(jnp.mean(values * values, axis=-1, keepdims=True) + EPS_NORM) * scaling
    )


def temporal_attention(
    queries, key_rows, value_rows, window_mask, first_frame, total_frames, window
):
    frames = queries.shape[0]
    numerator = jnp.zeros(queries.shape, jnp.float32)
    denominator = jnp.zeros(queries.shape[:-1], jnp.float32)
    for offset in range(2 * window + 1):
        near_keys = key_rows[offset : offset + frames].astype(jnp.float32)
        near_values = value_rows[offset : offset + frames].astype(jnp.float32)
        scores = jnp.sum(queries * near_keys, axis=-1) * queries.shape[-1] ** (-0.5)
        target = first_frame + jnp.arange(frames, dtype=jnp.int32) + (offset - window)
        allowed = (window_mask[:, offset] == 1) & (target >= 0) & (target < total_frames)
        weights = jnp.exp(scores) * allowed.astype(jnp.float32)[:, None, None]
        numerator = numerator + weights[..., None] * near_values
        denominator = denominator + weights
    return numerator / denominator[..., None]


def on_device_general(
    latents,
    fresh_noise,
    levels,
    window_mask,
    cond_embed,
    level_mod,
    embed_weight,
    qkv_weight,
    query_gain,
    key_gain,
    out_weight,
    final_gain,
    final_weight,
    guide_table,
    guide_index,
):
    frames = latents.shape[0]
    tok_count = latents.shape[2]
    model_width = embed_weight.shape[1]
    head_dim = query_gain.shape[0]
    levels_all = level_mod.shape[0]
    queue_count = lax.axis_size("queue")
    all_tokens = lax.all_gather(latents, "tok", axis=2, tiled=True)
    seq_tokens = all_tokens.shape[2]
    row_count = frames * seq_tokens
    embedded = (
        jnp.einsum(
            "fcs,cd->fsd",
            all_tokens.astype(jnp.bfloat16),
            embed_weight,
            preferred_element_type=jnp.float32,
        )
        + cond_embed[0]
    )
    one_hot = (levels[:, None] == jnp.arange(levels_all, dtype=jnp.int32)[None, :]).astype(
        jnp.float32
    )
    modulate = jnp.dot(
        one_hot, level_mod.reshape(levels_all, 3 * model_width), precision=lax.Precision.HIGHEST
    ).reshape(frames, 3, model_width)
    normed = (layer_norm(embedded) * (1.0 + modulate[:, None, 1]) + modulate[:, None, 0]).astype(
        jnp.bfloat16
    )
    norm_rows = normed.reshape(row_count, model_width)
    local_cols = qkv_weight.shape[2]
    shard_piece = lax.all_gather(qkv_weight, ("queue", "cfg"), axis=0, tiled=True)
    flat_piece = shard_piece.reshape(shard_piece.shape[0], 3 * local_cols)
    projected = jnp.dot(norm_rows, flat_piece, preferred_element_type=jnp.float32)
    projected = projected.reshape(frames, seq_tokens, 3, local_cols // head_dim, head_dim)
    queries = rms_norm(projected[:, :, 0], query_gain)
    keys_values = jnp.stack(
        [
            rms_norm(projected[:, :, 1], key_gain).astype(jnp.bfloat16),
            projected[:, :, 2].astype(jnp.bfloat16),
        ]
    )
    window = window_mask.shape[1] // 2
    widened = with_halo(keys_values, (("queue", 1),), window)
    first_frame = lax.axis_index("queue") * frames
    attended = temporal_attention(
        queries, widened[0], widened[1], window_mask, first_frame, frames * queue_count, window
    )
    attended = attended.astype(jnp.bfloat16).reshape(frames, seq_tokens, local_cols)
    flat_heads = attended.reshape(row_count, local_cols)
    partial_value = jnp.dot(
        flat_heads,
        lax.all_gather(out_weight, ("queue", "cfg"), axis=1, tiled=True),
        preferred_element_type=jnp.float32,
    )
    mixed_out = lax.psum_scatter(
        partial_value.reshape(frames, seq_tokens, model_width).astype(jnp.bfloat16),
        "tok",
        scatter_dimension=1,
        tiled=True,
    ).astype(jnp.float32)
    own_start = lax.axis_index("tok") * tok_count
    own_embed = lax.dynamic_slice_in_dim(embedded, own_start, tok_count, 1)
    summed = own_embed + modulate[:, None, 2] * mixed_out
    final_rows = (layer_norm(summed) * final_gain).astype(jnp.bfloat16)
    velocity = jnp.einsum(
        "ftd,dc->fct", final_rows, final_weight, preferred_element_type=jnp.float32
    )
    half_values = velocity.shape[1] // 2
    branch_index = lax.axis_index("cfg")
    own_first = branch_index * half_values
    other_first = (1 - branch_index) * half_values
    outgoing = lax.dynamic_slice_in_dim(velocity, other_first, half_values, 1)
    partner = from_partner(outgoing, "cfg", 0)
    mine = lax.dynamic_slice_in_dim(velocity, own_first, half_values, 1)
    is_cond = branch_index == 0
    cond_vel = jnp.where(is_cond, mine, partner)
    uncond_vel = jnp.where(is_cond, partner, mine)
    entries = guide_table.shape[0]
    guidance = jnp.sum(
        guide_table * (jnp.arange(entries, dtype=jnp.int32) == guide_index[0]).astype(jnp.float32)
    )
    guided = uncond_vel + guidance * (cond_vel - uncond_vel)
    current = noise_sigma((levels + 1).astype(jnp.float32) / levels_all)
    upcoming = noise_sigma(levels.astype(jnp.float32) / levels_all)
    own_latents = lax.dynamic_slice_in_dim(latents, own_first, half_values, 1)
    updated = own_latents + (upcoming - current)[:, None, None] * guided
    incoming = shifted(updated[:1], "queue", -1)
    is_last = lax.axis_index("queue") == queue_count - 1
    incoming = jnp.where(is_last, fresh_noise[None], incoming)
    new_queue = jnp.concatenate([updated[1:], incoming], axis=0)
    return (guided, new_queue)


def kernel_call(body, out_shapes, spaces, scratch=(), vmem=VMEM_BYTES, **cost):
    kinds = {
        "v": pl.BlockSpec(),
        "s": pl.BlockSpec(memory_space=pltpu.SMEM),
        "a": pl.BlockSpec(memory_space=pl.ANY),
        "h": pl.BlockSpec(memory_space=pltpu.HBM),
    }
    many = isinstance(out_shapes, (list, tuple))
    return pl.pallas_call(
        body,
        out_shape=out_shapes,
        in_specs=[kinds[k] for k in spaces],
        out_specs=[pl.BlockSpec() for _ in out_shapes] if many else pl.BlockSpec(),
        scratch_shapes=list(scratch),
        compiler_params=pltpu.CompilerParams(vmem_limit_bytes=vmem),
        cost_estimate=pl.CostEstimate(
            flops=cost.get("flops", 1000000),
            bytes_accessed=cost.get("bytes_accessed", 1000000),
            transcendentals=0,
        ),
    )


def split_terms(values, terms):
    parts = []
    for _ in range(terms):
        part = values.astype(BF16)
        parts.append(part)
        values = values - part.astype(F32)
    return parts


def dot_tn(left, right):
    return lax.dot_general(
        left, right, (((0,), (0,)), ((), ())), preferred_element_type=F32
    )


def place_of(axis):
    return lax.axis_index(axis)


def pack_kernel(head_dim, copies_frames, latents, levels, window_mask, qkv, out_w, cond, *outs):
    scratch = outs[-1]
    copies, packed, first = outs[-4:-1]
    chunks = outs[:-4]
    scene, q, tok, core = (place_of(a) for a in ("scene", "queue", "tok", "cfg"))
    for h in range(scratch.shape[0]):
        start = h * head_dim
        scratch[h] = jnp.concatenate(
            [qkv[part, :, start : start + head_dim] for part in range(3)], axis=1
        )
    group = out_w.shape[1] // 2
    half = jnp.where(scene == 0, out_w[:, :group], out_w[:, group:])
    for k, chunk in enumerate(chunks):
        chunk[...] = jnp.concatenate([half, scratch[scene * len(chunks) + (q ^ k)]], axis=1)
    frames, values, tokens = latents.shape
    span = window_mask.shape[1]
    shares = []
    own = []
    for f in range(frames):
        level = levels[:, f : f + 1].astype(F32)
        side = jnp.zeros((copies.shape[1] - values, tokens), F32)
        row_id = lax.broadcasted_iota(jnp.int32, side.shape, 0)
        for o in range(span):
            side = jnp.where(row_id == o, window_mask[f : f + 1, o : o + 1].astype(F32), side)
        side = jnp.where(row_id == span, level, side)
        shares.append(jnp.concatenate([latents[f], side], axis=0))
        fill = jnp.broadcast_to(level, (packed.shape[0] - values, tokens))
        own.append(jnp.concatenate([latents[f], fill], axis=0))
    lower = jnp.concatenate(shares[:copies_frames], axis=1)
    upper = jnp.concatenate(shares[copies_frames:], axis=1)
    share = jnp.where(core == 0, lower, upper)
    spots = lax.axis_size("queue") * lax.axis_size("tok")
    length = cond.shape[1] // spots
    piece = jnp.zeros((1, length), F32)
    for i in range(spots):
        chosen = q * lax.axis_size("tok") + tok == i
        piece = jnp.where(chosen, cond[:, i * length : (i + 1) * length], piece)
    row_id = lax.broadcasted_iota(jnp.int32, share.shape, 0)
    at_row, step = values + span + 1, share.shape[1]
    for term in split_terms(piece, 3):
        for start in range(0, length, step):
            line = term.astype(F32)[:, start : start + step]
            fill = jnp.zeros((1, step - line.shape[1]), F32)
            line = jnp.concatenate([line, fill], axis=1) if fill.shape[1] else line
            share = jnp.where(row_id == at_row, line, share)
            at_row += 1
    share = share.astype(BF16)
    for at in range(copies.shape[0]):
        copies[at] = share
    packed[...] = jnp.concatenate(own, axis=1)
    first[...] = own[0]


def prepare_kernel(
    frames,
    values,
    span,
    mine,
    other,
    level_mod,
    embed,
    lhs,
    xin,
    rstd_out,
    mask_out,
):
    width = embed.shape[1]
    scenes, all_frames = mask_out.shape[:2]
    rows = xin.shape[1] // scenes
    queues = all_frames // frames
    toks = mine.shape[0] // (scenes * queues)
    per_core = frames // 2
    tokens = mine.shape[2] // per_core
    core = place_of("cfg")
    weights = embed[...].astype(F32)
    weights = weights - jnp.mean(weights, axis=1, keepdims=True)
    length, step = width // (queues * toks), mine.shape[2]
    lines = -(-length // step)
    conds = []
    for y in range(scenes):
        pieces = []
        for at in range(y * queues * toks, (y + 1) * queues * toks):
            info = mine[at].astype(F32)
            first = values + span + 1
            terms = sum(info[first + i * lines : first + (i + 1) * lines] for i in range(3))
            for i in range(lines):
                pieces.append(terms[i : i + 1, : min(step, length - i * step)])
        conds.append(jnp.concatenate(pieces, axis=1))
    conds = jnp.concatenate(conds, axis=0)
    conds = conds - jnp.mean(conds, axis=1, keepdims=True)
    basis = jnp.concatenate(
        [weights, conds, jnp.zeros((rows - values - scenes, width), F32)], axis=0
    )
    gram = lax.dot_general(
        basis,
        basis,
        (((1,), (1,)), ((), ())),
        preferred_element_type=F32,
        precision=lax.Precision.HIGHEST,
    ) * (1.0 / width)
    row_id = lax.broadcasted_iota(jnp.int32, (rows, LANES), 0)
    wide_id = lax.broadcasted_iota(jnp.int32, (rows, width), 0)
    level_id = lax.broadcasted_iota(jnp.int32, (level_mod.shape[1], width), 0).astype(F32)
    shift_row = values + scenes
    fill = LANES - toks * tokens
    for y in range(scenes):
        for q in range(queues):
            first = (y * queues + q) * toks
            held = []
            for t in range(toks):
                one, two = mine[first + t].astype(F32), other[first + t].astype(F32)
                held.append((jnp.where(core == 0, one, two), jnp.where(core == 0, two, one)))
            for part in range(frames):
                f = q * frames + part
                at = part % per_core * tokens
                info = [pair[part // per_core][:, at : at + tokens] for pair in held]
                level = info[0][values + span : values + span + 1, 0:1]
                chosen = level_id == level
                shift = jnp.sum(jnp.where(chosen, level_mod[0], 0.0), axis=0, keepdims=True)
                scale = jnp.sum(jnp.where(chosen, level_mod[1], 0.0), axis=0, keepdims=True)
                block = basis * (1.0 + scale)
                block = jnp.where((wide_id == shift_row) | (wide_id == shift_row + 1), shift, block)
                to = (f * scenes + y) * rows
                lhs[to : to + rows, :] = block.astype(BF16)
                info = jnp.concatenate(info + [jnp.ones((info[0].shape[0], fill), F32)], axis=1)
                mask_out[y, f] = info[values : values + mask_out.shape[2]]
                vec = jnp.where(row_id < values, info[:rows], 0.0)
                vec = jnp.where(row_id == values + y, 1.0, vec)
                spread = jnp.sum(
                    vec
                    * jnp.dot(
                        gram, vec, preferred_element_type=F32, precision=lax.Precision.HIGHEST
                    ),
                    axis=0,
                    keepdims=True,
                )
                spread = jnp.maximum(spread, 0.0) + EPS_NORM
                rstd = lax.rsqrt(spread)
                std = spread * rstd
                high = std.astype(BF16).astype(F32)
                vec = jnp.where(row_id == shift_row, high, vec)
                vec = jnp.where(row_id == shift_row + 1, std - high, vec)
                blank = jnp.zeros(vec.shape, F32)
                blocks = [vec if n == y else blank for n in range(scenes)]
                xin[f, y * rows : (y + 1) * rows] = jnp.concatenate(blocks, axis=1).astype(BF16)
                rstd_out[f, :, y * LANES : (y + 1) * LANES] = rstd


def attend_kernel(frames, tokens, queues, *refs):
    pieces = refs[: 2 * queues]
    lhs, xin, rstd_in, mask_in, gain_q, gain_k, out, whole, proj, kfac, vfac, att = refs[
        2 * queues :
    ]
    scenes, all_frames = mask_in.shape[:2]
    rows = xin.shape[1]
    head_dim = gain_q.shape[1]
    window = (proj.shape[0] - all_frames) // 2
    span = 2 * window + 1
    q_at, core = place_of("queue"), place_of("cfg")
    part_rows = pieces[0].shape[0]
    for k in range(queues):
        for side in range(2):
            owner = core if side == 0 else 1 - core
            first = pl.multiple_of(((q_at ^ k) * 2 + owner) * part_rows, 16)
            piece = pieces[side * queues + k]
            whole[pl.ds(first, part_rows), :] = piece[:, piece.shape[1] - 3 * head_dim :]
    folded = jnp.dot(lhs[...], whole[...], preferred_element_type=F32)
    high, low = split_terms(folded, 2)
    gains = split_terms(gain_q[...] * gain_k[...] * head_dim ** (-0.5), 3)
    gains = jnp.concatenate(gains + [jnp.zeros((13, head_dim), BF16)], axis=0)
    gains = dot_tn(gains, jnp.ones((16, LANES), BF16))
    for side in range(window):
        for at in (side, all_frames + window + side):
            proj[at] = jnp.zeros(proj.shape[1:], F32)
            kfac[at] = jnp.zeros(kfac.shape[1:], F32)
            vfac[at] = jnp.zeros(vfac.shape[1:], F32)
    for f in range(all_frames):
        piece = slice(f * rows, (f + 1) * rows)
        made = dot_tn(
            jnp.concatenate([high[piece], low[piece]], axis=0),
            jnp.concatenate([xin[f], xin[f]], axis=0),
        )
        proj[f + window] = made
        rstd = rstd_in[f]
        keys = made[head_dim : 2 * head_dim]
        square = jnp.mean(keys * keys, axis=0, keepdims=True)
        kfac[f + window] = rstd * lax.rsqrt(rstd * rstd * square + EPS_NORM)
        vfac[f + window] = rstd

    def one_frame(f, carry):
        for y in range(scenes):
            lane = slice(y * LANES, (y + 1) * LANES)
            query = proj[f + window, 0:head_dim, lane]
            rstd = vfac[f + window, :, lane]
            square = jnp.mean(query * query, axis=0, keepdims=True)
            qfac = rstd * lax.rsqrt(rstd * rstd * square + EPS_NORM)
            query = query * gains
            total = jnp.zeros((head_dim, LANES), F32)
            norm = jnp.zeros((1, LANES), F32)
            for o in range(span):
                keys = proj[f + o, head_dim : 2 * head_dim, lane]
                score = jnp.sum(query * keys, axis=0, keepdims=True)
                score = score * (qfac * kfac[f + o, :, lane])
                part = jnp.exp(score) * mask_in[y, f, o : o + 1, :]
                norm = norm + part
                total = total + (part * vfac[f + o, :, lane]) * proj[f + o, 2 * head_dim :, lane]
            att[f, y] = total * (1.0 / norm)
        return carry

    lax.fori_loop(0, all_frames, one_frame, 0)
    toks = out.shape[0] // (scenes * queues)
    for t in range(toks):
        for y in range(scenes):
            for q in range(queues):
                parts = [
                    att[min(q * frames + i, all_frames - 1), y, :, t * tokens : (t + 1) * tokens]
                    for i in range(frames + 1)
                ]
                at = (t * queues + q) * scenes + y
                out[at] = jnp.concatenate(parts, axis=1).astype(BF16)


def stage_kernel(own_source, level_source, embed_source, own, level_mod, embed, sems):
    copies = [
        pltpu.make_async_copy(own_source, own, sems.at[0]),
        pltpu.make_async_copy(level_source.at[pl.ds(0, 2)], level_mod, sems.at[1]),
        pltpu.make_async_copy(embed_source, embed, sems.at[2]),
    ]
    for copy in copies:
        copy.start()
    for copy in copies:
        copy.wait()


def side_kernel(group, *refs):
    for k, piece in enumerate(refs[:-1]):
        refs[-1][:, k * group : (k + 1) * group] = piece[:, :group]


def ready_kernel(values, half, *refs):
    sources, table, index = refs[:8], refs[8], refs[9]
    left, right, base, factor, noise_out, guide, final_out = refs[10:17]
    held, sems = refs[17:25], refs[25]
    copies = []
    for i, (source, to) in enumerate(zip(sources, held)):
        source = source.at[2] if i == 3 else source
        copies.append(pltpu.make_async_copy(source, to, sems.at[i]))
    for copy in copies:
        copy.start()
    for copy in copies:
        copy.wait()
    packed, following, cond, gates, embed, final_gain, final_w, noise = held
    levels_all, width = gates.shape
    info = jnp.concatenate([packed[...], following[...]], axis=1)
    lanes = info.shape[1]
    ones = jnp.ones((16, lanes), BF16)
    zero = jnp.zeros((13, width), BF16)
    left[...] = jnp.concatenate(
        [embed[...]]
        + split_terms(cond[...], 3)
        + [zero]
        + split_terms(gates[...], 3)
        + split_terms(final_gain[...], 3)
        + [zero],
        axis=0,
    )
    level = info[values : values + 1]
    one_hot = (lax.broadcasted_iota(jnp.int32, (levels_all, lanes), 0).astype(F32) == level).astype(
        F32
    ).astype(BF16)
    right[...] = jnp.concatenate(
        [info[:values].astype(BF16), ones, one_hot, one_hot, one_hot, ones], axis=0
    )
    own = pl.multiple_of(place_of("cfg") * half, half)
    current = noise_sigma((level + 1.0) / levels_all)
    upcoming = noise_sigma(level / levels_all)
    factor[...] = jnp.broadcast_to(upcoming - current, factor.shape)
    base[...] = jnp.concatenate(
        [packed[pl.ds(own, half), :], following[pl.ds(own, half), :]], axis=1
    )
    noise_out[...] = noise[...]
    final_out[...] = final_w[...]
    guide[...] = jnp.full(guide.shape, table[index[0]], F32)


def finish_kernel(half, values, queues, *refs):
    parts = [refs[:5], refs[5:10]]
    attended, left, right, final_w, mine, send, scratch, mixed = refs[10:]
    scene, q_at, tok, core = (place_of(a) for a in ("scene", "queue", "tok", "cfg"))
    group = parts[0][0].shape[1] // queues
    columns = parts[0][0].shape[0]

    def weights_of(c, t, y, k):
        lane = slice(k * group, (k + 1) * group)
        if t == y == 1:
            return [parts[c][3][:, lane], parts[c][4][:, lane]]
        return [parts[c][2 * y + t][:, lane]]

    total = None
    for t in range(2):
        made = None
        for y in range(2):
            pieces = []
            for c in range(2):
                for k in range(queues):
                    pieces += weights_of(c, t, y, k)
            rows = [
                attended[((tok ^ t) * queues + k) * 2 + (scene ^ y)].astype(F32)
                for k in range(queues)
            ]
            rows = jnp.concatenate(rows, axis=0).astype(BF16)
            term = jnp.dot(jnp.concatenate(pieces, axis=0), rows, preferred_element_type=F32)
            made = term if made is None else made + term
        made = made.astype(BF16).astype(F32)
        total = made if total is None else total + made
    for c in range(2):
        for k in range(queues):
            first = ((q_at ^ k) * 2 + (core ^ c)) * columns
            at = (c * queues + k) * columns
            mixed[pl.ds(pl.multiple_of(first, 8), columns), :] = total[at : at + columns]

    first, last = values + 16, left.shape[0] - 16
    emb = dot_tn(left[:first], right[:first])
    gate = dot_tn(left[first:last], right[first:last])
    gain = dot_tn(left[last:], right[last:])
    summed = emb + gate * mixed[...]
    center = jnp.mean(summed, axis=0, keepdims=True)
    deviate = summed - center
    spread = jnp.mean(deviate * deviate, axis=0, keepdims=True)
    final = (deviate * lax.rsqrt(spread + EPS_NORM) * gain).astype(BF16)
    scratch[...] = jnp.dot(final_w[...], final, preferred_element_type=F32)
    own = pl.multiple_of(core * half, half)
    other = pl.multiple_of((1 - core) * half, half)
    mine[...] = scratch[pl.ds(own, half), :]
    send[...] = scratch[pl.ds(other, half), :]


def update_kernel(mine, partner, base, factor, noise, guide, vel, new):
    frames, _, tokens = vel.shape
    is_cond = place_of("cfg") == 0
    here, there = mine[...], partner[...]
    cond = jnp.where(is_cond, here, there)
    uncond = jnp.where(is_cond, there, here)
    guided = uncond + guide[0:1, 0:1] * (cond - uncond)
    updated = base[...] + factor[...] * guided
    is_last = place_of("queue") == lax.axis_size("queue") - 1
    for f in range(frames):
        vel[f] = guided[:, f * tokens : (f + 1) * tokens]
        moved = updated[:, (f + 1) * tokens : (f + 2) * tokens]
        if f == frames - 1:
            moved = jnp.where(is_last, noise[...], moved)
        new[f] = moved


def swapped(value, axis, mask):
    count = lax.axis_size(axis)
    return lax.ppermute(value, axis, [(i, i ^ mask) for i in range(count)])


def on_device_heads(
    latents,
    fresh_noise,
    levels,
    window_mask,
    cond_embed,
    level_mod,
    embed_weight,
    qkv_weight,
    query_gain,
    key_gain,
    out_weight,
    final_gain,
    final_weight,
    guide_table,
    guide_index,
):
    frames, values, tokens = latents.shape
    width = embed_weight.shape[1]
    head_dim = query_gain.shape[0]
    levels_all = level_mod.shape[0]
    span = window_mask.shape[1]
    window = span // 2
    scenes, queues, toks = (lax.axis_size(a) for a in ("scene", "queue", "tok"))
    chips = scenes * queues * toks
    all_frames = queues * frames
    per_core = frames // 2
    cond_rows = 3 * -(-(width // (queues * toks)) // (per_core * tokens))
    rows = -(-max(values + scenes + 2, values + span + 1 + cond_rows) // 16) * 16
    own_rows = -(-(values + 1) // 8) * 8
    local_rows = qkv_weight.shape[0]
    local_heads = qkv_weight.shape[2] // head_dim
    lanes = scenes * LANES
    row_lanes = (frames + 1) * tokens
    mods = jnp.transpose(level_mod, (1, 0, 2))

    group = out_weight.shape[0] // scenes
    chunk = jax.ShapeDtypeStruct((local_rows, group + 3 * head_dim), BF16)
    *chunks, copies, packed, first = kernel_call(
        functools.partial(pack_kernel, head_dim, per_core),
        [chunk] * queues
        + [
            jax.ShapeDtypeStruct((chips, rows, per_core * tokens), BF16),
            jax.ShapeDtypeStruct((own_rows, frames * tokens), F32),
            jax.ShapeDtypeStruct((own_rows, tokens), F32),
        ],
        "vvvvvv",
        [pltpu.VMEM((local_heads, local_rows, 3 * head_dim), BF16)],
        vmem=WHOLE_VMEM,
        bytes_accessed=8_000_000,
    )(
        latents,
        levels[None],
        window_mask,
        jnp.transpose(qkv_weight, (1, 0, 2)),
        out_weight.T,
        cond_embed,
    )

    near = [chunks[0]] + [swapped(chunks[k], "queue", k) for k in range(1, queues)]
    far = [swapped(piece, "cfg", 1) for piece in near]
    shares = lax.all_to_all(copies, ("scene", "queue", "tok"), 0, 0)
    other_shares = swapped(shares, "cfg", 1)

    own, level_rows, embed_held = kernel_call(
        stage_kernel,
        [
            chunk,
            jax.ShapeDtypeStruct((2, levels_all, width), F32),
            jax.ShapeDtypeStruct(embed_weight.shape, BF16),
        ],
        "hhh",
        [pltpu.SemaphoreType.DMA((3,))],
    )(chunks[0], mods, embed_weight)
    following = lax.ppermute(first, "queue", [(i + 1, i) for i in range(queues - 1)])
    near[-1], following, *far[:-1] = lax.optimization_barrier((near[-1], following, *far[:-1]))
    part = kernel_call(
        functools.partial(side_kernel, group),
        jax.ShapeDtypeStruct((local_rows, queues * group), BF16),
        "v" * queues,
    )(own, *near[1:])
    part_tok, part_scene = swapped(part, "tok", 1), swapped(part, "scene", 1)

    lhs, xin, rstd, masks = kernel_call(
        functools.partial(prepare_kernel, frames, values, span),
        [
            jax.ShapeDtypeStruct((scenes * all_frames * rows, width), BF16),
            jax.ShapeDtypeStruct((all_frames, scenes * rows, lanes), BF16),
            jax.ShapeDtypeStruct((all_frames, 1, lanes), F32),
            jax.ShapeDtypeStruct((scenes, all_frames, rows - values, LANES), F32),
        ],
        "vvvv",
        bytes_accessed=8_000_000,
    )(shares, other_shares, level_rows, embed_held)
    attended = kernel_call(
        functools.partial(attend_kernel, frames, tokens, queues),
        jax.ShapeDtypeStruct((chips, head_dim, row_lanes), BF16),
        "v" * (2 * queues + 6),
        [
            pltpu.VMEM((width, 3 * head_dim), BF16),
            pltpu.VMEM((all_frames + 2 * window, 3 * head_dim, lanes), F32),
            pltpu.VMEM((all_frames + 2 * window, 1, lanes), F32),
            pltpu.VMEM((all_frames + 2 * window, 1, lanes), F32),
            pltpu.VMEM((all_frames, scenes, head_dim, LANES), F32),
        ],
        bytes_accessed=100_000_000,
    )(own, *near[1:], *far, lhs, xin, rstd, masks, query_gain[None], key_gain[None])
    attended, part, part_tok, part_scene = lax.optimization_barrier(
        (attended, part, part_tok, part_scene)
    )
    received = lax.all_to_all(attended, ("tok", "queue", "scene"), 0, 0)
    cut = -(-local_rows // 32) * 16
    upper = swapped(part_tok[:cut], "scene", 1)
    lower = swapped(part_scene[cut:], "tok", 1)
    half = values // 2
    half_shape = jax.ShapeDtypeStruct((half, row_lanes), F32)
    smalls = (
        packed,
        following,
        cond_embed,
        mods,
        embed_weight,
        final_gain[None],
        final_weight.T,
        fresh_noise,
    )
    places = [
        pltpu.VMEM(a.shape[1:] if i == 3 else a.shape, a.dtype) for i, a in enumerate(smalls)
    ]
    terms = values + 16 + 3 * levels_all + 16
    left, right, *rest, final_held = kernel_call(
        functools.partial(ready_kernel, values, half),
        [
            jax.ShapeDtypeStruct((terms, width), BF16),
            jax.ShapeDtypeStruct((terms, row_lanes), BF16),
            half_shape,
            half_shape,
            jax.ShapeDtypeStruct(fresh_noise.shape, F32),
            jax.ShapeDtypeStruct((8, LANES), F32),
            jax.ShapeDtypeStruct((values, width), BF16),
        ],
        "ha" + "h" * 6 + "ss",
        places + [pltpu.SemaphoreType.DMA((len(smalls),))],
    )(*smalls, guide_table, guide_index)
    upper, lower, right = lax.optimization_barrier((upper, lower, right))
    away = [part, part_tok, part_scene, upper, lower]
    away_far = [swapped(piece, "cfg", 1) for piece in away]

    mine, send = kernel_call(
        functools.partial(finish_kernel, half, values, queues),
        [half_shape] * 2,
        "v" * 14,
        [pltpu.VMEM((values, row_lanes), F32), pltpu.VMEM((width, row_lanes), F32)],
        bytes_accessed=8_000_000,
    )(*away, *away_far, received, left, right, final_held)
    partner = swapped(send, "cfg", 1)
    shape = jax.ShapeDtypeStruct((frames, half, tokens), F32)
    return kernel_call(update_kernel, [shape, shape], "v" * 6)(mine, partner, *rest)


def on_device(*args):
    latents, qkv_weight, query_gain = args[0], args[7], args[8]
    local_heads = qkv_weight.shape[2] // query_gain.shape[0]
    scenes, queues, toks, cores = (lax.axis_size(a) for a in ("scene", "queue", "tok", "cfg"))
    pairs = scenes == toks == cores == 2 and queues & (queues - 1) == 0
    fits = latents.shape[2] * toks <= LANES and latents.shape[0] % cores == 0
    if pairs and fits and local_heads == scenes * queues:
        return tuple(on_device_heads(*args))
    return on_device_general(*args)


def solution(mesh):
    placed = (
        P(("scene", "queue"), None, "tok"),
        P(("scene", "cfg"), "tok"),
        P(("scene", "queue")),
        P(("scene", "queue"), None),
        P(("scene", "cfg"), None),
        P(),
        P(),
        P(("queue", "cfg"), None, "tok"),
        P(),
        P(),
        P("tok", ("queue", "cfg")),
        P(),
        P(),
        P(),
        P(),
    )
    return jax.shard_map(
        on_device,
        mesh=mesh,
        in_specs=placed,
        out_specs=(P(("scene", "queue"), "cfg", "tok"), P(("scene", "queue"), "cfg", "tok")),
        check_vma=False,
    )
```

```python
import functools

import jax
import jax.numpy as jnp
from jax import lax
from jax.experimental import pallas as pl
from jax.experimental.pallas import tpu as pltpu
from jax.sharding import PartitionSpec as P

EPS_NORM = 1e-06
TIME_SHIFT = 3.0
LANES = 128
VMEM_BYTES = 20 * 1024 * 1024
WHOLE_VMEM = 62 * 1024 * 1024
F32 = jnp.float32
BF16 = jnp.bfloat16


def noise_sigma(fraction):
    return TIME_SHIFT * fraction / (1.0 + (TIME_SHIFT - 1.0) * fraction)


def from_partner(value, axis, bit):
    return lax.ppermute(value, axis, [(i, i ^ 1 << bit) for i in range(lax.axis_size(axis))])


def with_halo(cells, sides, width):
    for axis, dim in sides:
        count = lax.axis_size(axis)
        ends = count - 1
        head = lax.slice_in_dim(cells, 0, width, axis=dim)
        tail = lax.slice_in_dim(cells, cells.shape[dim] - width, cells.shape[dim], axis=dim)
        cells = jnp.concatenate(
            [
                lax.ppermute(tail, axis, [(i, (i + 1) % count) for i in range(ends)]),
                cells,
                lax.ppermute(head, axis, [((i + 1) % count, i) for i in range(ends)]),
            ],
            axis=dim,
        )
    return cells


def shifted(value, axis, steps):
    count = lax.axis_size(axis)
    initial, last = (max(0, -steps), min(count, count - steps))
    return lax.ppermute(value, axis, [(source, source + steps) for source in range(initial, last)])


def layer_norm(values):
    center = jnp.mean(values, axis=-1, keepdims=True)
    deviate = values - center
    spread = jnp.mean(deviate * deviate, axis=-1, keepdims=True)
    return deviate * lax.rsqrt(spread + EPS_NORM)


def rms_norm(values, scaling):
    return (
        values * lax.rsqrt(jnp.mean(values * values, axis=-1, keepdims=True) + EPS_NORM) * scaling
    )


def temporal_attention(
    queries, key_rows, value_rows, window_mask, first_frame, total_frames, window
):
    frames = queries.shape[0]
    numerator = jnp.zeros(queries.shape, jnp.float32)
    denominator = jnp.zeros(queries.shape[:-1], jnp.float32)
    for offset in range(2 * window + 1):
        near_keys = key_rows[offset : offset + frames].astype(jnp.float32)
        near_values = value_rows[offset : offset + frames].astype(jnp.float32)
        scores = jnp.sum(queries * near_keys, axis=-1) * queries.shape[-1] ** (-0.5)
        target = first_frame + jnp.arange(frames, dtype=jnp.int32) + (offset - window)
        allowed = (window_mask[:, offset] == 1) & (target >= 0) & (target < total_frames)
        weights = jnp.exp(scores) * allowed.astype(jnp.float32)[:, None, None]
        numerator = numerator + weights[..., None] * near_values
        denominator = denominator + weights
    return numerator / denominator[..., None]


def on_device_general(
    latents,
    fresh_noise,
    levels,
    window_mask,
    cond_embed,
    level_mod,
    embed_weight,
    qkv_weight,
    query_gain,
    key_gain,
    out_weight,
    final_gain,
    final_weight,
    guide_table,
    guide_index,
):
    frames = latents.shape[0]
    tok_count = latents.shape[2]
    model_width = embed_weight.shape[1]
    head_dim = query_gain.shape[0]
    levels_all = level_mod.shape[0]
    queue_count = lax.axis_size("queue")
    all_tokens = lax.all_gather(latents, "tok", axis=2, tiled=True)
    seq_tokens = all_tokens.shape[2]
    row_count = frames * seq_tokens
    embedded = (
        jnp.einsum(
            "fcs,cd->fsd",
            all_tokens.astype(jnp.bfloat16),
            embed_weight,
            preferred_element_type=jnp.float32,
        )
        + cond_embed[0]
    )
    one_hot = (levels[:, None] == jnp.arange(levels_all, dtype=jnp.int32)[None, :]).astype(
        jnp.float32
    )
    modulate = jnp.dot(
        one_hot, level_mod.reshape(levels_all, 3 * model_width), precision=lax.Precision.HIGHEST
    ).reshape(frames, 3, model_width)
    normed = (layer_norm(embedded) * (1.0 + modulate[:, None, 1]) + modulate[:, None, 0]).astype(
        jnp.bfloat16
    )
    norm_rows = normed.reshape(row_count, model_width)
    local_cols = qkv_weight.shape[2]
    shard_piece = lax.all_gather(qkv_weight, ("queue", "cfg"), axis=0, tiled=True)
    flat_piece = shard_piece.reshape(shard_piece.shape[0], 3 * local_cols)
    projected = jnp.dot(norm_rows, flat_piece, preferred_element_type=jnp.float32)
    projected = projected.reshape(frames, seq_tokens, 3, local_cols // head_dim, head_dim)
    queries = rms_norm(projected[:, :, 0], query_gain)
    keys_values = jnp.stack(
        [
            rms_norm(projected[:, :, 1], key_gain).astype(jnp.bfloat16),
            projected[:, :, 2].astype(jnp.bfloat16),
        ]
    )
    window = window_mask.shape[1] // 2
    widened = with_halo(keys_values, (("queue", 1),), window)
    first_frame = lax.axis_index("queue") * frames
    attended = temporal_attention(
        queries, widened[0], widened[1], window_mask, first_frame, frames * queue_count, window
    )
    attended = attended.astype(jnp.bfloat16).reshape(frames, seq_tokens, local_cols)
    flat_heads = attended.reshape(row_count, local_cols)
    partial_value = jnp.dot(
        flat_heads,
        lax.all_gather(out_weight, ("queue", "cfg"), axis=1, tiled=True),
        preferred_element_type=jnp.float32,
    )
    mixed_out = lax.psum_scatter(
        partial_value.reshape(frames, seq_tokens, model_width).astype(jnp.bfloat16),
        "tok",
        scatter_dimension=1,
        tiled=True,
    ).astype(jnp.float32)
    own_start = lax.axis_index("tok") * tok_count
    own_embed = lax.dynamic_slice_in_dim(embedded, own_start, tok_count, 1)
    summed = own_embed + modulate[:, None, 2] * mixed_out
    final_rows = (layer_norm(summed) * final_gain).astype(jnp.bfloat16)
    velocity = jnp.einsum(
        "ftd,dc->fct", final_rows, final_weight, preferred_element_type=jnp.float32
    )
    half_values = velocity.shape[1] // 2
    branch_index = lax.axis_index("cfg")
    own_first = branch_index * half_values
    other_first = (1 - branch_index) * half_values
    outgoing = lax.dynamic_slice_in_dim(velocity, other_first, half_values, 1)
    partner = from_partner(outgoing, "cfg", 0)
    mine = lax.dynamic_slice_in_dim(velocity, own_first, half_values, 1)
    is_cond = branch_index == 0
    cond_vel = jnp.where(is_cond, mine, partner)
    uncond_vel = jnp.where(is_cond, partner, mine)
    entries = guide_table.shape[0]
    guidance = jnp.sum(
        guide_table * (jnp.arange(entries, dtype=jnp.int32) == guide_index[0]).astype(jnp.float32)
    )
    guided = uncond_vel + guidance * (cond_vel - uncond_vel)
    current = noise_sigma((levels + 1).astype(jnp.float32) / levels_all)
    upcoming = noise_sigma(levels.astype(jnp.float32) / levels_all)
    own_latents = lax.dynamic_slice_in_dim(latents, own_first, half_values, 1)
    updated = own_latents + (upcoming - current)[:, None, None] * guided
    incoming = shifted(updated[:1], "queue", -1)
    is_last = lax.axis_index("queue") == queue_count - 1
    incoming = jnp.where(is_last, fresh_noise[None], incoming)
    new_queue = jnp.concatenate([updated[1:], incoming], axis=0)
    return (guided, new_queue)


def kernel_call(body, out_shapes, spaces, scratch=(), vmem=VMEM_BYTES, **cost):
    kinds = {
        "v": pl.BlockSpec(),
        "s": pl.BlockSpec(memory_space=pltpu.SMEM),
        "a": pl.BlockSpec(memory_space=pl.ANY),
        "h": pl.BlockSpec(memory_space=pltpu.HBM),
    }
    many = isinstance(out_shapes, (list, tuple))
    return pl.pallas_call(
        body,
        out_shape=out_shapes,
        in_specs=[kinds[k] for k in spaces],
        out_specs=[pl.BlockSpec() for _ in out_shapes] if many else pl.BlockSpec(),
        scratch_shapes=list(scratch),
        compiler_params=pltpu.CompilerParams(vmem_limit_bytes=vmem),
        cost_estimate=pl.CostEstimate(
            flops=cost.get("flops", 1000000),
            bytes_accessed=cost.get("bytes_accessed", 1000000),
            transcendentals=0,
        ),
    )


def split_terms(values, terms):
    parts = []
    for _ in range(terms):
        part = values.astype(BF16)
        parts.append(part)
        values = values - part.astype(F32)
    return parts


def dot_tn(left, right):
    return lax.dot_general(
        left, right, (((0,), (0,)), ((), ())), preferred_element_type=F32
    )


def place_of(axis):
    return lax.axis_index(axis)


def pack_kernel(head_dim, copies_frames, latents, levels, window_mask, qkv, out_w, cond, *outs):
    scratch = outs[-1]
    copies, packed, first = outs[-4:-1]
    chunks = outs[:-4]
    scene, q, tok, core = (place_of(a) for a in ("scene", "queue", "tok", "cfg"))
    for h in range(scratch.shape[0]):
        start = h * head_dim
        scratch[h] = jnp.concatenate(
            [qkv[part, :, start : start + head_dim] for part in range(3)], axis=1
        )
    group = out_w.shape[1] // 2
    half = jnp.where(scene == 0, out_w[:, :group], out_w[:, group:])
    for k, chunk in enumerate(chunks):
        chunk[...] = jnp.concatenate([half, scratch[scene * len(chunks) + (q ^ k)]], axis=1)
    frames, values, tokens = latents.shape
    span = window_mask.shape[1]
    shares = []
    own = []
    for f in range(frames):
        level = levels[:, f : f + 1].astype(F32)
        side = jnp.zeros((copies.shape[1] - values, tokens), F32)
        row_id = lax.broadcasted_iota(jnp.int32, side.shape, 0)
        for o in range(span):
            side = jnp.where(row_id == o, window_mask[f : f + 1, o : o + 1].astype(F32), side)
        side = jnp.where(row_id == span, level, side)
        shares.append(jnp.concatenate([latents[f], side], axis=0))
        fill = jnp.broadcast_to(level, (packed.shape[0] - values, tokens))
        own.append(jnp.concatenate([latents[f], fill], axis=0))
    lower = jnp.concatenate(shares[:copies_frames], axis=1)
    upper = jnp.concatenate(shares[copies_frames:], axis=1)
    share = jnp.where(core == 0, lower, upper)
    spots = lax.axis_size("queue") * lax.axis_size("tok")
    length = cond.shape[1] // spots
    piece = jnp.zeros((1, length), F32)
    for i in range(spots):
        chosen = q * lax.axis_size("tok") + tok == i
        piece = jnp.where(chosen, cond[:, i * length : (i + 1) * length], piece)
    row_id = lax.broadcasted_iota(jnp.int32, share.shape, 0)
    at_row, step = values + span + 1, share.shape[1]
    for term in split_terms(piece, 3):
        for start in range(0, length, step):
            line = term.astype(F32)[:, start : start + step]
            fill = jnp.zeros((1, step - line.shape[1]), F32)
            line = jnp.concatenate([line, fill], axis=1) if fill.shape[1] else line
            share = jnp.where(row_id == at_row, line, share)
            at_row += 1
    share = share.astype(BF16)
    for at in range(copies.shape[0]):
        copies[at] = share
    packed[...] = jnp.concatenate(own, axis=1)
    first[...] = own[0]


def prepare_kernel(
    frames,
    values,
    span,
    mine,
    other,
    level_mod,
    embed,
    lhs,
    xin,
    rstd_out,
    mask_out,
):
    width = embed.shape[1]
    scenes, all_frames = mask_out.shape[:2]
    rows = xin.shape[1] // scenes
    queues = all_frames // frames
    toks = mine.shape[0] // (scenes * queues)
    per_core = frames // 2
    tokens = mine.shape[2] // per_core
    core = place_of("cfg")
    weights = embed[...].astype(F32)
    weights = weights - jnp.mean(weights, axis=1, keepdims=True)
    length, step = width // (queues * toks), mine.shape[2]
    lines = -(-length // step)
    conds = []
    for y in range(scenes):
        pieces = []
        for at in range(y * queues * toks, (y + 1) * queues * toks):
            info = mine[at].astype(F32)
            first = values + span + 1
            terms = sum(info[first + i * lines : first + (i + 1) * lines] for i in range(3))
            for i in range(lines):
                pieces.append(terms[i : i + 1, : min(step, length - i * step)])
        conds.append(jnp.concatenate(pieces, axis=1))
    conds = jnp.concatenate(conds, axis=0)
    conds = conds - jnp.mean(conds, axis=1, keepdims=True)
    basis = jnp.concatenate(
        [weights, conds, jnp.zeros((rows - values - scenes, width), F32)], axis=0
    )
    gram = lax.dot_general(
        basis,
        basis,
        (((1,), (1,)), ((), ())),
        preferred_element_type=F32,
        precision=lax.Precision.HIGHEST,
    ) * (1.0 / width)
    row_id = lax.broadcasted_iota(jnp.int32, (rows, LANES), 0)
    wide_id = lax.broadcasted_iota(jnp.int32, (rows, width), 0)
    level_id = lax.broadcasted_iota(jnp.int32, (level_mod.shape[1], width), 0).astype(F32)
    shift_row = values + scenes
    fill = LANES - toks * tokens
    for y in range(scenes):
        for q in range(queues):
            first = (y * queues + q) * toks
            held = []
            for t in range(toks):
                one, two = mine[first + t].astype(F32), other[first + t].astype(F32)
                held.append((jnp.where(core == 0, one, two), jnp.where(core == 0, two, one)))
            for part in range(frames):
                f = q * frames + part
                at = part % per_core * tokens
                info = [pair[part // per_core][:, at : at + tokens] for pair in held]
                level = info[0][values + span : values + span + 1, 0:1]
                chosen = level_id == level
                shift = jnp.sum(jnp.where(chosen, level_mod[0], 0.0), axis=0, keepdims=True)
                scale = jnp.sum(jnp.where(chosen, level_mod[1], 0.0), axis=0, keepdims=True)
                block = basis * (1.0 + scale)
                block = jnp.where((wide_id == shift_row) | (wide_id == shift_row + 1), shift, block)
                to = (f * scenes + y) * rows
                lhs[to : to + rows, :] = block.astype(BF16)
                info = jnp.concatenate(info + [jnp.ones((info[0].shape[0], fill), F32)], axis=1)
                mask_out[y, f] = info[values : values + mask_out.shape[2]]
                vec = jnp.where(row_id < values, info[:rows], 0.0)
                vec = jnp.where(row_id == values + y, 1.0, vec)
                spread = jnp.sum(
                    vec
                    * jnp.dot(
                        gram, vec, preferred_element_type=F32, precision=lax.Precision.HIGHEST
                    ),
                    axis=0,
                    keepdims=True,
                )
                spread = jnp.maximum(spread, 0.0) + EPS_NORM
                rstd = lax.rsqrt(spread)
                std = spread * rstd
                high = std.astype(BF16).astype(F32)
                vec = jnp.where(row_id == shift_row, high, vec)
                vec = jnp.where(row_id == shift_row + 1, std - high, vec)
                blank = jnp.zeros(vec.shape, F32)
                blocks = [vec if n == y else blank for n in range(scenes)]
                xin[f, y * rows : (y + 1) * rows] = jnp.concatenate(blocks, axis=1).astype(BF16)
                rstd_out[f, :, y * LANES : (y + 1) * LANES] = rstd


def attend_kernel(frames, tokens, queues, *refs):
    pieces = refs[: 2 * queues]
    lhs, xin, rstd_in, mask_in, gain_q, gain_k, out, whole, proj, kfac, vfac, att = refs[
        2 * queues :
    ]
    scenes, all_frames = mask_in.shape[:2]
    rows = xin.shape[1]
    head_dim = gain_q.shape[1]
    window = (proj.shape[0] - all_frames) // 2
    span = 2 * window + 1
    q_at, core = place_of("queue"), place_of("cfg")
    part_rows = pieces[0].shape[0]
    for k in range(queues):
        for side in range(2):
            owner = core if side == 0 else 1 - core
            first = pl.multiple_of(((q_at ^ k) * 2 + owner) * part_rows, 16)
            piece = pieces[side * queues + k]
            whole[pl.ds(first, part_rows), :] = piece[:, piece.shape[1] - 3 * head_dim :]
    folded = jnp.dot(lhs[...], whole[...], preferred_element_type=F32)
    high, low = split_terms(folded, 2)
    gains = split_terms(gain_q[...] * gain_k[...] * head_dim ** (-0.5), 3)
    gains = jnp.concatenate(gains + [jnp.zeros((13, head_dim), BF16)], axis=0)
    gains = dot_tn(gains, jnp.ones((16, LANES), BF16))
    for side in range(window):
        for at in (side, all_frames + window + side):
            proj[at] = jnp.zeros(proj.shape[1:], F32)
            kfac[at] = jnp.zeros(kfac.shape[1:], F32)
            vfac[at] = jnp.zeros(vfac.shape[1:], F32)
    for f in range(all_frames):
        piece = slice(f * rows, (f + 1) * rows)
        made = dot_tn(
            jnp.concatenate([high[piece], low[piece]], axis=0),
            jnp.concatenate([xin[f], xin[f]], axis=0),
        )
        proj[f + window] = made
        rstd = rstd_in[f]
        keys = made[head_dim : 2 * head_dim]
        square = jnp.mean(keys * keys, axis=0, keepdims=True)
        kfac[f + window] = rstd * lax.rsqrt(rstd * rstd * square + EPS_NORM)
        vfac[f + window] = rstd

    def one_frame(f, carry):
        for y in range(scenes):
            lane = slice(y * LANES, (y + 1) * LANES)
            query = proj[f + window, 0:head_dim, lane]
            rstd = vfac[f + window, :, lane]
            square = jnp.mean(query * query, axis=0, keepdims=True)
            qfac = rstd * lax.rsqrt(rstd * rstd * square + EPS_NORM)
            query = query * gains
            total = jnp.zeros((head_dim, LANES), F32)
            norm = jnp.zeros((1, LANES), F32)
            for o in range(span):
                keys = proj[f + o, head_dim : 2 * head_dim, lane]
                score = jnp.sum(query * keys, axis=0, keepdims=True)
                score = score * (qfac * kfac[f + o, :, lane])
                part = jnp.exp(score) * mask_in[y, f, o : o + 1, :]
                norm = norm + part
                total = total + (part * vfac[f + o, :, lane]) * proj[f + o, 2 * head_dim :, lane]
            att[f, y] = total * (1.0 / norm)
        return carry

    lax.fori_loop(0, all_frames, one_frame, 0)
    toks = out.shape[0] // (scenes * queues)
    for t in range(toks):
        for y in range(scenes):
            for q in range(queues):
                parts = [
                    att[min(q * frames + i, all_frames - 1), y, :, t * tokens : (t + 1) * tokens]
                    for i in range(frames + 1)
                ]
                at = (t * queues + q) * scenes + y
                out[at] = jnp.concatenate(parts, axis=1).astype(BF16)


def stage_kernel(own_source, level_source, embed_source, own, level_mod, embed, sems):
    copies = [
        pltpu.make_async_copy(own_source, own, sems.at[0]),
        pltpu.make_async_copy(level_source.at[pl.ds(0, 2)], level_mod, sems.at[1]),
        pltpu.make_async_copy(embed_source, embed, sems.at[2]),
    ]
    for copy in copies:
        copy.start()
    for copy in copies:
        copy.wait()


def side_kernel(group, *refs):
    for k, piece in enumerate(refs[:-1]):
        refs[-1][:, k * group : (k + 1) * group] = piece[:, :group]


def ready_kernel(values, half, *refs):
    sources, table, index = refs[:8], refs[8], refs[9]
    left, right, base, factor, noise_out, guide, final_out = refs[10:17]
    held, sems = refs[17:25], refs[25]
    copies = []
    for i, (source, to) in enumerate(zip(sources, held)):
        source = source.at[2] if i == 3 else source
        copies.append(pltpu.make_async_copy(source, to, sems.at[i]))
    for copy in copies:
        copy.start()
    for copy in copies:
        copy.wait()
    packed, following, cond, gates, embed, final_gain, final_w, noise = held
    levels_all, width = gates.shape
    info = jnp.concatenate([packed[...], following[...]], axis=1)
    lanes = info.shape[1]
    ones = jnp.ones((16, lanes), BF16)
    zero = jnp.zeros((13, width), BF16)
    left[...] = jnp.concatenate(
        [embed[...]]
        + split_terms(cond[...], 3)
        + [zero]
        + split_terms(gates[...], 3)
        + split_terms(final_gain[...], 3)
        + [zero],
        axis=0,
    )
    level = info[values : values + 1]
    one_hot = (lax.broadcasted_iota(jnp.int32, (levels_all, lanes), 0).astype(F32) == level).astype(
        F32
    ).astype(BF16)
    right[...] = jnp.concatenate(
        [info[:values].astype(BF16), ones, one_hot, one_hot, one_hot, ones], axis=0
    )
    own = pl.multiple_of(place_of("cfg") * half, half)
    current = noise_sigma((level + 1.0) / levels_all)
    upcoming = noise_sigma(level / levels_all)
    factor[...] = jnp.broadcast_to(upcoming - current, factor.shape)
    base[...] = jnp.concatenate(
        [packed[pl.ds(own, half), :], following[pl.ds(own, half), :]], axis=1
    )
    noise_out[...] = noise[...]
    final_out[...] = final_w[...]
    guide[...] = jnp.full(guide.shape, table[index[0]], F32)


def finish_kernel(half, values, queues, *refs):
    parts = [refs[:5], refs[5:10]]
    attended, left, right, final_w, mine, send, scratch, mixed = refs[10:]
    scene, q_at, tok, core = (place_of(a) for a in ("scene", "queue", "tok", "cfg"))
    group = parts[0][0].shape[1] // queues
    columns = parts[0][0].shape[0]

    def weights_of(c, t, y, k):
        lane = slice(k * group, (k + 1) * group)
        if t == y == 1:
            return [parts[c][3][:, lane], parts[c][4][:, lane]]
        return [parts[c][2 * y + t][:, lane]]

    total = None
    for t in range(2):
        made = None
        for y in range(2):
            pieces = []
            for c in range(2):
                for k in range(queues):
                    pieces += weights_of(c, t, y, k)
            rows = [
                attended[((tok ^ t) * queues + k) * 2 + (scene ^ y)].astype(F32)
                for k in range(queues)
            ]
            rows = jnp.concatenate(rows, axis=0).astype(BF16)
            term = jnp.dot(jnp.concatenate(pieces, axis=0), rows, preferred_element_type=F32)
            made = term if made is None else made + term
        made = made.astype(BF16).astype(F32)
        total = made if total is None else total + made
    for c in range(2):
        for k in range(queues):
            first = ((q_at ^ k) * 2 + (core ^ c)) * columns
            at = (c * queues + k) * columns
            mixed[pl.ds(pl.multiple_of(first, 8), columns), :] = total[at : at + columns]

    first, last = values + 16, left.shape[0] - 16
    emb = dot_tn(left[:first], right[:first])
    gate = dot_tn(left[first:last], right[first:last])
    gain = dot_tn(left[last:], right[last:])
    summed = emb + gate * mixed[...]
    center = jnp.mean(summed, axis=0, keepdims=True)
    deviate = summed - center
    spread = jnp.mean(deviate * deviate, axis=0, keepdims=True)
    final = (deviate * lax.rsqrt(spread + EPS_NORM) * gain).astype(BF16)
    scratch[...] = jnp.dot(final_w[...], final, preferred_element_type=F32)
    own = pl.multiple_of(core * half, half)
    other = pl.multiple_of((1 - core) * half, half)
    mine[...] = scratch[pl.ds(own, half), :]
    send[...] = scratch[pl.ds(other, half), :]


def update_kernel(mine, partner, base, factor, noise, guide, vel, new):
    frames, _, tokens = vel.shape
    is_cond = place_of("cfg") == 0
    here, there = mine[...], partner[...]
    cond = jnp.where(is_cond, here, there)
    uncond = jnp.where(is_cond, there, here)
    guided = uncond + guide[0:1, 0:1] * (cond - uncond)
    updated = base[...] + factor[...] * guided
    is_last = place_of("queue") == lax.axis_size("queue") - 1
    for f in range(frames):
        vel[f] = guided[:, f * tokens : (f + 1) * tokens]
        moved = updated[:, (f + 1) * tokens : (f + 2) * tokens]
        if f == frames - 1:
            moved = jnp.where(is_last, noise[...], moved)
        new[f] = moved


def swapped(value, axis, mask):
    count = lax.axis_size(axis)
    return lax.ppermute(value, axis, [(i, i ^ mask) for i in range(count)])


def on_device_heads(
    latents,
    fresh_noise,
    levels,
    window_mask,
    cond_embed,
    level_mod,
    embed_weight,
    qkv_weight,
    query_gain,
    key_gain,
    out_weight,
    final_gain,
    final_weight,
    guide_table,
    guide_index,
):
    frames, values, tokens = latents.shape
    width = embed_weight.shape[1]
    head_dim = query_gain.shape[0]
    levels_all = level_mod.shape[0]
    span = window_mask.shape[1]
    window = span // 2
    scenes, queues, toks = (lax.axis_size(a) for a in ("scene", "queue", "tok"))
    chips = scenes * queues * toks
    all_frames = queues * frames
    per_core = frames // 2
    cond_rows = 3 * -(-(width // (queues * toks)) // (per_core * tokens))
    rows = -(-max(values + scenes + 2, values + span + 1 + cond_rows) // 16) * 16
    own_rows = -(-(values + 1) // 8) * 8
    local_rows = qkv_weight.shape[0]
    local_heads = qkv_weight.shape[2] // head_dim
    lanes = scenes * LANES
    row_lanes = (frames + 1) * tokens
    mods = jnp.transpose(level_mod, (1, 0, 2))

    group = out_weight.shape[0] // scenes
    chunk = jax.ShapeDtypeStruct((local_rows, group + 3 * head_dim), BF16)
    *chunks, copies, packed, first = kernel_call(
        functools.partial(pack_kernel, head_dim, per_core),
        [chunk] * queues
        + [
            jax.ShapeDtypeStruct((chips, rows, per_core * tokens), BF16),
            jax.ShapeDtypeStruct((own_rows, frames * tokens), F32),
            jax.ShapeDtypeStruct((own_rows, tokens), F32),
        ],
        "vvvvvv",
        [pltpu.VMEM((local_heads, local_rows, 3 * head_dim), BF16)],
        vmem=WHOLE_VMEM,
        bytes_accessed=8_000_000,
    )(
        latents,
        levels[None],
        window_mask,
        jnp.transpose(qkv_weight, (1, 0, 2)),
        out_weight.T,
        cond_embed,
    )

    near = [chunks[0]] + [swapped(chunks[k], "queue", k) for k in range(1, queues)]
    far = [swapped(piece, "cfg", 1) for piece in near]
    shares = lax.all_to_all(copies, ("scene", "queue", "tok"), 0, 0)
    other_shares = swapped(shares, "cfg", 1)

    own, level_rows, embed_held = kernel_call(
        stage_kernel,
        [
            chunk,
            jax.ShapeDtypeStruct((2, levels_all, width), F32),
            jax.ShapeDtypeStruct(embed_weight.shape, BF16),
        ],
        "hhh",
        [pltpu.SemaphoreType.DMA((3,))],
    )(chunks[0], mods, embed_weight)
    following = lax.ppermute(first, "queue", [(i + 1, i) for i in range(queues - 1)])
    near[-1], following, shares, *far[:-1] = lax.optimization_barrier(
        (near[-1], following, shares, *far[:-1])
    )
    part = kernel_call(
        functools.partial(side_kernel, group),
        jax.ShapeDtypeStruct((local_rows, queues * group), BF16),
        "v" * queues,
    )(own, *near[1:])
    part_tok, part_scene = swapped(part, "tok", 1), swapped(part, "scene", 1)

    lhs, xin, rstd, masks = kernel_call(
        functools.partial(prepare_kernel, frames, values, span),
        [
            jax.ShapeDtypeStruct((scenes * all_frames * rows, width), BF16),
            jax.ShapeDtypeStruct((all_frames, scenes * rows, lanes), BF16),
            jax.ShapeDtypeStruct((all_frames, 1, lanes), F32),
            jax.ShapeDtypeStruct((scenes, all_frames, rows - values, LANES), F32),
        ],
        "vvvv",
        bytes_accessed=8_000_000,
    )(shares, other_shares, level_rows, embed_held)
    attended = kernel_call(
        functools.partial(attend_kernel, frames, tokens, queues),
        jax.ShapeDtypeStruct((chips, head_dim, row_lanes), BF16),
        "v" * (2 * queues + 6),
        [
            pltpu.VMEM((width, 3 * head_dim), BF16),
            pltpu.VMEM((all_frames + 2 * window, 3 * head_dim, lanes), F32),
            pltpu.VMEM((all_frames + 2 * window, 1, lanes), F32),
            pltpu.VMEM((all_frames + 2 * window, 1, lanes), F32),
            pltpu.VMEM((all_frames, scenes, head_dim, LANES), F32),
        ],
        bytes_accessed=100_000_000,
    )(own, *near[1:], *far, lhs, xin, rstd, masks, query_gain[None], key_gain[None])
    attended, part, part_tok, part_scene = lax.optimization_barrier(
        (attended, part, part_tok, part_scene)
    )
    received = lax.all_to_all(attended, ("tok", "queue", "scene"), 0, 0)
    cut = -(-local_rows // 32) * 16
    upper = swapped(part_tok[:cut], "scene", 1)
    lower = swapped(part_scene[cut:], "tok", 1)
    half = values // 2
    half_shape = jax.ShapeDtypeStruct((half, row_lanes), F32)
    smalls = (
        packed,
        following,
        cond_embed,
        mods,
        embed_weight,
        final_gain[None],
        final_weight.T,
        fresh_noise,
    )
    places = [
        pltpu.VMEM(a.shape[1:] if i == 3 else a.shape, a.dtype) for i, a in enumerate(smalls)
    ]
    terms = values + 16 + 3 * levels_all + 16
    left, right, *rest, final_held = kernel_call(
        functools.partial(ready_kernel, values, half),
        [
            jax.ShapeDtypeStruct((terms, width), BF16),
            jax.ShapeDtypeStruct((terms, row_lanes), BF16),
            half_shape,
            half_shape,
            jax.ShapeDtypeStruct(fresh_noise.shape, F32),
            jax.ShapeDtypeStruct((8, LANES), F32),
            jax.ShapeDtypeStruct((values, width), BF16),
        ],
        "ha" + "h" * 6 + "ss",
        places + [pltpu.SemaphoreType.DMA((len(smalls),))],
    )(*smalls, guide_table, guide_index)
    upper, lower, right = lax.optimization_barrier((upper, lower, right))
    away = [part, part_tok, part_scene, upper, lower]
    away_far = [swapped(piece, "cfg", 1) for piece in away]

    mine, send = kernel_call(
        functools.partial(finish_kernel, half, values, queues),
        [half_shape] * 2,
        "v" * 14,
        [pltpu.VMEM((values, row_lanes), F32), pltpu.VMEM((width, row_lanes), F32)],
        bytes_accessed=8_000_000,
    )(*away, *away_far, received, left, right, final_held)
    partner = swapped(send, "cfg", 1)
    shape = jax.ShapeDtypeStruct((frames, half, tokens), F32)
    return kernel_call(update_kernel, [shape, shape], "v" * 6)(mine, partner, *rest)


def on_device(*args):
    latents, qkv_weight, query_gain = args[0], args[7], args[8]
    local_heads = qkv_weight.shape[2] // query_gain.shape[0]
    scenes, queues, toks, cores = (lax.axis_size(a) for a in ("scene", "queue", "tok", "cfg"))
    pairs = scenes == toks == cores == 2 and queues & (queues - 1) == 0
    fits = latents.shape[2] * toks <= LANES and latents.shape[0] % cores == 0
    if pairs and fits and local_heads == scenes * queues:
        return tuple(on_device_heads(*args))
    return on_device_general(*args)


def solution(mesh):
    placed = (
        P(("scene", "queue"), None, "tok"),
        P(("scene", "cfg"), "tok"),
        P(("scene", "queue")),
        P(("scene", "queue"), None),
        P(("scene", "cfg"), None),
        P(),
        P(),
        P(("queue", "cfg"), None, "tok"),
        P(),
        P(),
        P("tok", ("queue", "cfg")),
        P(),
        P(),
        P(),
        P(),
    )
    return jax.shard_map(
        on_device,
        mesh=mesh,
        in_specs=placed,
        out_specs=(P(("scene", "queue"), "cfg", "tok"), P(("scene", "queue"), "cfg", "tok")),
        check_vma=False,
    )
```

```python
import functools

import jax
import jax.numpy as jnp
from jax import lax
from jax.experimental import pallas as pl
from jax.experimental.pallas import tpu as pltpu
from jax.sharding import PartitionSpec as P

EPS_NORM = 1e-06
TIME_SHIFT = 3.0
LANES = 128
VMEM_BYTES = 20 * 1024 * 1024
WHOLE_VMEM = 62 * 1024 * 1024
F32 = jnp.float32
BF16 = jnp.bfloat16


def noise_sigma(fraction):
    return TIME_SHIFT * fraction / (1.0 + (TIME_SHIFT - 1.0) * fraction)


def from_partner(value, axis, bit):
    return lax.ppermute(value, axis, [(i, i ^ 1 << bit) for i in range(lax.axis_size(axis))])


def with_halo(cells, sides, width):
    for axis, dim in sides:
        count = lax.axis_size(axis)
        ends = count - 1
        head = lax.slice_in_dim(cells, 0, width, axis=dim)
        tail = lax.slice_in_dim(cells, cells.shape[dim] - width, cells.shape[dim], axis=dim)
        cells = jnp.concatenate(
            [
                lax.ppermute(tail, axis, [(i, (i + 1) % count) for i in range(ends)]),
                cells,
                lax.ppermute(head, axis, [((i + 1) % count, i) for i in range(ends)]),
            ],
            axis=dim,
        )
    return cells


def shifted(value, axis, steps):
    count = lax.axis_size(axis)
    initial, last = (max(0, -steps), min(count, count - steps))
    return lax.ppermute(value, axis, [(source, source + steps) for source in range(initial, last)])


def layer_norm(values):
    center = jnp.mean(values, axis=-1, keepdims=True)
    deviate = values - center
    spread = jnp.mean(deviate * deviate, axis=-1, keepdims=True)
    return deviate * lax.rsqrt(spread + EPS_NORM)


def rms_norm(values, scaling):
    return (
        values * lax.rsqrt(jnp.mean(values * values, axis=-1, keepdims=True) + EPS_NORM) * scaling
    )


def temporal_attention(
    queries, key_rows, value_rows, window_mask, first_frame, total_frames, window
):
    frames = queries.shape[0]
    numerator = jnp.zeros(queries.shape, jnp.float32)
    denominator = jnp.zeros(queries.shape[:-1], jnp.float32)
    for offset in range(2 * window + 1):
        near_keys = key_rows[offset : offset + frames].astype(jnp.float32)
        near_values = value_rows[offset : offset + frames].astype(jnp.float32)
        scores = jnp.sum(queries * near_keys, axis=-1) * queries.shape[-1] ** (-0.5)
        target = first_frame + jnp.arange(frames, dtype=jnp.int32) + (offset - window)
        allowed = (window_mask[:, offset] == 1) & (target >= 0) & (target < total_frames)
        weights = jnp.exp(scores) * allowed.astype(jnp.float32)[:, None, None]
        numerator = numerator + weights[..., None] * near_values
        denominator = denominator + weights
    return numerator / denominator[..., None]


def on_device_general(
    latents,
    fresh_noise,
    levels,
    window_mask,
    cond_embed,
    level_mod,
    embed_weight,
    qkv_weight,
    query_gain,
    key_gain,
    out_weight,
    final_gain,
    final_weight,
    guide_table,
    guide_index,
):
    frames = latents.shape[0]
    tok_count = latents.shape[2]
    model_width = embed_weight.shape[1]
    head_dim = query_gain.shape[0]
    levels_all = level_mod.shape[0]
    queue_count = lax.axis_size("queue")
    all_tokens = lax.all_gather(latents, "tok", axis=2, tiled=True)
    seq_tokens = all_tokens.shape[2]
    row_count = frames * seq_tokens
    embedded = (
        jnp.einsum(
            "fcs,cd->fsd",
            all_tokens.astype(jnp.bfloat16),
            embed_weight,
            preferred_element_type=jnp.float32,
        )
        + cond_embed[0]
    )
    one_hot = (levels[:, None] == jnp.arange(levels_all, dtype=jnp.int32)[None, :]).astype(
        jnp.float32
    )
    modulate = jnp.dot(
        one_hot, level_mod.reshape(levels_all, 3 * model_width), precision=lax.Precision.HIGHEST
    ).reshape(frames, 3, model_width)
    normed = (layer_norm(embedded) * (1.0 + modulate[:, None, 1]) + modulate[:, None, 0]).astype(
        jnp.bfloat16
    )
    norm_rows = normed.reshape(row_count, model_width)
    local_cols = qkv_weight.shape[2]
    shard_piece = lax.all_gather(qkv_weight, ("queue", "cfg"), axis=0, tiled=True)
    flat_piece = shard_piece.reshape(shard_piece.shape[0], 3 * local_cols)
    projected = jnp.dot(norm_rows, flat_piece, preferred_element_type=jnp.float32)
    projected = projected.reshape(frames, seq_tokens, 3, local_cols // head_dim, head_dim)
    queries = rms_norm(projected[:, :, 0], query_gain)
    keys_values = jnp.stack(
        [
            rms_norm(projected[:, :, 1], key_gain).astype(jnp.bfloat16),
            projected[:, :, 2].astype(jnp.bfloat16),
        ]
    )
    window = window_mask.shape[1] // 2
    widened = with_halo(keys_values, (("queue", 1),), window)
    first_frame = lax.axis_index("queue") * frames
    attended = temporal_attention(
        queries, widened[0], widened[1], window_mask, first_frame, frames * queue_count, window
    )
    attended = attended.astype(jnp.bfloat16).reshape(frames, seq_tokens, local_cols)
    flat_heads = attended.reshape(row_count, local_cols)
    partial_value = jnp.dot(
        flat_heads,
        lax.all_gather(out_weight, ("queue", "cfg"), axis=1, tiled=True),
        preferred_element_type=jnp.float32,
    )
    mixed_out = lax.psum_scatter(
        partial_value.reshape(frames, seq_tokens, model_width).astype(jnp.bfloat16),
        "tok",
        scatter_dimension=1,
        tiled=True,
    ).astype(jnp.float32)
    own_start = lax.axis_index("tok") * tok_count
    own_embed = lax.dynamic_slice_in_dim(embedded, own_start, tok_count, 1)
    summed = own_embed + modulate[:, None, 2] * mixed_out
    final_rows = (layer_norm(summed) * final_gain).astype(jnp.bfloat16)
    velocity = jnp.einsum(
        "ftd,dc->fct", final_rows, final_weight, preferred_element_type=jnp.float32
    )
    half_values = velocity.shape[1] // 2
    branch_index = lax.axis_index("cfg")
    own_first = branch_index * half_values
    other_first = (1 - branch_index) * half_values
    outgoing = lax.dynamic_slice_in_dim(velocity, other_first, half_values, 1)
    partner = from_partner(outgoing, "cfg", 0)
    mine = lax.dynamic_slice_in_dim(velocity, own_first, half_values, 1)
    is_cond = branch_index == 0
    cond_vel = jnp.where(is_cond, mine, partner)
    uncond_vel = jnp.where(is_cond, partner, mine)
    entries = guide_table.shape[0]
    guidance = jnp.sum(
        guide_table * (jnp.arange(entries, dtype=jnp.int32) == guide_index[0]).astype(jnp.float32)
    )
    guided = uncond_vel + guidance * (cond_vel - uncond_vel)
    current = noise_sigma((levels + 1).astype(jnp.float32) / levels_all)
    upcoming = noise_sigma(levels.astype(jnp.float32) / levels_all)
    own_latents = lax.dynamic_slice_in_dim(latents, own_first, half_values, 1)
    updated = own_latents + (upcoming - current)[:, None, None] * guided
    incoming = shifted(updated[:1], "queue", -1)
    is_last = lax.axis_index("queue") == queue_count - 1
    incoming = jnp.where(is_last, fresh_noise[None], incoming)
    new_queue = jnp.concatenate([updated[1:], incoming], axis=0)
    return (guided, new_queue)


def kernel_call(body, out_shapes, spaces, scratch=(), vmem=VMEM_BYTES, **cost):
    kinds = {
        "v": pl.BlockSpec(),
        "s": pl.BlockSpec(memory_space=pltpu.SMEM),
        "a": pl.BlockSpec(memory_space=pl.ANY),
        "h": pl.BlockSpec(memory_space=pltpu.HBM),
    }
    many = isinstance(out_shapes, (list, tuple))
    return pl.pallas_call(
        body,
        out_shape=out_shapes,
        in_specs=[kinds[k] for k in spaces],
        out_specs=[pl.BlockSpec() for _ in out_shapes] if many else pl.BlockSpec(),
        scratch_shapes=list(scratch),
        compiler_params=pltpu.CompilerParams(vmem_limit_bytes=vmem),
        cost_estimate=pl.CostEstimate(
            flops=cost.get("flops", 1000000),
            bytes_accessed=cost.get("bytes_accessed", 1000000),
            transcendentals=0,
        ),
    )


def split_terms(values, terms):
    parts = []
    for _ in range(terms):
        part = values.astype(BF16)
        parts.append(part)
        values = values - part.astype(F32)
    return parts


def dot_tn(left, right):
    return lax.dot_general(
        left, right, (((0,), (0,)), ((), ())), preferred_element_type=F32
    )


def place_of(axis):
    return lax.axis_index(axis)


def pack_kernel(head_dim, copies_frames, latents, levels, window_mask, qkv, out_w, cond, *outs):
    scratch = outs[-1]
    copies, packed, first = outs[-4:-1]
    chunks = outs[:-4]
    scene, q, tok, core = (place_of(a) for a in ("scene", "queue", "tok", "cfg"))
    for h in range(scratch.shape[0]):
        start = h * head_dim
        scratch[h] = jnp.concatenate(
            [qkv[part, :, start : start + head_dim] for part in range(3)], axis=1
        )
    group = out_w.shape[1] // 2
    half = jnp.where(scene == 0, out_w[:, :group], out_w[:, group:])
    for k, chunk in enumerate(chunks):
        chunk[...] = jnp.concatenate([half, scratch[scene * len(chunks) + (q ^ k)]], axis=1)
    frames, values, tokens = latents.shape
    span = window_mask.shape[1]
    shares = []
    own = []
    for f in range(frames):
        level = levels[:, f : f + 1].astype(F32)
        side = jnp.zeros((copies.shape[1] - values, tokens), F32)
        row_id = lax.broadcasted_iota(jnp.int32, side.shape, 0)
        for o in range(span):
            side = jnp.where(row_id == o, window_mask[f : f + 1, o : o + 1].astype(F32), side)
        side = jnp.where(row_id == span, level, side)
        shares.append(jnp.concatenate([latents[f], side], axis=0))
        fill = jnp.broadcast_to(level, (packed.shape[0] - values, tokens))
        own.append(jnp.concatenate([latents[f], fill], axis=0))
    lower = jnp.concatenate(shares[:copies_frames], axis=1)
    upper = jnp.concatenate(shares[copies_frames:], axis=1)
    share = jnp.where(core == 0, lower, upper)
    spots = lax.axis_size("queue") * lax.axis_size("tok")
    length = cond.shape[1] // spots
    piece = jnp.zeros((1, length), F32)
    for i in range(spots):
        chosen = q * lax.axis_size("tok") + tok == i
        piece = jnp.where(chosen, cond[:, i * length : (i + 1) * length], piece)
    row_id = lax.broadcasted_iota(jnp.int32, share.shape, 0)
    at_row, step = values + span + 1, share.shape[1]
    for term in split_terms(piece, 3):
        for start in range(0, length, step):
            line = term.astype(F32)[:, start : start + step]
            fill = jnp.zeros((1, step - line.shape[1]), F32)
            line = jnp.concatenate([line, fill], axis=1) if fill.shape[1] else line
            share = jnp.where(row_id == at_row, line, share)
            at_row += 1
    share = share.astype(BF16)
    for at in range(copies.shape[0]):
        copies[at] = share
    packed[...] = jnp.concatenate(own, axis=1)
    first[...] = own[0]


def prepare_kernel(
    frames,
    values,
    span,
    mine,
    other,
    level_mod,
    embed,
    lhs,
    xin,
    rstd_out,
    mask_out,
):
    width = embed.shape[1]
    scenes, all_frames = mask_out.shape[:2]
    rows = xin.shape[1] // scenes
    queues = all_frames // frames
    toks = mine.shape[0] // (scenes * queues)
    per_core = frames // 2
    tokens = mine.shape[2] // per_core
    core = place_of("cfg")
    weights = embed[...].astype(F32)
    weights = weights - jnp.mean(weights, axis=1, keepdims=True)
    length, step = width // (queues * toks), mine.shape[2]
    lines = -(-length // step)
    conds = []
    for y in range(scenes):
        pieces = []
        for at in range(y * queues * toks, (y + 1) * queues * toks):
            info = mine[at].astype(F32)
            first = values + span + 1
            terms = sum(info[first + i * lines : first + (i + 1) * lines] for i in range(3))
            for i in range(lines):
                pieces.append(terms[i : i + 1, : min(step, length - i * step)])
        conds.append(jnp.concatenate(pieces, axis=1))
    conds = jnp.concatenate(conds, axis=0)
    conds = conds - jnp.mean(conds, axis=1, keepdims=True)
    basis = jnp.concatenate(
        [weights, conds, jnp.zeros((rows - values - scenes, width), F32)], axis=0
    )
    gram = lax.dot_general(
        basis,
        basis,
        (((1,), (1,)), ((), ())),
        preferred_element_type=F32,
        precision=lax.Precision.HIGHEST,
    ) * (1.0 / width)
    row_id = lax.broadcasted_iota(jnp.int32, (rows, LANES), 0)
    wide_id = lax.broadcasted_iota(jnp.int32, (rows, width), 0)
    level_id = lax.broadcasted_iota(jnp.int32, (level_mod.shape[1], width), 0).astype(F32)
    shift_row = values + scenes
    fill = LANES - toks * tokens
    for y in range(scenes):
        for q in range(queues):
            first = (y * queues + q) * toks
            held = []
            for t in range(toks):
                one, two = mine[first + t].astype(F32), other[first + t].astype(F32)
                held.append((jnp.where(core == 0, one, two), jnp.where(core == 0, two, one)))
            for part in range(frames):
                f = q * frames + part
                at = part % per_core * tokens
                info = [pair[part // per_core][:, at : at + tokens] for pair in held]
                level = info[0][values + span : values + span + 1, 0:1]
                chosen = level_id == level
                shift = jnp.sum(jnp.where(chosen, level_mod[0], 0.0), axis=0, keepdims=True)
                scale = jnp.sum(jnp.where(chosen, level_mod[1], 0.0), axis=0, keepdims=True)
                block = basis * (1.0 + scale)
                block = jnp.where((wide_id == shift_row) | (wide_id == shift_row + 1), shift, block)
                to = (f * scenes + y) * rows
                lhs[to : to + rows, :] = block.astype(BF16)
                info = jnp.concatenate(info + [jnp.ones((info[0].shape[0], fill), F32)], axis=1)
                mask_out[y, f] = info[values : values + mask_out.shape[2]]
                vec = jnp.where(row_id < values, info[:rows], 0.0)
                vec = jnp.where(row_id == values + y, 1.0, vec)
                spread = jnp.sum(
                    vec
                    * jnp.dot(
                        gram, vec, preferred_element_type=F32, precision=lax.Precision.HIGHEST
                    ),
                    axis=0,
                    keepdims=True,
                )
                spread = jnp.maximum(spread, 0.0) + EPS_NORM
                rstd = lax.rsqrt(spread)
                std = spread * rstd
                high = std.astype(BF16).astype(F32)
                vec = jnp.where(row_id == shift_row, high, vec)
                vec = jnp.where(row_id == shift_row + 1, std - high, vec)
                blank = jnp.zeros(vec.shape, F32)
                blocks = [vec if n == y else blank for n in range(scenes)]
                xin[f, y * rows : (y + 1) * rows] = jnp.concatenate(blocks, axis=1).astype(BF16)
                rstd_out[f, :, y * LANES : (y + 1) * LANES] = rstd


def attend_kernel(frames, tokens, queues, *refs):
    pieces = refs[: 2 * queues]
    lhs, xin, rstd_in, mask_in, gain_q, gain_k, out, whole, proj, kfac, vfac, att = refs[
        2 * queues :
    ]
    scenes, all_frames = mask_in.shape[:2]
    rows = xin.shape[1]
    head_dim = gain_q.shape[1]
    window = (proj.shape[0] - all_frames) // 2
    span = 2 * window + 1
    q_at, core = place_of("queue"), place_of("cfg")
    part_rows = pieces[0].shape[0]
    for k in range(queues):
        for side in range(2):
            owner = core if side == 0 else 1 - core
            first = pl.multiple_of(((q_at ^ k) * 2 + owner) * part_rows, 16)
            piece = pieces[side * queues + k]
            whole[pl.ds(first, part_rows), :] = piece[:, piece.shape[1] - 3 * head_dim :]
    folded = jnp.dot(lhs[...], whole[...], preferred_element_type=F32)
    high, low = split_terms(folded, 2)
    gains = split_terms(gain_q[...] * gain_k[...] * head_dim ** (-0.5), 3)
    gains = jnp.concatenate(gains + [jnp.zeros((13, head_dim), BF16)], axis=0)
    gains = dot_tn(gains, jnp.ones((16, LANES), BF16))
    for side in range(window):
        for at in (side, all_frames + window + side):
            proj[at] = jnp.zeros(proj.shape[1:], F32)
            kfac[at] = jnp.zeros(kfac.shape[1:], F32)
            vfac[at] = jnp.zeros(vfac.shape[1:], F32)
    for f in range(all_frames):
        piece = slice(f * rows, (f + 1) * rows)
        made = dot_tn(
            jnp.concatenate([high[piece], low[piece]], axis=0),
            jnp.concatenate([xin[f], xin[f]], axis=0),
        )
        proj[f + window] = made
        rstd = rstd_in[f]
        keys = made[head_dim : 2 * head_dim]
        square = jnp.mean(keys * keys, axis=0, keepdims=True)
        kfac[f + window] = rstd * lax.rsqrt(rstd * rstd * square + EPS_NORM)
        vfac[f + window] = rstd

    def one_frame(f, carry):
        for y in range(scenes):
            lane = slice(y * LANES, (y + 1) * LANES)
            query = proj[f + window, 0:head_dim, lane]
            rstd = vfac[f + window, :, lane]
            square = jnp.mean(query * query, axis=0, keepdims=True)
            qfac = rstd * lax.rsqrt(rstd * rstd * square + EPS_NORM)
            query = query * gains
            total = jnp.zeros((head_dim, LANES), F32)
            norm = jnp.zeros((1, LANES), F32)
            for o in range(span):
                keys = proj[f + o, head_dim : 2 * head_dim, lane]
                score = jnp.sum(query * keys, axis=0, keepdims=True)
                score = score * (qfac * kfac[f + o, :, lane])
                part = jnp.exp(score) * mask_in[y, f, o : o + 1, :]
                norm = norm + part
                total = total + (part * vfac[f + o, :, lane]) * proj[f + o, 2 * head_dim :, lane]
            att[f, y] = total * (1.0 / norm)
        return carry

    lax.fori_loop(0, all_frames, one_frame, 0)
    toks = out.shape[0] // (scenes * queues)
    for t in range(toks):
        for y in range(scenes):
            for q in range(queues):
                parts = [
                    att[min(q * frames + i, all_frames - 1), y, :, t * tokens : (t + 1) * tokens]
                    for i in range(frames + 1)
                ]
                at = (t * queues + q) * scenes + y
                out[at] = jnp.concatenate(parts, axis=1).astype(BF16)


def stage_kernel(own_source, level_source, embed_source, own, level_mod, embed, sems):
    copies = [
        pltpu.make_async_copy(own_source, own, sems.at[0]),
        pltpu.make_async_copy(level_source.at[pl.ds(0, 2)], level_mod, sems.at[1]),
        pltpu.make_async_copy(embed_source, embed, sems.at[2]),
    ]
    for copy in copies:
        copy.start()
    for copy in copies:
        copy.wait()


def side_kernel(group, *refs):
    for k, piece in enumerate(refs[:-1]):
        refs[-1][:, k * group : (k + 1) * group] = piece[:, :group]


def ready_kernel(values, half, *refs):
    sources, table, index = refs[:8], refs[8], refs[9]
    left, right, base, factor, noise_out, guide = refs[10:16]
    held, sems = refs[16:24], refs[24]
    copies = []
    for i, (source, to) in enumerate(zip(sources, held)):
        source = source.at[2] if i == 3 else source
        copies.append(pltpu.make_async_copy(source, to, sems.at[i]))
    for copy in copies:
        copy.start()
    for copy in copies:
        copy.wait()
    packed, following, cond, gates, embed, final_gain, final_w, noise = held
    levels_all, width = gates.shape
    info = jnp.concatenate([packed[...], following[...]], axis=1)
    lanes = info.shape[1]
    ones = jnp.ones((16, lanes), BF16)
    zero = jnp.zeros((13, width), BF16)
    left[...] = jnp.concatenate(
        [embed[...]]
        + split_terms(cond[...], 3)
        + [zero]
        + split_terms(gates[...], 3)
        + split_terms(final_gain[...], 3)
        + [zero, final_w[...]],
        axis=0,
    )
    level = info[values : values + 1]
    one_hot = (lax.broadcasted_iota(jnp.int32, (levels_all, lanes), 0).astype(F32) == level).astype(
        F32
    ).astype(BF16)
    right[...] = jnp.concatenate(
        [info[:values].astype(BF16), ones, one_hot, one_hot, one_hot, ones], axis=0
    )
    own = pl.multiple_of(place_of("cfg") * half, half)
    current = noise_sigma((level + 1.0) / levels_all)
    upcoming = noise_sigma(level / levels_all)
    factor[...] = jnp.broadcast_to(upcoming - current, factor.shape)
    base[...] = jnp.concatenate(
        [packed[pl.ds(own, half), :], following[pl.ds(own, half), :]], axis=1
    )
    noise_out[...] = noise[...]
    guide[...] = jnp.full(guide.shape, table[index[0]], F32)


def finish_kernel(half, values, queues, *refs):
    parts = [refs[:5], refs[5:10]]
    attended, left, right, mine, send, scratch, mixed = refs[10:]
    scene, q_at, tok, core = (place_of(a) for a in ("scene", "queue", "tok", "cfg"))
    group = parts[0][0].shape[1] // queues
    columns = parts[0][0].shape[0]

    def weights_of(c, t, y, k):
        lane = slice(k * group, (k + 1) * group)
        if t == y == 1:
            return [parts[c][3][:, lane], parts[c][4][:, lane]]
        return [parts[c][2 * y + t][:, lane]]

    total = None
    for t in range(2):
        made = None
        for y in range(2):
            pieces = []
            for c in range(2):
                for k in range(queues):
                    pieces += weights_of(c, t, y, k)
            rows = [
                attended[((tok ^ t) * queues + k) * 2 + (scene ^ y)].astype(F32)
                for k in range(queues)
            ]
            rows = jnp.concatenate(rows, axis=0).astype(BF16)
            term = jnp.dot(jnp.concatenate(pieces, axis=0), rows, preferred_element_type=F32)
            made = term if made is None else made + term
        made = made.astype(BF16).astype(F32)
        total = made if total is None else total + made
    for c in range(2):
        for k in range(queues):
            first = ((q_at ^ k) * 2 + (core ^ c)) * columns
            at = (c * queues + k) * columns
            mixed[pl.ds(pl.multiple_of(first, 8), columns), :] = total[at : at + columns]

    first, terms = values + 16, right.shape[0]
    last = terms - 16
    emb = dot_tn(left[:first], right[:first])
    gate = dot_tn(left[first:last], right[first:last])
    gain = dot_tn(left[last:terms], right[last:])
    summed = emb + gate * mixed[...]
    center = jnp.mean(summed, axis=0, keepdims=True)
    deviate = summed - center
    spread = jnp.mean(deviate * deviate, axis=0, keepdims=True)
    final = (deviate * lax.rsqrt(spread + EPS_NORM) * gain).astype(BF16)
    scratch[...] = jnp.dot(left[terms:], final, preferred_element_type=F32)
    own = pl.multiple_of(core * half, half)
    other = pl.multiple_of((1 - core) * half, half)
    mine[...] = scratch[pl.ds(own, half), :]
    send[...] = scratch[pl.ds(other, half), :]


def update_kernel(mine, partner, base, factor, noise, guide, vel, new):
    frames, _, tokens = vel.shape
    is_cond = place_of("cfg") == 0
    here, there = mine[...], partner[...]
    cond = jnp.where(is_cond, here, there)
    uncond = jnp.where(is_cond, there, here)
    guided = uncond + guide[0:1, 0:1] * (cond - uncond)
    updated = base[...] + factor[...] * guided
    is_last = place_of("queue") == lax.axis_size("queue") - 1
    for f in range(frames):
        vel[f] = guided[:, f * tokens : (f + 1) * tokens]
        moved = updated[:, (f + 1) * tokens : (f + 2) * tokens]
        if f == frames - 1:
            moved = jnp.where(is_last, noise[...], moved)
        new[f] = moved


def swapped(value, axis, mask):
    count = lax.axis_size(axis)
    return lax.ppermute(value, axis, [(i, i ^ mask) for i in range(count)])


def on_device_heads(
    latents,
    fresh_noise,
    levels,
    window_mask,
    cond_embed,
    level_mod,
    embed_weight,
    qkv_weight,
    query_gain,
    key_gain,
    out_weight,
    final_gain,
    final_weight,
    guide_table,
    guide_index,
):
    frames, values, tokens = latents.shape
    width = embed_weight.shape[1]
    head_dim = query_gain.shape[0]
    levels_all = level_mod.shape[0]
    span = window_mask.shape[1]
    window = span // 2
    scenes, queues, toks = (lax.axis_size(a) for a in ("scene", "queue", "tok"))
    chips = scenes * queues * toks
    all_frames = queues * frames
    per_core = frames // 2
    cond_rows = 3 * -(-(width // (queues * toks)) // (per_core * tokens))
    rows = -(-max(values + scenes + 2, values + span + 1 + cond_rows) // 16) * 16
    own_rows = -(-(values + 1) // 8) * 8
    local_rows = qkv_weight.shape[0]
    local_heads = qkv_weight.shape[2] // head_dim
    lanes = scenes * LANES
    row_lanes = (frames + 1) * tokens
    mods = jnp.transpose(level_mod, (1, 0, 2))

    group = out_weight.shape[0] // scenes
    chunk = jax.ShapeDtypeStruct((local_rows, group + 3 * head_dim), BF16)
    *chunks, copies, packed, first = kernel_call(
        functools.partial(pack_kernel, head_dim, per_core),
        [chunk] * queues
        + [
            jax.ShapeDtypeStruct((chips, rows, per_core * tokens), BF16),
            jax.ShapeDtypeStruct((own_rows, frames * tokens), F32),
            jax.ShapeDtypeStruct((own_rows, tokens), F32),
        ],
        "vvvvvv",
        [pltpu.VMEM((local_heads, local_rows, 3 * head_dim), BF16)],
        vmem=WHOLE_VMEM,
        bytes_accessed=8_000_000,
    )(
        latents,
        levels[None],
        window_mask,
        jnp.transpose(qkv_weight, (1, 0, 2)),
        out_weight.T,
        cond_embed,
    )

    near = [chunks[0]] + [swapped(chunks[k], "queue", k) for k in range(1, queues)]
    own, level_rows, embed_held = kernel_call(
        stage_kernel,
        [
            chunk,
            jax.ShapeDtypeStruct((2, levels_all, width), F32),
            jax.ShapeDtypeStruct(embed_weight.shape, BF16),
        ],
        "hhh",
        [pltpu.SemaphoreType.DMA((3,))],
    )(chunks[0], mods, embed_weight)
    near[1], own, level_rows, embed_held = lax.optimization_barrier(
        (near[1], own, level_rows, embed_held)
    )
    far = [swapped(piece, "cfg", 1) for piece in near]
    shares = lax.all_to_all(copies, ("scene", "queue", "tok"), 0, 0)
    other_shares = swapped(shares, "cfg", 1)

    following = lax.ppermute(first, "queue", [(i + 1, i) for i in range(queues - 1)])
    near[-1], following, shares, *far[:-1] = lax.optimization_barrier(
        (near[-1], following, shares, *far[:-1])
    )
    part = kernel_call(
        functools.partial(side_kernel, group),
        jax.ShapeDtypeStruct((local_rows, queues * group), BF16),
        "v" * queues,
    )(own, *near[1:])
    part_tok, part_scene = swapped(part, "tok", 1), swapped(part, "scene", 1)

    lhs, xin, rstd, masks = kernel_call(
        functools.partial(prepare_kernel, frames, values, span),
        [
            jax.ShapeDtypeStruct((scenes * all_frames * rows, width), BF16),
            jax.ShapeDtypeStruct((all_frames, scenes * rows, lanes), BF16),
            jax.ShapeDtypeStruct((all_frames, 1, lanes), F32),
            jax.ShapeDtypeStruct((scenes, all_frames, rows - values, LANES), F32),
        ],
        "vvvv",
        bytes_accessed=8_000_000,
    )(shares, other_shares, level_rows, embed_held)
    attended = kernel_call(
        functools.partial(attend_kernel, frames, tokens, queues),
        jax.ShapeDtypeStruct((chips, head_dim, row_lanes), BF16),
        "v" * (2 * queues + 6),
        [
            pltpu.VMEM((width, 3 * head_dim), BF16),
            pltpu.VMEM((all_frames + 2 * window, 3 * head_dim, lanes), F32),
            pltpu.VMEM((all_frames + 2 * window, 1, lanes), F32),
            pltpu.VMEM((all_frames + 2 * window, 1, lanes), F32),
            pltpu.VMEM((all_frames, scenes, head_dim, LANES), F32),
        ],
        bytes_accessed=100_000_000,
    )(own, *near[1:], *far, lhs, xin, rstd, masks, query_gain[None], key_gain[None])
    attended, part, part_tok, part_scene = lax.optimization_barrier(
        (attended, part, part_tok, part_scene)
    )
    received = lax.all_to_all(attended, ("tok", "queue", "scene"), 0, 0)
    cut = -(-local_rows // 32) * 16
    upper = swapped(part_tok[:cut], "scene", 1)
    lower = swapped(part_scene[cut:], "tok", 1)
    half = values // 2
    half_shape = jax.ShapeDtypeStruct((half, row_lanes), F32)
    smalls = (
        packed,
        following,
        cond_embed,
        mods,
        embed_weight,
        final_gain[None],
        final_weight.T,
        fresh_noise,
    )
    places = [
        pltpu.VMEM(a.shape[1:] if i == 3 else a.shape, a.dtype) for i, a in enumerate(smalls)
    ]
    terms = values + 16 + 3 * levels_all + 16
    left, right, *rest = kernel_call(
        functools.partial(ready_kernel, values, half),
        [
            jax.ShapeDtypeStruct((terms + values, width), BF16),
            jax.ShapeDtypeStruct((terms, row_lanes), BF16),
            half_shape,
            half_shape,
            jax.ShapeDtypeStruct(fresh_noise.shape, F32),
            jax.ShapeDtypeStruct((8, LANES), F32),
        ],
        "ha" + "h" * 6 + "ss",
        places + [pltpu.SemaphoreType.DMA((len(smalls),))],
    )(*smalls, guide_table, guide_index)
    upper, lower, right = lax.optimization_barrier((upper, lower, right))
    away = [part, part_tok, part_scene, upper, lower]
    away_far = [swapped(piece, "cfg", 1) for piece in away]

    mine, send = kernel_call(
        functools.partial(finish_kernel, half, values, queues),
        [half_shape] * 2,
        "v" * 13,
        [pltpu.VMEM((values, row_lanes), F32), pltpu.VMEM((width, row_lanes), F32)],
        bytes_accessed=8_000_000,
    )(*away, *away_far, received, left, right)
    partner = swapped(send, "cfg", 1)
    shape = jax.ShapeDtypeStruct((frames, half, tokens), F32)
    return kernel_call(update_kernel, [shape, shape], "v" * 6)(mine, partner, *rest)


def on_device(*args):
    latents, qkv_weight, query_gain = args[0], args[7], args[8]
    local_heads = qkv_weight.shape[2] // query_gain.shape[0]
    scenes, queues, toks, cores = (lax.axis_size(a) for a in ("scene", "queue", "tok", "cfg"))
    pairs = scenes == toks == cores == 2 and queues & (queues - 1) == 0
    fits = latents.shape[2] * toks <= LANES and latents.shape[0] % cores == 0
    if pairs and fits and local_heads == scenes * queues:
        return tuple(on_device_heads(*args))
    return on_device_general(*args)


def solution(mesh):
    placed = (
        P(("scene", "queue"), None, "tok"),
        P(("scene", "cfg"), "tok"),
        P(("scene", "queue")),
        P(("scene", "queue"), None),
        P(("scene", "cfg"), None),
        P(),
        P(),
        P(("queue", "cfg"), None, "tok"),
        P(),
        P(),
        P("tok", ("queue", "cfg")),
        P(),
        P(),
        P(),
        P(),
    )
    return jax.shard_map(
        on_device,
        mesh=mesh,
        in_specs=placed,
        out_specs=(P(("scene", "queue"), "cfg", "tok"), P(("scene", "queue"), "cfg", "tok")),
        check_vma=False,
    )
```

```python
import functools

import jax
import jax.numpy as jnp
from jax import lax
from jax.experimental import pallas as pl
from jax.experimental.pallas import tpu as pltpu
from jax.sharding import PartitionSpec as P

EPS_NORM = 1e-06
TIME_SHIFT = 3.0
LANES = 128
VMEM_BYTES = 20 * 1024 * 1024
WHOLE_VMEM = 62 * 1024 * 1024
F32 = jnp.float32
BF16 = jnp.bfloat16


def noise_sigma(fraction):
    return TIME_SHIFT * fraction / (1.0 + (TIME_SHIFT - 1.0) * fraction)


def from_partner(value, axis, bit):
    return lax.ppermute(value, axis, [(i, i ^ 1 << bit) for i in range(lax.axis_size(axis))])


def with_halo(cells, sides, width):
    for axis, dim in sides:
        count = lax.axis_size(axis)
        ends = count - 1
        head = lax.slice_in_dim(cells, 0, width, axis=dim)
        tail = lax.slice_in_dim(cells, cells.shape[dim] - width, cells.shape[dim], axis=dim)
        cells = jnp.concatenate(
            [
                lax.ppermute(tail, axis, [(i, (i + 1) % count) for i in range(ends)]),
                cells,
                lax.ppermute(head, axis, [((i + 1) % count, i) for i in range(ends)]),
            ],
            axis=dim,
        )
    return cells


def shifted(value, axis, steps):
    count = lax.axis_size(axis)
    initial, last = (max(0, -steps), min(count, count - steps))
    return lax.ppermute(value, axis, [(source, source + steps) for source in range(initial, last)])


def layer_norm(values):
    center = jnp.mean(values, axis=-1, keepdims=True)
    deviate = values - center
    spread = jnp.mean(deviate * deviate, axis=-1, keepdims=True)
    return deviate * lax.rsqrt(spread + EPS_NORM)


def rms_norm(values, scaling):
    return (
        values * lax.rsqrt(jnp.mean(values * values, axis=-1, keepdims=True) + EPS_NORM) * scaling
    )


def temporal_attention(
    queries, key_rows, value_rows, window_mask, first_frame, total_frames, window
):
    frames = queries.shape[0]
    numerator = jnp.zeros(queries.shape, jnp.float32)
    denominator = jnp.zeros(queries.shape[:-1], jnp.float32)
    for offset in range(2 * window + 1):
        near_keys = key_rows[offset : offset + frames].astype(jnp.float32)
        near_values = value_rows[offset : offset + frames].astype(jnp.float32)
        scores = jnp.sum(queries * near_keys, axis=-1) * queries.shape[-1] ** (-0.5)
        target = first_frame + jnp.arange(frames, dtype=jnp.int32) + (offset - window)
        allowed = (window_mask[:, offset] == 1) & (target >= 0) & (target < total_frames)
        weights = jnp.exp(scores) * allowed.astype(jnp.float32)[:, None, None]
        numerator = numerator + weights[..., None] * near_values
        denominator = denominator + weights
    return numerator / denominator[..., None]


def on_device_general(
    latents,
    fresh_noise,
    levels,
    window_mask,
    cond_embed,
    level_mod,
    embed_weight,
    qkv_weight,
    query_gain,
    key_gain,
    out_weight,
    final_gain,
    final_weight,
    guide_table,
    guide_index,
):
    frames = latents.shape[0]
    tok_count = latents.shape[2]
    model_width = embed_weight.shape[1]
    head_dim = query_gain.shape[0]
    levels_all = level_mod.shape[0]
    queue_count = lax.axis_size("queue")
    all_tokens = lax.all_gather(latents, "tok", axis=2, tiled=True)
    seq_tokens = all_tokens.shape[2]
    row_count = frames * seq_tokens
    embedded = (
        jnp.einsum(
            "fcs,cd->fsd",
            all_tokens.astype(jnp.bfloat16),
            embed_weight,
            preferred_element_type=jnp.float32,
        )
        + cond_embed[0]
    )
    one_hot = (levels[:, None] == jnp.arange(levels_all, dtype=jnp.int32)[None, :]).astype(
        jnp.float32
    )
    modulate = jnp.dot(
        one_hot, level_mod.reshape(levels_all, 3 * model_width), precision=lax.Precision.HIGHEST
    ).reshape(frames, 3, model_width)
    normed = (layer_norm(embedded) * (1.0 + modulate[:, None, 1]) + modulate[:, None, 0]).astype(
        jnp.bfloat16
    )
    norm_rows = normed.reshape(row_count, model_width)
    local_cols = qkv_weight.shape[2]
    shard_piece = lax.all_gather(qkv_weight, ("queue", "cfg"), axis=0, tiled=True)
    flat_piece = shard_piece.reshape(shard_piece.shape[0], 3 * local_cols)
    projected = jnp.dot(norm_rows, flat_piece, preferred_element_type=jnp.float32)
    projected = projected.reshape(frames, seq_tokens, 3, local_cols // head_dim, head_dim)
    queries = rms_norm(projected[:, :, 0], query_gain)
    keys_values = jnp.stack(
        [
            rms_norm(projected[:, :, 1], key_gain).astype(jnp.bfloat16),
            projected[:, :, 2].astype(jnp.bfloat16),
        ]
    )
    window = window_mask.shape[1] // 2
    widened = with_halo(keys_values, (("queue", 1),), window)
    first_frame = lax.axis_index("queue") * frames
    attended = temporal_attention(
        queries, widened[0], widened[1], window_mask, first_frame, frames * queue_count, window
    )
    attended = attended.astype(jnp.bfloat16).reshape(frames, seq_tokens, local_cols)
    flat_heads = attended.reshape(row_count, local_cols)
    partial_value = jnp.dot(
        flat_heads,
        lax.all_gather(out_weight, ("queue", "cfg"), axis=1, tiled=True),
        preferred_element_type=jnp.float32,
    )
    mixed_out = lax.psum_scatter(
        partial_value.reshape(frames, seq_tokens, model_width).astype(jnp.bfloat16),
        "tok",
        scatter_dimension=1,
        tiled=True,
    ).astype(jnp.float32)
    own_start = lax.axis_index("tok") * tok_count
    own_embed = lax.dynamic_slice_in_dim(embedded, own_start, tok_count, 1)
    summed = own_embed + modulate[:, None, 2] * mixed_out
    final_rows = (layer_norm(summed) * final_gain).astype(jnp.bfloat16)
    velocity = jnp.einsum(
        "ftd,dc->fct", final_rows, final_weight, preferred_element_type=jnp.float32
    )
    half_values = velocity.shape[1] // 2
    branch_index = lax.axis_index("cfg")
    own_first = branch_index * half_values
    other_first = (1 - branch_index) * half_values
    outgoing = lax.dynamic_slice_in_dim(velocity, other_first, half_values, 1)
    partner = from_partner(outgoing, "cfg", 0)
    mine = lax.dynamic_slice_in_dim(velocity, own_first, half_values, 1)
    is_cond = branch_index == 0
    cond_vel = jnp.where(is_cond, mine, partner)
    uncond_vel = jnp.where(is_cond, partner, mine)
    entries = guide_table.shape[0]
    guidance = jnp.sum(
        guide_table * (jnp.arange(entries, dtype=jnp.int32) == guide_index[0]).astype(jnp.float32)
    )
    guided = uncond_vel + guidance * (cond_vel - uncond_vel)
    current = noise_sigma((levels + 1).astype(jnp.float32) / levels_all)
    upcoming = noise_sigma(levels.astype(jnp.float32) / levels_all)
    own_latents = lax.dynamic_slice_in_dim(latents, own_first, half_values, 1)
    updated = own_latents + (upcoming - current)[:, None, None] * guided
    incoming = shifted(updated[:1], "queue", -1)
    is_last = lax.axis_index("queue") == queue_count - 1
    incoming = jnp.where(is_last, fresh_noise[None], incoming)
    new_queue = jnp.concatenate([updated[1:], incoming], axis=0)
    return (guided, new_queue)


def kernel_call(body, out_shapes, spaces, scratch=(), vmem=VMEM_BYTES, **cost):
    kinds = {
        "v": pl.BlockSpec(),
        "s": pl.BlockSpec(memory_space=pltpu.SMEM),
        "a": pl.BlockSpec(memory_space=pl.ANY),
        "h": pl.BlockSpec(memory_space=pltpu.HBM),
    }
    many = isinstance(out_shapes, (list, tuple))
    return pl.pallas_call(
        body,
        out_shape=out_shapes,
        in_specs=[kinds[k] for k in spaces],
        out_specs=[pl.BlockSpec() for _ in out_shapes] if many else pl.BlockSpec(),
        scratch_shapes=list(scratch),
        compiler_params=pltpu.CompilerParams(vmem_limit_bytes=vmem),
        cost_estimate=pl.CostEstimate(
            flops=cost.get("flops", 1000000),
            bytes_accessed=cost.get("bytes_accessed", 1000000),
            transcendentals=0,
        ),
    )


def split_terms(values, terms):
    parts = []
    for _ in range(terms):
        part = values.astype(BF16)
        parts.append(part)
        values = values - part.astype(F32)
    return parts


def dot_tn(left, right):
    return lax.dot_general(
        left, right, (((0,), (0,)), ((), ())), preferred_element_type=F32
    )


def place_of(axis):
    return lax.axis_index(axis)


def pack_kernel(head_dim, copies_frames, latents, levels, window_mask, qkv, out_w, cond, *outs):
    scratch = outs[-1]
    copies, packed, first = outs[-4:-1]
    chunks = outs[:-4]
    scene, q, tok, core = (place_of(a) for a in ("scene", "queue", "tok", "cfg"))
    for h in range(scratch.shape[0]):
        start = h * head_dim
        scratch[h] = jnp.concatenate(
            [qkv[part, :, start : start + head_dim] for part in range(3)], axis=1
        )
    group = out_w.shape[1] // 2
    half = jnp.where(scene == 0, out_w[:, :group], out_w[:, group:])
    for k, chunk in enumerate(chunks):
        chunk[...] = jnp.concatenate([half, scratch[scene * len(chunks) + (q ^ k)]], axis=1)
    frames, values, tokens = latents.shape
    span = window_mask.shape[1]
    shares = []
    own = []
    for f in range(frames):
        level = levels[:, f : f + 1].astype(F32)
        side = jnp.zeros((copies.shape[1] - values, tokens), F32)
        row_id = lax.broadcasted_iota(jnp.int32, side.shape, 0)
        for o in range(span):
            side = jnp.where(row_id == o, window_mask[f : f + 1, o : o + 1].astype(F32), side)
        side = jnp.where(row_id == span, level, side)
        shares.append(jnp.concatenate([latents[f], side], axis=0))
        fill = jnp.broadcast_to(level, (packed.shape[0] - values, tokens))
        own.append(jnp.concatenate([latents[f], fill], axis=0))
    lower = jnp.concatenate(shares[:copies_frames], axis=1)
    upper = jnp.concatenate(shares[copies_frames:], axis=1)
    share = jnp.where(core == 0, lower, upper)
    spots = lax.axis_size("queue") * lax.axis_size("tok")
    length = cond.shape[1] // spots
    piece = jnp.zeros((1, length), F32)
    for i in range(spots):
        chosen = q * lax.axis_size("tok") + tok == i
        piece = jnp.where(chosen, cond[:, i * length : (i + 1) * length], piece)
    row_id = lax.broadcasted_iota(jnp.int32, share.shape, 0)
    at_row, step = values + span + 1, share.shape[1]
    for term in split_terms(piece, 3):
        for start in range(0, length, step):
            line = term.astype(F32)[:, start : start + step]
            fill = jnp.zeros((1, step - line.shape[1]), F32)
            line = jnp.concatenate([line, fill], axis=1) if fill.shape[1] else line
            share = jnp.where(row_id == at_row, line, share)
            at_row += 1
    share = share.astype(BF16)
    for at in range(copies.shape[0]):
        copies[at] = share
    packed[...] = jnp.concatenate(own, axis=1)
    first[...] = own[0]


def prepare_kernel(
    frames,
    values,
    span,
    mine,
    other,
    level_mod,
    embed,
    lhs,
    xin,
    rstd_out,
    mask_out,
):
    width = embed.shape[1]
    scenes, all_frames = mask_out.shape[:2]
    rows = xin.shape[1] // scenes
    queues = all_frames // frames
    toks = mine.shape[0] // (scenes * queues)
    per_core = frames // 2
    tokens = mine.shape[2] // per_core
    core = place_of("cfg")
    weights = embed[...].astype(F32)
    weights = weights - jnp.mean(weights, axis=1, keepdims=True)
    length, step = width // (queues * toks), mine.shape[2]
    lines = -(-length // step)
    conds = []
    for y in range(scenes):
        pieces = []
        for at in range(y * queues * toks, (y + 1) * queues * toks):
            info = mine[at].astype(F32)
            first = values + span + 1
            terms = sum(info[first + i * lines : first + (i + 1) * lines] for i in range(3))
            for i in range(lines):
                pieces.append(terms[i : i + 1, : min(step, length - i * step)])
        conds.append(jnp.concatenate(pieces, axis=1))
    conds = jnp.concatenate(conds, axis=0)
    conds = conds - jnp.mean(conds, axis=1, keepdims=True)
    basis = jnp.concatenate(
        [weights, conds, jnp.zeros((rows - values - scenes, width), F32)], axis=0
    )
    gram = lax.dot_general(
        basis,
        basis,
        (((1,), (1,)), ((), ())),
        preferred_element_type=F32,
        precision=lax.Precision.HIGHEST,
    ) * (1.0 / width)
    row_id = lax.broadcasted_iota(jnp.int32, (rows, LANES), 0)
    wide_id = lax.broadcasted_iota(jnp.int32, (rows, width), 0)
    level_id = lax.broadcasted_iota(jnp.int32, (level_mod.shape[1], width), 0).astype(F32)
    shift_row = values + scenes
    fill = LANES - toks * tokens
    for y in range(scenes):
        for q in range(queues):
            first = (y * queues + q) * toks
            held = []
            for t in range(toks):
                one, two = mine[first + t].astype(F32), other[first + t].astype(F32)
                held.append((jnp.where(core == 0, one, two), jnp.where(core == 0, two, one)))
            for part in range(frames):
                f = q * frames + part
                at = part % per_core * tokens
                info = [pair[part // per_core][:, at : at + tokens] for pair in held]
                level = info[0][values + span : values + span + 1, 0:1]
                chosen = level_id == level
                shift = jnp.sum(jnp.where(chosen, level_mod[0], 0.0), axis=0, keepdims=True)
                scale = jnp.sum(jnp.where(chosen, level_mod[1], 0.0), axis=0, keepdims=True)
                block = basis * (1.0 + scale)
                block = jnp.where((wide_id == shift_row) | (wide_id == shift_row + 1), shift, block)
                to = (f * scenes + y) * rows
                lhs[to : to + rows, :] = block.astype(BF16)
                info = jnp.concatenate(info + [jnp.ones((info[0].shape[0], fill), F32)], axis=1)
                mask_out[y, f] = info[values : values + mask_out.shape[2]]
                vec = jnp.where(row_id < values, info[:rows], 0.0)
                vec = jnp.where(row_id == values + y, 1.0, vec)
                spread = jnp.sum(
                    vec
                    * jnp.dot(
                        gram, vec, preferred_element_type=F32, precision=lax.Precision.HIGHEST
                    ),
                    axis=0,
                    keepdims=True,
                )
                spread = jnp.maximum(spread, 0.0) + EPS_NORM
                rstd = lax.rsqrt(spread)
                std = spread * rstd
                high = std.astype(BF16).astype(F32)
                vec = jnp.where(row_id == shift_row, high, vec)
                vec = jnp.where(row_id == shift_row + 1, std - high, vec)
                blank = jnp.zeros(vec.shape, F32)
                blocks = [vec if n == y else blank for n in range(scenes)]
                xin[f, y * rows : (y + 1) * rows] = jnp.concatenate(blocks, axis=1).astype(BF16)
                rstd_out[f, :, y * LANES : (y + 1) * LANES] = rstd


def attend_kernel(frames, tokens, queues, *refs):
    pieces = refs[: 2 * queues]
    lhs, xin, rstd_in, mask_in, gain_q, gain_k, out, whole, proj, kfac, vfac, att = refs[
        2 * queues :
    ]
    scenes, all_frames = mask_in.shape[:2]
    rows = xin.shape[1]
    head_dim = gain_q.shape[1]
    window = (proj.shape[0] - all_frames) // 2
    span = 2 * window + 1
    q_at, core = place_of("queue"), place_of("cfg")
    part_rows = pieces[0].shape[0]
    for k in range(queues):
        for side in range(2):
            owner = core if side == 0 else 1 - core
            first = pl.multiple_of(((q_at ^ k) * 2 + owner) * part_rows, 16)
            piece = pieces[side * queues + k]
            whole[pl.ds(first, part_rows), :] = piece[:, piece.shape[1] - 3 * head_dim :]
    folded = jnp.dot(lhs[...], whole[...], preferred_element_type=F32)
    high, low = split_terms(folded, 2)
    gains = split_terms(gain_q[...] * gain_k[...] * head_dim ** (-0.5), 3)
    gains = jnp.concatenate(gains + [jnp.zeros((13, head_dim), BF16)], axis=0)
    gains = dot_tn(gains, jnp.ones((16, LANES), BF16))
    for side in range(window):
        for at in (side, all_frames + window + side):
            proj[at] = jnp.zeros(proj.shape[1:], F32)
            kfac[at] = jnp.zeros(kfac.shape[1:], F32)
            vfac[at] = jnp.zeros(vfac.shape[1:], F32)
    for f in range(all_frames):
        piece = slice(f * rows, (f + 1) * rows)
        made = dot_tn(
            jnp.concatenate([high[piece], low[piece]], axis=0),
            jnp.concatenate([xin[f], xin[f]], axis=0),
        )
        proj[f + window] = made
        rstd = rstd_in[f]
        keys = made[head_dim : 2 * head_dim]
        square = jnp.mean(keys * keys, axis=0, keepdims=True)
        kfac[f + window] = rstd * lax.rsqrt(rstd * rstd * square + EPS_NORM)
        vfac[f + window] = rstd

    def one_frame(f, carry):
        for y in range(scenes):
            lane = slice(y * LANES, (y + 1) * LANES)
            query = proj[f + window, 0:head_dim, lane]
            rstd = vfac[f + window, :, lane]
            square = jnp.mean(query * query, axis=0, keepdims=True)
            qfac = rstd * lax.rsqrt(rstd * rstd * square + EPS_NORM)
            query = query * gains
            total = jnp.zeros((head_dim, LANES), F32)
            norm = jnp.zeros((1, LANES), F32)
            for o in range(span):
                keys = proj[f + o, head_dim : 2 * head_dim, lane]
                score = jnp.sum(query * keys, axis=0, keepdims=True)
                score = score * (qfac * kfac[f + o, :, lane])
                part = jnp.exp(score) * mask_in[y, f, o : o + 1, :]
                norm = norm + part
                total = total + (part * vfac[f + o, :, lane]) * proj[f + o, 2 * head_dim :, lane]
            att[f, y] = total * (1.0 / norm)
        return carry

    lax.fori_loop(0, all_frames, one_frame, 0, unroll=2)
    toks = out.shape[0] // (scenes * queues)
    for t in range(toks):
        for y in range(scenes):
            for q in range(queues):
                parts = [
                    att[min(q * frames + i, all_frames - 1), y, :, t * tokens : (t + 1) * tokens]
                    for i in range(frames + 1)
                ]
                at = (t * queues + q) * scenes + y
                out[at] = jnp.concatenate(parts, axis=1).astype(BF16)


def stage_kernel(own_source, level_source, embed_source, own, level_mod, embed, sems):
    copies = [
        pltpu.make_async_copy(own_source, own, sems.at[0]),
        pltpu.make_async_copy(level_source.at[pl.ds(0, 2)], level_mod, sems.at[1]),
        pltpu.make_async_copy(embed_source, embed, sems.at[2]),
    ]
    for copy in copies:
        copy.start()
    for copy in copies:
        copy.wait()


def side_kernel(group, *refs):
    for k, piece in enumerate(refs[:-1]):
        refs[-1][:, k * group : (k + 1) * group] = piece[:, :group]


def ready_kernel(values, half, *refs):
    sources, table, index = refs[:8], refs[8], refs[9]
    left, right, base, factor, noise_out, guide = refs[10:16]
    held, sems = refs[16:24], refs[24]
    copies = []
    for i, (source, to) in enumerate(zip(sources, held)):
        source = source.at[2] if i == 3 else source
        copies.append(pltpu.make_async_copy(source, to, sems.at[i]))
    for copy in copies:
        copy.start()
    for copy in copies:
        copy.wait()
    packed, following, cond, gates, embed, final_gain, final_w, noise = held
    levels_all, width = gates.shape
    info = jnp.concatenate([packed[...], following[...]], axis=1)
    lanes = info.shape[1]
    ones = jnp.ones((16, lanes), BF16)
    zero = jnp.zeros((13, width), BF16)
    left[...] = jnp.concatenate(
        [embed[...]]
        + split_terms(cond[...], 3)
        + [zero]
        + split_terms(gates[...], 3)
        + split_terms(final_gain[...], 3)
        + [zero, final_w[...]],
        axis=0,
    )
    level = info[values : values + 1]
    one_hot = (lax.broadcasted_iota(jnp.int32, (levels_all, lanes), 0).astype(F32) == level).astype(
        F32
    ).astype(BF16)
    right[...] = jnp.concatenate(
        [info[:values].astype(BF16), ones, one_hot, one_hot, one_hot, ones], axis=0
    )
    own = pl.multiple_of(place_of("cfg") * half, half)
    current = noise_sigma((level + 1.0) / levels_all)
    upcoming = noise_sigma(level / levels_all)
    factor[...] = jnp.broadcast_to(upcoming - current, factor.shape)
    base[...] = jnp.concatenate(
        [packed[pl.ds(own, half), :], following[pl.ds(own, half), :]], axis=1
    )
    noise_out[...] = noise[...]
    guide[...] = jnp.full(guide.shape, table[index[0]], F32)


def finish_kernel(half, values, queues, *refs):
    parts = [refs[:5], refs[5:10]]
    attended, left, right, mine, send, scratch, mixed = refs[10:]
    scene, q_at, tok, core = (place_of(a) for a in ("scene", "queue", "tok", "cfg"))
    group = parts[0][0].shape[1] // queues
    columns = parts[0][0].shape[0]

    def weights_of(c, t, y, k):
        lane = slice(k * group, (k + 1) * group)
        if t == y == 1:
            return [parts[c][3][:, lane], parts[c][4][:, lane]]
        return [parts[c][2 * y + t][:, lane]]

    total = None
    for t in range(2):
        made = None
        for y in range(2):
            pieces = []
            for c in range(2):
                for k in range(queues):
                    pieces += weights_of(c, t, y, k)
            rows = [
                attended[((tok ^ t) * queues + k) * 2 + (scene ^ y)].astype(F32)
                for k in range(queues)
            ]
            rows = jnp.concatenate(rows, axis=0).astype(BF16)
            term = jnp.dot(jnp.concatenate(pieces, axis=0), rows, preferred_element_type=F32)
            made = term if made is None else made + term
        made = made.astype(BF16).astype(F32)
        total = made if total is None else total + made
    for c in range(2):
        for k in range(queues):
            first = ((q_at ^ k) * 2 + (core ^ c)) * columns
            at = (c * queues + k) * columns
            mixed[pl.ds(pl.multiple_of(first, 8), columns), :] = total[at : at + columns]

    first, terms = values + 16, right.shape[0]
    last = terms - 16
    emb = dot_tn(left[:first], right[:first])
    gate = dot_tn(left[first:last], right[first:last])
    gain = dot_tn(left[last:terms], right[last:])
    summed = emb + gate * mixed[...]
    center = jnp.mean(summed, axis=0, keepdims=True)
    deviate = summed - center
    spread = jnp.mean(deviate * deviate, axis=0, keepdims=True)
    final = (deviate * lax.rsqrt(spread + EPS_NORM) * gain).astype(BF16)
    scratch[...] = jnp.dot(left[terms:], final, preferred_element_type=F32)
    own = pl.multiple_of(core * half, half)
    other = pl.multiple_of((1 - core) * half, half)
    mine[...] = scratch[pl.ds(own, half), :]
    send[...] = scratch[pl.ds(other, half), :]


def update_kernel(mine, partner, base, factor, noise, guide, vel, new):
    frames, _, tokens = vel.shape
    is_cond = place_of("cfg") == 0
    here, there = mine[...], partner[...]
    cond = jnp.where(is_cond, here, there)
    uncond = jnp.where(is_cond, there, here)
    guided = uncond + guide[0:1, 0:1] * (cond - uncond)
    updated = base[...] + factor[...] * guided
    is_last = place_of("queue") == lax.axis_size("queue") - 1
    for f in range(frames):
        vel[f] = guided[:, f * tokens : (f + 1) * tokens]
        moved = updated[:, (f + 1) * tokens : (f + 2) * tokens]
        if f == frames - 1:
            moved = jnp.where(is_last, noise[...], moved)
        new[f] = moved


def swapped(value, axis, mask):
    count = lax.axis_size(axis)
    return lax.ppermute(value, axis, [(i, i ^ mask) for i in range(count)])


def on_device_heads(
    latents,
    fresh_noise,
    levels,
    window_mask,
    cond_embed,
    level_mod,
    embed_weight,
    qkv_weight,
    query_gain,
    key_gain,
    out_weight,
    final_gain,
    final_weight,
    guide_table,
    guide_index,
):
    frames, values, tokens = latents.shape
    width = embed_weight.shape[1]
    head_dim = query_gain.shape[0]
    levels_all = level_mod.shape[0]
    span = window_mask.shape[1]
    window = span // 2
    scenes, queues, toks = (lax.axis_size(a) for a in ("scene", "queue", "tok"))
    chips = scenes * queues * toks
    all_frames = queues * frames
    per_core = frames // 2
    cond_rows = 3 * -(-(width // (queues * toks)) // (per_core * tokens))
    rows = -(-max(values + scenes + 2, values + span + 1 + cond_rows) // 16) * 16
    own_rows = -(-(values + 1) // 8) * 8
    local_rows = qkv_weight.shape[0]
    local_heads = qkv_weight.shape[2] // head_dim
    lanes = scenes * LANES
    row_lanes = (frames + 1) * tokens
    mods = jnp.transpose(level_mod, (1, 0, 2))

    group = out_weight.shape[0] // scenes
    chunk = jax.ShapeDtypeStruct((local_rows, group + 3 * head_dim), BF16)
    *chunks, copies, packed, first = kernel_call(
        functools.partial(pack_kernel, head_dim, per_core),
        [chunk] * queues
        + [
            jax.ShapeDtypeStruct((chips, rows, per_core * tokens), BF16),
            jax.ShapeDtypeStruct((own_rows, frames * tokens), F32),
            jax.ShapeDtypeStruct((own_rows, tokens), F32),
        ],
        "vvvvvv",
        [pltpu.VMEM((local_heads, local_rows, 3 * head_dim), BF16)],
        vmem=WHOLE_VMEM,
        bytes_accessed=8_000_000,
    )(
        latents,
        levels[None],
        window_mask,
        jnp.transpose(qkv_weight, (1, 0, 2)),
        out_weight.T,
        cond_embed,
    )

    near = [chunks[0]] + [swapped(chunks[k], "queue", k) for k in range(1, queues)]
    own, level_rows, embed_held = kernel_call(
        stage_kernel,
        [
            chunk,
            jax.ShapeDtypeStruct((2, levels_all, width), F32),
            jax.ShapeDtypeStruct(embed_weight.shape, BF16),
        ],
        "hhh",
        [pltpu.SemaphoreType.DMA((3,))],
    )(chunks[0], mods, embed_weight)
    near[1], own, level_rows, embed_held = lax.optimization_barrier(
        (near[1], own, level_rows, embed_held)
    )
    far = [swapped(piece, "cfg", 1) for piece in near]
    shares = lax.all_to_all(copies, ("scene", "queue", "tok"), 0, 0)
    other_shares = swapped(shares, "cfg", 1)

    following = lax.ppermute(first, "queue", [(i + 1, i) for i in range(queues - 1)])
    near[-1], following, shares, *far[:-1] = lax.optimization_barrier(
        (near[-1], following, shares, *far[:-1])
    )
    part = kernel_call(
        functools.partial(side_kernel, group),
        jax.ShapeDtypeStruct((local_rows, queues * group), BF16),
        "v" * queues,
    )(own, *near[1:])
    part_tok, part_scene = swapped(part, "tok", 1), swapped(part, "scene", 1)

    lhs, xin, rstd, masks = kernel_call(
        functools.partial(prepare_kernel, frames, values, span),
        [
            jax.ShapeDtypeStruct((scenes * all_frames * rows, width), BF16),
            jax.ShapeDtypeStruct((all_frames, scenes * rows, lanes), BF16),
            jax.ShapeDtypeStruct((all_frames, 1, lanes), F32),
            jax.ShapeDtypeStruct((scenes, all_frames, rows - values, LANES), F32),
        ],
        "vvvv",
        bytes_accessed=8_000_000,
    )(shares, other_shares, level_rows, embed_held)
    attended = kernel_call(
        functools.partial(attend_kernel, frames, tokens, queues),
        jax.ShapeDtypeStruct((chips, head_dim, row_lanes), BF16),
        "v" * (2 * queues + 6),
        [
            pltpu.VMEM((width, 3 * head_dim), BF16),
            pltpu.VMEM((all_frames + 2 * window, 3 * head_dim, lanes), F32),
            pltpu.VMEM((all_frames + 2 * window, 1, lanes), F32),
            pltpu.VMEM((all_frames + 2 * window, 1, lanes), F32),
            pltpu.VMEM((all_frames, scenes, head_dim, LANES), F32),
        ],
        bytes_accessed=100_000_000,
    )(own, *near[1:], *far, lhs, xin, rstd, masks, query_gain[None], key_gain[None])
    attended, part, part_tok, part_scene = lax.optimization_barrier(
        (attended, part, part_tok, part_scene)
    )
    received = lax.all_to_all(attended, ("tok", "queue", "scene"), 0, 0)
    cut = -(-local_rows // 32) * 16
    upper = swapped(part_tok[:cut], "scene", 1)
    lower = swapped(part_scene[cut:], "tok", 1)
    half = values // 2
    half_shape = jax.ShapeDtypeStruct((half, row_lanes), F32)
    smalls = (
        packed,
        following,
        cond_embed,
        mods,
        embed_weight,
        final_gain[None],
        final_weight.T,
        fresh_noise,
    )
    places = [
        pltpu.VMEM(a.shape[1:] if i == 3 else a.shape, a.dtype) for i, a in enumerate(smalls)
    ]
    terms = values + 16 + 3 * levels_all + 16
    left, right, *rest = kernel_call(
        functools.partial(ready_kernel, values, half),
        [
            jax.ShapeDtypeStruct((terms + values, width), BF16),
            jax.ShapeDtypeStruct((terms, row_lanes), BF16),
            half_shape,
            half_shape,
            jax.ShapeDtypeStruct(fresh_noise.shape, F32),
            jax.ShapeDtypeStruct((8, LANES), F32),
        ],
        "ha" + "h" * 6 + "ss",
        places + [pltpu.SemaphoreType.DMA((len(smalls),))],
    )(*smalls, guide_table, guide_index)
    upper, lower, right = lax.optimization_barrier((upper, lower, right))
    away = [part, part_tok, part_scene, upper, lower]
    away_far = [swapped(piece, "cfg", 1) for piece in away]

    mine, send = kernel_call(
        functools.partial(finish_kernel, half, values, queues),
        [half_shape] * 2,
        "v" * 13,
        [pltpu.VMEM((values, row_lanes), F32), pltpu.VMEM((width, row_lanes), F32)],
        bytes_accessed=8_000_000,
    )(*away, *away_far, received, left, right)
    partner = swapped(send, "cfg", 1)
    shape = jax.ShapeDtypeStruct((frames, half, tokens), F32)
    return kernel_call(update_kernel, [shape, shape], "v" * 6)(mine, partner, *rest)


def on_device(*args):
    latents, qkv_weight, query_gain = args[0], args[7], args[8]
    local_heads = qkv_weight.shape[2] // query_gain.shape[0]
    scenes, queues, toks, cores = (lax.axis_size(a) for a in ("scene", "queue", "tok", "cfg"))
    pairs = scenes == toks == cores == 2 and queues & (queues - 1) == 0
    fits = latents.shape[2] * toks <= LANES and latents.shape[0] % cores == 0
    if pairs and fits and local_heads == scenes * queues:
        return tuple(on_device_heads(*args))
    return on_device_general(*args)


def solution(mesh):
    placed = (
        P(("scene", "queue"), None, "tok"),
        P(("scene", "cfg"), "tok"),
        P(("scene", "queue")),
        P(("scene", "queue"), None),
        P(("scene", "cfg"), None),
        P(),
        P(),
        P(("queue", "cfg"), None, "tok"),
        P(),
        P(),
        P("tok", ("queue", "cfg")),
        P(),
        P(),
        P(),
        P(),
    )
    return jax.shard_map(
        on_device,
        mesh=mesh,
        in_specs=placed,
        out_specs=(P(("scene", "queue"), "cfg", "tok"), P(("scene", "queue"), "cfg", "tok")),
        check_vma=False,
    )
```

```python
import functools

import jax
import jax.numpy as jnp
from jax import lax
from jax.experimental import pallas as pl
from jax.experimental.pallas import tpu as pltpu
from jax.sharding import PartitionSpec as P

EPS_NORM = 1e-06
TIME_SHIFT = 3.0
LANES = 128
VMEM_BYTES = 20 * 1024 * 1024
WHOLE_VMEM = 62 * 1024 * 1024
F32 = jnp.float32
BF16 = jnp.bfloat16


def noise_sigma(fraction):
    return TIME_SHIFT * fraction / (1.0 + (TIME_SHIFT - 1.0) * fraction)


def from_partner(value, axis, bit):
    return lax.ppermute(value, axis, [(i, i ^ 1 << bit) for i in range(lax.axis_size(axis))])


def with_halo(cells, sides, width):
    for axis, dim in sides:
        count = lax.axis_size(axis)
        ends = count - 1
        head = lax.slice_in_dim(cells, 0, width, axis=dim)
        tail = lax.slice_in_dim(cells, cells.shape[dim] - width, cells.shape[dim], axis=dim)
        cells = jnp.concatenate(
            [
                lax.ppermute(tail, axis, [(i, (i + 1) % count) for i in range(ends)]),
                cells,
                lax.ppermute(head, axis, [((i + 1) % count, i) for i in range(ends)]),
            ],
            axis=dim,
        )
    return cells


def shifted(value, axis, steps):
    count = lax.axis_size(axis)
    initial, last = (max(0, -steps), min(count, count - steps))
    return lax.ppermute(value, axis, [(source, source + steps) for source in range(initial, last)])


def layer_norm(values):
    center = jnp.mean(values, axis=-1, keepdims=True)
    deviate = values - center
    spread = jnp.mean(deviate * deviate, axis=-1, keepdims=True)
    return deviate * lax.rsqrt(spread + EPS_NORM)


def rms_norm(values, scaling):
    return (
        values * lax.rsqrt(jnp.mean(values * values, axis=-1, keepdims=True) + EPS_NORM) * scaling
    )


def temporal_attention(
    queries, key_rows, value_rows, window_mask, first_frame, total_frames, window
):
    frames = queries.shape[0]
    numerator = jnp.zeros(queries.shape, jnp.float32)
    denominator = jnp.zeros(queries.shape[:-1], jnp.float32)
    for offset in range(2 * window + 1):
        near_keys = key_rows[offset : offset + frames].astype(jnp.float32)
        near_values = value_rows[offset : offset + frames].astype(jnp.float32)
        scores = jnp.sum(queries * near_keys, axis=-1) * queries.shape[-1] ** (-0.5)
        target = first_frame + jnp.arange(frames, dtype=jnp.int32) + (offset - window)
        allowed = (window_mask[:, offset] == 1) & (target >= 0) & (target < total_frames)
        weights = jnp.exp(scores) * allowed.astype(jnp.float32)[:, None, None]
        numerator = numerator + weights[..., None] * near_values
        denominator = denominator + weights
    return numerator / denominator[..., None]


def on_device_general(
    latents,
    fresh_noise,
    levels,
    window_mask,
    cond_embed,
    level_mod,
    embed_weight,
    qkv_weight,
    query_gain,
    key_gain,
    out_weight,
    final_gain,
    final_weight,
    guide_table,
    guide_index,
):
    frames = latents.shape[0]
    tok_count = latents.shape[2]
    model_width = embed_weight.shape[1]
    head_dim = query_gain.shape[0]
    levels_all = level_mod.shape[0]
    queue_count = lax.axis_size("queue")
    all_tokens = lax.all_gather(latents, "tok", axis=2, tiled=True)
    seq_tokens = all_tokens.shape[2]
    row_count = frames * seq_tokens
    embedded = (
        jnp.einsum(
            "fcs,cd->fsd",
            all_tokens.astype(jnp.bfloat16),
            embed_weight,
            preferred_element_type=jnp.float32,
        )
        + cond_embed[0]
    )
    one_hot = (levels[:, None] == jnp.arange(levels_all, dtype=jnp.int32)[None, :]).astype(
        jnp.float32
    )
    modulate = jnp.dot(
        one_hot, level_mod.reshape(levels_all, 3 * model_width), precision=lax.Precision.HIGHEST
    ).reshape(frames, 3, model_width)
    normed = (layer_norm(embedded) * (1.0 + modulate[:, None, 1]) + modulate[:, None, 0]).astype(
        jnp.bfloat16
    )
    norm_rows = normed.reshape(row_count, model_width)
    local_cols = qkv_weight.shape[2]
    shard_piece = lax.all_gather(qkv_weight, ("queue", "cfg"), axis=0, tiled=True)
    flat_piece = shard_piece.reshape(shard_piece.shape[0], 3 * local_cols)
    projected = jnp.dot(norm_rows, flat_piece, preferred_element_type=jnp.float32)
    projected = projected.reshape(frames, seq_tokens, 3, local_cols // head_dim, head_dim)
    queries = rms_norm(projected[:, :, 0], query_gain)
    keys_values = jnp.stack(
        [
            rms_norm(projected[:, :, 1], key_gain).astype(jnp.bfloat16),
            projected[:, :, 2].astype(jnp.bfloat16),
        ]
    )
    window = window_mask.shape[1] // 2
    widened = with_halo(keys_values, (("queue", 1),), window)
    first_frame = lax.axis_index("queue") * frames
    attended = temporal_attention(
        queries, widened[0], widened[1], window_mask, first_frame, frames * queue_count, window
    )
    attended = attended.astype(jnp.bfloat16).reshape(frames, seq_tokens, local_cols)
    flat_heads = attended.reshape(row_count, local_cols)
    partial_value = jnp.dot(
        flat_heads,
        lax.all_gather(out_weight, ("queue", "cfg"), axis=1, tiled=True),
        preferred_element_type=jnp.float32,
    )
    mixed_out = lax.psum_scatter(
        partial_value.reshape(frames, seq_tokens, model_width).astype(jnp.bfloat16),
        "tok",
        scatter_dimension=1,
        tiled=True,
    ).astype(jnp.float32)
    own_start = lax.axis_index("tok") * tok_count
    own_embed = lax.dynamic_slice_in_dim(embedded, own_start, tok_count, 1)
    summed = own_embed + modulate[:, None, 2] * mixed_out
    final_rows = (layer_norm(summed) * final_gain).astype(jnp.bfloat16)
    velocity = jnp.einsum(
        "ftd,dc->fct", final_rows, final_weight, preferred_element_type=jnp.float32
    )
    half_values = velocity.shape[1] // 2
    branch_index = lax.axis_index("cfg")
    own_first = branch_index * half_values
    other_first = (1 - branch_index) * half_values
    outgoing = lax.dynamic_slice_in_dim(velocity, other_first, half_values, 1)
    partner = from_partner(outgoing, "cfg", 0)
    mine = lax.dynamic_slice_in_dim(velocity, own_first, half_values, 1)
    is_cond = branch_index == 0
    cond_vel = jnp.where(is_cond, mine, partner)
    uncond_vel = jnp.where(is_cond, partner, mine)
    entries = guide_table.shape[0]
    guidance = jnp.sum(
        guide_table * (jnp.arange(entries, dtype=jnp.int32) == guide_index[0]).astype(jnp.float32)
    )
    guided = uncond_vel + guidance * (cond_vel - uncond_vel)
    current = noise_sigma((levels + 1).astype(jnp.float32) / levels_all)
    upcoming = noise_sigma(levels.astype(jnp.float32) / levels_all)
    own_latents = lax.dynamic_slice_in_dim(latents, own_first, half_values, 1)
    updated = own_latents + (upcoming - current)[:, None, None] * guided
    incoming = shifted(updated[:1], "queue", -1)
    is_last = lax.axis_index("queue") == queue_count - 1
    incoming = jnp.where(is_last, fresh_noise[None], incoming)
    new_queue = jnp.concatenate([updated[1:], incoming], axis=0)
    return (guided, new_queue)


def kernel_call(body, out_shapes, spaces, scratch=(), vmem=VMEM_BYTES, **cost):
    kinds = {
        "v": pl.BlockSpec(),
        "s": pl.BlockSpec(memory_space=pltpu.SMEM),
        "a": pl.BlockSpec(memory_space=pl.ANY),
        "h": pl.BlockSpec(memory_space=pltpu.HBM),
    }
    many = isinstance(out_shapes, (list, tuple))
    return pl.pallas_call(
        body,
        out_shape=out_shapes,
        in_specs=[kinds[k] for k in spaces],
        out_specs=[pl.BlockSpec() for _ in out_shapes] if many else pl.BlockSpec(),
        scratch_shapes=list(scratch),
        compiler_params=pltpu.CompilerParams(vmem_limit_bytes=vmem),
        cost_estimate=pl.CostEstimate(
            flops=cost.get("flops", 1000000),
            bytes_accessed=cost.get("bytes_accessed", 1000000),
            transcendentals=0,
        ),
    )


def split_terms(values, terms):
    parts = []
    for _ in range(terms):
        part = values.astype(BF16)
        parts.append(part)
        values = values - part.astype(F32)
    return parts


def dot_tn(left, right):
    return lax.dot_general(
        left, right, (((0,), (0,)), ((), ())), preferred_element_type=F32
    )


def place_of(axis):
    return lax.axis_index(axis)


def pack_kernel(head_dim, copies_frames, latents, levels, window_mask, qkv, out_w, cond, *outs):
    scratch = outs[-1]
    copies, packed, first = outs[-4:-1]
    chunks = outs[:-4]
    scene, q, tok, core = (place_of(a) for a in ("scene", "queue", "tok", "cfg"))
    for h in range(scratch.shape[0]):
        start = h * head_dim
        scratch[h] = jnp.concatenate(
            [qkv[part, :, start : start + head_dim] for part in range(3)], axis=1
        )
    group = out_w.shape[1] // 2
    half = jnp.where(scene == 0, out_w[:, :group], out_w[:, group:])
    for k, chunk in enumerate(chunks):
        chunk[...] = jnp.concatenate([half, scratch[scene * len(chunks) + (q ^ k)]], axis=1)
    frames, values, tokens = latents.shape
    span = window_mask.shape[1]
    shares = []
    own = []
    for f in range(frames):
        level = levels[:, f : f + 1].astype(F32)
        side = jnp.zeros((copies.shape[1] - values, tokens), F32)
        row_id = lax.broadcasted_iota(jnp.int32, side.shape, 0)
        for o in range(span):
            side = jnp.where(row_id == o, window_mask[f : f + 1, o : o + 1].astype(F32), side)
        side = jnp.where(row_id == span, level, side)
        shares.append(jnp.concatenate([latents[f], side], axis=0))
        fill = jnp.broadcast_to(level, (packed.shape[0] - values, tokens))
        own.append(jnp.concatenate([latents[f], fill], axis=0))
    lower = jnp.concatenate(shares[:copies_frames], axis=1)
    upper = jnp.concatenate(shares[copies_frames:], axis=1)
    share = jnp.where(core == 0, lower, upper)
    spots = lax.axis_size("queue") * lax.axis_size("tok")
    length = cond.shape[1] // spots
    piece = jnp.zeros((1, length), F32)
    for i in range(spots):
        chosen = q * lax.axis_size("tok") + tok == i
        piece = jnp.where(chosen, cond[:, i * length : (i + 1) * length], piece)
    row_id = lax.broadcasted_iota(jnp.int32, share.shape, 0)
    at_row, step = values + span + 1, share.shape[1]
    for term in split_terms(piece, 3):
        for start in range(0, length, step):
            line = term.astype(F32)[:, start : start + step]
            fill = jnp.zeros((1, step - line.shape[1]), F32)
            line = jnp.concatenate([line, fill], axis=1) if fill.shape[1] else line
            share = jnp.where(row_id == at_row, line, share)
            at_row += 1
    share = share.astype(BF16)
    for at in range(copies.shape[0]):
        copies[at] = share
    packed[...] = jnp.concatenate(own, axis=1)
    first[...] = own[0]


def prepare_kernel(
    frames,
    values,
    span,
    mine,
    other,
    level_mod,
    embed,
    lhs,
    xin,
    rstd_out,
    mask_out,
):
    width = embed.shape[1]
    scenes, all_frames = mask_out.shape[:2]
    rows = xin.shape[1] // scenes
    queues = all_frames // frames
    toks = mine.shape[0] // (scenes * queues)
    per_core = frames // 2
    tokens = mine.shape[2] // per_core
    core = place_of("cfg")
    weights = embed[...].astype(F32)
    weights = weights - jnp.mean(weights, axis=1, keepdims=True)
    length, step = width // (queues * toks), mine.shape[2]
    lines = -(-length // step)
    conds = []
    for y in range(scenes):
        pieces = []
        for at in range(y * queues * toks, (y + 1) * queues * toks):
            info = mine[at].astype(F32)
            first = values + span + 1
            terms = sum(info[first + i * lines : first + (i + 1) * lines] for i in range(3))
            for i in range(lines):
                pieces.append(terms[i : i + 1, : min(step, length - i * step)])
        conds.append(jnp.concatenate(pieces, axis=1))
    conds = jnp.concatenate(conds, axis=0)
    conds = conds - jnp.mean(conds, axis=1, keepdims=True)
    basis = jnp.concatenate(
        [weights, conds, jnp.zeros((rows - values - scenes, width), F32)], axis=0
    )
    gram = lax.dot_general(
        basis,
        basis,
        (((1,), (1,)), ((), ())),
        preferred_element_type=F32,
        precision=lax.Precision.HIGHEST,
    ) * (1.0 / width)
    gram = jnp.concatenate(split_terms(gram, 3), axis=1)
    row_id = lax.broadcasted_iota(jnp.int32, (rows, LANES), 0)
    wide_id = lax.broadcasted_iota(jnp.int32, (rows, width), 0)
    level_id = lax.broadcasted_iota(jnp.int32, (level_mod.shape[1], width), 0).astype(F32)
    shift_row = values + scenes
    fill = LANES - toks * tokens
    for y in range(scenes):
        for q in range(queues):
            first = (y * queues + q) * toks
            held = []
            for t in range(toks):
                one, two = mine[first + t].astype(F32), other[first + t].astype(F32)
                held.append((jnp.where(core == 0, one, two), jnp.where(core == 0, two, one)))
            for part in range(frames):
                f = q * frames + part
                at = part % per_core * tokens
                info = [pair[part // per_core][:, at : at + tokens] for pair in held]
                level = info[0][values + span : values + span + 1, 0:1]
                chosen = level_id == level
                shift = jnp.sum(jnp.where(chosen, level_mod[0], 0.0), axis=0, keepdims=True)
                scale = jnp.sum(jnp.where(chosen, level_mod[1], 0.0), axis=0, keepdims=True)
                block = basis * (1.0 + scale)
                block = jnp.where((wide_id == shift_row) | (wide_id == shift_row + 1), shift, block)
                to = (f * scenes + y) * rows
                lhs[to : to + rows, :] = block.astype(BF16)
                info = jnp.concatenate(info + [jnp.ones((info[0].shape[0], fill), F32)], axis=1)
                mask_out[y, f] = info[values : values + mask_out.shape[2]]
                vec = jnp.where(row_id < values, info[:rows], 0.0)
                vec = jnp.where(row_id == values + y, 1.0, vec)
                short = vec.astype(BF16)
                met = jnp.dot(
                    gram,
                    jnp.concatenate([short, short, short], axis=0),
                    preferred_element_type=F32,
                )
                spread = jnp.sum(vec * met, axis=0, keepdims=True)
                spread = jnp.maximum(spread, 0.0) + EPS_NORM
                rstd = lax.rsqrt(spread)
                std = spread * rstd
                high = std.astype(BF16).astype(F32)
                vec = jnp.where(row_id == shift_row, high, vec)
                vec = jnp.where(row_id == shift_row + 1, std - high, vec)
                blank = jnp.zeros(vec.shape, F32)
                blocks = [vec if n == y else blank for n in range(scenes)]
                xin[f, y * rows : (y + 1) * rows] = jnp.concatenate(blocks, axis=1).astype(BF16)
                rstd_out[f, :, y * LANES : (y + 1) * LANES] = rstd


def attend_kernel(frames, tokens, queues, *refs):
    pieces = refs[: 2 * queues]
    lhs, xin, rstd_in, mask_in, gain_q, gain_k, out, whole, proj, kfac, vfac, att = refs[
        2 * queues :
    ]
    scenes, all_frames = mask_in.shape[:2]
    rows = xin.shape[1]
    head_dim = gain_q.shape[1]
    window = (proj.shape[0] - all_frames) // 2
    span = 2 * window + 1
    q_at, core = place_of("queue"), place_of("cfg")
    part_rows = pieces[0].shape[0]
    for k in range(queues):
        for side in range(2):
            owner = core if side == 0 else 1 - core
            first = pl.multiple_of(((q_at ^ k) * 2 + owner) * part_rows, 16)
            piece = pieces[side * queues + k]
            whole[pl.ds(first, part_rows), :] = piece[:, piece.shape[1] - 3 * head_dim :]
    folded = jnp.dot(lhs[...], whole[...], preferred_element_type=F32)
    high, low = split_terms(folded, 2)
    gains = split_terms(gain_q[...] * gain_k[...] * head_dim ** (-0.5), 3)
    gains = jnp.concatenate(gains + [jnp.zeros((13, head_dim), BF16)], axis=0)
    gains = dot_tn(gains, jnp.ones((16, LANES), BF16))
    for side in range(window):
        for at in (side, all_frames + window + side):
            proj[at] = jnp.zeros(proj.shape[1:], F32)
            kfac[at] = jnp.zeros(kfac.shape[1:], F32)
            vfac[at] = jnp.zeros(vfac.shape[1:], F32)
    for f in range(all_frames):
        piece = slice(f * rows, (f + 1) * rows)
        made = dot_tn(
            jnp.concatenate([high[piece], low[piece]], axis=0),
            jnp.concatenate([xin[f], xin[f]], axis=0),
        )
        proj[f + window] = made
        rstd = rstd_in[f]
        keys = made[head_dim : 2 * head_dim]
        square = jnp.mean(keys * keys, axis=0, keepdims=True)
        kfac[f + window] = rstd * lax.rsqrt(rstd * rstd * square + EPS_NORM)
        vfac[f + window] = rstd

    def one_frame(f, carry):
        for y in range(scenes):
            lane = slice(y * LANES, (y + 1) * LANES)
            query = proj[f + window, 0:head_dim, lane]
            rstd = vfac[f + window, :, lane]
            square = jnp.mean(query * query, axis=0, keepdims=True)
            qfac = rstd * lax.rsqrt(rstd * rstd * square + EPS_NORM)
            query = query * gains
            total = jnp.zeros((head_dim, LANES), F32)
            norm = jnp.zeros((1, LANES), F32)
            for o in range(span):
                keys = proj[f + o, head_dim : 2 * head_dim, lane]
                score = jnp.sum(query * keys, axis=0, keepdims=True)
                score = score * (qfac * kfac[f + o, :, lane])
                part = jnp.exp(score) * mask_in[y, f, o : o + 1, :]
                norm = norm + part
                total = total + (part * vfac[f + o, :, lane]) * proj[f + o, 2 * head_dim :, lane]
            att[f, y] = total * (1.0 / norm)
        return carry

    lax.fori_loop(0, all_frames, one_frame, 0)
    toks = out.shape[0] // (scenes * queues)
    for t in range(toks):
        for y in range(scenes):
            for q in range(queues):
                parts = [
                    att[min(q * frames + i, all_frames - 1), y, :, t * tokens : (t + 1) * tokens]
                    for i in range(frames + 1)
                ]
                at = (t * queues + q) * scenes + y
                out[at] = jnp.concatenate(parts, axis=1).astype(BF16)


def stage_kernel(own_source, level_source, embed_source, own, level_mod, embed, sems):
    copies = [
        pltpu.make_async_copy(own_source, own, sems.at[0]),
        pltpu.make_async_copy(level_source.at[pl.ds(0, 2)], level_mod, sems.at[1]),
        pltpu.make_async_copy(embed_source, embed, sems.at[2]),
    ]
    for copy in copies:
        copy.start()
    for copy in copies:
        copy.wait()


def side_kernel(group, *refs):
    for k, piece in enumerate(refs[:-1]):
        refs[-1][:, k * group : (k + 1) * group] = piece[:, :group]


def ready_kernel(values, half, *refs):
    sources, table, index = refs[:8], refs[8], refs[9]
    left, right, base, factor, noise_out, guide = refs[10:16]
    held, sems = refs[16:24], refs[24]
    copies = []
    for i, (source, to) in enumerate(zip(sources, held)):
        source = source.at[2] if i == 3 else source
        copies.append(pltpu.make_async_copy(source, to, sems.at[i]))
    for copy in copies:
        copy.start()
    for copy in copies:
        copy.wait()
    packed, following, cond, gates, embed, final_gain, final_w, noise = held
    levels_all, width = gates.shape
    info = jnp.concatenate([packed[...], following[...]], axis=1)
    lanes = info.shape[1]
    ones = jnp.ones((16, lanes), BF16)
    zero = jnp.zeros((13, width), BF16)
    left[...] = jnp.concatenate(
        [embed[...]]
        + split_terms(cond[...], 3)
        + [zero]
        + split_terms(gates[...], 3)
        + split_terms(final_gain[...], 3)
        + [zero, final_w[...]],
        axis=0,
    )
    level = info[values : values + 1]
    one_hot = (lax.broadcasted_iota(jnp.int32, (levels_all, lanes), 0).astype(F32) == level).astype(
        F32
    ).astype(BF16)
    right[...] = jnp.concatenate(
        [info[:values].astype(BF16), ones, one_hot, one_hot, one_hot, ones], axis=0
    )
    own = pl.multiple_of(place_of("cfg") * half, half)
    current = noise_sigma((level + 1.0) / levels_all)
    upcoming = noise_sigma(level / levels_all)
    factor[...] = jnp.broadcast_to(upcoming - current, factor.shape)
    base[...] = jnp.concatenate(
        [packed[pl.ds(own, half), :], following[pl.ds(own, half), :]], axis=1
    )
    noise_out[...] = noise[...]
    guide[...] = jnp.full(guide.shape, table[index[0]], F32)


def finish_kernel(half, values, queues, *refs):
    parts = [refs[:5], refs[5:10]]
    attended, left, right, mine, send, scratch, mixed = refs[10:]
    scene, q_at, tok, core = (place_of(a) for a in ("scene", "queue", "tok", "cfg"))
    group = parts[0][0].shape[1] // queues
    columns = parts[0][0].shape[0]

    def weights_of(c, t, y, k):
        lane = slice(k * group, (k + 1) * group)
        if t == y == 1:
            return [parts[c][3][:, lane], parts[c][4][:, lane]]
        return [parts[c][2 * y + t][:, lane]]

    total = None
    for t in range(2):
        made = None
        for y in range(2):
            pieces = []
            for c in range(2):
                for k in range(queues):
                    pieces += weights_of(c, t, y, k)
            rows = [
                attended[((tok ^ t) * queues + k) * 2 + (scene ^ y)].astype(F32)
                for k in range(queues)
            ]
            rows = jnp.concatenate(rows, axis=0).astype(BF16)
            term = jnp.dot(jnp.concatenate(pieces, axis=0), rows, preferred_element_type=F32)
            made = term if made is None else made + term
        made = made.astype(BF16).astype(F32)
        total = made if total is None else total + made
    for c in range(2):
        for k in range(queues):
            first = ((q_at ^ k) * 2 + (core ^ c)) * columns
            at = (c * queues + k) * columns
            mixed[pl.ds(pl.multiple_of(first, 8), columns), :] = total[at : at + columns]

    first, terms = values + 16, right.shape[0]
    last = terms - 16
    emb = dot_tn(left[:first], right[:first])
    gate = dot_tn(left[first:last], right[first:last])
    gain = dot_tn(left[last:terms], right[last:])
    summed = emb + gate * mixed[...]
    center = jnp.mean(summed, axis=0, keepdims=True)
    deviate = summed - center
    spread = jnp.mean(deviate * deviate, axis=0, keepdims=True)
    final = (deviate * lax.rsqrt(spread + EPS_NORM) * gain).astype(BF16)
    scratch[...] = jnp.dot(left[terms:], final, preferred_element_type=F32)
    own = pl.multiple_of(core * half, half)
    other = pl.multiple_of((1 - core) * half, half)
    mine[...] = scratch[pl.ds(own, half), :]
    send[...] = scratch[pl.ds(other, half), :]


def update_kernel(mine, partner, base, factor, noise, guide, vel, new):
    frames, _, tokens = vel.shape
    is_cond = place_of("cfg") == 0
    here, there = mine[...], partner[...]
    cond = jnp.where(is_cond, here, there)
    uncond = jnp.where(is_cond, there, here)
    guided = uncond + guide[0:1, 0:1] * (cond - uncond)
    updated = base[...] + factor[...] * guided
    is_last = place_of("queue") == lax.axis_size("queue") - 1
    for f in range(frames):
        vel[f] = guided[:, f * tokens : (f + 1) * tokens]
        moved = updated[:, (f + 1) * tokens : (f + 2) * tokens]
        if f == frames - 1:
            moved = jnp.where(is_last, noise[...], moved)
        new[f] = moved


def swapped(value, axis, mask):
    count = lax.axis_size(axis)
    return lax.ppermute(value, axis, [(i, i ^ mask) for i in range(count)])


def on_device_heads(
    latents,
    fresh_noise,
    levels,
    window_mask,
    cond_embed,
    level_mod,
    embed_weight,
    qkv_weight,
    query_gain,
    key_gain,
    out_weight,
    final_gain,
    final_weight,
    guide_table,
    guide_index,
):
    frames, values, tokens = latents.shape
    width = embed_weight.shape[1]
    head_dim = query_gain.shape[0]
    levels_all = level_mod.shape[0]
    span = window_mask.shape[1]
    window = span // 2
    scenes, queues, toks = (lax.axis_size(a) for a in ("scene", "queue", "tok"))
    chips = scenes * queues * toks
    all_frames = queues * frames
    per_core = frames // 2
    cond_rows = 3 * -(-(width // (queues * toks)) // (per_core * tokens))
    rows = -(-max(values + scenes + 2, values + span + 1 + cond_rows) // 16) * 16
    own_rows = -(-(values + 1) // 8) * 8
    local_rows = qkv_weight.shape[0]
    local_heads = qkv_weight.shape[2] // head_dim
    lanes = scenes * LANES
    row_lanes = (frames + 1) * tokens
    mods = jnp.transpose(level_mod, (1, 0, 2))

    group = out_weight.shape[0] // scenes
    chunk = jax.ShapeDtypeStruct((local_rows, group + 3 * head_dim), BF16)
    *chunks, copies, packed, first = kernel_call(
        functools.partial(pack_kernel, head_dim, per_core),
        [chunk] * queues
        + [
            jax.ShapeDtypeStruct((chips, rows, per_core * tokens), BF16),
            jax.ShapeDtypeStruct((own_rows, frames * tokens), F32),
            jax.ShapeDtypeStruct((own_rows, tokens), F32),
        ],
        "vvvvvv",
        [pltpu.VMEM((local_heads, local_rows, 3 * head_dim), BF16)],
        vmem=WHOLE_VMEM,
        bytes_accessed=8_000_000,
    )(
        latents,
        levels[None],
        window_mask,
        jnp.transpose(qkv_weight, (1, 0, 2)),
        out_weight.T,
        cond_embed,
    )

    near = [chunks[0]] + [swapped(chunks[k], "queue", k) for k in range(1, queues)]
    own, level_rows, embed_held = kernel_call(
        stage_kernel,
        [
            chunk,
            jax.ShapeDtypeStruct((2, levels_all, width), F32),
            jax.ShapeDtypeStruct(embed_weight.shape, BF16),
        ],
        "hhh",
        [pltpu.SemaphoreType.DMA((3,))],
    )(chunks[0], mods, embed_weight)
    near[1], own, level_rows, embed_held = lax.optimization_barrier(
        (near[1], own, level_rows, embed_held)
    )
    far = [swapped(piece, "cfg", 1) for piece in near]
    shares = lax.all_to_all(copies, ("scene", "queue", "tok"), 0, 0)
    other_shares = swapped(shares, "cfg", 1)

    following = lax.ppermute(first, "queue", [(i + 1, i) for i in range(queues - 1)])
    near[-1], following, shares, *far[:-1] = lax.optimization_barrier(
        (near[-1], following, shares, *far[:-1])
    )
    part = kernel_call(
        functools.partial(side_kernel, group),
        jax.ShapeDtypeStruct((local_rows, queues * group), BF16),
        "v" * queues,
    )(own, *near[1:])
    part_tok, part_scene = swapped(part, "tok", 1), swapped(part, "scene", 1)

    lhs, xin, rstd, masks = kernel_call(
        functools.partial(prepare_kernel, frames, values, span),
        [
            jax.ShapeDtypeStruct((scenes * all_frames * rows, width), BF16),
            jax.ShapeDtypeStruct((all_frames, scenes * rows, lanes), BF16),
            jax.ShapeDtypeStruct((all_frames, 1, lanes), F32),
            jax.ShapeDtypeStruct((scenes, all_frames, rows - values, LANES), F32),
        ],
        "vvvv",
        bytes_accessed=8_000_000,
    )(shares, other_shares, level_rows, embed_held)
    attended = kernel_call(
        functools.partial(attend_kernel, frames, tokens, queues),
        jax.ShapeDtypeStruct((chips, head_dim, row_lanes), BF16),
        "v" * (2 * queues + 6),
        [
            pltpu.VMEM((width, 3 * head_dim), BF16),
            pltpu.VMEM((all_frames + 2 * window, 3 * head_dim, lanes), F32),
            pltpu.VMEM((all_frames + 2 * window, 1, lanes), F32),
            pltpu.VMEM((all_frames + 2 * window, 1, lanes), F32),
            pltpu.VMEM((all_frames, scenes, head_dim, LANES), F32),
        ],
        bytes_accessed=100_000_000,
    )(own, *near[1:], *far, lhs, xin, rstd, masks, query_gain[None], key_gain[None])
    attended, part, part_tok, part_scene = lax.optimization_barrier(
        (attended, part, part_tok, part_scene)
    )
    received = lax.all_to_all(attended, ("tok", "queue", "scene"), 0, 0)
    cut = -(-local_rows // 32) * 16
    upper = swapped(part_tok[:cut], "scene", 1)
    lower = swapped(part_scene[cut:], "tok", 1)
    half = values // 2
    half_shape = jax.ShapeDtypeStruct((half, row_lanes), F32)
    smalls = (
        packed,
        following,
        cond_embed,
        mods,
        embed_weight,
        final_gain[None],
        final_weight.T,
        fresh_noise,
    )
    places = [
        pltpu.VMEM(a.shape[1:] if i == 3 else a.shape, a.dtype) for i, a in enumerate(smalls)
    ]
    terms = values + 16 + 3 * levels_all + 16
    left, right, *rest = kernel_call(
        functools.partial(ready_kernel, values, half),
        [
            jax.ShapeDtypeStruct((terms + values, width), BF16),
            jax.ShapeDtypeStruct((terms, row_lanes), BF16),
            half_shape,
            half_shape,
            jax.ShapeDtypeStruct(fresh_noise.shape, F32),
            jax.ShapeDtypeStruct((8, LANES), F32),
        ],
        "ha" + "h" * 6 + "ss",
        places + [pltpu.SemaphoreType.DMA((len(smalls),))],
    )(*smalls, guide_table, guide_index)
    upper, lower, right = lax.optimization_barrier((upper, lower, right))
    away = [part, part_tok, part_scene, upper, lower]
    away_far = [swapped(piece, "cfg", 1) for piece in away]

    mine, send = kernel_call(
        functools.partial(finish_kernel, half, values, queues),
        [half_shape] * 2,
        "v" * 13,
        [pltpu.VMEM((values, row_lanes), F32), pltpu.VMEM((width, row_lanes), F32)],
        bytes_accessed=8_000_000,
    )(*away, *away_far, received, left, right)
    partner = swapped(send, "cfg", 1)
    shape = jax.ShapeDtypeStruct((frames, half, tokens), F32)
    return kernel_call(update_kernel, [shape, shape], "v" * 6)(mine, partner, *rest)


def on_device(*args):
    latents, qkv_weight, query_gain = args[0], args[7], args[8]
    local_heads = qkv_weight.shape[2] // query_gain.shape[0]
    scenes, queues, toks, cores = (lax.axis_size(a) for a in ("scene", "queue", "tok", "cfg"))
    pairs = scenes == toks == cores == 2 and queues & (queues - 1) == 0
    fits = latents.shape[2] * toks <= LANES and latents.shape[0] % cores == 0
    if pairs and fits and local_heads == scenes * queues:
        return tuple(on_device_heads(*args))
    return on_device_general(*args)


def solution(mesh):
    placed = (
        P(("scene", "queue"), None, "tok"),
        P(("scene", "cfg"), "tok"),
        P(("scene", "queue")),
        P(("scene", "queue"), None),
        P(("scene", "cfg"), None),
        P(),
        P(),
        P(("queue", "cfg"), None, "tok"),
        P(),
        P(),
        P("tok", ("queue", "cfg")),
        P(),
        P(),
        P(),
        P(),
    )
    return jax.shard_map(
        on_device,
        mesh=mesh,
        in_specs=placed,
        out_specs=(P(("scene", "queue"), "cfg", "tok"), P(("scene", "queue"), "cfg", "tok")),
        check_vma=False,
    )
```

```python
import functools

import jax
import jax.numpy as jnp
from jax import lax
from jax.experimental import pallas as pl
from jax.experimental.pallas import tpu as pltpu
from jax.sharding import PartitionSpec as P

EPS_NORM = 1e-06
TIME_SHIFT = 3.0
LANES = 128
VMEM_BYTES = 20 * 1024 * 1024
WHOLE_VMEM = 62 * 1024 * 1024
F32 = jnp.float32
BF16 = jnp.bfloat16


def noise_sigma(fraction):
    return TIME_SHIFT * fraction / (1.0 + (TIME_SHIFT - 1.0) * fraction)


def from_partner(value, axis, bit):
    return lax.ppermute(value, axis, [(i, i ^ 1 << bit) for i in range(lax.axis_size(axis))])


def with_halo(cells, sides, width):
    for axis, dim in sides:
        count = lax.axis_size(axis)
        ends = count - 1
        head = lax.slice_in_dim(cells, 0, width, axis=dim)
        tail = lax.slice_in_dim(cells, cells.shape[dim] - width, cells.shape[dim], axis=dim)
        cells = jnp.concatenate(
            [
                lax.ppermute(tail, axis, [(i, (i + 1) % count) for i in range(ends)]),
                cells,
                lax.ppermute(head, axis, [((i + 1) % count, i) for i in range(ends)]),
            ],
            axis=dim,
        )
    return cells


def shifted(value, axis, steps):
    count = lax.axis_size(axis)
    initial, last = (max(0, -steps), min(count, count - steps))
    return lax.ppermute(value, axis, [(source, source + steps) for source in range(initial, last)])


def layer_norm(values):
    center = jnp.mean(values, axis=-1, keepdims=True)
    deviate = values - center
    spread = jnp.mean(deviate * deviate, axis=-1, keepdims=True)
    return deviate * lax.rsqrt(spread + EPS_NORM)


def rms_norm(values, scaling):
    return (
        values * lax.rsqrt(jnp.mean(values * values, axis=-1, keepdims=True) + EPS_NORM) * scaling
    )


def temporal_attention(
    queries, key_rows, value_rows, window_mask, first_frame, total_frames, window
):
    frames = queries.shape[0]
    numerator = jnp.zeros(queries.shape, jnp.float32)
    denominator = jnp.zeros(queries.shape[:-1], jnp.float32)
    for offset in range(2 * window + 1):
        near_keys = key_rows[offset : offset + frames].astype(jnp.float32)
        near_values = value_rows[offset : offset + frames].astype(jnp.float32)
        scores = jnp.sum(queries * near_keys, axis=-1) * queries.shape[-1] ** (-0.5)
        target = first_frame + jnp.arange(frames, dtype=jnp.int32) + (offset - window)
        allowed = (window_mask[:, offset] == 1) & (target >= 0) & (target < total_frames)
        weights = jnp.exp(scores) * allowed.astype(jnp.float32)[:, None, None]
        numerator = numerator + weights[..., None] * near_values
        denominator = denominator + weights
    return numerator / denominator[..., None]


def on_device_general(
    latents,
    fresh_noise,
    levels,
    window_mask,
    cond_embed,
    level_mod,
    embed_weight,
    qkv_weight,
    query_gain,
    key_gain,
    out_weight,
    final_gain,
    final_weight,
    guide_table,
    guide_index,
):
    frames = latents.shape[0]
    tok_count = latents.shape[2]
    model_width = embed_weight.shape[1]
    head_dim = query_gain.shape[0]
    levels_all = level_mod.shape[0]
    queue_count = lax.axis_size("queue")
    all_tokens = lax.all_gather(latents, "tok", axis=2, tiled=True)
    seq_tokens = all_tokens.shape[2]
    row_count = frames * seq_tokens
    embedded = (
        jnp.einsum(
            "fcs,cd->fsd",
            all_tokens.astype(jnp.bfloat16),
            embed_weight,
            preferred_element_type=jnp.float32,
        )
        + cond_embed[0]
    )
    one_hot = (levels[:, None] == jnp.arange(levels_all, dtype=jnp.int32)[None, :]).astype(
        jnp.float32
    )
    modulate = jnp.dot(
        one_hot, level_mod.reshape(levels_all, 3 * model_width), precision=lax.Precision.HIGHEST
    ).reshape(frames, 3, model_width)
    normed = (layer_norm(embedded) * (1.0 + modulate[:, None, 1]) + modulate[:, None, 0]).astype(
        jnp.bfloat16
    )
    norm_rows = normed.reshape(row_count, model_width)
    local_cols = qkv_weight.shape[2]
    shard_piece = lax.all_gather(qkv_weight, ("queue", "cfg"), axis=0, tiled=True)
    flat_piece = shard_piece.reshape(shard_piece.shape[0], 3 * local_cols)
    projected = jnp.dot(norm_rows, flat_piece, preferred_element_type=jnp.float32)
    projected = projected.reshape(frames, seq_tokens, 3, local_cols // head_dim, head_dim)
    queries = rms_norm(projected[:, :, 0], query_gain)
    keys_values = jnp.stack(
        [
            rms_norm(projected[:, :, 1], key_gain).astype(jnp.bfloat16),
            projected[:, :, 2].astype(jnp.bfloat16),
        ]
    )
    window = window_mask.shape[1] // 2
    widened = with_halo(keys_values, (("queue", 1),), window)
    first_frame = lax.axis_index("queue") * frames
    attended = temporal_attention(
        queries, widened[0], widened[1], window_mask, first_frame, frames * queue_count, window
    )
    attended = attended.astype(jnp.bfloat16).reshape(frames, seq_tokens, local_cols)
    flat_heads = attended.reshape(row_count, local_cols)
    partial_value = jnp.dot(
        flat_heads,
        lax.all_gather(out_weight, ("queue", "cfg"), axis=1, tiled=True),
        preferred_element_type=jnp.float32,
    )
    mixed_out = lax.psum_scatter(
        partial_value.reshape(frames, seq_tokens, model_width).astype(jnp.bfloat16),
        "tok",
        scatter_dimension=1,
        tiled=True,
    ).astype(jnp.float32)
    own_start = lax.axis_index("tok") * tok_count
    own_embed = lax.dynamic_slice_in_dim(embedded, own_start, tok_count, 1)
    summed = own_embed + modulate[:, None, 2] * mixed_out
    final_rows = (layer_norm(summed) * final_gain).astype(jnp.bfloat16)
    velocity = jnp.einsum(
        "ftd,dc->fct", final_rows, final_weight, preferred_element_type=jnp.float32
    )
    half_values = velocity.shape[1] // 2
    branch_index = lax.axis_index("cfg")
    own_first = branch_index * half_values
    other_first = (1 - branch_index) * half_values
    outgoing = lax.dynamic_slice_in_dim(velocity, other_first, half_values, 1)
    partner = from_partner(outgoing, "cfg", 0)
    mine = lax.dynamic_slice_in_dim(velocity, own_first, half_values, 1)
    is_cond = branch_index == 0
    cond_vel = jnp.where(is_cond, mine, partner)
    uncond_vel = jnp.where(is_cond, partner, mine)
    entries = guide_table.shape[0]
    guidance = jnp.sum(
        guide_table * (jnp.arange(entries, dtype=jnp.int32) == guide_index[0]).astype(jnp.float32)
    )
    guided = uncond_vel + guidance * (cond_vel - uncond_vel)
    current = noise_sigma((levels + 1).astype(jnp.float32) / levels_all)
    upcoming = noise_sigma(levels.astype(jnp.float32) / levels_all)
    own_latents = lax.dynamic_slice_in_dim(latents, own_first, half_values, 1)
    updated = own_latents + (upcoming - current)[:, None, None] * guided
    incoming = shifted(updated[:1], "queue", -1)
    is_last = lax.axis_index("queue") == queue_count - 1
    incoming = jnp.where(is_last, fresh_noise[None], incoming)
    new_queue = jnp.concatenate([updated[1:], incoming], axis=0)
    return (guided, new_queue)


def kernel_call(body, out_shapes, spaces, scratch=(), vmem=VMEM_BYTES, **cost):
    kinds = {
        "v": pl.BlockSpec(),
        "s": pl.BlockSpec(memory_space=pltpu.SMEM),
        "a": pl.BlockSpec(memory_space=pl.ANY),
        "h": pl.BlockSpec(memory_space=pltpu.HBM),
    }
    many = isinstance(out_shapes, (list, tuple))
    return pl.pallas_call(
        body,
        out_shape=out_shapes,
        in_specs=[kinds[k] for k in spaces],
        out_specs=[pl.BlockSpec() for _ in out_shapes] if many else pl.BlockSpec(),
        scratch_shapes=list(scratch),
        compiler_params=pltpu.CompilerParams(vmem_limit_bytes=vmem),
        cost_estimate=pl.CostEstimate(
            flops=cost.get("flops", 1000000),
            bytes_accessed=cost.get("bytes_accessed", 1000000),
            transcendentals=0,
        ),
    )


def split_terms(values, terms):
    parts = []
    for _ in range(terms):
        part = values.astype(BF16)
        parts.append(part)
        values = values - part.astype(F32)
    return parts


def dot_tn(left, right):
    return lax.dot_general(
        left, right, (((0,), (0,)), ((), ())), preferred_element_type=F32
    )


def place_of(axis):
    return lax.axis_index(axis)


def pack_kernel(head_dim, copies_frames, latents, levels, window_mask, qkv, out_w, cond, *outs):
    scratch = outs[-1]
    copies, packed, first = outs[-4:-1]
    chunks = outs[:-4]
    scene, q, tok, core = (place_of(a) for a in ("scene", "queue", "tok", "cfg"))
    for h in range(scratch.shape[0]):
        start = h * head_dim
        scratch[h] = jnp.concatenate(
            [qkv[part, :, start : start + head_dim] for part in range(3)], axis=1
        )
    group = out_w.shape[1] // 2
    half = jnp.where(scene == 0, out_w[:, :group], out_w[:, group:])
    for k, chunk in enumerate(chunks):
        chunk[...] = jnp.concatenate([half, scratch[scene * len(chunks) + (q ^ k)]], axis=1)
    frames, values, tokens = latents.shape
    span = window_mask.shape[1]
    shares = []
    own = []
    for f in range(frames):
        level = levels[:, f : f + 1].astype(F32)
        side = jnp.zeros((copies.shape[1] - values, tokens), F32)
        row_id = lax.broadcasted_iota(jnp.int32, side.shape, 0)
        for o in range(span):
            side = jnp.where(row_id == o, window_mask[f : f + 1, o : o + 1].astype(F32), side)
        side = jnp.where(row_id == span, level, side)
        shares.append(jnp.concatenate([latents[f], side], axis=0))
        fill = jnp.broadcast_to(level, (packed.shape[0] - values, tokens))
        own.append(jnp.concatenate([latents[f], fill], axis=0))
    lower = jnp.concatenate(shares[:copies_frames], axis=1)
    upper = jnp.concatenate(shares[copies_frames:], axis=1)
    share = jnp.where(core == 0, lower, upper)
    spots = lax.axis_size("queue") * lax.axis_size("tok")
    length = cond.shape[1] // spots
    piece = jnp.zeros((1, length), F32)
    for i in range(spots):
        chosen = q * lax.axis_size("tok") + tok == i
        piece = jnp.where(chosen, cond[:, i * length : (i + 1) * length], piece)
    row_id = lax.broadcasted_iota(jnp.int32, share.shape, 0)
    at_row, step = values + span + 1, share.shape[1]
    for term in split_terms(piece, 3):
        for start in range(0, length, step):
            line = term.astype(F32)[:, start : start + step]
            fill = jnp.zeros((1, step - line.shape[1]), F32)
            line = jnp.concatenate([line, fill], axis=1) if fill.shape[1] else line
            share = jnp.where(row_id == at_row, line, share)
            at_row += 1
    share = share.astype(BF16)
    for at in range(copies.shape[0]):
        copies[at] = share
    packed[...] = jnp.concatenate(own, axis=1)
    first[...] = own[0]


def prepare_kernel(
    frames,
    values,
    span,
    mine,
    other,
    level_mod,
    embed,
    lhs,
    xin,
    rstd_out,
    mask_out,
):
    width = embed.shape[1]
    scenes, all_frames = mask_out.shape[:2]
    rows = xin.shape[1] // scenes
    queues = all_frames // frames
    toks = mine.shape[0] // (scenes * queues)
    per_core = frames // 2
    tokens = mine.shape[2] // per_core
    core = place_of("cfg")
    weights = embed[...].astype(F32)
    weights = weights - jnp.mean(weights, axis=1, keepdims=True)
    length, step = width // (queues * toks), mine.shape[2]
    lines = -(-length // step)
    conds = []
    for y in range(scenes):
        pieces = []
        for at in range(y * queues * toks, (y + 1) * queues * toks):
            info = mine[at].astype(F32)
            first = values + span + 1
            terms = sum(info[first + i * lines : first + (i + 1) * lines] for i in range(3))
            for i in range(lines):
                pieces.append(terms[i : i + 1, : min(step, length - i * step)])
        conds.append(jnp.concatenate(pieces, axis=1))
    conds = jnp.concatenate(conds, axis=0)
    conds = conds - jnp.mean(conds, axis=1, keepdims=True)
    basis = jnp.concatenate(
        [weights, conds, jnp.zeros((rows - values - scenes, width), F32)], axis=0
    )
    gram = lax.dot_general(
        basis,
        basis,
        (((1,), (1,)), ((), ())),
        preferred_element_type=F32,
        precision=lax.Precision.HIGHEST,
    ) * (1.0 / width)
    gram = jnp.concatenate(split_terms(gram, 3), axis=1)
    row_id = lax.broadcasted_iota(jnp.int32, (rows, LANES), 0)
    wide_id = lax.broadcasted_iota(jnp.int32, (rows, width), 0)
    level_id = lax.broadcasted_iota(jnp.int32, (level_mod.shape[1], width), 0).astype(F32)
    shift_row = values + scenes
    fill = LANES - toks * tokens
    for y in range(scenes):
        for q in range(queues):
            first = (y * queues + q) * toks
            held = []
            for t in range(toks):
                one, two = mine[first + t].astype(F32), other[first + t].astype(F32)
                held.append((jnp.where(core == 0, one, two), jnp.where(core == 0, two, one)))
            for part in range(frames):
                f = q * frames + part
                at = part % per_core * tokens
                info = [pair[part // per_core][:, at : at + tokens] for pair in held]
                level = info[0][values + span : values + span + 1, 0:1]
                chosen = level_id == level
                shift = jnp.sum(jnp.where(chosen, level_mod[0], 0.0), axis=0, keepdims=True)
                scale = jnp.sum(jnp.where(chosen, level_mod[1], 0.0), axis=0, keepdims=True)
                block = basis * (1.0 + scale)
                block = jnp.where((wide_id == shift_row) | (wide_id == shift_row + 1), shift, block)
                to = (f * scenes + y) * rows
                lhs[to : to + rows, :] = block.astype(BF16)
                info = jnp.concatenate(info + [jnp.ones((info[0].shape[0], fill), F32)], axis=1)
                mask_out[y, f] = info[values : values + mask_out.shape[2]]
                vec = jnp.where(row_id < values, info[:rows], 0.0)
                vec = jnp.where(row_id == values + y, 1.0, vec)
                short = vec.astype(BF16)
                met = jnp.dot(
                    gram,
                    jnp.concatenate([short, short, short], axis=0),
                    preferred_element_type=F32,
                )
                spread = jnp.sum(vec * met, axis=0, keepdims=True)
                spread = jnp.maximum(spread, 0.0) + EPS_NORM
                rstd = lax.rsqrt(spread)
                std = spread * rstd
                high = std.astype(BF16).astype(F32)
                vec = jnp.where(row_id == shift_row, high, vec)
                vec = jnp.where(row_id == shift_row + 1, std - high, vec)
                blank = jnp.zeros(vec.shape, F32)
                blocks = [vec if n == y else blank for n in range(scenes)]
                xin[f, y * rows : (y + 1) * rows] = jnp.concatenate(blocks, axis=1).astype(BF16)
                rstd_out[f, :, y * LANES : (y + 1) * LANES] = rstd


def attend_kernel(frames, tokens, queues, *refs):
    pieces = refs[: 2 * queues]
    lhs, xin, rstd_in, mask_in, gain_q, gain_k, out, whole, proj, kfac, vfac, att = refs[
        2 * queues :
    ]
    scenes, all_frames = mask_in.shape[:2]
    rows = xin.shape[1]
    head_dim = gain_q.shape[1]
    window = (proj.shape[0] - all_frames) // 2
    span = 2 * window + 1
    q_at, core = place_of("queue"), place_of("cfg")
    part_rows = pieces[0].shape[0]
    for k in range(queues):
        for side in range(2):
            owner = core if side == 0 else 1 - core
            first = pl.multiple_of(((q_at ^ k) * 2 + owner) * part_rows, 16)
            piece = pieces[side * queues + k]
            whole[pl.ds(first, part_rows), :] = piece[:, piece.shape[1] - 3 * head_dim :]
    folded = jnp.dot(lhs[...], whole[...], preferred_element_type=F32)
    high, low = split_terms(folded, 2)
    gains = split_terms(gain_q[...] * gain_k[...] * head_dim ** (-0.5), 3)
    gains = jnp.concatenate(gains + [jnp.zeros((13, head_dim), BF16)], axis=0)
    gains = dot_tn(gains, jnp.ones((16, LANES), BF16))
    for side in range(window):
        for at in (side, all_frames + window + side):
            proj[at] = jnp.zeros(proj.shape[1:], F32)
            kfac[at] = jnp.zeros(kfac.shape[1:], F32)
            vfac[at] = jnp.zeros(vfac.shape[1:], F32)
    for f in range(all_frames):
        piece = slice(f * rows, (f + 1) * rows)
        made = dot_tn(
            jnp.concatenate([high[piece], low[piece]], axis=0),
            jnp.concatenate([xin[f], xin[f]], axis=0),
        )
        proj[f + window] = made
        rstd = rstd_in[f]
        keys = made[head_dim : 2 * head_dim]
        square = jnp.mean(keys * keys, axis=0, keepdims=True)
        kfac[f + window] = rstd * lax.rsqrt(rstd * rstd * square + EPS_NORM)
        vfac[f + window] = rstd

    def one_frame(f, carry):
        for y in range(scenes):
            lane = slice(y * LANES, (y + 1) * LANES)
            query = proj[f + window, 0:head_dim, lane]
            rstd = vfac[f + window, :, lane]
            square = jnp.mean(query * query, axis=0, keepdims=True)
            qfac = rstd * lax.rsqrt(rstd * rstd * square + EPS_NORM)
            query = query * gains
            total = jnp.zeros((head_dim, LANES), F32)
            norm = jnp.zeros((1, LANES), F32)
            for o in range(span):
                keys = proj[f + o, head_dim : 2 * head_dim, lane]
                score = jnp.sum(query * keys, axis=0, keepdims=True)
                score = score * (qfac * kfac[f + o, :, lane])
                part = jnp.exp(score) * mask_in[y, f, o : o + 1, :]
                norm = norm + part
                total = total + (part * vfac[f + o, :, lane]) * proj[f + o, 2 * head_dim :, lane]
            att[f, y] = total * (1.0 / norm)
        return carry

    lax.fori_loop(0, all_frames, one_frame, 0)
    toks = out.shape[0] // (scenes * queues)
    for t in range(toks):
        for y in range(scenes):
            for q in range(queues):
                parts = [
                    att[min(q * frames + i, all_frames - 1), y, :, t * tokens : (t + 1) * tokens]
                    for i in range(frames + 1)
                ]
                at = (t * queues + q) * scenes + y
                out[at] = jnp.concatenate(parts, axis=1).astype(BF16)


def stage_kernel(own_source, level_source, embed_source, own, level_mod, embed, sems):
    copies = [
        pltpu.make_async_copy(own_source, own, sems.at[0]),
        pltpu.make_async_copy(level_source.at[pl.ds(0, 2)], level_mod, sems.at[1]),
        pltpu.make_async_copy(embed_source, embed, sems.at[2]),
    ]
    for copy in copies:
        copy.start()
    for copy in copies:
        copy.wait()


def side_kernel(group, *refs):
    for k, piece in enumerate(refs[:-1]):
        refs[-1][:, k * group : (k + 1) * group] = piece[:, :group]


def ready_kernel(values, half, *refs):
    sources, table, index = refs[:8], refs[8], refs[9]
    both, base, factor, noise_out, guide = refs[10:15]
    held, sems = refs[15:23], refs[23]
    copies = []
    for i, (source, to) in enumerate(zip(sources, held)):
        source = source.at[2] if i == 3 else source
        copies.append(pltpu.make_async_copy(source, to, sems.at[i]))
    for copy in copies:
        copy.start()
    for copy in copies:
        copy.wait()
    packed, following, cond, gates, embed, final_gain, final_w, noise = held
    levels_all, width = gates.shape
    info = jnp.concatenate([packed[...], following[...]], axis=1)
    lanes = info.shape[1]
    ones = jnp.ones((16, lanes), BF16)
    zero = jnp.zeros((13, width), BF16)
    both[:, :width] = jnp.concatenate(
        [embed[...]]
        + split_terms(cond[...], 3)
        + [zero]
        + split_terms(gates[...], 3)
        + split_terms(final_gain[...], 3)
        + [zero, final_w[...]],
        axis=0,
    )
    level = info[values : values + 1]
    one_hot = (lax.broadcasted_iota(jnp.int32, (levels_all, lanes), 0).astype(F32) == level).astype(
        F32
    ).astype(BF16)
    unused = jnp.zeros((final_w.shape[0], lanes), BF16)
    both[:, width:] = jnp.concatenate(
        [info[:values].astype(BF16), ones, one_hot, one_hot, one_hot, ones, unused], axis=0
    )
    own = pl.multiple_of(place_of("cfg") * half, half)
    current = noise_sigma((level + 1.0) / levels_all)
    upcoming = noise_sigma(level / levels_all)
    factor[...] = jnp.broadcast_to(upcoming - current, factor.shape)
    base[...] = jnp.concatenate(
        [packed[pl.ds(own, half), :], following[pl.ds(own, half), :]], axis=1
    )
    noise_out[...] = noise[...]
    guide[...] = jnp.full(guide.shape, table[index[0]], F32)


def finish_kernel(half, values, queues, *refs):
    parts = [refs[:5], refs[5:10]]
    attended, both, mine, send, scratch, mixed = refs[10:]
    scene, q_at, tok, core = (place_of(a) for a in ("scene", "queue", "tok", "cfg"))
    group = parts[0][0].shape[1] // queues
    columns = parts[0][0].shape[0]

    def weights_of(c, t, y, k):
        lane = slice(k * group, (k + 1) * group)
        if t == y == 1:
            return [parts[c][3][:, lane], parts[c][4][:, lane]]
        return [parts[c][2 * y + t][:, lane]]

    total = None
    for t in range(2):
        made = None
        for y in range(2):
            pieces = []
            for c in range(2):
                for k in range(queues):
                    pieces += weights_of(c, t, y, k)
            rows = [
                attended[((tok ^ t) * queues + k) * 2 + (scene ^ y)].astype(F32)
                for k in range(queues)
            ]
            rows = jnp.concatenate(rows, axis=0).astype(BF16)
            term = jnp.dot(jnp.concatenate(pieces, axis=0), rows, preferred_element_type=F32)
            made = term if made is None else made + term
        made = made.astype(BF16).astype(F32)
        total = made if total is None else total + made
    for c in range(2):
        for k in range(queues):
            first = ((q_at ^ k) * 2 + (core ^ c)) * columns
            at = (c * queues + k) * columns
            mixed[pl.ds(pl.multiple_of(first, 8), columns), :] = total[at : at + columns]

    width, terms = mixed.shape[0], both.shape[0] - values
    first, last = values + 16, terms - 16
    emb = dot_tn(both[:first, :width], both[:first, width:])
    gate = dot_tn(both[first:last, :width], both[first:last, width:])
    gain = dot_tn(both[last:terms, :width], both[last:terms, width:])
    summed = emb + gate * mixed[...]
    center = jnp.mean(summed, axis=0, keepdims=True)
    deviate = summed - center
    spread = jnp.mean(deviate * deviate, axis=0, keepdims=True)
    final = (deviate * lax.rsqrt(spread + EPS_NORM) * gain).astype(BF16)
    scratch[...] = jnp.dot(both[terms:, :width], final, preferred_element_type=F32)
    own = pl.multiple_of(core * half, half)
    other = pl.multiple_of((1 - core) * half, half)
    mine[...] = scratch[pl.ds(own, half), :]
    send[...] = scratch[pl.ds(other, half), :]


def update_kernel(mine, partner, base, factor, noise, guide, vel, new):
    frames, _, tokens = vel.shape
    is_cond = place_of("cfg") == 0
    here, there = mine[...], partner[...]
    cond = jnp.where(is_cond, here, there)
    uncond = jnp.where(is_cond, there, here)
    guided = uncond + guide[0:1, 0:1] * (cond - uncond)
    updated = base[...] + factor[...] * guided
    is_last = place_of("queue") == lax.axis_size("queue") - 1
    for f in range(frames):
        vel[f] = guided[:, f * tokens : (f + 1) * tokens]
        moved = updated[:, (f + 1) * tokens : (f + 2) * tokens]
        if f == frames - 1:
            moved = jnp.where(is_last, noise[...], moved)
        new[f] = moved


def swapped(value, axis, mask):
    count = lax.axis_size(axis)
    return lax.ppermute(value, axis, [(i, i ^ mask) for i in range(count)])


def on_device_heads(
    latents,
    fresh_noise,
    levels,
    window_mask,
    cond_embed,
    level_mod,
    embed_weight,
    qkv_weight,
    query_gain,
    key_gain,
    out_weight,
    final_gain,
    final_weight,
    guide_table,
    guide_index,
):
    frames, values, tokens = latents.shape
    width = embed_weight.shape[1]
    head_dim = query_gain.shape[0]
    levels_all = level_mod.shape[0]
    span = window_mask.shape[1]
    window = span // 2
    scenes, queues, toks = (lax.axis_size(a) for a in ("scene", "queue", "tok"))
    chips = scenes * queues * toks
    all_frames = queues * frames
    per_core = frames // 2
    cond_rows = 3 * -(-(width // (queues * toks)) // (per_core * tokens))
    rows = -(-max(values + scenes + 2, values + span + 1 + cond_rows) // 16) * 16
    own_rows = -(-(values + 1) // 8) * 8
    local_rows = qkv_weight.shape[0]
    local_heads = qkv_weight.shape[2] // head_dim
    lanes = scenes * LANES
    row_lanes = (frames + 1) * tokens
    mods = jnp.transpose(level_mod, (1, 0, 2))

    group = out_weight.shape[0] // scenes
    chunk = jax.ShapeDtypeStruct((local_rows, group + 3 * head_dim), BF16)
    *chunks, copies, packed, first = kernel_call(
        functools.partial(pack_kernel, head_dim, per_core),
        [chunk] * queues
        + [
            jax.ShapeDtypeStruct((chips, rows, per_core * tokens), BF16),
            jax.ShapeDtypeStruct((own_rows, frames * tokens), F32),
            jax.ShapeDtypeStruct((own_rows, tokens), F32),
        ],
        "vvvvvv",
        [pltpu.VMEM((local_heads, local_rows, 3 * head_dim), BF16)],
        vmem=WHOLE_VMEM,
        bytes_accessed=8_000_000,
    )(
        latents,
        levels[None],
        window_mask,
        jnp.transpose(qkv_weight, (1, 0, 2)),
        out_weight.T,
        cond_embed,
    )

    near = [chunks[0]] + [swapped(chunks[k], "queue", k) for k in range(1, queues)]
    own, level_rows, embed_held = kernel_call(
        stage_kernel,
        [
            chunk,
            jax.ShapeDtypeStruct((2, levels_all, width), F32),
            jax.ShapeDtypeStruct(embed_weight.shape, BF16),
        ],
        "hhh",
        [pltpu.SemaphoreType.DMA((3,))],
    )(chunks[0], mods, embed_weight)
    near[1], own, level_rows, embed_held = lax.optimization_barrier(
        (near[1], own, level_rows, embed_held)
    )
    far = [swapped(piece, "cfg", 1) for piece in near]
    shares = lax.all_to_all(copies, ("scene", "queue", "tok"), 0, 0)
    other_shares = swapped(shares, "cfg", 1)

    following = lax.ppermute(first, "queue", [(i + 1, i) for i in range(queues - 1)])
    near[-1], following, shares, *far[:-1] = lax.optimization_barrier(
        (near[-1], following, shares, *far[:-1])
    )
    part = kernel_call(
        functools.partial(side_kernel, group),
        jax.ShapeDtypeStruct((local_rows, queues * group), BF16),
        "v" * queues,
    )(own, *near[1:])
    part_tok, part_scene = swapped(part, "tok", 1), swapped(part, "scene", 1)

    lhs, xin, rstd, masks = kernel_call(
        functools.partial(prepare_kernel, frames, values, span),
        [
            jax.ShapeDtypeStruct((scenes * all_frames * rows, width), BF16),
            jax.ShapeDtypeStruct((all_frames, scenes * rows, lanes), BF16),
            jax.ShapeDtypeStruct((all_frames, 1, lanes), F32),
            jax.ShapeDtypeStruct((scenes, all_frames, rows - values, LANES), F32),
        ],
        "vvvv",
        bytes_accessed=8_000_000,
    )(shares, other_shares, level_rows, embed_held)
    attended = kernel_call(
        functools.partial(attend_kernel, frames, tokens, queues),
        jax.ShapeDtypeStruct((chips, head_dim, row_lanes), BF16),
        "v" * (2 * queues + 6),
        [
            pltpu.VMEM((width, 3 * head_dim), BF16),
            pltpu.VMEM((all_frames + 2 * window, 3 * head_dim, lanes), F32),
            pltpu.VMEM((all_frames + 2 * window, 1, lanes), F32),
            pltpu.VMEM((all_frames + 2 * window, 1, lanes), F32),
            pltpu.VMEM((all_frames, scenes, head_dim, LANES), F32),
        ],
        bytes_accessed=100_000_000,
    )(own, *near[1:], *far, lhs, xin, rstd, masks, query_gain[None], key_gain[None])
    attended, part, part_tok, part_scene = lax.optimization_barrier(
        (attended, part, part_tok, part_scene)
    )
    received = lax.all_to_all(attended, ("tok", "queue", "scene"), 0, 0)
    cut = -(-local_rows // 32) * 16
    upper = swapped(part_tok[:cut], "scene", 1)
    lower = swapped(part_scene[cut:], "tok", 1)
    half = values // 2
    half_shape = jax.ShapeDtypeStruct((half, row_lanes), F32)
    smalls = (
        packed,
        following,
        cond_embed,
        mods,
        embed_weight,
        final_gain[None],
        final_weight.T,
        fresh_noise,
    )
    places = [
        pltpu.VMEM(a.shape[1:] if i == 3 else a.shape, a.dtype) for i, a in enumerate(smalls)
    ]
    terms = values + 16 + 3 * levels_all + 16
    both, *rest = kernel_call(
        functools.partial(ready_kernel, values, half),
        [
            jax.ShapeDtypeStruct((terms + values, width + row_lanes), BF16),
            half_shape,
            half_shape,
            jax.ShapeDtypeStruct(fresh_noise.shape, F32),
            jax.ShapeDtypeStruct((8, LANES), F32),
        ],
        "ha" + "h" * 6 + "ss",
        places + [pltpu.SemaphoreType.DMA((len(smalls),))],
    )(*smalls, guide_table, guide_index)
    upper, lower, both = lax.optimization_barrier((upper, lower, both))
    away = [part, part_tok, part_scene, upper, lower]
    away_far = [swapped(piece, "cfg", 1) for piece in away]

    mine, send = kernel_call(
        functools.partial(finish_kernel, half, values, queues),
        [half_shape] * 2,
        "v" * 12,
        [pltpu.VMEM((values, row_lanes), F32), pltpu.VMEM((width, row_lanes), F32)],
        bytes_accessed=8_000_000,
    )(*away, *away_far, received, both)
    partner = swapped(send, "cfg", 1)
    shape = jax.ShapeDtypeStruct((frames, half, tokens), F32)
    return kernel_call(update_kernel, [shape, shape], "v" * 6)(mine, partner, *rest)


def on_device(*args):
    latents, qkv_weight, query_gain = args[0], args[7], args[8]
    local_heads = qkv_weight.shape[2] // query_gain.shape[0]
    scenes, queues, toks, cores = (lax.axis_size(a) for a in ("scene", "queue", "tok", "cfg"))
    pairs = scenes == toks == cores == 2 and queues & (queues - 1) == 0
    fits = latents.shape[2] * toks <= LANES and latents.shape[0] % cores == 0
    if pairs and fits and local_heads == scenes * queues:
        return tuple(on_device_heads(*args))
    return on_device_general(*args)


def solution(mesh):
    placed = (
        P(("scene", "queue"), None, "tok"),
        P(("scene", "cfg"), "tok"),
        P(("scene", "queue")),
        P(("scene", "queue"), None),
        P(("scene", "cfg"), None),
        P(),
        P(),
        P(("queue", "cfg"), None, "tok"),
        P(),
        P(),
        P("tok", ("queue", "cfg")),
        P(),
        P(),
        P(),
        P(),
    )
    return jax.shard_map(
        on_device,
        mesh=mesh,
        in_specs=placed,
        out_specs=(P(("scene", "queue"), "cfg", "tok"), P(("scene", "queue"), "cfg", "tok")),
        check_vma=False,
    )
```
